32 devices in a mesh: seq: 4 (over y, x), fsdp: 8 (over z, core).
Axes of the slice: x: 2, y: 2, z: 4, core: 2. Of those that a mesh axis runs over, the one named last changes fastest.
Arguments:
- hidden: bfloat16 [8, 1024, 1024], P('fsdp', 'seq'), may hold values from -6 to 6
- lengths: int32 [8], P('fsdp'), may hold values from 1 to 1024, 5120 in all
- expert_ids: int32 [8, 1024, 1], P('fsdp', 'seq'), may hold values from 0 to 15; in each aligned block of 256 rows (0 to 255, 256 to 511, ..., all dimensions but the last counted through in order) at most 32 rows name the same one
- attn_gain: bfloat16 [1024], P(('seq', 'fsdp')), may hold values from 0.5 to 1.5
- qkv_weight: bfloat16 [1024, 3072], P(('seq', 'fsdp')), may hold values from -0.1875 to 0.1875
- out_weight: bfloat16 [1024, 1024], P(('seq', 'fsdp')), may hold values from -2 to 2
- moe_gain: bfloat16 [1024], P(('seq', 'fsdp')), may hold values from 0.5 to 1.5
- router_weight: bfloat16 [1024, 16], P(('seq', 'fsdp')), may hold values from -0.09375 to 0.09375
- expert_in: bfloat16 [16, 1024, 4096], P('fsdp', None, 'seq'), may hold values from -0.1875 to 0.1875
- expert_out: bfloat16 [16, 4096, 1024], P('fsdp', 'seq'), may hold values from -12 to 12
- out_grad: bfloat16 [8, 1024, 1024], P('fsdp', 'seq'), may hold values from -6 to 6
Outputs:
- output: bfloat16 [8, 1024, 1024], P('fsdp', 'seq')
- input_grad: float32 [8, 1024, 1024], P('fsdp', 'seq')
- attn_gain_grad: float32 [1024], P(('seq', 'fsdp'))
- qkv_grad: float32 [1024, 3072], P(('seq', 'fsdp'))
- out_weight_grad: float32 [1024, 1024], P(('seq', 'fsdp'))
- moe_gain_grad: float32 [1024], P(('seq', 'fsdp'))
- router_grad: float32 [1024, 16], P(('seq', 'fsdp'))
- expert_in_grad: float32 [16, 1024, 4096], P('fsdp', None, 'seq')
- expert_out_grad: float32 [16, 4096, 1024], P('fsdp', 'seq')
The draws below stay inside these ranges and needn't reach their ends.
Inputs may be any that keep to these rules, and one draw needn't show every extreme that they name: `lengths`: the longest slot holds exactly 1024 valid positions. `expert_ids`: in each aligned block of 256 tokens (the tokens of one device, slots first, then positions), no expert is named more than 32 times, and in some block one expert is named exactly 32 times.
All inputs are finite; a program needn't handle non-finite values. No bound on the sum of `lengths` on one device may be relied on, other than what follows from the above.
Results may differ from the reference program's by a relative error of at most 0.017.
Values may be sent and summed in bfloat16 or wider, within the bound.
A program may use at most 192 MiB of HBM per device.

```python
import math
import jax
import jax.numpy as jnp
import numpy as np
from jax import lax

D = 1024
HEADS = 16
HEAD_DIM = 64
FF = 4096
LEN = 1024
EXPERTS = 16
SLOTS = 8
TOK_DEV = 256
CAP = 32
QBLOCK = 512


def block_scale(stream_key, extent, shards, smallest, top_value):
    level, own = 1.0, jax.random.fold_in(stream_key, 6)
    for dim, parts in shards:
        draws = jnp.exp(jax.random.uniform(jax.random.fold_in(own, dim), (parts,), jnp.float32, smallest / len(shards), top_value / len(shards)))
        level = level * jnp.repeat(draws, extent[dim] // parts).reshape([-1 if axis == dim else 1 for axis in range(len(extent))])
    return level


def split_up(amount, total, reach, lean):
    weights = [(1 << 20) // math.isqrt(rank ** lean) + 1 for rank in range(2, amount + 1)]
    surplus, given = total - reach - (amount - 1), [1] * (amount - 1)
    while surplus > 0:
        free = [i for i in range(amount - 1) if given[i] < reach]
        whole, remaining = sum([weights[i] for i in free]), surplus
        for i in free:
            more = min(reach - given[i], max(1, remaining * weights[i] // whole), surplus)
            given[i] = given[i] + more
            surplus = surplus - more
    return np.array([reach] + given)


def ragged(rng, amount, total, most, lean):
    if amount == 2:
        one = jax.random.randint(rng, (), max(1, total - most), min(most, total - 1) + 1)
        return jnp.stack([one, total - one])
    tallies = jnp.asarray(split_up(amount, total, most, lean), jnp.int32)
    twos = (amount - 1) // 2
    donor, sink = tallies[1:1 + 2 * twos:2], tallies[2:2 + 2 * twos:2]
    slack = jnp.minimum(donor - 1, most - sink)
    moved = jax.random.randint(jax.random.fold_in(rng, 1), (twos,), 0, 1 << 20) % (slack + 1)
    tallies = tallies.at[1:1 + 2 * twos:2].set(donor - moved).at[2:2 + 2 * twos:2].set(sink + moved)
    return tallies[jax.random.permutation(jax.random.fold_in(rng, 2), amount)]


def deal_out(stream_key, own, number, rows, count, top, reach, lean):
    sequence = jax.random.permutation(stream_key, count)
    packed, common = shares(count, rows * top, reach, lean, True), shares(count, rows * top, reach, lean, False)
    places = jnp.arange(count)

    def named(sizes, rotation):
        used = int((sizes > 0).sum())
        fixed = max(1, used // 4)
        moved = fixed + (places - fixed + rotation * (used - fixed)) % max(1, count - fixed)
        return jnp.zeros((count,), jnp.int32).at[sequence[jnp.where(places < fixed, places, moved)]].set(jnp.asarray(sizes, jnp.int32))

    sizes = jnp.where(number % 4 == 0, named(packed, number // 4), named(common, number - number // 4 - 1))
    mixed = jax.random.permutation(jax.random.fold_in(own, 3), count)
    giver, sink = mixed[0:count // 2 * 2:2], mixed[1:count // 2 * 2:2]
    slack = jnp.minimum(sizes[giver] - 1, reach - sizes[sink]) // 2
    slack = jnp.where((giver == sequence[0]) | (sink == sequence[0]) | (sizes[sink] == 0), 0, jnp.maximum(slack, 0))
    moved = jax.random.randint(jax.random.fold_in(own, 4), (count // 2,), 0, 1 << 20) % (slack + 1)
    sizes = sizes.at[giver].add(-moved).at[sink].add(moved)
    items = jnp.searchsorted(jnp.cumsum(sizes), jnp.arange(rows * top), side="right").astype(jnp.int32)
    table = items.reshape(top, rows).T
    table = table[jax.random.permutation(jax.random.fold_in(own, 1), rows)]
    rotation = jax.random.randint(jax.random.fold_in(own, 2), (rows, 1), 0, top)
    return jnp.take_along_axis(table, (jnp.arange(top)[None, :] + rotation) % top, axis=1)


def shares(count, total, most, slope, full):
    loads = [(1 << 20) // math.isqrt(standing ** slope) + 1 for standing in range(1, count + 1)]
    largest = most if full else min(most, max(-(-total // count), total * loads[0] // sum(loads)))
    least = 1 if total - largest >= count - 1 else 0
    given, spare = [largest] + [least] * (count - 1), total - largest - least * (count - 1)
    while spare > 0:
        free = [i for i in range(1, count) if given[i] < largest] or [i for i in range(1, count) if given[i] < most]
        pool, budget = sum([loads[i] for i in free]), spare
        for i in free:
            more = min(most - given[i], max(1, budget * loads[i] // pool), spare)
            given[i] = given[i] + more
            spare = spare - more
    return np.array(given)


def noise(rng, shape, scale, limit, pieces=(), kind=jnp.bfloat16):
    level = block_scale(rng, shape, pieces, -0.22, 0.18) if pieces else 1.0
    array = jax.random.normal(rng, shape, jnp.float32) * scale * level
    return jnp.minimum(jnp.maximum(array, -limit), limit).astype(kind)


def setup_inputs(seed: int = 0) -> dict:
    key_list = jax.random.split(jax.random.key(seed), 12)
    hidden = noise(key_list[0], (SLOTS, LEN, D), 1.0, 6.0, ((0, 8), (1, 4)))
    lengths = ragged(key_list[1], SLOTS, SLOTS * LEN * 5 // 8, LEN, 0).astype(jnp.int32)
    expert_ids_keys = jax.random.split(jax.random.fold_in(key_list[2], 1), SLOTS * LEN // TOK_DEV)
    expert_ids_turns = jax.random.permutation(jax.random.fold_in(key_list[2], 3), SLOTS * LEN // TOK_DEV)
    expert_ids = jax.vmap(lambda own, number: deal_out(jax.random.fold_in(key_list[2], 2), own, number, TOK_DEV, EXPERTS, 1, CAP, 2))(expert_ids_keys, expert_ids_turns).reshape((SLOTS, LEN, 1))
    attn_gain = jnp.clip(1.0 + 0.1 * jax.random.normal(key_list[3], (D,), jnp.float32), 0.5, 1.5).astype(jnp.bfloat16)
    qkv_weight = noise(key_list[4], (D, 3 * D), D ** -0.5, 0.1875, ((0, 32),))
    out_weight = noise(key_list[5], (D, D), (max(D * 8 // LEN, 1)) ** -0.5, 2.0, ((0, 32),))
    moe_gain = jnp.clip(1.0 + 0.1 * jax.random.normal(key_list[6], (D,), jnp.float32), 0.5, 1.5).astype(jnp.bfloat16)
    router_weight = noise(key_list[7], (D, EXPERTS), (4 * D) ** -0.5, 0.09375, ((0, 32),))
    expert_in = noise(key_list[8], (EXPERTS, D, FF), D ** -0.5, 0.1875, ((0, 8), (2, 4)))
    expert_out = noise(key_list[9], (EXPERTS, FF, D), (2 + 8 // (FF // 128)), 12.0, ((0, 8), (1, 4)))
    out_grad = noise(key_list[10], (SLOTS, LEN, D), 1.0, 6.0, ((0, 8), (1, 4)))
    return dict(hidden=hidden, lengths=lengths, expert_ids=expert_ids, attn_gain=attn_gain, qkv_weight=qkv_weight, out_weight=out_weight, moe_gain=moe_gain, router_weight=router_weight, expert_in=expert_in, expert_out=expert_out, out_grad=out_grad)


@jax.custom_vjp
def low(v):
    return lax.optimization_barrier(v.astype(jnp.bfloat16)).astype(jnp.float32)

@jax.custom_vjp
def low_back(v):
    return v

def low_keep(v):
    return (low(v), None)

def low_pass(kept, grad):
    return (grad,)

def back_keep(v):
    return (v, None)

def back_low(kept, grad):
    return (low(grad),)
low.defvjp(low_keep, low_pass)
low_back.defvjp(back_keep, back_low)
EPS = 1e-05
MASKED = -1e+30

def scaled_norm(value, gain):
    return value * lax.rsqrt(lax.optimization_barrier(jnp.mean(value * value, axis=-1, keepdims=True)) + EPS) * gain

def matmul(left, right):
    return jnp.dot(left, right, precision=lax.Precision.HIGHEST, preferred_element_type=jnp.float32)

def attend_slot(qkv_slot, length):
    query = qkv_slot[:, 0].reshape(LEN, HEADS, HEAD_DIM)
    keys = qkv_slot[:, 1].reshape(LEN, HEADS, HEAD_DIM)
    values = qkv_slot[:, 2].reshape(LEN, HEADS, HEAD_DIM)
    scale = HEAD_DIM ** (-0.5)
    columns = jnp.arange(LEN, dtype=jnp.int32)

    def one_block(start):
        block_query = lax.dynamic_slice_in_dim(query, start, QBLOCK, 0)
        scores = jnp.einsum('qhd,khd->hqk', block_query, keys, precision=lax.Precision.HIGHEST) * scale
        scores = low_back(scores)
        rows = start + jnp.arange(QBLOCK, dtype=jnp.int32)
        keep = (columns[None, :] <= rows[:, None]) & (columns[None, :] < length)
        scores = jnp.where(keep[None], scores, MASKED)
        probs = low(jax.nn.softmax(scores, axis=-1))
        return jnp.einsum('hqk,khd->qhd', probs, values, precision=lax.Precision.HIGHEST)
    starts = jnp.arange(LEN // QBLOCK, dtype=jnp.int32) * QBLOCK
    blocks = lax.map(jax.checkpoint(one_block), starts)
    return blocks.reshape(LEN, D)

def run_experts(rows_in, chosen, choose, expert_in, expert_out):
    count = chosen.shape[0]
    blocks = count // TOK_DEV
    counts = choose.astype(jnp.int32).reshape(blocks, TOK_DEV, EXPERTS)
    ranks = (lax.optimization_barrier(jnp.sum(jnp.cumsum(counts, axis=1) * counts, axis=-1)).reshape(count) - 1).astype(jnp.int32)
    block_of = (jnp.arange(count, dtype=jnp.int32) // TOK_DEV).astype(jnp.int32)
    slot = (block_of * CAP + ranks).astype(jnp.int32)
    width_slots = blocks * CAP
    token_index = jnp.arange(count, dtype=jnp.int32)

    def one_expert(carry, item):
        number, weight_in, weight_out = item
        place = jnp.where(chosen == number, slot, width_slots).astype(jnp.int32)
        index = jnp.full((width_slots,), count, jnp.int32).at[place].set(token_index, mode='drop')
        rows = low_back(jnp.take(rows_in, index, axis=0, mode='fill', fill_value=0.0))
        inner = low_back(matmul(rows, weight_in))
        active = low(jax.nn.gelu(inner, approximate=True))
        return (carry, low_back(low(matmul(active, weight_out))))
    numbers = jnp.arange(EXPERTS, dtype=jnp.int32)
    _, outputs = lax.scan(jax.checkpoint(one_expert), None, (numbers, expert_in, expert_out))
    return outputs[chosen, slot]

def forward(hidden, attn_gain, qkv_weight, out_weight, moe_gain, router_weight, expert_in, expert_out, lengths, expert_ids):
    positions = jnp.arange(LEN, dtype=jnp.int32)
    valid = (positions[None, :] < lengths[:, None]).astype(hidden.dtype)[..., None]
    flat = hidden.reshape(SLOTS * LEN, D)
    normed = low(scaled_norm(flat, attn_gain))
    qkv = low_back(low(matmul(normed, qkv_weight))).reshape(SLOTS, LEN, 3, D)

    def slot_step(carry, item):
        return (carry, attend_slot(item[0], item[1]))
    _, mixed = lax.scan(jax.checkpoint(slot_step), None, (qkv, lengths))
    mixed = low_back(low(mixed.reshape(SLOTS * LEN, D)))
    middle = flat + low_back(matmul(mixed, out_weight))
    normed_two = low(scaled_norm(middle, moe_gain))
    logits = low_back(matmul(normed_two, router_weight))
    probs = jax.nn.softmax(logits, axis=-1)
    chosen = expert_ids.reshape(SLOTS * LEN).astype(jnp.int32)
    choose = chosen[:, None] == jnp.arange(EXPERTS, dtype=jnp.int32)[None, :]
    gate = lax.optimization_barrier(jnp.sum(jnp.where(choose, probs, 0.0), axis=-1))
    returned = run_experts(normed_two, chosen, choose, expert_in, expert_out)
    result = middle + gate[:, None] * returned
    return valid * result.reshape(SLOTS, LEN, D)

def reference(hidden, lengths, expert_ids, attn_gain, qkv_weight, out_weight, moe_gain, router_weight, expert_in, expert_out, out_grad):
    floats = (hidden.astype(jnp.float32), attn_gain.astype(jnp.float32), qkv_weight.astype(jnp.float32), out_weight.astype(jnp.float32), moe_gain.astype(jnp.float32), router_weight.astype(jnp.float32), expert_in.astype(jnp.float32), expert_out.astype(jnp.float32))

    def wrapped(*values):
        return forward(*values, lengths, expert_ids)
    result, pullback = jax.vjp(wrapped, *floats)
    grads = pullback(out_grad.astype(jnp.float32))
    return (result.astype(jnp.bfloat16), grads[0], grads[1], grads[2], grads[3], grads[4], grads[5], grads[6], grads[7])
```

```python
import jax
import jax.numpy as jnp
from jax import lax
from jax.sharding import PartitionSpec as P

HEAD_DIM = 64
QBLOCK = 512


EPS = 1e-05
MASKED = -1e30


def scaled_norm(value, gain):
    return value * lax.rsqrt(jnp.mean(value * value, axis=-1, keepdims=True) + EPS) * gain


def gelu_tanh(value):
    return jax.nn.gelu(value, approximate=True)


def times_transposed(left, right):
    return lax.dot_general(
        left, right, (((1,), (1,)), ((), ())), preferred_element_type=jnp.float32
    )


def transposed_times(left, right):
    return lax.dot_general(
        left, right, (((0,), (0,)), ((), ())), preferred_element_type=jnp.float32
    )


def to_heads(value):
    return lax.all_to_all(value, "seq", split_axis=2, concat_axis=0, tiled=True)


def to_tokens(value):
    return lax.all_to_all(value, "seq", split_axis=0, concat_axis=2, tiled=True)


def to_owners(value):
    return lax.all_to_all(value, "fsdp", split_axis=0, concat_axis=0, tiled=True)


def to_sources(value):
    return lax.all_to_all(value, "fsdp", split_axis=0, concat_axis=0, tiled=True)


def spread_rows(value):
    return lax.all_gather(value, "seq", axis=2, tiled=True)


def collect_rows(value):
    return lax.psum_scatter(value, "seq", scatter_dimension=2, tiled=True)


def masked_scores(block_query, keys, start, length, scale):
    scores = (
        jnp.einsum("qhd,khd->hqk", block_query, keys, preferred_element_type=jnp.float32) * scale
    )
    rows = start + jnp.arange(block_query.shape[0], dtype=jnp.int32)
    columns = jnp.arange(keys.shape[0], dtype=jnp.int32)
    keep = (columns[None, :] <= rows[:, None]) & (columns[None, :] < length)
    return jnp.where(keep[None], scores, MASKED)


def shards(
    hidden,
    lengths,
    expert_ids,
    attn_gain,
    qkv_weight,
    out_weight,
    moe_gain,
    router_weight,
    expert_in,
    expert_out,
    out_grad,
):
    seq_count = lax.axis_size("seq")
    seq_place = lax.axis_index("seq")
    tokens = hidden.shape[1]
    width = hidden.shape[2]
    full_len = tokens * seq_count
    gain_one, weight_qkv, weight_mix, gain_two, weight_route = (
        lax.all_gather(attn_gain, ("seq", "fsdp"), axis=0, tiled=True),
        lax.all_gather(qkv_weight, ("seq", "fsdp"), axis=0, tiled=True),
        lax.all_gather(out_weight, ("seq", "fsdp"), axis=0, tiled=True),
        lax.all_gather(moe_gain, ("seq", "fsdp"), axis=0, tiled=True),
        lax.all_gather(router_weight, ("seq", "fsdp"), axis=0, tiled=True),
    )
    experts_all = weight_route.shape[1]
    expert_local = expert_in.shape[0]
    owners = experts_all // expert_local
    capacity = max(2, 2 * tokens // experts_all)
    heads_local = width // seq_count // HEAD_DIM
    group_width = width // seq_count
    scale = HEAD_DIM ** (-0.5)
    length = lengths[0]
    position = seq_place * tokens + jnp.arange(tokens, dtype=jnp.int32)
    valid = (position < length).astype(jnp.float32)[:, None]
    inputs = hidden[0].astype(jnp.float32)
    normed, norm_back = jax.vjp(scaled_norm, inputs, gain_one.astype(jnp.float32))
    normed = normed.astype(jnp.bfloat16)
    projected = jnp.dot(normed, weight_qkv, preferred_element_type=jnp.float32).astype(jnp.bfloat16)
    grouped = to_heads(projected.reshape(tokens, 3, width))
    query = grouped[:, 0].reshape(full_len, heads_local, HEAD_DIM)
    keys = grouped[:, 1].reshape(full_len, heads_local, HEAD_DIM)
    values = grouped[:, 2].reshape(full_len, heads_local, HEAD_DIM)
    starts = list(range(0, full_len, QBLOCK))
    outputs = []
    totals = []
    for start in starts:
        reach = full_len
        block_query = query[start : start + QBLOCK]
        scores = masked_scores(block_query, keys, start, length, scale)
        top = jnp.max(scores, axis=-1, keepdims=True)
        total = top + jnp.log(jnp.sum(jnp.exp(scores - top), axis=-1, keepdims=True))
        probs = jnp.exp(scores - total).astype(jnp.bfloat16)
        block_out = jnp.einsum("hqk,khd->qhd", probs, values, preferred_element_type=jnp.float32)
        outputs.append(block_out.astype(jnp.bfloat16))
        totals.append(total)
    attended = jnp.concatenate(outputs, axis=0).reshape(full_len, 1, group_width)
    mixed = to_tokens(attended).reshape(tokens, width)
    middle = inputs + jnp.dot(mixed, weight_mix, preferred_element_type=jnp.float32)
    normed_two, norm_two_back = jax.vjp(scaled_norm, middle, gain_two.astype(jnp.float32))
    normed_two = normed_two.astype(jnp.bfloat16)
    logits = jnp.dot(normed_two, weight_route, preferred_element_type=jnp.float32)
    chosen = expert_ids[0, :, 0]
    choose = chosen[:, None] == jnp.arange(experts_all, dtype=jnp.int32)[None, :]

    def gate_of(logit_rows):
        return jnp.sum(jnp.where(choose, jax.nn.softmax(logit_rows, axis=-1), 0.0), axis=-1)

    gate, gate_back = jax.vjp(gate_of, logits)
    order = jnp.arange(tokens, dtype=jnp.int32)
    earlier = (order[None, :] < order[:, None]) & (chosen[None, :] == chosen[:, None])
    ranks = jnp.sum(earlier.astype(jnp.int32), axis=1)
    slot = chosen * capacity + ranks
    dispatch = (
        jnp.arange(experts_all * capacity, dtype=jnp.int32)[:, None] == slot[None, :]
    ).astype(jnp.bfloat16)
    sent = jnp.dot(dispatch, normed_two, preferred_element_type=jnp.float32).astype(jnp.bfloat16)
    arrived = to_owners(sent.reshape(owners, expert_local, capacity, width))
    rows_all = spread_rows(arrived)
    weight_in, weight_out = (expert_in, expert_out)
    inner = jnp.einsum("sjcd,jdf->sjcf", rows_all, weight_in, preferred_element_type=jnp.float32)
    active, active_back = jax.vjp(gelu_tanh, inner)
    active = active.astype(jnp.bfloat16)
    partial_out = jnp.einsum(
        "sjcf,jfd->sjcd", active, weight_out, preferred_element_type=jnp.float32
    )
    produced = collect_rows(partial_out)
    returned = to_sources(produced.astype(jnp.bfloat16)).reshape(experts_all * capacity, width)
    back_rows = jnp.einsum("st,sd->td", dispatch, returned, preferred_element_type=jnp.float32)
    output = valid * (middle + gate[:, None] * back_rows)
    upstream = out_grad[0].astype(jnp.float32) * valid
    grad_returned = (upstream * gate[:, None]).astype(jnp.bfloat16)
    grad_gate = jnp.sum(upstream * back_rows, axis=1)
    grad_logits = gate_back(grad_gate)[0].astype(jnp.bfloat16)
    grad_route = transposed_times(normed_two, grad_logits)
    grad_normed_two = times_transposed(grad_logits, weight_route)
    grad_sent = jnp.dot(dispatch, grad_returned, preferred_element_type=jnp.float32).astype(
        jnp.bfloat16
    )
    grad_arrived = to_owners(grad_sent.reshape(owners, expert_local, capacity, width))
    grad_rows = spread_rows(grad_arrived)
    grad_active = jnp.einsum(
        "sjcd,jfd->sjcf", grad_rows, weight_out, preferred_element_type=jnp.float32
    )
    grad_weight_out = jnp.einsum(
        "sjcf,sjcd->jfd", active, grad_rows, preferred_element_type=jnp.float32
    )
    grad_inner = active_back(grad_active)[0].astype(jnp.bfloat16)
    grad_weight_in = jnp.einsum(
        "sjcd,sjcf->jdf", rows_all, grad_inner, preferred_element_type=jnp.float32
    )
    grad_rows_in = jnp.einsum(
        "sjcf,jdf->sjcd", grad_inner, weight_in, preferred_element_type=jnp.float32
    )
    grad_input_rows = collect_rows(grad_rows_in)
    expert_in_grad, expert_out_grad = (grad_weight_in, grad_weight_out)
    grad_back_rows = to_sources(grad_input_rows.astype(jnp.bfloat16)).reshape(
        experts_all * capacity, width
    )
    grad_normed_two = grad_normed_two + jnp.einsum(
        "st,sd->td", dispatch, grad_back_rows, preferred_element_type=jnp.float32
    )
    grad_middle, grad_gain_two = norm_two_back(grad_normed_two)
    grad_middle = grad_middle + upstream
    grad_attn = grad_middle.astype(jnp.bfloat16)
    grad_mix = transposed_times(mixed, grad_attn)
    grad_mixed = times_transposed(grad_attn, weight_mix).astype(jnp.bfloat16)
    grad_heads = to_heads(grad_mixed.reshape(tokens, 1, width)).reshape(
        full_len, heads_local, HEAD_DIM
    )
    grad_query = []
    grad_keys = jnp.zeros((full_len, heads_local, HEAD_DIM), jnp.float32)
    grad_values = jnp.zeros((full_len, heads_local, HEAD_DIM), jnp.float32)
    for number, start in enumerate(starts):
        reach = full_len
        block_query = query[start : start + QBLOCK]
        scores = masked_scores(block_query, keys, start, length, scale)
        probs = jnp.exp(scores - totals[number])
        probs_low = probs.astype(jnp.bfloat16)
        grad_out = grad_heads[start : start + QBLOCK]
        grad_values = grad_values.at[:reach].add(
            jnp.einsum("hqk,qhd->khd", probs_low, grad_out, preferred_element_type=jnp.float32)
        )
        grad_probs = jnp.einsum(
            "qhd,khd->hqk", grad_out, values, preferred_element_type=jnp.float32
        )
        grad_scores = (
            probs * (grad_probs - jnp.sum(grad_probs * probs, axis=-1, keepdims=True))
        ).astype(jnp.bfloat16)
        grad_query.append(
            jnp.einsum("hqk,khd->qhd", grad_scores, keys, preferred_element_type=jnp.float32)
            * scale
        )
        grad_keys = grad_keys.at[:reach].add(
            jnp.einsum("hqk,qhd->khd", grad_scores, block_query, preferred_element_type=jnp.float32)
            * scale
        )
    grad_grouped = jnp.stack([jnp.concatenate(grad_query, axis=0), grad_keys, grad_values], axis=1)
    grad_grouped = grad_grouped.astype(jnp.bfloat16).reshape(full_len, 3, group_width)
    grad_projected = to_tokens(grad_grouped).reshape(tokens, 3 * width)
    grad_qkv_weight = transposed_times(normed, grad_projected)
    grad_normed = times_transposed(grad_projected, weight_qkv)
    grad_inputs, grad_gain_one = norm_back(grad_normed)
    grad_inputs = grad_inputs + grad_middle
    gain_one_grad, qkv_weight_grad, mix_grad, gain_two_grad, route_grad = (
        lax.psum_scatter(grad_gain_one, ("seq", "fsdp"), scatter_dimension=0, tiled=True),
        lax.psum_scatter(grad_qkv_weight, ("seq", "fsdp"), scatter_dimension=0, tiled=True),
        lax.psum_scatter(grad_mix, ("seq", "fsdp"), scatter_dimension=0, tiled=True),
        lax.psum_scatter(grad_gain_two, ("seq", "fsdp"), scatter_dimension=0, tiled=True),
        lax.psum_scatter(grad_route, ("seq", "fsdp"), scatter_dimension=0, tiled=True),
    )
    return (
        output.astype(jnp.bfloat16)[None],
        grad_inputs[None],
        gain_one_grad,
        qkv_weight_grad,
        mix_grad,
        gain_two_grad,
        route_grad,
        expert_in_grad,
        expert_out_grad,
    )


def solution(mesh):
    placed = (
        P("fsdp", "seq", None),
        P("fsdp"),
        P("fsdp", "seq", None),
        P(("seq", "fsdp")),
        P(("seq", "fsdp"), None),
        P(("seq", "fsdp"), None),
        P(("seq", "fsdp")),
        P(("seq", "fsdp"), None),
        P("fsdp", None, "seq"),
        P("fsdp", "seq", None),
        P("fsdp", "seq", None),
    )
    return jax.shard_map(
        shards,
        mesh=mesh,
        in_specs=placed,
        out_specs=(
            P("fsdp", "seq", None),
            P("fsdp", "seq", None),
            P(("seq", "fsdp")),
            P(("seq", "fsdp"), None),
            P(("seq", "fsdp"), None),
            P(("seq", "fsdp")),
            P(("seq", "fsdp"), None),
            P("fsdp", None, "seq"),
            P("fsdp", "seq", None),
        ),
        check_vma=False,
    )
```

```python
import functools

import jax
import jax.numpy as jnp
from jax import lax
from jax.experimental import pallas as pl
from jax.experimental.pallas import tpu as pltpu
from jax.sharding import PartitionSpec as P

HEAD_DIM = 64
QBLOCK = 512
EPS = 1e-05
MASKED = -1e30
MESH = pl.DeviceIdType.MESH
ANY = pl.BlockSpec(memory_space=pl.ANY)


def scaled_norm(value, gain):
    return value * lax.rsqrt(jnp.mean(value * value, axis=-1, keepdims=True) + EPS) * gain


def gelu_tanh(value):
    return jax.nn.gelu(value, approximate=True)


def times(left, right):
    return jnp.dot(left, right, preferred_element_type=jnp.float32)


def times_transposed(left, right):
    return lax.dot_general(
        left, right, (((1,), (1,)), ((), ())), preferred_element_type=jnp.float32
    )


def transposed_times(left, right):
    return lax.dot_general(
        left, right, (((0,), (0,)), ((), ())), preferred_element_type=jnp.float32
    )


def greet(axis, peers):
    barrier = pltpu.get_barrier_semaphore()
    for peer in peers:
        pl.semaphore_signal(barrier, inc=1, device_id={axis: peer}, device_id_type=MESH)
    pl.semaphore_wait(barrier, len(peers))


def remote(axis, peer, source, target, send, receive):
    copy = pltpu.make_async_remote_copy(
        source, target, send, receive, device_id={axis: peer}, device_id_type=MESH
    )
    copy.start()
    return copy


def call(kernel, inputs, outputs, scratch, number):
    return pl.pallas_call(
        kernel,
        out_shape=outputs,
        in_specs=[ANY] * len(inputs),
        out_specs=jax.tree.map(lambda _: ANY, outputs),
        scratch_shapes=scratch,
        compiler_params=pltpu.CompilerParams(
            collective_id=number, has_side_effects=True, vmem_limit_bytes=48 * 2**20
        ),
    )(*inputs)


def exchange_kernel(axis, count, views, *refs):
    arrays = len(views)
    sources, targets = refs[:arrays], refs[arrays : 2 * arrays]
    send, receive, local = refs[2 * arrays :]
    me = lax.axis_index(axis)
    peers = [lax.rem(me + step, count) for step in range(1, count)]
    greet(axis, peers)
    copies = []
    for step, peer in enumerate(peers):
        for a, (out_of, into) in enumerate(views):
            copies.append(
                remote(
                    axis,
                    peer,
                    out_of(sources[a], peer),
                    into(targets[a], me),
                    send.at[a, step],
                    receive.at[a, step],
                )
            )
    for a, (out_of, into) in enumerate(views):
        copy = pltpu.make_async_copy(out_of(sources[a], me), into(targets[a], me), local.at[a])
        copy.start()
        copies.append(copy)
    for copy in copies:
        copy.wait()


def exchange(axis, count, inputs, outputs, views, number):
    arrays = len(views)
    return call(
        functools.partial(exchange_kernel, axis, count, views),
        inputs,
        outputs,
        [
            pltpu.SemaphoreType.DMA((arrays, count - 1)),
            pltpu.SemaphoreType.DMA((arrays, count - 1)),
            pltpu.SemaphoreType.DMA((arrays,)),
        ],
        number,
    )


def lead(ref, place):
    return ref.at[place]


def second(ref, place):
    return ref.at[:, place]


def whole(ref, place):
    return ref


def spread_kernel(source, target, send, receive, local):
    me = lax.axis_index("seq")
    one, two, both = me ^ 1, me ^ 2, me ^ 3
    half = source.shape[1] // 2
    greet("seq", [one, two])
    parts = (pl.ds(0, half), pl.ds(half, half))
    own = pltpu.make_async_copy(source, target.at[:, me], local)
    own.start()
    copies = {}
    for side, peer in enumerate((one, two)):
        for order in range(2):
            part = (order + side) % 2
            copies[side, part] = remote(
                "seq",
                peer,
                source.at[:, parts[part]],
                target.at[:, me, parts[part]],
                send.at[side, part],
                receive.at[side, part],
            )
    relayed = []
    for side, (origin, peer) in enumerate(((one, two), (two, one))):
        copies[side, side].wait_recv()
        block = target.at[:, origin, parts[side]]
        relayed.append(remote("seq", peer, block, block, send.at[2, side], receive.at[2, side]))
    for side in range(2):
        copies[side, 1 - side].wait_recv()
        for part in range(2):
            copies[side, part].wait_send()
    for copy in relayed:
        copy.wait()
    own.wait()


def spread(source, number):
    return call(
        spread_kernel,
        (source,),
        jax.ShapeDtypeStruct((source.shape[0], 4, *source.shape[1:]), source.dtype),
        [
            pltpu.SemaphoreType.DMA((3, 2)),
            pltpu.SemaphoreType.DMA((3, 2)),
            pltpu.SemaphoreType.DMA,
        ],
        number,
    )


def columns_kernel(count, source, target, staged, send, receive, local, far_send, far_receive, near_send, near_receive):
    me, place = lax.axis_index("seq"), lax.axis_index("fsdp")
    barrier = pltpu.get_barrier_semaphore()
    others = [lax.rem(me + step, 4) for step in range(1, 4)]
    sibling = place ^ 1
    chips = count // 2
    chip, core = place // 2, lax.rem(place, 2)
    far = [lax.rem(chip + step, chips) * 2 + core for step in range(1, chips)]
    for other in others:
        pl.semaphore_signal(barrier, inc=1, device_id={"seq": other}, device_id_type=MESH)
    for other in [sibling, *far]:
        pl.semaphore_signal(barrier, inc=1, device_id={"fsdp": other}, device_id_type=MESH)
    pl.semaphore_wait(barrier, 3 + chips)
    copies = []
    for step, other in enumerate(others):
        copies.append(
            remote("seq", other, source.at[other], staged.at[me], send.at[step], receive.at[step])
        )
    own = pltpu.make_async_copy(source.at[me], staged.at[me], local.at[0])
    own.start()
    own.wait()
    for copy in copies:
        copy.wait()
    block = target.at[:, place]
    keep = pltpu.make_async_copy(staged, block, local.at[1])
    keep.start()
    away = [
        remote("fsdp", other, staged, block, far_send.at[step], far_receive.at[step])
        for step, other in enumerate(far)
    ]
    near = [remote("fsdp", sibling, staged, block, near_send.at[chips - 1], near_receive.at[chips - 1])]
    for step in range(1, chips):
        away[step - 1].wait_recv()
        origin = lax.rem(chip + chips - step, chips) * 2 + core
        arrived = target.at[:, origin]
        near.append(
            remote("fsdp", sibling, arrived, arrived, near_send.at[step - 1], near_receive.at[step - 1])
        )
    for copy in away:
        copy.wait_send()
    for copy in near:
        copy.wait()
    keep.wait()


def columns_of(weight, count, number):
    chips = count // 2
    dma = pltpu.SemaphoreType.DMA
    return call(
        functools.partial(columns_kernel, count),
        (weight,),
        jax.ShapeDtypeStruct((4, count, *weight.shape[1:]), weight.dtype),
        [
            pltpu.VMEM(weight.shape, weight.dtype),
            dma((3,)),
            dma((3,)),
            dma((2,)),
            dma((chips - 1,)),
            dma((chips - 1,)),
            dma((chips,)),
            dma((chips,)),
        ],
        number,
    )


def collect_kernel(source, target, mine, first, second_in, outgoing, load, send, receive, store):
    me = lax.axis_index("seq")
    one, two, both = me ^ 1, me ^ 2, me ^ 3
    width = source.shape[3] // 2
    greet("seq", [one, two])
    copies = []
    for side, (near, rest) in enumerate(((one, two), (two, one))):
        lanes = pl.ds(side * width, width)
        for order, block in enumerate((both, near)):
            copies.append(
                remote(
                    "seq",
                    near,
                    source.at[:, block, :, lanes],
                    first.at[side, order],
                    send.at[side, order],
                    receive.at[side, order],
                )
            )
        for order, block in enumerate((rest, me)):
            pltpu.make_async_copy(
                source.at[:, block, :, lanes], mine.at[side, order], load.at[side, order]
            ).start()
    passed = []
    for side, rest in enumerate((two, one)):
        copies[side * 2].wait_recv()
        pltpu.make_async_copy(mine.at[side, 0], mine.at[side, 0], load.at[side, 0]).wait()
        outgoing[side] = (
            mine[side, 0].astype(jnp.float32) + first[side, 0].astype(jnp.float32)
        ).astype(outgoing.dtype)
        passed.append(
            remote("seq", rest, outgoing.at[side], second_in.at[side], send.at[2, side], receive.at[2, side])
        )
    for side in range(2):
        copies[side * 2 + 1].wait_recv()
        pltpu.make_async_copy(mine.at[side, 1], mine.at[side, 1], load.at[side, 1]).wait()
        passed[side].wait_recv()
        mine[side, 1] = (
            mine[side, 1].astype(jnp.float32)
            + first[side, 1].astype(jnp.float32)
            + second_in[side].astype(jnp.float32)
        ).astype(mine.dtype)
        out = pltpu.make_async_copy(
            mine.at[side, 1], target.at[:, :, pl.ds(side * width, width)], store.at[side]
        )
        out.start()
    for side in range(2):
        pltpu.make_async_copy(
            mine.at[side, 1], target.at[:, :, pl.ds(side * width, width)], store.at[side]
        ).wait()
    for copy in copies + passed:
        copy.wait_send()


def collect(source, number):
    a, _, rows, width = source.shape
    dma = pltpu.SemaphoreType.DMA
    block = (a, rows, width // 2)
    return call(
        collect_kernel,
        (source,),
        jax.ShapeDtypeStruct((a, rows, width), source.dtype),
        [
            pltpu.VMEM((2, 2, *block), source.dtype),
            pltpu.VMEM((2, 2, *block), source.dtype),
            pltpu.VMEM((2, *block), source.dtype),
            pltpu.VMEM((2, *block), source.dtype),
            dma((2, 2)),
            dma((3, 2)),
            dma((3, 2)),
            dma((2,)),
        ],
        number,
    )


def masked_scores(block_query, keys, start, length, scale):
    scores = (
        jnp.einsum("qhd,khd->hqk", block_query, keys, preferred_element_type=jnp.float32) * scale
    )
    rows = start + jnp.arange(block_query.shape[0], dtype=jnp.int32)
    columns = jnp.arange(keys.shape[0], dtype=jnp.int32)
    keep = (columns[None, :] <= rows[:, None]) & (columns[None, :] < length)
    return jnp.where(keep[None], scores, MASKED)


def shards(
    hidden,
    lengths,
    expert_ids,
    attn_gain,
    qkv_weight,
    out_weight,
    moe_gain,
    router_weight,
    expert_in,
    expert_out,
    out_grad,
):
    S = jax.ShapeDtypeStruct
    low = jnp.bfloat16
    owners = lax.axis_size("fsdp")
    seq_place = lax.axis_index("seq")
    seq_count = lax.axis_size("seq")
    tokens, width = hidden.shape[1], hidden.shape[2]
    full_len = tokens * seq_count
    group_width = width // seq_count
    heads_local = group_width // HEAD_DIM
    rows_own = qkv_weight.shape[0]
    scale = HEAD_DIM ** (-0.5)
    length = lengths[0]
    experts_all = router_weight.shape[1]
    small = jnp.concatenate([router_weight, attn_gain[:, None], moe_gain[:, None]], axis=1)
    small = jnp.pad(small, ((0, 0), (0, -small.shape[1] % 128)))
    small = lax.all_gather(small, ("seq", "fsdp"), axis=0, tiled=True)
    weight_mix = lax.all_gather(out_weight, ("seq", "fsdp"), axis=0, tiled=True)
    weight_route = small[:, :experts_all]
    gain_one = small[:, experts_all].astype(jnp.float32)
    gain_two = small[:, experts_all + 1].astype(jnp.float32)
    mix_rows = lax.dynamic_slice_in_dim(weight_mix, seq_place * group_width, group_width, 0)

    expert_local = expert_in.shape[0]
    capacity = -(-max(2, 2 * tokens // experts_all) // 16) * 16
    slots = experts_all * capacity

    position = seq_place * tokens + jnp.arange(tokens, dtype=jnp.int32)
    valid = (position < length).astype(jnp.float32)[:, None]
    chosen = expert_ids[0, :, 0]
    choose = chosen[:, None] == jnp.arange(experts_all, dtype=jnp.int32)[None, :]
    order = jnp.arange(tokens, dtype=jnp.int32)
    earlier = (order[None, :] < order[:, None]) & (chosen[None, :] == chosen[:, None])
    ranks = jnp.sum(earlier.astype(jnp.int32), axis=1)
    slot = chosen * capacity + ranks
    hit = jnp.arange(slots, dtype=jnp.int32)[:, None] == slot[None, :]
    dispatch = hit.astype(low)

    def to_owners(rows, number):
        return exchange(
            "fsdp",
            owners,
            (rows.reshape(owners, expert_local, capacity, width),),
            (S((expert_local, owners, capacity, width), low),),
            ((lead, second),),
            number,
        )[0].reshape(expert_local, owners * capacity, width)

    def to_sources(rows, number):
        return exchange(
            "fsdp",
            owners,
            (rows.reshape(expert_local, owners, capacity, width),),
            (S((owners, expert_local, capacity, width), low),),
            ((second, lead),),
            number,
        )[0].reshape(slots, width)

    upstream_low = jnp.where(valid > 0, out_grad[0], 0).astype(low)
    upstream = upstream_low.astype(jnp.float32)
    up_rows = times(dispatch, upstream_low).astype(low)
    up_all = spread(to_owners(up_rows, 0), 1)

    weight_qkv = columns_of(
        qkv_weight.reshape(rows_own, 3, seq_count, group_width)
        .transpose(2, 0, 1, 3)
        .reshape(seq_count, rows_own, 3 * group_width),
        owners,
        2,
    ).reshape(width, 3 * group_width)
    hidden_all = spread(hidden, 3).reshape(full_len, width)

    normed = scaled_norm(hidden_all.astype(jnp.float32), gain_one).astype(low)
    projected = times(normed, weight_qkv).astype(low)
    query = projected[:, :group_width].reshape(full_len, heads_local, HEAD_DIM)
    keys = projected[:, group_width : 2 * group_width].reshape(full_len, heads_local, HEAD_DIM)
    values = projected[:, 2 * group_width :].reshape(full_len, heads_local, HEAD_DIM)
    starts = list(range(0, full_len, QBLOCK))
    outputs = []
    totals = []
    for start in starts:
        block_query = query[start : start + QBLOCK]
        reach = start + QBLOCK
        scores = masked_scores(block_query, keys[:reach], start, length, scale)
        top = jnp.max(scores, axis=-1, keepdims=True)
        total = top + jnp.log(jnp.sum(jnp.exp(scores - top), axis=-1, keepdims=True))
        probs = jnp.exp(scores - total).astype(low)
        block_out = jnp.einsum("hqk,khd->qhd", probs, values[:reach], preferred_element_type=jnp.float32)
        outputs.append(block_out.astype(low))
        totals.append(total)
    attended = jnp.concatenate(outputs, axis=0).reshape(full_len, group_width)
    mixed = exchange(
        "seq",
        seq_count,
        (attended.reshape(seq_count, tokens, group_width),),
        (S((seq_count, tokens, group_width), low),),
        ((lead, lead),),
        4,
    )[0]
    mixed = mixed.transpose(1, 0, 2).reshape(tokens, width)
    inputs = hidden[0].astype(jnp.float32)
    middle = inputs + times(mixed, weight_mix)
    normed_two, norm_two_back = jax.vjp(scaled_norm, middle, gain_two)
    normed_two = normed_two.astype(low)
    logits = times(normed_two, weight_route)

    def gate_of(logit_rows):
        return jnp.sum(jnp.where(choose, jax.nn.softmax(logit_rows, axis=-1), 0.0), axis=-1)

    gate, gate_back = jax.vjp(gate_of, logits)
    gate_rows = jnp.sum(jnp.where(hit, gate[None, :], 0.0), axis=1)
    gates = lax.all_to_all(
        gate_rows.reshape(owners, expert_local, capacity), "fsdp", split_axis=0, concat_axis=0, tiled=True
    )
    gates = lax.all_gather(gates, "seq", axis=0)
    gates = gates.transpose(2, 0, 1, 3).reshape(expert_local, seq_count * owners * capacity, 1)

    sent = times(dispatch, normed_two).astype(low)
    rows_all = spread(to_owners(sent, 5), 6)
    count = seq_count * owners * capacity
    rows_all = rows_all.reshape(expert_local, count, width)
    up_all = up_all.reshape(expert_local, count, width)
    grad_rows = (up_all.astype(jnp.float32) * gates).astype(low)

    def per_expert(form, left, right):
        return jnp.einsum(form, left, right, preferred_element_type=jnp.float32)

    inner = per_expert("jrd,jdf->jrf", rows_all, expert_in)
    active, active_back = jax.vjp(gelu_tanh, inner)
    active = active.astype(low)
    partial_out = per_expert("jrf,jfd->jrd", active, expert_out).astype(low)
    grad_active = per_expert("jrd,jfd->jrf", grad_rows, expert_out)
    grad_inner = active_back(grad_active)[0].astype(low)
    partial_back = per_expert("jrf,jdf->jrd", grad_inner, expert_in).astype(low)
    expert_out_grad = per_expert("jrf,jrd->jfd", active, grad_rows)
    expert_in_grad = per_expert("jrd,jrf->jdf", rows_all, grad_inner)

    shape = (expert_local, seq_count, owners * capacity, width)
    returned = to_sources(collect(partial_out.reshape(shape), 7), 8)
    grad_back = to_sources(collect(partial_back.reshape(shape), 9), 10)

    back_rows = transposed_times(dispatch, returned)
    output = valid * (middle + gate[:, None] * back_rows)
    grad_gate = jnp.sum(upstream * back_rows, axis=1)
    grad_logits = gate_back(grad_gate)[0].astype(low)
    grad_route = transposed_times(normed_two, grad_logits)
    grad_normed_two = times_transposed(grad_logits, weight_route) + transposed_times(dispatch, grad_back)
    grad_middle, grad_gain_two = norm_two_back(grad_normed_two)
    grad_middle = grad_middle + upstream
    grad_attn = grad_middle.astype(low)

    grad_attn_all = spread(grad_attn[None], 11).reshape(full_len, width)
    grad_mix = transposed_times(attended, grad_attn_all)
    grad_heads = times_transposed(grad_attn_all, mix_rows).astype(low)
    grad_heads = grad_heads.reshape(full_len, heads_local, HEAD_DIM)
    grad_query = []
    grad_keys = jnp.zeros((full_len, heads_local, HEAD_DIM), jnp.float32)
    grad_values = jnp.zeros((full_len, heads_local, HEAD_DIM), jnp.float32)
    for number, start in enumerate(starts):
        reach = start + QBLOCK
        block_query = query[start : start + QBLOCK]
        scores = masked_scores(block_query, keys[:reach], start, length, scale)
        probs = jnp.exp(scores - totals[number])
        probs_low = probs.astype(low)
        grad_out = grad_heads[start : start + QBLOCK]
        grad_values = grad_values.at[:reach].add(
            jnp.einsum("hqk,qhd->khd", probs_low, grad_out, preferred_element_type=jnp.float32)
        )
        grad_probs = jnp.einsum(
            "qhd,khd->hqk", grad_out, values[:reach], preferred_element_type=jnp.float32
        )
        grad_scores = (
            probs * (grad_probs - jnp.sum(grad_probs * probs, axis=-1, keepdims=True))
        ).astype(low)
        grad_query.append(
            jnp.einsum("hqk,khd->qhd", grad_scores, keys[:reach], preferred_element_type=jnp.float32)
            * scale
        )
        grad_keys = grad_keys.at[:reach].add(
            jnp.einsum("hqk,qhd->khd", grad_scores, block_query, preferred_element_type=jnp.float32)
            * scale
        )
    grad_projected = jnp.concatenate(
        [
            part.astype(low).reshape(full_len, group_width)
            for part in (jnp.concatenate(grad_query, axis=0), grad_keys, grad_values)
        ],
        axis=1,
    )
    grad_qkv_cols = transposed_times(normed, grad_projected).astype(low)
    partial_normed = times_transposed(grad_projected, weight_qkv).astype(low)
    grad_normed = collect(partial_normed.reshape(1, seq_count, tokens, width), 12)[0]

    qkv_parts, mix_parts = exchange(
        "fsdp",
        owners,
        (
            grad_qkv_cols.reshape(seq_count, owners, rows_own, 3 * group_width),
            grad_mix.astype(low).reshape(owners, rows_own, width),
        ),
        (
            S((owners, seq_count, rows_own, 3 * group_width), low),
            S((owners, rows_own, width), low),
        ),
        ((second, lead), (lead, lead)),
        13,
    )
    mix_grad = jnp.sum(mix_parts.astype(jnp.float32), axis=0)
    qkv_sum = jnp.sum(qkv_parts.astype(jnp.float32), axis=0)
    qkv_sum = exchange(
        "seq", seq_count, (qkv_sum,), (S(qkv_sum.shape, jnp.float32),), ((lead, lead),), 14
    )[0]
    qkv_weight_grad = (
        qkv_sum.reshape(seq_count, rows_own, 3, group_width)
        .transpose(1, 2, 0, 3)
        .reshape(rows_own, 3 * width)
    )
    _, norm_back = jax.vjp(scaled_norm, inputs, gain_one)
    grad_inputs, grad_gain_one = norm_back(grad_normed.astype(jnp.float32))
    grad_inputs = grad_inputs + grad_middle
    small_grad = jnp.concatenate(
        [grad_route, grad_gain_one[:, None], grad_gain_two[:, None]], axis=1
    )
    small_grad = jnp.pad(small_grad, ((0, 0), (0, -small_grad.shape[1] % 128)))
    small_grad = lax.psum_scatter(small_grad, ("seq", "fsdp"), scatter_dimension=0, tiled=True)
    return (
        output.astype(low)[None],
        grad_inputs[None],
        small_grad[:, experts_all],
        qkv_weight_grad,
        mix_grad,
        small_grad[:, experts_all + 1],
        small_grad[:, :experts_all],
        expert_in_grad,
        expert_out_grad,
    )


def solution(mesh):
    placed = (
        P("fsdp", "seq", None),
        P("fsdp"),
        P("fsdp", "seq", None),
        P(("seq", "fsdp")),
        P(("seq", "fsdp"), None),
        P(("seq", "fsdp"), None),
        P(("seq", "fsdp")),
        P(("seq", "fsdp"), None),
        P("fsdp", None, "seq"),
        P("fsdp", "seq", None),
        P("fsdp", "seq", None),
    )
    return jax.shard_map(
        shards,
        mesh=mesh,
        in_specs=placed,
        out_specs=(
            P("fsdp", "seq", None),
            P("fsdp", "seq", None),
            P(("seq", "fsdp")),
            P(("seq", "fsdp"), None),
            P(("seq", "fsdp"), None),
            P(("seq", "fsdp")),
            P(("seq", "fsdp"), None),
            P("fsdp", None, "seq"),
            P("fsdp", "seq", None),
        ),
        check_vma=False,
    )
```

```python
import functools

import jax
import jax.numpy as jnp
from jax import lax
from jax.experimental import pallas as pl
from jax.experimental.pallas import tpu as pltpu
from jax.sharding import PartitionSpec as P

HEAD_DIM = 64
QBLOCK = 512
EPS = 1e-05
MASKED = -1e30
ROOT = 0.7978845608028654
TILE = 256
GRAD = 256
MESH = pl.DeviceIdType.MESH
ANY = pl.BlockSpec(memory_space=pl.ANY)


def scaled_norm(value, gain):
    return value * lax.rsqrt(jnp.mean(value * value, axis=-1, keepdims=True) + EPS) * gain


def gelu_tanh(value):
    return jax.nn.gelu(value, approximate=True)


def times(left, right):
    return jnp.dot(left, right, preferred_element_type=jnp.float32)


def times_transposed(left, right):
    return lax.dot_general(
        left, right, (((1,), (1,)), ((), ())), preferred_element_type=jnp.float32
    )


def transposed_times(left, right):
    return lax.dot_general(
        left, right, (((0,), (0,)), ((), ())), preferred_element_type=jnp.float32
    )


def greet(axis, peers):
    barrier = pltpu.get_barrier_semaphore()
    for peer in peers:
        pl.semaphore_signal(barrier, inc=1, device_id={axis: peer}, device_id_type=MESH)
    pl.semaphore_wait(barrier, len(peers))


def remote(axis, peer, source, target, send, receive):
    copy = pltpu.make_async_remote_copy(
        source, target, send, receive, device_id={axis: peer}, device_id_type=MESH
    )
    copy.start()
    return copy


def call(kernel, inputs, outputs, scratch, number):
    return pl.pallas_call(
        kernel,
        out_shape=outputs,
        in_specs=[ANY] * len(inputs),
        out_specs=jax.tree.map(lambda _: ANY, outputs),
        scratch_shapes=scratch,
        compiler_params=pltpu.CompilerParams(
            collective_id=number, has_side_effects=True, vmem_limit_bytes=48 * 2**20
        ),
    )(*inputs)


def exchange_kernel(axis, count, views, *refs):
    arrays = len(views)
    sources, targets = refs[:arrays], refs[arrays : 2 * arrays]
    send, receive, local = refs[2 * arrays :]
    me = lax.axis_index(axis)
    peers = [lax.rem(me + step, count) for step in range(1, count)]
    greet(axis, peers)
    copies = []
    for step, peer in enumerate(peers):
        for a, (out_of, into) in enumerate(views):
            copies.append(
                remote(
                    axis,
                    peer,
                    out_of(sources[a], peer),
                    into(targets[a], me),
                    send.at[a, step],
                    receive.at[a, step],
                )
            )
    for a, (out_of, into) in enumerate(views):
        copy = pltpu.make_async_copy(out_of(sources[a], me), into(targets[a], me), local.at[a])
        copy.start()
        copies.append(copy)
    for copy in copies:
        copy.wait()


def exchange(axis, count, inputs, outputs, views, number):
    arrays = len(views)
    return call(
        functools.partial(exchange_kernel, axis, count, views),
        inputs,
        outputs,
        [
            pltpu.SemaphoreType.DMA((arrays, count - 1)),
            pltpu.SemaphoreType.DMA((arrays, count - 1)),
            pltpu.SemaphoreType.DMA((arrays,)),
        ],
        number,
    )


def lead(ref, place):
    return ref.at[place]


def second(ref, place):
    return ref.at[:, place]


def whole(ref, place):
    return ref


def spread_kernel(source, target, send, receive, local):
    me = lax.axis_index("seq")
    one, two, both = me ^ 1, me ^ 2, me ^ 3
    half = source.shape[1] // 2
    greet("seq", [one, two])
    parts = (pl.ds(0, half), pl.ds(half, half))
    own = pltpu.make_async_copy(source, target.at[:, me], local)
    own.start()
    copies = {}
    for side, peer in enumerate((one, two)):
        for order in range(2):
            part = (order + side) % 2
            copies[side, part] = remote(
                "seq",
                peer,
                source.at[:, parts[part]],
                target.at[:, me, parts[part]],
                send.at[side, part],
                receive.at[side, part],
            )
    relayed = []
    for side, (origin, peer) in enumerate(((one, two), (two, one))):
        copies[side, side].wait_recv()
        block = target.at[:, origin, parts[side]]
        relayed.append(remote("seq", peer, block, block, send.at[2, side], receive.at[2, side]))
    for side in range(2):
        copies[side, 1 - side].wait_recv()
        for part in range(2):
            copies[side, part].wait_send()
    for copy in relayed:
        copy.wait()
    own.wait()


def spread(source, number):
    return call(
        spread_kernel,
        (source,),
        jax.ShapeDtypeStruct((source.shape[0], 4, *source.shape[1:]), source.dtype),
        [
            pltpu.SemaphoreType.DMA((3, 2)),
            pltpu.SemaphoreType.DMA((3, 2)),
            pltpu.SemaphoreType.DMA,
        ],
        number,
    )


def columns_kernel(count, source, target, staged, send, receive, local, far_send, far_receive, near_send, near_receive):
    me, place = lax.axis_index("seq"), lax.axis_index("fsdp")
    barrier = pltpu.get_barrier_semaphore()
    others = [lax.rem(me + step, 4) for step in range(1, 4)]
    sibling = place ^ 1
    chips = count // 2
    chip, core = place // 2, lax.rem(place, 2)
    far = [lax.rem(chip + step, chips) * 2 + core for step in range(1, chips)]
    for other in others:
        pl.semaphore_signal(barrier, inc=1, device_id={"seq": other}, device_id_type=MESH)
    for other in [sibling, *far]:
        pl.semaphore_signal(barrier, inc=1, device_id={"fsdp": other}, device_id_type=MESH)
    pl.semaphore_wait(barrier, 3 + chips)
    copies = []
    for step, other in enumerate(others):
        copies.append(
            remote("seq", other, source.at[other], staged.at[me], send.at[step], receive.at[step])
        )
    own = pltpu.make_async_copy(source.at[me], staged.at[me], local.at[0])
    own.start()
    own.wait()
    for copy in copies:
        copy.wait()
    block = target.at[:, place]
    keep = pltpu.make_async_copy(staged, block, local.at[1])
    keep.start()
    away = [
        remote("fsdp", other, staged, block, far_send.at[step], far_receive.at[step])
        for step, other in enumerate(far)
    ]
    near = [remote("fsdp", sibling, staged, block, near_send.at[chips - 1], near_receive.at[chips - 1])]
    for step in range(1, chips):
        away[step - 1].wait_recv()
        origin = lax.rem(chip + chips - step, chips) * 2 + core
        arrived = target.at[:, origin]
        near.append(
            remote("fsdp", sibling, arrived, arrived, near_send.at[step - 1], near_receive.at[step - 1])
        )
    for copy in away:
        copy.wait_send()
    for copy in near:
        copy.wait()
    keep.wait()


def columns_of(weight, count, number):
    chips = count // 2
    dma = pltpu.SemaphoreType.DMA
    return call(
        functools.partial(columns_kernel, count),
        (weight,),
        jax.ShapeDtypeStruct((4, count, *weight.shape[1:]), weight.dtype),
        [
            pltpu.VMEM(weight.shape, weight.dtype),
            dma((3,)),
            dma((3,)),
            dma((2,)),
            dma((chips - 1,)),
            dma((chips - 1,)),
            dma((chips,)),
            dma((chips,)),
        ],
        number,
    )


def collect_kernel(source, target, mine, first, second_in, outgoing, load, send, receive, store):
    me = lax.axis_index("seq")
    one, two, both = me ^ 1, me ^ 2, me ^ 3
    width = source.shape[3] // 2
    greet("seq", [one, two])
    copies = []
    for side, (near, rest) in enumerate(((one, two), (two, one))):
        lanes = pl.ds(side * width, width)
        for order, block in enumerate((both, near)):
            copies.append(
                remote(
                    "seq",
                    near,
                    source.at[:, block, :, lanes],
                    first.at[side, order],
                    send.at[side, order],
                    receive.at[side, order],
                )
            )
        for order, block in enumerate((rest, me)):
            pltpu.make_async_copy(
                source.at[:, block, :, lanes], mine.at[side, order], load.at[side, order]
            ).start()
    passed = []
    for side, rest in enumerate((two, one)):
        copies[side * 2].wait_recv()
        pltpu.make_async_copy(mine.at[side, 0], mine.at[side, 0], load.at[side, 0]).wait()
        outgoing[side] = (
            mine[side, 0].astype(jnp.float32) + first[side, 0].astype(jnp.float32)
        ).astype(outgoing.dtype)
        passed.append(
            remote("seq", rest, outgoing.at[side], second_in.at[side], send.at[2, side], receive.at[2, side])
        )
    for side in range(2):
        copies[side * 2 + 1].wait_recv()
        pltpu.make_async_copy(mine.at[side, 1], mine.at[side, 1], load.at[side, 1]).wait()
        passed[side].wait_recv()
        mine[side, 1] = (
            mine[side, 1].astype(jnp.float32)
            + first[side, 1].astype(jnp.float32)
            + second_in[side].astype(jnp.float32)
        ).astype(mine.dtype)
        out = pltpu.make_async_copy(
            mine.at[side, 1], target.at[:, :, pl.ds(side * width, width)], store.at[side]
        )
        out.start()
    for side in range(2):
        pltpu.make_async_copy(
            mine.at[side, 1], target.at[:, :, pl.ds(side * width, width)], store.at[side]
        ).wait()
    for copy in copies + passed:
        copy.wait_send()


def collect(source, number):
    a, _, rows, width = source.shape
    dma = pltpu.SemaphoreType.DMA
    block = (a, rows, width // 2)
    return call(
        collect_kernel,
        (source,),
        jax.ShapeDtypeStruct((a, rows, width), source.dtype),
        [
            pltpu.VMEM((2, 2, *block), source.dtype),
            pltpu.VMEM((2, 2, *block), source.dtype),
            pltpu.VMEM((2, *block), source.dtype),
            pltpu.VMEM((2, *block), source.dtype),
            dma((2, 2)),
            dma((3, 2)),
            dma((3, 2)),
            dma((2,)),
        ],
        number,
    )


def moe_kernel(
    chips, cap, experts_all, send_rows, up_rows, route, w_in, w_out,
    ret, dw_in, dw_out,
    R, U, G, A, I, PB, first, second, W1, W2, RT, stage,
    load, own, z_send, z_recv, s_send, s_recv, y_send, y_recv,
    c_send, c_recv, d_send, d_recv, r_send, r_recv, store,
):
    me, place = lax.axis_index("seq"), lax.axis_index("fsdp")
    one, two, both = me ^ 1, me ^ 2, me ^ 3
    chip, core = place // 2, lax.rem(place, 2)
    sibling = place ^ 1
    count = chips * 2
    part = 2 * cap
    chunk = 4 * part
    barrier = pltpu.get_barrier_semaphore()
    for peer in (one, two):
        pl.semaphore_signal(barrier, inc=1, device_id={"seq": peer}, device_id_type=MESH)
    for step in range(1, count):
        pl.semaphore_signal(
            barrier, inc=1, device_id={"fsdp": lax.rem(place + step, count)}, device_id_type=MESH
        )
    pl.semaphore_wait(barrier, 2 + count - 1)

    def rows_of(k, s):
        return pl.ds(k * chunk + s * part, part)

    loads = []

    def local(source, target, sem):
        copy = pltpu.make_async_copy(source, target, sem)
        copy.start()
        return copy

    dispatched = []
    own_rows = None
    for k in range(chips):
        to = lax.rem(chip - k + chips, chips)
        for c in range(2):
            target = R.at[:, pl.ds(k * chunk + me * part + core * cap, cap)]
            if k == 0:
                if c == 0:
                    own_rows = local(send_rows.at[place], target, own.at[0])
                    dispatched.append(
                        remote("fsdp", sibling, send_rows.at[sibling], target, z_send.at[0, 0], z_recv.at[0, 0])
                    )
                continue
            peer = to * 2 + (core ^ c)
            dispatched.append(
                remote("fsdp", peer, send_rows.at[peer], target, z_send.at[k, c], z_recv.at[k, c])
            )

    def z_arrived(k):
        if k == 0:
            own_rows.wait()
            dispatched[0].wait_recv()
        else:
            dispatched[2 * k - 1].wait_recv()
            dispatched[2 * k].wait_recv()

    sent = {}

    def spread_out(a, k):
        for side, peer in enumerate((one, two)):
            for order in range(2):
                j = (order + side) % 2
                target = (U, R)[a].at[j, rows_of(k, me)]
                source = up_rows.at[k, j] if a == 0 else target
                sent[a, k, side, j] = remote(
                    "seq", peer, source, target, s_send.at[a, k, side, j], s_recv.at[a, k, side, j]
                )

    def relay(a, k):
        for side, (origin, peer) in enumerate(((one, two), (two, one))):
            sent[a, k, side, side].wait_recv()
            block = (U, R)[a].at[side, rows_of(k, origin)]
            sent[a, k, 2, side] = remote(
                "seq", peer, block, block, y_send.at[a, k, side], y_recv.at[a, k, side]
            )

    def all_arrived(a, k):
        for side in range(2):
            sent[a, k, side, 1 - side].wait_recv()
        for side in range(2):
            sent[a, k, 2, side].wait_recv()

    def experts(k, j):
        rows = pl.ds(k * chunk, chunk)
        logits = times(R[j, rows, :], RT[...])
        lane = lax.broadcasted_iota(jnp.int32, logits.shape, 1)
        logits = jnp.where(lane < experts_all, logits, MASKED)
        powers = jnp.exp(logits - jnp.max(logits, axis=1, keepdims=True))
        picked = jnp.sum(jnp.where(lane == place * 2 + j, powers, 0.0), axis=1, keepdims=True)
        gate = picked / jnp.sum(powers, axis=1, keepdims=True)
        G[j, rows, :] = (U[j, rows, :].astype(jnp.float32) * gate).astype(G.dtype)

        @pl.loop(0, W1.shape[2] // TILE)
        def _(t):
            cols = pl.ds(pl.multiple_of(t * TILE, TILE), TILE)
            v = times(R[j, rows, :], W1[j, :, cols])
            grad = times_transposed(G[j, rows, :], W2[j, cols, :])
            square = v * v
            t = jnp.tanh(ROOT * v * (1.0 + 0.044715 * square))
            half = 0.5 * (1.0 + t)
            A[j, rows, cols] = (v * half).astype(A.dtype)
            slope = half + 0.5 * v * (1.0 - t * t) * (ROOT * (1.0 + 0.134145 * square))
            I[j, rows, cols] = (grad * slope).astype(I.dtype)

        @pl.loop(0, W1.shape[1] // TILE)
        def _(t):
            cols = pl.ds(pl.multiple_of(t * TILE, TILE), TILE)
            PB[0, j, rows, cols] = times(A[j, rows, :], W2[j, :, cols]).astype(PB.dtype)
            PB[1, j, rows, cols] = times_transposed(I[j, rows, :], W1[j, cols, :]).astype(PB.dtype)

    summed = {}

    def near_of(j):
        return (one, two) if j == 0 else (two, one)

    def collect_one(k, j):
        near, rest = near_of(j)
        for a in range(2):
            for order, block in enumerate((both, near)):
                summed[a, k, j, order] = remote(
                    "seq", near, PB.at[a, j, rows_of(k, block)], first.at[a, j, k, order],
                    c_send.at[a, j, k, order], c_recv.at[a, j, k, order],
                )

    def collect_two(k, j):
        near, rest = near_of(j)
        for a in range(2):
            summed[a, k, j, 0].wait_recv()
            first[a, j, k, 0] = (
                first[a, j, k, 0].astype(jnp.float32) + PB[a, j, rows_of(k, rest), :].astype(jnp.float32)
            ).astype(first.dtype)
            summed[a, k, j, 2] = remote(
                "seq", rest, first.at[a, j, k, 0], second.at[a, j, k], d_send.at[a, j, k], d_recv.at[a, j, k]
            )

    returns = {}

    def collect_three(k, j):
        for a in range(2):
            summed[a, k, j, 1].wait_recv()
            summed[a, k, j, 2].wait_recv()
            first[a, j, k, 1] = (
                first[a, j, k, 1].astype(jnp.float32)
                + PB[a, j, rows_of(k, me), :].astype(jnp.float32)
                + second[a, j, k].astype(jnp.float32)
            ).astype(first.dtype)
            to = lax.rem(chip + k, chips)
            target = ret.at[a, place, j]
            for c in range(2):
                if k == 0:
                    if c == 0:
                        returns[a, k, j, 0] = local(
                            first.at[a, j, k, 1, pl.ds(core * cap, cap)], target, own.at[1 + a * 2 + j]
                        )
                        returns[a, k, j, 1] = remote(
                            "fsdp", sibling, first.at[a, j, k, 1, pl.ds((core ^ 1) * cap, cap)], target,
                            r_send.at[a, j, k, 1], r_recv.at[a, j, k, 1],
                        )
                    continue
                returns[a, k, j, c] = remote(
                    "fsdp", to * 2 + (core ^ c), first.at[a, j, k, 1, pl.ds((core ^ c) * cap, cap)], target,
                    r_send.at[a, j, k, c], r_recv.at[a, j, k, c],
                )

    staged = {}

    def weight_grads(j, which):
        left, right, out = ((R, I, dw_in), (A, G, dw_out))[which]
        for m in range(left.shape[2] // GRAD):
            slot = m % 2
            lanes = slice(m * GRAD, (m + 1) * GRAD)
            if slot in staged:
                staged.pop(slot).wait()

            @pl.loop(0, right.shape[2] // TILE)
            def _(t):
                cols = pl.ds(pl.multiple_of(t * TILE, TILE), TILE)
                stage[slot, :, cols] = transposed_times(left[j, :, lanes], right[j, :, cols])

            staged[slot] = local(stage.at[slot], out.at[j, lanes], store.at[slot])

    mine = [
        local(up_rows.at[k, j], U.at[j, rows_of(k, me)], own.at[5 + k * 2 + j])
        for k in range(chips)
        for j in range(2)
    ]
    spread_out(0, 0)
    for j in range(2):
        loads.append(local(w_in.at[j], W1.at[j], load.at[j]))
        loads.append(local(w_out.at[j], W2.at[j], load.at[2 + j]))
    loads.append(local(route, RT, load.at[4]))
    z_arrived(0)
    spread_out(1, 0)
    spread_out(0, 1)
    for copy in mine + loads:
        copy.wait()
    for k in range(chips):
        relay(0, k)
        relay(1, k)
        if k + 1 < chips:
            z_arrived(k + 1)
            spread_out(1, k + 1)
        if k + 2 < chips:
            spread_out(0, k + 2)
        all_arrived(0, k)
        all_arrived(1, k)
        experts(k, 0)
        collect_one(k, 0)
        if k:
            collect_two(k - 1, 0)
            collect_two(k - 1, 1)
        experts(k, 1)
        collect_one(k, 1)
        if k:
            collect_three(k - 1, 0)
            collect_three(k - 1, 1)
    last = chips - 1
    weight_grads(0, 0)
    collect_two(last, 0)
    collect_two(last, 1)
    weight_grads(0, 1)
    weight_grads(1, 0)
    collect_three(last, 0)
    collect_three(last, 1)
    weight_grads(1, 1)
    for copy in staged.values():
        copy.wait()
    for copy in dispatched:
        copy.wait_send()
    for copy in sent.values():
        copy.wait_send()
    for copy in summed.values():
        copy.wait_send()
    for (a, k, j, c), copy in returns.items():
        copy.wait()


def moe(send_rows, up_rows, route, w_in, w_out, experts_all, number):
    S, low, dma = jax.ShapeDtypeStruct, jnp.bfloat16, pltpu.SemaphoreType.DMA
    owners, _, cap, width = send_rows.shape
    chips = owners // 2
    hidden_units = w_in.shape[2]
    count = owners * cap * 4
    part = 2 * cap

    def vmem(*shape, dtype=low):
        return pltpu.VMEM(shape, dtype)

    return pl.pallas_call(
        functools.partial(moe_kernel, chips, cap, experts_all),
        out_shape=(
            S((2, owners, 2, cap, width), low),
            S(w_in.shape, jnp.float32),
            S(w_out.shape, jnp.float32),
        ),
        in_specs=[ANY] * 5,
        out_specs=(ANY,) * 3,
        scratch_shapes=[
            vmem(2, count, width),
            vmem(2, count, width),
            vmem(2, count, width),
            vmem(2, count, hidden_units),
            vmem(2, count, hidden_units),
            vmem(2, 2, count, width),
            vmem(2, 2, chips, 2, part, width),
            vmem(2, 2, chips, part, width),
            vmem(*w_in.shape),
            vmem(*w_out.shape),
            vmem(*route.shape),
            vmem(2, GRAD, max(width, hidden_units), dtype=jnp.float32),
            dma((5,)),
            dma((5 + 2 * chips,)),
            dma((chips, 2)),
            dma((chips, 2)),
            dma((2, chips, 2, 2)),
            dma((2, chips, 2, 2)),
            dma((2, chips, 2)),
            dma((2, chips, 2)),
            dma((2, 2, chips, 2)),
            dma((2, 2, chips, 2)),
            dma((2, 2, chips)),
            dma((2, 2, chips)),
            dma((2, 2, chips, 2)),
            dma((2, 2, chips, 2)),
            dma((2,)),
        ],
        compiler_params=pltpu.CompilerParams(
            collective_id=number, has_side_effects=True, vmem_limit_bytes=58 * 2**20
        ),
        cost_estimate=pl.CostEstimate(
            flops=12 * 2 * count * width * hidden_units, bytes_accessed=2**25, transcendentals=0
        ),
    )(send_rows, up_rows, route, w_in, w_out)


def masked_scores(block_query, keys, start, length, scale):
    scores = (
        jnp.einsum("qhd,khd->hqk", block_query, keys, preferred_element_type=jnp.float32) * scale
    )
    rows = start + jnp.arange(block_query.shape[0], dtype=jnp.int32)
    columns = jnp.arange(keys.shape[0], dtype=jnp.int32)
    keep = (columns[None, :] <= rows[:, None]) & (columns[None, :] < length)
    return jnp.where(keep[None], scores, MASKED)


def shards(
    hidden,
    lengths,
    expert_ids,
    attn_gain,
    qkv_weight,
    out_weight,
    moe_gain,
    router_weight,
    expert_in,
    expert_out,
    out_grad,
):
    S = jax.ShapeDtypeStruct
    low = jnp.bfloat16
    owners = lax.axis_size("fsdp")
    seq_place = lax.axis_index("seq")
    seq_count = lax.axis_size("seq")
    tokens, width = hidden.shape[1], hidden.shape[2]
    full_len = tokens * seq_count
    group_width = width // seq_count
    heads_local = group_width // HEAD_DIM
    rows_own = qkv_weight.shape[0]
    scale = HEAD_DIM ** (-0.5)
    length = lengths[0]
    experts_all = router_weight.shape[1]
    small = jnp.concatenate([router_weight, attn_gain[:, None], moe_gain[:, None]], axis=1)
    small = jnp.pad(small, ((0, 0), (0, -small.shape[1] % 128)))
    small = lax.all_gather(small, ("seq", "fsdp"), axis=0, tiled=True)
    weight_mix = lax.all_gather(out_weight, ("seq", "fsdp"), axis=0, tiled=True)
    weight_route = small[:, :experts_all]
    gain_one = small[:, experts_all].astype(jnp.float32)
    gain_two = small[:, experts_all + 1].astype(jnp.float32)
    mix_rows = lax.dynamic_slice_in_dim(weight_mix, seq_place * group_width, group_width, 0)

    expert_local = expert_in.shape[0]
    capacity = -(-max(2, 2 * tokens // experts_all) // 16) * 16
    slots = experts_all * capacity

    position = seq_place * tokens + jnp.arange(tokens, dtype=jnp.int32)
    valid = (position < length).astype(jnp.float32)[:, None]
    chosen = expert_ids[0, :, 0]
    choose = chosen[:, None] == jnp.arange(experts_all, dtype=jnp.int32)[None, :]
    order = jnp.arange(tokens, dtype=jnp.int32)
    earlier = (order[None, :] < order[:, None]) & (chosen[None, :] == chosen[:, None])
    ranks = jnp.sum(earlier.astype(jnp.int32), axis=1)
    slot = chosen * capacity + ranks
    hit = jnp.arange(slots, dtype=jnp.int32)[:, None] == slot[None, :]
    dispatch = hit.astype(low)

    def to_owners(rows, number):
        return exchange(
            "fsdp",
            owners,
            (rows.reshape(owners, expert_local, capacity, width),),
            (S((expert_local, owners, capacity, width), low),),
            ((lead, second),),
            number,
        )[0].reshape(expert_local, owners * capacity, width)

    def to_sources(rows, number):
        return exchange(
            "fsdp",
            owners,
            (rows.reshape(expert_local, owners, capacity, width),),
            (S((owners, expert_local, capacity, width), low),),
            ((second, lead),),
            number,
        )[0].reshape(slots, width)

    upstream_low = jnp.where(valid > 0, out_grad[0], 0).astype(low)
    upstream = upstream_low.astype(jnp.float32)
    up_rows = times(dispatch, upstream_low).astype(low)
    up_all = to_owners(up_rows, 0)
    fused = expert_local == 2 and 4 * owners * capacity <= 1024
    if fused:
        up_all = up_all.reshape(expert_local, owners // 2, 2 * capacity, width).transpose(1, 0, 2, 3)
        up_all = jnp.roll(up_all, -(lax.axis_index("fsdp") // 2), axis=0)
    else:
        up_all = spread(up_all, 1)

    weight_qkv = columns_of(
        qkv_weight.reshape(rows_own, 3, seq_count, group_width)
        .transpose(2, 0, 1, 3)
        .reshape(seq_count, rows_own, 3 * group_width),
        owners,
        2,
    ).reshape(width, 3 * group_width)
    hidden_all = spread(hidden, 3).reshape(full_len, width)

    normed = scaled_norm(hidden_all.astype(jnp.float32), gain_one).astype(low)
    projected = times(normed, weight_qkv).astype(low)
    query = projected[:, :group_width].reshape(full_len, heads_local, HEAD_DIM)
    keys = projected[:, group_width : 2 * group_width].reshape(full_len, heads_local, HEAD_DIM)
    values = projected[:, 2 * group_width :].reshape(full_len, heads_local, HEAD_DIM)
    starts = list(range(0, full_len, QBLOCK))
    outputs = []
    totals = []
    for start in starts:
        block_query = query[start : start + QBLOCK]
        reach = start + QBLOCK
        scores = masked_scores(block_query, keys[:reach], start, length, scale)
        top = jnp.max(scores, axis=-1, keepdims=True)
        total = top + jnp.log(jnp.sum(jnp.exp(scores - top), axis=-1, keepdims=True))
        probs = jnp.exp(scores - total).astype(low)
        block_out = jnp.einsum("hqk,khd->qhd", probs, values[:reach], preferred_element_type=jnp.float32)
        outputs.append(block_out.astype(low))
        totals.append(total)
    attended = jnp.concatenate(outputs, axis=0).reshape(full_len, group_width)
    mixed = exchange(
        "seq",
        seq_count,
        (attended.reshape(seq_count, tokens, group_width),),
        (S((seq_count, tokens, group_width), low),),
        ((lead, lead),),
        4,
    )[0]
    mixed = mixed.transpose(1, 0, 2).reshape(tokens, width)
    inputs = hidden[0].astype(jnp.float32)
    middle = inputs + times(mixed, weight_mix)
    normed_two, norm_two_back = jax.vjp(scaled_norm, middle, gain_two)
    normed_two = normed_two.astype(low)
    logits = times(normed_two, weight_route)

    def gate_of(logit_rows):
        return jnp.sum(jnp.where(choose, jax.nn.softmax(logit_rows, axis=-1), 0.0), axis=-1)

    gate, gate_back = jax.vjp(gate_of, logits)
    sent = times(dispatch, normed_two).astype(low)
    if fused:
        (returned, grad_back), expert_in_grad, expert_out_grad = moe(
            sent.reshape(owners, expert_local, capacity, width),
            up_all,
            small,
            expert_in,
            expert_out,
            experts_all,
            5,
        )
        returned, grad_back = returned.reshape(slots, width), grad_back.reshape(slots, width)
    else:
        gate_rows = jnp.sum(jnp.where(hit, gate[None, :], 0.0), axis=1)
        gates = lax.all_to_all(
            gate_rows.reshape(owners, expert_local, capacity), "fsdp", split_axis=0, concat_axis=0, tiled=True
        )
        gates = lax.all_gather(gates, "seq", axis=0)
        gates = gates.transpose(2, 0, 1, 3).reshape(expert_local, seq_count * owners * capacity, 1)

        rows_all = spread(to_owners(sent, 5), 6)
        count = seq_count * owners * capacity
        rows_all = rows_all.reshape(expert_local, count, width)
        up_all = up_all.reshape(expert_local, count, width)
        grad_rows = (up_all.astype(jnp.float32) * gates).astype(low)

        def per_expert(form, left, right):
            return jnp.einsum(form, left, right, preferred_element_type=jnp.float32)

        inner = per_expert("jrd,jdf->jrf", rows_all, expert_in)
        active, active_back = jax.vjp(gelu_tanh, inner)
        active = active.astype(low)
        partial_out = per_expert("jrf,jfd->jrd", active, expert_out).astype(low)
        grad_active = per_expert("jrd,jfd->jrf", grad_rows, expert_out)
        grad_inner = active_back(grad_active)[0].astype(low)
        partial_back = per_expert("jrf,jdf->jrd", grad_inner, expert_in).astype(low)
        expert_out_grad = per_expert("jrf,jrd->jfd", active, grad_rows)
        expert_in_grad = per_expert("jrd,jrf->jdf", rows_all, grad_inner)

        shape = (expert_local, seq_count, owners * capacity, width)
        returned = to_sources(collect(partial_out.reshape(shape), 7), 8)
        grad_back = to_sources(collect(partial_back.reshape(shape), 9), 10)

    back_rows = transposed_times(dispatch, returned)
    output = valid * (middle + gate[:, None] * back_rows)
    grad_gate = jnp.sum(upstream * back_rows, axis=1)
    grad_logits = gate_back(grad_gate)[0].astype(low)
    grad_route = transposed_times(normed_two, grad_logits)
    grad_normed_two = times_transposed(grad_logits, weight_route) + transposed_times(dispatch, grad_back)
    grad_middle, grad_gain_two = norm_two_back(grad_normed_two)
    grad_middle = grad_middle + upstream
    grad_attn = grad_middle.astype(low)

    grad_attn_all = spread(grad_attn[None], 11).reshape(full_len, width)
    grad_mix = transposed_times(attended, grad_attn_all)
    grad_heads = times_transposed(grad_attn_all, mix_rows).astype(low)
    grad_heads = grad_heads.reshape(full_len, heads_local, HEAD_DIM)
    grad_query = []
    grad_keys = jnp.zeros((full_len, heads_local, HEAD_DIM), jnp.float32)
    grad_values = jnp.zeros((full_len, heads_local, HEAD_DIM), jnp.float32)
    for number, start in enumerate(starts):
        reach = start + QBLOCK
        block_query = query[start : start + QBLOCK]
        scores = masked_scores(block_query, keys[:reach], start, length, scale)
        probs = jnp.exp(scores - totals[number])
        probs_low = probs.astype(low)
        grad_out = grad_heads[start : start + QBLOCK]
        grad_values = grad_values.at[:reach].add(
            jnp.einsum("hqk,qhd->khd", probs_low, grad_out, preferred_element_type=jnp.float32)
        )
        grad_probs = jnp.einsum(
            "qhd,khd->hqk", grad_out, values[:reach], preferred_element_type=jnp.float32
        )
        grad_scores = (
            probs * (grad_probs - jnp.sum(grad_probs * probs, axis=-1, keepdims=True))
        ).astype(low)
        grad_query.append(
            jnp.einsum("hqk,khd->qhd", grad_scores, keys[:reach], preferred_element_type=jnp.float32)
            * scale
        )
        grad_keys = grad_keys.at[:reach].add(
            jnp.einsum("hqk,qhd->khd", grad_scores, block_query, preferred_element_type=jnp.float32)
            * scale
        )
    grad_projected = jnp.concatenate(
        [
            part.astype(low).reshape(full_len, group_width)
            for part in (jnp.concatenate(grad_query, axis=0), grad_keys, grad_values)
        ],
        axis=1,
    )
    grad_qkv_cols = transposed_times(normed, grad_projected).astype(low)
    partial_normed = times_transposed(grad_projected, weight_qkv).astype(low)
    grad_normed = collect(partial_normed.reshape(1, seq_count, tokens, width), 12)[0]

    qkv_parts, mix_parts = exchange(
        "fsdp",
        owners,
        (
            grad_qkv_cols.reshape(seq_count, owners, rows_own, 3 * group_width),
            grad_mix.astype(low).reshape(owners, rows_own, width),
        ),
        (
            S((owners, seq_count, rows_own, 3 * group_width), low),
            S((owners, rows_own, width), low),
        ),
        ((second, lead), (lead, lead)),
        13,
    )
    mix_grad = jnp.sum(mix_parts.astype(jnp.float32), axis=0)
    qkv_sum = jnp.sum(qkv_parts.astype(jnp.float32), axis=0)
    qkv_sum = exchange(
        "seq", seq_count, (qkv_sum,), (S(qkv_sum.shape, jnp.float32),), ((lead, lead),), 14
    )[0]
    qkv_weight_grad = (
        qkv_sum.reshape(seq_count, rows_own, 3, group_width)
        .transpose(1, 2, 0, 3)
        .reshape(rows_own, 3 * width)
    )
    _, norm_back = jax.vjp(scaled_norm, inputs, gain_one)
    grad_inputs, grad_gain_one = norm_back(grad_normed.astype(jnp.float32))
    grad_inputs = grad_inputs + grad_middle
    small_grad = jnp.concatenate(
        [grad_route, grad_gain_one[:, None], grad_gain_two[:, None]], axis=1
    )
    small_grad = jnp.pad(small_grad, ((0, 0), (0, -small_grad.shape[1] % 128)))
    small_grad = lax.psum_scatter(small_grad, ("seq", "fsdp"), scatter_dimension=0, tiled=True)
    return (
        output.astype(low)[None],
        grad_inputs[None],
        small_grad[:, experts_all],
        qkv_weight_grad,
        mix_grad,
        small_grad[:, experts_all + 1],
        small_grad[:, :experts_all],
        expert_in_grad,
        expert_out_grad,
    )


def solution(mesh):
    placed = (
        P("fsdp", "seq", None),
        P("fsdp"),
        P("fsdp", "seq", None),
        P(("seq", "fsdp")),
        P(("seq", "fsdp"), None),
        P(("seq", "fsdp"), None),
        P(("seq", "fsdp")),
        P(("seq", "fsdp"), None),
        P("fsdp", None, "seq"),
        P("fsdp", "seq", None),
        P("fsdp", "seq", None),
    )
    return jax.shard_map(
        shards,
        mesh=mesh,
        in_specs=placed,
        out_specs=(
            P("fsdp", "seq", None),
            P("fsdp", "seq", None),
            P(("seq", "fsdp")),
            P(("seq", "fsdp"), None),
            P(("seq", "fsdp"), None),
            P(("seq", "fsdp")),
            P(("seq", "fsdp"), None),
            P("fsdp", None, "seq"),
            P("fsdp", "seq", None),
        ),
        check_vma=False,
    )
```

```python
import functools

import jax
import jax.numpy as jnp
from jax import lax
from jax.experimental import pallas as pl
from jax.experimental.pallas import tpu as pltpu
from jax.sharding import PartitionSpec as P

HEAD_DIM = 64
QBLOCK = 512
EPS = 1e-05
MASKED = -1e30
ROOT = 0.7978845608028654
TILE = 256
GRAD = 256
MESH = pl.DeviceIdType.MESH
ANY = pl.BlockSpec(memory_space=pl.ANY)


def scaled_norm(value, gain):
    return value * lax.rsqrt(jnp.mean(value * value, axis=-1, keepdims=True) + EPS) * gain


def gelu_tanh(value):
    return jax.nn.gelu(value, approximate=True)


def times(left, right):
    return jnp.dot(left, right, preferred_element_type=jnp.float32)


def times_transposed(left, right):
    return lax.dot_general(
        left, right, (((1,), (1,)), ((), ())), preferred_element_type=jnp.float32
    )


def transposed_times(left, right):
    return lax.dot_general(
        left, right, (((0,), (0,)), ((), ())), preferred_element_type=jnp.float32
    )


def greet(axis, peers):
    barrier = pltpu.get_barrier_semaphore()
    for peer in peers:
        pl.semaphore_signal(barrier, inc=1, device_id={axis: peer}, device_id_type=MESH)
    pl.semaphore_wait(barrier, len(peers))


def remote(axis, peer, source, target, send, receive):
    copy = pltpu.make_async_remote_copy(
        source, target, send, receive, device_id={axis: peer}, device_id_type=MESH
    )
    copy.start()
    return copy


def call(kernel, inputs, outputs, scratch, number):
    return pl.pallas_call(
        kernel,
        out_shape=outputs,
        in_specs=[ANY] * len(inputs),
        out_specs=jax.tree.map(lambda _: ANY, outputs),
        scratch_shapes=scratch,
        compiler_params=pltpu.CompilerParams(
            collective_id=number, has_side_effects=True, vmem_limit_bytes=48 * 2**20
        ),
    )(*inputs)


def exchange_kernel(axis, count, views, *refs):
    arrays = len(views)
    sources, targets = refs[:arrays], refs[arrays : 2 * arrays]
    send, receive, local = refs[2 * arrays :]
    me = lax.axis_index(axis)
    peers = [lax.rem(me + step, count) for step in range(1, count)]
    greet(axis, peers)
    copies = []
    for step, peer in enumerate(peers):
        for a, (out_of, into) in enumerate(views):
            copies.append(
                remote(
                    axis,
                    peer,
                    out_of(sources[a], peer),
                    into(targets[a], me),
                    send.at[a, step],
                    receive.at[a, step],
                )
            )
    for a, (out_of, into) in enumerate(views):
        copy = pltpu.make_async_copy(out_of(sources[a], me), into(targets[a], me), local.at[a])
        copy.start()
        copies.append(copy)
    for copy in copies:
        copy.wait()


def exchange(axis, count, inputs, outputs, views, number):
    arrays = len(views)
    return call(
        functools.partial(exchange_kernel, axis, count, views),
        inputs,
        outputs,
        [
            pltpu.SemaphoreType.DMA((arrays, count - 1)),
            pltpu.SemaphoreType.DMA((arrays, count - 1)),
            pltpu.SemaphoreType.DMA((arrays,)),
        ],
        number,
    )


def lead(ref, place):
    return ref.at[place]


def second(ref, place):
    return ref.at[:, place]


def whole(ref, place):
    return ref


def spread_kernel(source, target, send, receive, local):
    me = lax.axis_index("seq")
    one, two, both = me ^ 1, me ^ 2, me ^ 3
    half = source.shape[1] // 2
    greet("seq", [one, two])
    parts = (pl.ds(0, half), pl.ds(half, half))
    own = pltpu.make_async_copy(source, target.at[:, me], local)
    own.start()
    copies = {}
    for side, peer in enumerate((one, two)):
        for order in range(2):
            part = (order + side) % 2
            copies[side, part] = remote(
                "seq",
                peer,
                source.at[:, parts[part]],
                target.at[:, me, parts[part]],
                send.at[side, part],
                receive.at[side, part],
            )
    relayed = []
    for side, (origin, peer) in enumerate(((one, two), (two, one))):
        copies[side, side].wait_recv()
        block = target.at[:, origin, parts[side]]
        relayed.append(remote("seq", peer, block, block, send.at[2, side], receive.at[2, side]))
    for side in range(2):
        copies[side, 1 - side].wait_recv()
        for part in range(2):
            copies[side, part].wait_send()
    for copy in relayed:
        copy.wait()
    own.wait()


def spread(source, number):
    return call(
        spread_kernel,
        (source,),
        jax.ShapeDtypeStruct((source.shape[0], 4, *source.shape[1:]), source.dtype),
        [
            pltpu.SemaphoreType.DMA((3, 2)),
            pltpu.SemaphoreType.DMA((3, 2)),
            pltpu.SemaphoreType.DMA,
        ],
        number,
    )


def collect_kernel(source, target, mine, first, second_in, outgoing, load, send, receive, store):
    me = lax.axis_index("seq")
    one, two, both = me ^ 1, me ^ 2, me ^ 3
    width = source.shape[3] // 2
    greet("seq", [one, two])
    copies = []
    for side, (near, rest) in enumerate(((one, two), (two, one))):
        lanes = pl.ds(side * width, width)
        for order, block in enumerate((both, near)):
            copies.append(
                remote(
                    "seq",
                    near,
                    source.at[:, block, :, lanes],
                    first.at[side, order],
                    send.at[side, order],
                    receive.at[side, order],
                )
            )
        for order, block in enumerate((rest, me)):
            pltpu.make_async_copy(
                source.at[:, block, :, lanes], mine.at[side, order], load.at[side, order]
            ).start()
    passed = []
    for side, rest in enumerate((two, one)):
        copies[side * 2].wait_recv()
        pltpu.make_async_copy(mine.at[side, 0], mine.at[side, 0], load.at[side, 0]).wait()
        outgoing[side] = (
            mine[side, 0].astype(jnp.float32) + first[side, 0].astype(jnp.float32)
        ).astype(outgoing.dtype)
        passed.append(
            remote("seq", rest, outgoing.at[side], second_in.at[side], send.at[2, side], receive.at[2, side])
        )
    for side in range(2):
        copies[side * 2 + 1].wait_recv()
        pltpu.make_async_copy(mine.at[side, 1], mine.at[side, 1], load.at[side, 1]).wait()
        passed[side].wait_recv()
        mine[side, 1] = (
            mine[side, 1].astype(jnp.float32)
            + first[side, 1].astype(jnp.float32)
            + second_in[side].astype(jnp.float32)
        ).astype(mine.dtype)
        out = pltpu.make_async_copy(
            mine.at[side, 1], target.at[:, :, pl.ds(side * width, width)], store.at[side]
        )
        out.start()
    for side in range(2):
        pltpu.make_async_copy(
            mine.at[side, 1], target.at[:, :, pl.ds(side * width, width)], store.at[side]
        ).wait()
    for copy in copies + passed:
        copy.wait_send()


def collect(source, number):
    a, _, rows, width = source.shape
    dma = pltpu.SemaphoreType.DMA
    block = (a, rows, width // 2)
    return call(
        collect_kernel,
        (source,),
        jax.ShapeDtypeStruct((a, rows, width), source.dtype),
        [
            pltpu.VMEM((2, 2, *block), source.dtype),
            pltpu.VMEM((2, 2, *block), source.dtype),
            pltpu.VMEM((2, *block), source.dtype),
            pltpu.VMEM((2, *block), source.dtype),
            dma((2, 2)),
            dma((3, 2)),
            dma((3, 2)),
            dma((2,)),
        ],
        number,
    )


def moe_kernel(
    chips, cap, experts_all, send_rows, up_rows, route, w_in, w_out,
    ret, dw_in, dw_out,
    R, U, G, A, I, PB, first, second, W1, W2, RT, stage,
    load, own, z_send, z_recv, s_send, s_recv, y_send, y_recv,
    c_send, c_recv, d_send, d_recv, r_send, r_recv, store,
):
    me, place = lax.axis_index("seq"), lax.axis_index("fsdp")
    one, two, both = me ^ 1, me ^ 2, me ^ 3
    chip, core = place // 2, lax.rem(place, 2)
    sibling = place ^ 1
    count = chips * 2
    part = 2 * cap
    chunk = 4 * part
    barrier = pltpu.get_barrier_semaphore()
    for peer in (one, two):
        pl.semaphore_signal(barrier, inc=1, device_id={"seq": peer}, device_id_type=MESH)
    for step in range(1, count):
        pl.semaphore_signal(
            barrier, inc=1, device_id={"fsdp": lax.rem(place + step, count)}, device_id_type=MESH
        )
    pl.semaphore_wait(barrier, 2 + count - 1)

    def rows_of(k, s):
        return pl.ds(k * chunk + s * part, part)

    loads = []

    def local(source, target, sem):
        copy = pltpu.make_async_copy(source, target, sem)
        copy.start()
        return copy

    dispatched = []
    own_rows = None
    for k in range(chips):
        to = lax.rem(chip - k + chips, chips)
        for c in range(2):
            target = R.at[:, pl.ds(k * chunk + me * part + core * cap, cap)]
            if k == 0:
                if c == 0:
                    own_rows = local(send_rows.at[place], target, own.at[0])
                    dispatched.append(
                        remote("fsdp", sibling, send_rows.at[sibling], target, z_send.at[0, 0], z_recv.at[0, 0])
                    )
                continue
            peer = to * 2 + (core ^ c)
            dispatched.append(
                remote("fsdp", peer, send_rows.at[peer], target, z_send.at[k, c], z_recv.at[k, c])
            )

    def z_arrived(k):
        if k == 0:
            own_rows.wait()
            dispatched[0].wait_recv()
        else:
            dispatched[2 * k - 1].wait_recv()
            dispatched[2 * k].wait_recv()

    sent = {}

    def spread_out(a, k):
        for side, peer in enumerate((one, two)):
            for order in range(2):
                j = (order + side) % 2
                target = (U, R)[a].at[j, rows_of(k, me)]
                source = up_rows.at[k, j] if a == 0 else target
                sent[a, k, side, j] = remote(
                    "seq", peer, source, target, s_send.at[a, k, side, j], s_recv.at[a, k, side, j]
                )

    def relay(a, k):
        for side, (origin, peer) in enumerate(((one, two), (two, one))):
            sent[a, k, side, side].wait_recv()
            block = (U, R)[a].at[side, rows_of(k, origin)]
            sent[a, k, 2, side] = remote(
                "seq", peer, block, block, y_send.at[a, k, side], y_recv.at[a, k, side]
            )

    def all_arrived(a, k):
        for side in range(2):
            sent[a, k, side, 1 - side].wait_recv()
        for side in range(2):
            sent[a, k, 2, side].wait_recv()

    def experts(k, j):
        rows = pl.ds(k * chunk, chunk)
        logits = times(R[j, rows, :], RT[...])
        lane = lax.broadcasted_iota(jnp.int32, logits.shape, 1)
        logits = jnp.where(lane < experts_all, logits, MASKED)
        powers = jnp.exp(logits - jnp.max(logits, axis=1, keepdims=True))
        picked = jnp.sum(jnp.where(lane == place * 2 + j, powers, 0.0), axis=1, keepdims=True)
        gate = picked / jnp.sum(powers, axis=1, keepdims=True)
        G[j, rows, :] = (U[j, rows, :].astype(jnp.float32) * gate).astype(G.dtype)

        @pl.loop(0, W1.shape[2] // TILE)
        def _(t):
            cols = pl.ds(pl.multiple_of(t * TILE, TILE), TILE)
            v = times(R[j, rows, :], W1[j, :, cols])
            grad = times_transposed(G[j, rows, :], W2[j, cols, :])
            square = v * v
            t = jnp.tanh(ROOT * v * (1.0 + 0.044715 * square))
            half = 0.5 * (1.0 + t)
            A[j, rows, cols] = (v * half).astype(A.dtype)
            slope = half + 0.5 * v * (1.0 - t * t) * (ROOT * (1.0 + 0.134145 * square))
            I[j, rows, cols] = (grad * slope).astype(I.dtype)

        @pl.loop(0, W1.shape[1] // TILE)
        def _(t):
            cols = pl.ds(pl.multiple_of(t * TILE, TILE), TILE)
            PB[0, j, rows, cols] = times(A[j, rows, :], W2[j, :, cols]).astype(PB.dtype)
            PB[1, j, rows, cols] = times_transposed(I[j, rows, :], W1[j, cols, :]).astype(PB.dtype)

    summed = {}

    def near_of(j):
        return (one, two) if j == 0 else (two, one)

    def collect_one(k, j):
        near, rest = near_of(j)
        for a in range(2):
            for order, block in enumerate((both, near)):
                summed[a, k, j, order] = remote(
                    "seq", near, PB.at[a, j, rows_of(k, block)], first.at[a, j, k, order],
                    c_send.at[a, j, k, order], c_recv.at[a, j, k, order],
                )

    def collect_two(k, j):
        near, rest = near_of(j)
        for a in range(2):
            summed[a, k, j, 0].wait_recv()
            first[a, j, k, 0] = (
                first[a, j, k, 0].astype(jnp.float32) + PB[a, j, rows_of(k, rest), :].astype(jnp.float32)
            ).astype(first.dtype)
            summed[a, k, j, 2] = remote(
                "seq", rest, first.at[a, j, k, 0], second.at[a, j, k], d_send.at[a, j, k], d_recv.at[a, j, k]
            )

    returns = {}

    def collect_three(k, j):
        for a in range(2):
            summed[a, k, j, 1].wait_recv()
            summed[a, k, j, 2].wait_recv()
            first[a, j, k, 1] = (
                first[a, j, k, 1].astype(jnp.float32)
                + PB[a, j, rows_of(k, me), :].astype(jnp.float32)
                + second[a, j, k].astype(jnp.float32)
            ).astype(first.dtype)
            to = lax.rem(chip + k, chips)
            target = ret.at[a, place, j]
            for c in range(2):
                if k == 0:
                    if c == 0:
                        returns[a, k, j, 0] = local(
                            first.at[a, j, k, 1, pl.ds(core * cap, cap)], target, own.at[1 + a * 2 + j]
                        )
                        returns[a, k, j, 1] = remote(
                            "fsdp", sibling, first.at[a, j, k, 1, pl.ds((core ^ 1) * cap, cap)], target,
                            r_send.at[a, j, k, 1], r_recv.at[a, j, k, 1],
                        )
                    continue
                returns[a, k, j, c] = remote(
                    "fsdp", to * 2 + (core ^ c), first.at[a, j, k, 1, pl.ds((core ^ c) * cap, cap)], target,
                    r_send.at[a, j, k, c], r_recv.at[a, j, k, c],
                )

    staged = {}

    def weight_grads(j, which):
        left, right, out = ((R, I, dw_in), (A, G, dw_out))[which]
        for m in range(left.shape[2] // GRAD):
            slot = m % 2
            lanes = slice(m * GRAD, (m + 1) * GRAD)
            if slot in staged:
                staged.pop(slot).wait()

            @pl.loop(0, right.shape[2] // TILE)
            def _(t):
                cols = pl.ds(pl.multiple_of(t * TILE, TILE), TILE)
                stage[slot, :, cols] = transposed_times(left[j, :, lanes], right[j, :, cols])

            staged[slot] = local(stage.at[slot], out.at[j, lanes], store.at[slot])

    mine = [
        local(up_rows.at[k, j], U.at[j, rows_of(k, me)], own.at[5 + k * 2 + j])
        for k in range(chips)
        for j in range(2)
    ]
    spread_out(0, 0)
    for j in range(2):
        loads.append(local(w_in.at[j], W1.at[j], load.at[j]))
        loads.append(local(w_out.at[j], W2.at[j], load.at[2 + j]))
    loads.append(local(route, RT, load.at[4]))
    z_arrived(0)
    spread_out(1, 0)
    spread_out(0, 1)
    for copy in mine + loads:
        copy.wait()
    for k in range(chips):
        relay(0, k)
        relay(1, k)
        if k + 1 < chips:
            z_arrived(k + 1)
            spread_out(1, k + 1)
        if k + 2 < chips:
            spread_out(0, k + 2)
        all_arrived(0, k)
        all_arrived(1, k)
        experts(k, 0)
        collect_one(k, 0)
        if k:
            collect_two(k - 1, 0)
            collect_two(k - 1, 1)
        experts(k, 1)
        collect_one(k, 1)
        if k:
            collect_three(k - 1, 0)
            collect_three(k - 1, 1)
    last = chips - 1
    weight_grads(0, 0)
    collect_two(last, 0)
    collect_two(last, 1)
    weight_grads(0, 1)
    weight_grads(1, 0)
    collect_three(last, 0)
    collect_three(last, 1)
    weight_grads(1, 1)
    for copy in staged.values():
        copy.wait()
    for copy in dispatched:
        copy.wait_send()
    for copy in sent.values():
        copy.wait_send()
    for copy in summed.values():
        copy.wait_send()
    for (a, k, j, c), copy in returns.items():
        copy.wait()


def moe(send_rows, up_rows, route, w_in, w_out, experts_all, number):
    S, low, dma = jax.ShapeDtypeStruct, jnp.bfloat16, pltpu.SemaphoreType.DMA
    owners, _, cap, width = send_rows.shape
    chips = owners // 2
    hidden_units = w_in.shape[2]
    count = owners * cap * 4
    part = 2 * cap

    def vmem(*shape, dtype=low):
        return pltpu.VMEM(shape, dtype)

    return pl.pallas_call(
        functools.partial(moe_kernel, chips, cap, experts_all),
        out_shape=(
            S((2, owners, 2, cap, width), low),
            S(w_in.shape, jnp.float32),
            S(w_out.shape, jnp.float32),
        ),
        in_specs=[ANY] * 5,
        out_specs=(ANY,) * 3,
        scratch_shapes=[
            vmem(2, count, width),
            vmem(2, count, width),
            vmem(2, count, width),
            vmem(2, count, hidden_units),
            vmem(2, count, hidden_units),
            vmem(2, 2, count, width),
            vmem(2, 2, chips, 2, part, width),
            vmem(2, 2, chips, part, width),
            vmem(*w_in.shape),
            vmem(*w_out.shape),
            vmem(*route.shape),
            vmem(2, GRAD, max(width, hidden_units), dtype=jnp.float32),
            dma((5,)),
            dma((5 + 2 * chips,)),
            dma((chips, 2)),
            dma((chips, 2)),
            dma((2, chips, 2, 2)),
            dma((2, chips, 2, 2)),
            dma((2, chips, 2)),
            dma((2, chips, 2)),
            dma((2, 2, chips, 2)),
            dma((2, 2, chips, 2)),
            dma((2, 2, chips)),
            dma((2, 2, chips)),
            dma((2, 2, chips, 2)),
            dma((2, 2, chips, 2)),
            dma((2,)),
        ],
        compiler_params=pltpu.CompilerParams(
            collective_id=number, has_side_effects=True, vmem_limit_bytes=58 * 2**20
        ),
        cost_estimate=pl.CostEstimate(
            flops=12 * 2 * count * width * hidden_units, bytes_accessed=2**25, transcendentals=0
        ),
    )(send_rows, up_rows, route, w_in, w_out)


def front_kernel(
    count, cap, hidden, heads, mix, small, rows,
    hidden_all, heads_all, mix_all, small_all, up, staged,
    h_send, h_recv, q_send, q_recv, f_send, f_recv, n_send, n_recv, u_send, u_recv, m_send, m_recv, local,
):
    me, place = lax.axis_index("seq"), lax.axis_index("fsdp")
    one, two, both = me ^ 1, me ^ 2, me ^ 3
    others = (one, two, both)
    chips = count // 2
    chip, core = place // 2, lax.rem(place, 2)
    sibling = place ^ 1
    barrier = pltpu.get_barrier_semaphore()
    for peer in others:
        pl.semaphore_signal(barrier, inc=1, device_id={"seq": peer}, device_id_type=MESH)
    for step in range(1, count):
        pl.semaphore_signal(
            barrier, inc=1, device_id={"fsdp": lax.rem(place + step, count)}, device_id_type=MESH
        )
    pl.semaphore_wait(barrier, 3 + count - 1)
    started = []

    def keep(source, target, number):
        copy = pltpu.make_async_copy(source, target, local.at[number])
        copy.start()
        return copy

    def far(k, sign):
        return lax.rem(chip + sign * k + chips, chips) * 2 + core

    exchanged = [
        remote("seq", peer, heads.at[peer], staged.at[me], q_send.at[i], q_recv.at[i])
        for i, peer in enumerate(others)
    ]
    own_heads = keep(heads.at[me], staged.at[me], 0)
    kept = [
        keep(hidden, hidden_all.at[me], 1),
        keep(mix, mix_all.at[me, place], 2),
        keep(small, small_all.at[me, place], 3),
        keep(rows.at[place], up.at[0, :, pl.ds(core * cap, cap)], 4),
    ]
    gathered = ((mix, mix_all), (small, small_all), (staged, heads_all))

    def block(a, owner):
        return gathered[a][1].at[:, owner] if a == 2 else gathered[a][1].at[me, owner]

    away, near = {}, {}

    def send_own(a):
        for k in range(1, chips):
            away[a, k] = remote(
                "fsdp", far(k, -1), gathered[a][0], block(a, place), f_send.at[a, k], f_recv.at[a, k]
            )
        near[a, 0] = remote(
            "fsdp", sibling, gathered[a][0], block(a, place), n_send.at[a, 0], n_recv.at[a, 0]
        )

    def pass_on(a, k):
        away[a, k].wait_recv()
        arrived = block(a, far(k, 1))
        near[a, k] = remote("fsdp", sibling, arrived, arrived, n_send.at[a, k], n_recv.at[a, k])

    send_own(0)
    send_own(1)
    half = hidden.shape[0] // 2
    parts = (pl.ds(0, half), pl.ds(half, half))
    direct = {}
    for side, peer in enumerate((one, two)):
        for order in range(2):
            p = (order + side) % 2
            direct[side, p] = remote(
                "seq", peer, hidden.at[parts[p]], hidden_all.at[me, parts[p]], h_send.at[side, p], h_recv.at[side, p]
            )
    own_heads.wait()
    for copy in exchanged:
        copy.wait_recv()
    kept.append(keep(staged, heads_all.at[:, place], 5))
    send_own(2)
    for k in range(chips):
        for c in range(2):
            if k == 0 and c == 0:
                continue
            peer = lax.rem(chip - k + chips, chips) * 2 + (core ^ c)
            started.append(
                remote(
                    "fsdp", peer, rows.at[peer], up.at[k, :, pl.ds(core * cap, cap)], u_send.at[k, c], u_recv.at[k, c]
                )
            )
    for side, (origin, peer) in enumerate(((one, two), (two, one))):
        direct[side, side].wait_recv()
        source = hidden_all.at[origin, parts[side]]
        direct[2, side] = remote("seq", peer, source, source, h_send.at[2, side], h_recv.at[2, side])
    for k in range(1, chips):
        pass_on(0, k)
        pass_on(1, k)
    for copy in kept[1:3]:
        copy.wait()
    for k in range(chips):
        near[0, k].wait_recv()
        near[1, k].wait_recv()
    shares = (pl.ds(0, count // 2), pl.ds(count // 2, count // 2))
    for side, peer in enumerate((one, two)):
        for order in range(2):
            p = (order + side) % 2
            source = mix_all.at[me, shares[p]]
            direct[3 + side, p] = remote("seq", peer, source, source, m_send.at[side, p], m_recv.at[side, p])
    for i, peer in enumerate(others):
        started.append(
            remote("seq", peer, small_all.at[me], small_all.at[me], m_send.at[3 + i, 0], m_recv.at[3 + i, 0])
        )
    for k in range(1, chips):
        pass_on(2, k)
    for side, (origin, peer) in enumerate(((one, two), (two, one))):
        direct[3 + side, side].wait_recv()
        source = mix_all.at[origin, shares[side]]
        direct[5, side] = remote("seq", peer, source, source, m_send.at[2, side], m_recv.at[2, side])
    for side in range(2):
        for first in (0, 3):
            direct[first + side, 1 - side].wait_recv()
        for last in (2, 5):
            direct[last, side].wait_recv()
    for k in range(chips):
        near[2, k].wait_recv()
    for copy in (*direct.values(), *exchanged, *away.values(), *near.values()):
        copy.wait_send()
    for copy in started:
        copy.wait()
    for i in (0, 3, 4):
        kept[i].wait()


def front(hidden, heads, mix, small, rows, number):
    S, dma = jax.ShapeDtypeStruct, pltpu.SemaphoreType.DMA
    count, _, cap, width = rows.shape
    chips = count // 2
    return call(
        functools.partial(front_kernel, count, cap),
        (hidden, heads, mix, small, rows),
        (
            S((4, *hidden.shape), hidden.dtype),
            S((4, count, *heads.shape[1:]), heads.dtype),
            S((4, count, *mix.shape), mix.dtype),
            S((4, count, *small.shape), small.dtype),
            S((chips, 2, 2 * cap, width), rows.dtype),
        ),
        [
            pltpu.VMEM(heads.shape, heads.dtype),
            dma((3, 2)), dma((3, 2)), dma((3,)), dma((3,)),
            dma((3, chips)), dma((3, chips)), dma((3, chips)), dma((3, chips)),
            dma((chips, 2)), dma((chips, 2)), dma((6, 2)), dma((6, 2)), dma((6,)),
        ],
        number,
    )


def tail_kernel(
    chips, part, grad_heads, grad_mix, grad_small, normed_out, heads_out, mix_out, small_out,
    own_a, own_b, own_c, sib_a, sib_b, sib_c, got_a, got_b, got_c, total_a, total_b, total_c, mine, first, second,
    b_send, b_recv, z_send, z_recv, x_send, x_recv, c_send, c_recv, load, hold, keep,
):
    grads = (grad_heads, grad_mix, grad_small)
    own, sib, got = (own_a, own_b, own_c), (sib_a, sib_b, sib_c), (got_a, got_b, got_c)
    totals = (total_a, total_b, total_c)
    me, place = lax.axis_index("seq"), lax.axis_index("fsdp")
    one, two, both = me ^ 1, me ^ 2, me ^ 3
    others = (one, two, both)
    chip, core = place // 2, lax.rem(place, 2)
    sibling = place ^ 1
    barrier = pltpu.get_barrier_semaphore()
    for peer in others:
        pl.semaphore_signal(barrier, inc=1, device_id={"seq": peer}, device_id_type=MESH)
    for k in range(1, chips):
        pl.semaphore_signal(
            barrier, inc=1, device_id={"fsdp": lax.rem(chip + k, chips) * 2 + core}, device_id_type=MESH
        )
    pl.semaphore_signal(barrier, inc=1, device_id={"fsdp": sibling}, device_id_type=MESH)
    pl.semaphore_wait(barrier, 3 + chips)

    def local(source, to, sem):
        copy = pltpu.make_async_copy(source, to, sem)
        copy.start()
        return copy

    def view(a, owner):
        return grads[a].at[owner] if a == 1 else grads[a].at[:, owner]

    half = part.shape[1] // 2
    sums, held = {}, {}
    to_sibling, owned, away = {}, {}, {}
    order_of = [*range(1, chips), 0]
    for k in order_of:
        to = lax.rem(chip + k, chips) * 2
        for a in range(3):
            to_sibling[a, k] = remote(
                "fsdp", sibling, view(a, to + (core ^ 1)), sib[a].at[k], b_send.at[a, k], b_recv.at[a, k]
            )
            owned[a, k] = local(view(a, to + core), own[a].at[k], load.at[a, k])
    for side, (near, rest) in enumerate(((one, two), (two, one))):
        rows = pl.ds(side * half, half)
        for order, block in enumerate((both, near)):
            sums[side, order] = remote(
                "seq", near, part.at[block, rows], first.at[side, order], c_send.at[side, order], c_recv.at[side, order]
            )
        for order, block in enumerate((rest, me)):
            held[side, order] = local(part.at[block, rows], mine.at[side, order], hold.at[side, order])
    for k in order_of:
        for a in range(3):
            owned[a, k].wait()
            to_sibling[a, k].wait_recv()
            own[a][k] = (own[a][k].astype(jnp.float32) + sib[a][k].astype(jnp.float32)).astype(own[a].dtype)
            if k:
                away[a, k] = remote(
                    "fsdp", lax.rem(chip + k, chips) * 2 + core, own[a].at[k], got[a].at[k], z_send.at[a, k], z_recv.at[a, k]
                )
    for side, rest in enumerate((two, one)):
        sums[side, 0].wait_recv()
        held[side, 0].wait()
        first[side, 0] = (
            first[side, 0].astype(jnp.float32) + mine[side, 0].astype(jnp.float32)
        ).astype(first.dtype)
        sums[side, 2] = remote("seq", rest, first.at[side, 0], second.at[side], c_send.at[2, side], c_recv.at[2, side])
    stored = []
    for side in range(2):
        sums[side, 1].wait_recv()
        held[side, 1].wait()
        sums[side, 2].wait_recv()
        mine[side, 1] = (
            mine[side, 1].astype(jnp.float32)
            + first[side, 1].astype(jnp.float32)
            + second[side].astype(jnp.float32)
        ).astype(mine.dtype)
        stored.append(local(mine.at[side, 1], normed_out.at[pl.ds(side * half, half)], keep.at[side]))
    for a in range(3):
        total = own[a][0].astype(jnp.float32)
        for k in range(1, chips):
            away[a, k].wait_recv()
            total = total + got[a][k].astype(jnp.float32)
        totals[a][...] = total.astype(totals[a].dtype)
    crossed = []
    for a, out in ((0, heads_out), (2, small_out)):
        for i, peer in enumerate(others):
            crossed.append(remote("seq", peer, totals[a].at[peer], out.at[me], x_send.at[a, i], x_recv.at[a, i]))
        stored.append(local(totals[a].at[me], out.at[me], keep.at[3 + a // 2]))
    stored.append(local(totals[1], mix_out, keep.at[2]))
    for copy in (*stored, *crossed):
        copy.wait()
    for copy in (*sums.values(), *to_sibling.values(), *away.values()):
        copy.wait_send()


def tail(part, grad_heads, grad_mix, grad_small, number):
    S, dma, f32 = jax.ShapeDtypeStruct, pltpu.SemaphoreType.DMA, jnp.float32
    owners = grad_mix.shape[0]
    chips = owners // 2
    pieces = (
        ((4, *grad_heads.shape[2:]), grad_heads.dtype),
        (grad_mix.shape[1:], grad_mix.dtype),
        ((4, *grad_small.shape[2:]), grad_small.dtype),
    )
    sets = [pltpu.VMEM((chips, *shape), dtype) for _ in range(3) for shape, dtype in pieces]
    half = (part.shape[1] // 2, part.shape[2])
    return call(
        functools.partial(tail_kernel, chips),
        (part, grad_heads, grad_mix, grad_small),
        (
            S(part.shape[1:], part.dtype),
            S(*pieces[0]),
            S(grad_mix.shape[1:], f32),
            S(*pieces[2]),
        ),
        [
            *sets,
            pltpu.VMEM(*pieces[0]),
            pltpu.VMEM(pieces[1][0], f32),
            pltpu.VMEM(*pieces[2]),
            pltpu.VMEM((2, 2, *half), part.dtype),
            pltpu.VMEM((2, 2, *half), part.dtype),
            pltpu.VMEM((2, *half), part.dtype),
            dma((3, chips)), dma((3, chips)), dma((3, chips)), dma((3, chips)),
            dma((3, 3)), dma((3, 3)), dma((3, 2)), dma((3, 2)),
            dma((3, chips)), dma((2, 2)), dma((5,)),
        ],
        number,
    )


def masked_scores(block_query, keys, start, length, scale):
    scores = (
        jnp.einsum("qhd,khd->hqk", block_query, keys, preferred_element_type=jnp.float32) * scale
    )
    rows = start + jnp.arange(block_query.shape[0], dtype=jnp.int32)
    columns = jnp.arange(keys.shape[0], dtype=jnp.int32)
    keep = (columns[None, :] <= rows[:, None]) & (columns[None, :] < length)
    return jnp.where(keep[None], scores, MASKED)


def shards(
    hidden,
    lengths,
    expert_ids,
    attn_gain,
    qkv_weight,
    out_weight,
    moe_gain,
    router_weight,
    expert_in,
    expert_out,
    out_grad,
):
    S = jax.ShapeDtypeStruct
    low = jnp.bfloat16
    owners = lax.axis_size("fsdp")
    seq_place = lax.axis_index("seq")
    seq_count = lax.axis_size("seq")
    tokens, width = hidden.shape[1], hidden.shape[2]
    full_len = tokens * seq_count
    group_width = width // seq_count
    heads_local = group_width // HEAD_DIM
    rows_own = qkv_weight.shape[0]
    scale = HEAD_DIM ** (-0.5)
    length = lengths[0]
    experts_all = router_weight.shape[1]
    small = jnp.concatenate([router_weight, attn_gain[:, None], moe_gain[:, None]], axis=1)
    small = jnp.pad(small, ((0, 0), (0, -small.shape[1] % 128)))
    expert_local = expert_in.shape[0]
    capacity = -(-max(2, 2 * tokens // experts_all) // 16) * 16
    slots = experts_all * capacity

    position = seq_place * tokens + jnp.arange(tokens, dtype=jnp.int32)
    valid = (position < length).astype(jnp.float32)[:, None]
    chosen = expert_ids[0, :, 0]
    choose = chosen[:, None] == jnp.arange(experts_all, dtype=jnp.int32)[None, :]
    order = jnp.arange(tokens, dtype=jnp.int32)
    earlier = (order[None, :] < order[:, None]) & (chosen[None, :] == chosen[:, None])
    ranks = jnp.sum(earlier.astype(jnp.int32), axis=1)
    slot = chosen * capacity + ranks
    hit = jnp.arange(slots, dtype=jnp.int32)[:, None] == slot[None, :]
    dispatch = hit.astype(low)

    def to_owners(rows, number):
        return exchange(
            "fsdp",
            owners,
            (rows.reshape(owners, expert_local, capacity, width),),
            (S((expert_local, owners, capacity, width), low),),
            ((lead, second),),
            number,
        )[0].reshape(expert_local, owners * capacity, width)

    def to_sources(rows, number):
        return exchange(
            "fsdp",
            owners,
            (rows.reshape(expert_local, owners, capacity, width),),
            (S((owners, expert_local, capacity, width), low),),
            ((second, lead),),
            number,
        )[0].reshape(slots, width)

    upstream_low = jnp.where(valid > 0, out_grad[0], 0).astype(low)
    upstream = upstream_low.astype(jnp.float32)
    up_rows = times(dispatch, upstream_low).astype(low)
    hidden_all, weight_qkv, weight_mix, small, up_all = front(
        hidden[0],
        qkv_weight.reshape(rows_own, 3, seq_count, group_width)
        .transpose(2, 0, 1, 3)
        .reshape(seq_count, rows_own, 3 * group_width),
        out_weight,
        small,
        up_rows.reshape(owners, expert_local, capacity, width),
        0,
    )
    hidden_all = hidden_all.reshape(full_len, width)
    weight_qkv = weight_qkv.reshape(width, 3 * group_width)
    weight_mix = weight_mix.reshape(width, width)
    small = small.reshape(width, -1)
    weight_route = small[:, :experts_all]
    gain_one = small[:, experts_all].astype(jnp.float32)
    gain_two = small[:, experts_all + 1].astype(jnp.float32)
    mix_rows = lax.dynamic_slice_in_dim(weight_mix, seq_place * group_width, group_width, 0)
    fused = expert_local == 2 and 4 * owners * capacity <= 1024
    if not fused:
        up_all = jnp.roll(up_all, lax.axis_index("fsdp") // 2, axis=0)
        up_all = up_all.transpose(1, 0, 2, 3).reshape(expert_local, owners * capacity, width)
        up_all = spread(up_all, 1)

    hidden_wide = hidden_all.astype(jnp.float32)
    shrunk = hidden_wide * lax.rsqrt(jnp.mean(hidden_wide * hidden_wide, axis=-1, keepdims=True) + EPS)
    normed = (shrunk * gain_one).astype(low)
    projected = times(normed, weight_qkv).astype(low)
    query = projected[:, :group_width].reshape(full_len, heads_local, HEAD_DIM)
    keys = projected[:, group_width : 2 * group_width].reshape(full_len, heads_local, HEAD_DIM)
    values = projected[:, 2 * group_width :].reshape(full_len, heads_local, HEAD_DIM)
    starts = list(range(0, full_len, QBLOCK))
    outputs = []
    totals = []
    for start in starts:
        block_query = query[start : start + QBLOCK]
        reach = start + QBLOCK
        scores = masked_scores(block_query, keys[:reach], start, length, scale)
        top = jnp.max(scores, axis=-1, keepdims=True)
        total = top + jnp.log(jnp.sum(jnp.exp(scores - top), axis=-1, keepdims=True))
        probs = jnp.exp(scores - total).astype(low)
        block_out = jnp.einsum("hqk,khd->qhd", probs, values[:reach], preferred_element_type=jnp.float32)
        outputs.append(block_out.astype(low))
        totals.append(total)
    attended = jnp.concatenate(outputs, axis=0).reshape(full_len, group_width)
    mixed = exchange(
        "seq",
        seq_count,
        (attended.reshape(seq_count, tokens, group_width),),
        (S((seq_count, tokens, group_width), low),),
        ((lead, lead),),
        4,
    )[0]
    mixed = mixed.transpose(1, 0, 2).reshape(tokens, width)
    inputs = hidden[0].astype(jnp.float32)
    middle = inputs + times(mixed, weight_mix)
    normed_two, norm_two_back = jax.vjp(scaled_norm, middle, gain_two)
    normed_two = normed_two.astype(low)
    logits = times(normed_two, weight_route)

    def gate_of(logit_rows):
        return jnp.sum(jnp.where(choose, jax.nn.softmax(logit_rows, axis=-1), 0.0), axis=-1)

    gate, gate_back = jax.vjp(gate_of, logits)
    sent = times(dispatch, normed_two).astype(low)
    if fused:
        (returned, grad_back), expert_in_grad, expert_out_grad = moe(
            sent.reshape(owners, expert_local, capacity, width),
            up_all,
            small,
            expert_in,
            expert_out,
            experts_all,
            5,
        )
        returned, grad_back = returned.reshape(slots, width), grad_back.reshape(slots, width)
    else:
        gate_rows = jnp.sum(jnp.where(hit, gate[None, :], 0.0), axis=1)
        gates = lax.all_to_all(
            gate_rows.reshape(owners, expert_local, capacity), "fsdp", split_axis=0, concat_axis=0, tiled=True
        )
        gates = lax.all_gather(gates, "seq", axis=0)
        gates = gates.transpose(2, 0, 1, 3).reshape(expert_local, seq_count * owners * capacity, 1)

        rows_all = spread(to_owners(sent, 5), 6)
        count = seq_count * owners * capacity
        rows_all = rows_all.reshape(expert_local, count, width)
        up_all = up_all.reshape(expert_local, count, width)
        grad_rows = (up_all.astype(jnp.float32) * gates).astype(low)

        def per_expert(form, left, right):
            return jnp.einsum(form, left, right, preferred_element_type=jnp.float32)

        inner = per_expert("jrd,jdf->jrf", rows_all, expert_in)
        active, active_back = jax.vjp(gelu_tanh, inner)
        active = active.astype(low)
        partial_out = per_expert("jrf,jfd->jrd", active, expert_out).astype(low)
        grad_active = per_expert("jrd,jfd->jrf", grad_rows, expert_out)
        grad_inner = active_back(grad_active)[0].astype(low)
        partial_back = per_expert("jrf,jdf->jrd", grad_inner, expert_in).astype(low)
        expert_out_grad = per_expert("jrf,jrd->jfd", active, grad_rows)
        expert_in_grad = per_expert("jrd,jrf->jdf", rows_all, grad_inner)

        shape = (expert_local, seq_count, owners * capacity, width)
        returned = to_sources(collect(partial_out.reshape(shape), 7), 8)
        grad_back = to_sources(collect(partial_back.reshape(shape), 9), 10)

    back_rows = transposed_times(dispatch, returned)
    output = valid * (middle + gate[:, None] * back_rows)
    grad_gate = jnp.sum(upstream * back_rows, axis=1)
    grad_logits = gate_back(grad_gate)[0].astype(low)
    grad_normed_two = times_transposed(grad_logits, weight_route) + transposed_times(dispatch, grad_back)
    grad_middle, grad_gain_two = norm_two_back(grad_normed_two)
    grad_middle = grad_middle + upstream
    grad_attn = grad_middle.astype(low)

    grad_attn_all = spread(grad_attn[None], 11).reshape(full_len, width)
    grad_mix = transposed_times(attended, grad_attn_all)
    grad_heads = times_transposed(grad_attn_all, mix_rows).astype(low)
    grad_heads = grad_heads.reshape(full_len, heads_local, HEAD_DIM)
    grad_query = []
    grad_keys = jnp.zeros((full_len, heads_local, HEAD_DIM), jnp.float32)
    grad_values = jnp.zeros((full_len, heads_local, HEAD_DIM), jnp.float32)
    for number, start in enumerate(starts):
        reach = start + QBLOCK
        block_query = query[start : start + QBLOCK]
        scores = masked_scores(block_query, keys[:reach], start, length, scale)
        probs = jnp.exp(scores - totals[number])
        probs_low = probs.astype(low)
        grad_out = grad_heads[start : start + QBLOCK]
        grad_values = grad_values.at[:reach].add(
            jnp.einsum("hqk,qhd->khd", probs_low, grad_out, preferred_element_type=jnp.float32)
        )
        grad_probs = jnp.einsum(
            "qhd,khd->hqk", grad_out, values[:reach], preferred_element_type=jnp.float32
        )
        grad_scores = (
            probs * (grad_probs - jnp.sum(grad_probs * probs, axis=-1, keepdims=True))
        ).astype(low)
        grad_query.append(
            jnp.einsum("hqk,khd->qhd", grad_scores, keys[:reach], preferred_element_type=jnp.float32)
            * scale
        )
        grad_keys = grad_keys.at[:reach].add(
            jnp.einsum("hqk,qhd->khd", grad_scores, block_query, preferred_element_type=jnp.float32)
            * scale
        )
    grad_projected = jnp.concatenate(
        [
            part.astype(low).reshape(full_len, group_width)
            for part in (jnp.concatenate(grad_query, axis=0), grad_keys, grad_values)
        ],
        axis=1,
    )
    grad_qkv_cols = transposed_times(normed, grad_projected).astype(low)
    partial_normed = times_transposed(grad_projected, weight_qkv)
    grad_gain_one = jnp.sum(partial_normed * shrunk, axis=0)
    small_grad = jnp.concatenate(
        [transposed_times(grad_logits, normed_two), grad_gain_one[None], grad_gain_two[None]], axis=0
    )
    kinds = small_grad.shape[0]
    small_grad = (
        small_grad.reshape(kinds, seq_count, owners, rows_own)
        .transpose(1, 2, 0, 3)
        .reshape(seq_count, owners, kinds * rows_own)
    )
    padded = -(-kinds * rows_own // 1024) * 1024
    small_grad = jnp.pad(small_grad, ((0, 0), (0, 0), (0, padded - kinds * rows_own)))
    grad_normed, qkv_sum, mix_grad, small_sum = tail(
        partial_normed.astype(low).reshape(seq_count, tokens, width),
        grad_qkv_cols.reshape(seq_count, owners, rows_own, 3 * group_width),
        grad_mix.astype(low).reshape(owners, rows_own, width),
        small_grad.reshape(seq_count, owners, padded // 128, 128),
        12,
    )
    qkv_weight_grad = (
        qkv_sum.astype(jnp.float32)
        .reshape(seq_count, rows_own, 3, group_width)
        .transpose(1, 2, 0, 3)
        .reshape(rows_own, 3 * width)
    )
    small_sum = jnp.sum(small_sum, axis=0).reshape(padded)[: kinds * rows_own].reshape(kinds, rows_own)
    _, norm_back = jax.vjp(scaled_norm, inputs, gain_one)
    grad_inputs = norm_back(grad_normed.astype(jnp.float32))[0] + grad_middle
    return (
        output.astype(low)[None],
        grad_inputs[None],
        small_sum[experts_all],
        qkv_weight_grad,
        mix_grad,
        small_sum[experts_all + 1],
        small_sum[:experts_all].T,
        expert_in_grad,
        expert_out_grad,
    )


def solution(mesh):
    placed = (
        P("fsdp", "seq", None),
        P("fsdp"),
        P("fsdp", "seq", None),
        P(("seq", "fsdp")),
        P(("seq", "fsdp"), None),
        P(("seq", "fsdp"), None),
        P(("seq", "fsdp")),
        P(("seq", "fsdp"), None),
        P("fsdp", None, "seq"),
        P("fsdp", "seq", None),
        P("fsdp", "seq", None),
    )
    return jax.shard_map(
        shards,
        mesh=mesh,
        in_specs=placed,
        out_specs=(
            P("fsdp", "seq", None),
            P("fsdp", "seq", None),
            P(("seq", "fsdp")),
            P(("seq", "fsdp"), None),
            P(("seq", "fsdp"), None),
            P(("seq", "fsdp")),
            P(("seq", "fsdp"), None),
            P("fsdp", None, "seq"),
            P("fsdp", "seq", None),
        ),
        check_vma=False,
    )
```

```python
import functools

import jax
import jax.numpy as jnp
from jax import lax
from jax.experimental import pallas as pl
from jax.experimental.pallas import tpu as pltpu
from jax.sharding import PartitionSpec as P

HEAD_DIM = 64
EPS = 1e-05
MASKED = -1e30
ROOT = 0.7978845608028654
TILE = 256
GRAD = 256
MESH = pl.DeviceIdType.MESH
ANY = pl.BlockSpec(memory_space=pl.ANY)


def scaled_norm(value, gain):
    return value * lax.rsqrt(jnp.mean(value * value, axis=-1, keepdims=True) + EPS) * gain


def gelu_tanh(value):
    return jax.nn.gelu(value, approximate=True)


def times(left, right):
    return jnp.dot(left, right, preferred_element_type=jnp.float32)


def times_transposed(left, right):
    return lax.dot_general(
        left, right, (((1,), (1,)), ((), ())), preferred_element_type=jnp.float32
    )


def transposed_times(left, right):
    return lax.dot_general(
        left, right, (((0,), (0,)), ((), ())), preferred_element_type=jnp.float32
    )


def greet(axis, peers):
    barrier = pltpu.get_barrier_semaphore()
    for peer in peers:
        pl.semaphore_signal(barrier, inc=1, device_id={axis: peer}, device_id_type=MESH)
    pl.semaphore_wait(barrier, len(peers))


def remote(axis, peer, source, target, send, receive):
    copy = pltpu.make_async_remote_copy(
        source, target, send, receive, device_id={axis: peer}, device_id_type=MESH
    )
    copy.start()
    return copy


def call(kernel, inputs, outputs, scratch, number):
    return pl.pallas_call(
        kernel,
        out_shape=outputs,
        in_specs=[ANY] * len(inputs),
        out_specs=jax.tree.map(lambda _: ANY, outputs),
        scratch_shapes=scratch,
        compiler_params=pltpu.CompilerParams(
            collective_id=number, has_side_effects=True, vmem_limit_bytes=48 * 2**20
        ),
    )(*inputs)


def exchange_kernel(axis, count, views, *refs):
    arrays = len(views)
    sources, targets = refs[:arrays], refs[arrays : 2 * arrays]
    send, receive, local = refs[2 * arrays :]
    me = lax.axis_index(axis)
    peers = [lax.rem(me + step, count) for step in range(1, count)]
    greet(axis, peers)
    copies = []
    for step, peer in enumerate(peers):
        for a, (out_of, into) in enumerate(views):
            copies.append(
                remote(
                    axis,
                    peer,
                    out_of(sources[a], peer),
                    into(targets[a], me),
                    send.at[a, step],
                    receive.at[a, step],
                )
            )
    for a, (out_of, into) in enumerate(views):
        copy = pltpu.make_async_copy(out_of(sources[a], me), into(targets[a], me), local.at[a])
        copy.start()
        copies.append(copy)
    for copy in copies:
        copy.wait()


def exchange(axis, count, inputs, outputs, views, number):
    arrays = len(views)
    return call(
        functools.partial(exchange_kernel, axis, count, views),
        inputs,
        outputs,
        [
            pltpu.SemaphoreType.DMA((arrays, count - 1)),
            pltpu.SemaphoreType.DMA((arrays, count - 1)),
            pltpu.SemaphoreType.DMA((arrays,)),
        ],
        number,
    )


def lead(ref, place):
    return ref.at[place]


def second(ref, place):
    return ref.at[:, place]


def whole(ref, place):
    return ref


def spread_kernel(source, target, send, receive, local):
    me = lax.axis_index("seq")
    one, two, both = me ^ 1, me ^ 2, me ^ 3
    half = source.shape[1] // 2
    greet("seq", [one, two])
    parts = (pl.ds(0, half), pl.ds(half, half))
    own = pltpu.make_async_copy(source, target.at[:, me], local)
    own.start()
    copies = {}
    for side, peer in enumerate((one, two)):
        for order in range(2):
            part = (order + side) % 2
            copies[side, part] = remote(
                "seq",
                peer,
                source.at[:, parts[part]],
                target.at[:, me, parts[part]],
                send.at[side, part],
                receive.at[side, part],
            )
    relayed = []
    for side, (origin, peer) in enumerate(((one, two), (two, one))):
        copies[side, side].wait_recv()
        block = target.at[:, origin, parts[side]]
        relayed.append(remote("seq", peer, block, block, send.at[2, side], receive.at[2, side]))
    for side in range(2):
        copies[side, 1 - side].wait_recv()
        for part in range(2):
            copies[side, part].wait_send()
    for copy in relayed:
        copy.wait()
    own.wait()


def spread(source, number):
    return call(
        spread_kernel,
        (source,),
        jax.ShapeDtypeStruct((source.shape[0], 4, *source.shape[1:]), source.dtype),
        [
            pltpu.SemaphoreType.DMA((3, 2)),
            pltpu.SemaphoreType.DMA((3, 2)),
            pltpu.SemaphoreType.DMA,
        ],
        number,
    )


def collect_kernel(source, target, mine, first, second_in, outgoing, load, send, receive, store):
    me = lax.axis_index("seq")
    one, two, both = me ^ 1, me ^ 2, me ^ 3
    width = source.shape[3] // 2
    greet("seq", [one, two])
    copies = []
    for side, (near, rest) in enumerate(((one, two), (two, one))):
        lanes = pl.ds(side * width, width)
        for order, block in enumerate((both, near)):
            copies.append(
                remote(
                    "seq",
                    near,
                    source.at[:, block, :, lanes],
                    first.at[side, order],
                    send.at[side, order],
                    receive.at[side, order],
                )
            )
        for order, block in enumerate((rest, me)):
            pltpu.make_async_copy(
                source.at[:, block, :, lanes], mine.at[side, order], load.at[side, order]
            ).start()
    passed = []
    for side, rest in enumerate((two, one)):
        copies[side * 2].wait_recv()
        pltpu.make_async_copy(mine.at[side, 0], mine.at[side, 0], load.at[side, 0]).wait()
        outgoing[side] = (
            mine[side, 0].astype(jnp.float32) + first[side, 0].astype(jnp.float32)
        ).astype(outgoing.dtype)
        passed.append(
            remote("seq", rest, outgoing.at[side], second_in.at[side], send.at[2, side], receive.at[2, side])
        )
    for side in range(2):
        copies[side * 2 + 1].wait_recv()
        pltpu.make_async_copy(mine.at[side, 1], mine.at[side, 1], load.at[side, 1]).wait()
        passed[side].wait_recv()
        mine[side, 1] = (
            mine[side, 1].astype(jnp.float32)
            + first[side, 1].astype(jnp.float32)
            + second_in[side].astype(jnp.float32)
        ).astype(mine.dtype)
        out = pltpu.make_async_copy(
            mine.at[side, 1], target.at[:, :, pl.ds(side * width, width)], store.at[side]
        )
        out.start()
    for side in range(2):
        pltpu.make_async_copy(
            mine.at[side, 1], target.at[:, :, pl.ds(side * width, width)], store.at[side]
        ).wait()
    for copy in copies + passed:
        copy.wait_send()


def collect(source, number):
    a, _, rows, width = source.shape
    dma = pltpu.SemaphoreType.DMA
    block = (a, rows, width // 2)
    return call(
        collect_kernel,
        (source,),
        jax.ShapeDtypeStruct((a, rows, width), source.dtype),
        [
            pltpu.VMEM((2, 2, *block), source.dtype),
            pltpu.VMEM((2, 2, *block), source.dtype),
            pltpu.VMEM((2, *block), source.dtype),
            pltpu.VMEM((2, *block), source.dtype),
            dma((2, 2)),
            dma((3, 2)),
            dma((3, 2)),
            dma((2,)),
        ],
        number,
    )


def moe_kernel(
    chips, cap, experts_all, send_rows, up_rows, route, w_in, w_out,
    ret, dw_in, dw_out,
    R, U, G, A, I, PB, first, second, W1, W2, RT, stage,
    load, own, z_send, z_recv, s_send, s_recv, y_send, y_recv,
    c_send, c_recv, d_send, d_recv, r_send, r_recv, store,
):
    me, place = lax.axis_index("seq"), lax.axis_index("fsdp")
    one, two, both = me ^ 1, me ^ 2, me ^ 3
    chip, core = place // 2, lax.rem(place, 2)
    sibling = place ^ 1
    count = chips * 2
    part = 2 * cap
    chunk = 4 * part
    barrier = pltpu.get_barrier_semaphore()
    for peer in (one, two):
        pl.semaphore_signal(barrier, inc=1, device_id={"seq": peer}, device_id_type=MESH)
    for step in range(1, count):
        pl.semaphore_signal(
            barrier, inc=1, device_id={"fsdp": lax.rem(place + step, count)}, device_id_type=MESH
        )
    pl.semaphore_wait(barrier, 2 + count - 1)

    def rows_of(k, s):
        return pl.ds(k * chunk + s * part, part)

    loads = []

    def local(source, target, sem):
        copy = pltpu.make_async_copy(source, target, sem)
        copy.start()
        return copy

    dispatched = []
    own_rows = None
    for k in range(chips):
        to = lax.rem(chip - k + chips, chips)
        for c in range(2):
            target = R.at[:, pl.ds(k * chunk + me * part + core * cap, cap)]
            if k == 0:
                if c == 0:
                    own_rows = local(send_rows.at[place], target, own.at[0])
                    dispatched.append(
                        remote("fsdp", sibling, send_rows.at[sibling], target, z_send.at[0, 0], z_recv.at[0, 0])
                    )
                continue
            peer = to * 2 + (core ^ c)
            dispatched.append(
                remote("fsdp", peer, send_rows.at[peer], target, z_send.at[k, c], z_recv.at[k, c])
            )

    def z_arrived(k):
        if k == 0:
            own_rows.wait()
            dispatched[0].wait_recv()
        else:
            dispatched[2 * k - 1].wait_recv()
            dispatched[2 * k].wait_recv()

    sent = {}

    def spread_out(k):
        for side, peer in enumerate((one, two)):
            for order in range(2):
                j = (order + side) % 2
                block = R.at[j, rows_of(k, me)]
                sent[k, side, j] = remote("seq", peer, block, block, s_send.at[k, side, j], s_recv.at[k, side, j])

    def relay(k):
        for side, (origin, peer) in enumerate(((one, two), (two, one))):
            sent[k, side, side].wait_recv()
            block = R.at[side, rows_of(k, origin)]
            sent[k, 2, side] = remote("seq", peer, block, block, y_send.at[k, side], y_recv.at[k, side])

    def all_arrived(k):
        for side in range(2):
            sent[k, side, 1 - side].wait_recv()
            sent[k, 2, side].wait_recv()

    def experts(k, j):
        rows = pl.ds(k * chunk, chunk)
        logits = times(R[j, rows, :], RT[...])
        lane = lax.broadcasted_iota(jnp.int32, logits.shape, 1)
        logits = jnp.where(lane < experts_all, logits, MASKED)
        powers = jnp.exp(logits - jnp.max(logits, axis=1, keepdims=True))
        picked = jnp.sum(jnp.where(lane == place * 2 + j, powers, 0.0), axis=1, keepdims=True)
        gate = picked / jnp.sum(powers, axis=1, keepdims=True)
        G[j, rows, :] = (U[j, rows, :].astype(jnp.float32) * gate).astype(G.dtype)

        @pl.loop(0, W1.shape[2] // TILE)
        def _(t):
            cols = pl.ds(pl.multiple_of(t * TILE, TILE), TILE)
            v = times(R[j, rows, :], W1[j, :, cols])
            grad = times_transposed(G[j, rows, :], W2[j, cols, :])
            square = v * v
            t = jnp.tanh(ROOT * v * (1.0 + 0.044715 * square))
            half = 0.5 * (1.0 + t)
            A[j, rows, cols] = (v * half).astype(A.dtype)
            slope = half + 0.5 * v * (1.0 - t * t) * (ROOT * (1.0 + 0.134145 * square))
            I[j, rows, cols] = (grad * slope).astype(I.dtype)

        @pl.loop(0, W1.shape[1] // TILE)
        def _(t):
            cols = pl.ds(pl.multiple_of(t * TILE, TILE), TILE)
            PB[0, j, rows, cols] = times(A[j, rows, :], W2[j, :, cols]).astype(PB.dtype)
            PB[1, j, rows, cols] = times_transposed(I[j, rows, :], W1[j, cols, :]).astype(PB.dtype)

    summed = {}

    def near_of(j):
        return (one, two) if j == 0 else (two, one)

    def collect_one(k, j):
        near, rest = near_of(j)
        for a in range(2):
            for order, block in enumerate((both, near)):
                summed[a, k, j, order] = remote(
                    "seq", near, PB.at[a, j, rows_of(k, block)], first.at[a, j, k, order],
                    c_send.at[a, j, k, order], c_recv.at[a, j, k, order],
                )

    def collect_two(k, j):
        near, rest = near_of(j)
        for a in range(2):
            summed[a, k, j, 0].wait_recv()
            first[a, j, k, 0] = (
                first[a, j, k, 0].astype(jnp.float32) + PB[a, j, rows_of(k, rest), :].astype(jnp.float32)
            ).astype(first.dtype)
            summed[a, k, j, 2] = remote(
                "seq", rest, first.at[a, j, k, 0], second.at[a, j, k], d_send.at[a, j, k], d_recv.at[a, j, k]
            )

    returns = {}

    def collect_three(k, j):
        for a in range(2):
            summed[a, k, j, 1].wait_recv()
            summed[a, k, j, 2].wait_recv()
            first[a, j, k, 1] = (
                first[a, j, k, 1].astype(jnp.float32)
                + PB[a, j, rows_of(k, me), :].astype(jnp.float32)
                + second[a, j, k].astype(jnp.float32)
            ).astype(first.dtype)
            to = lax.rem(chip + k, chips)
            target = ret.at[a, place, j]
            for c in range(2):
                if k == 0:
                    if c == 0:
                        returns[a, k, j, 0] = local(
                            first.at[a, j, k, 1, pl.ds(core * cap, cap)], target, own.at[1 + a * 2 + j]
                        )
                        returns[a, k, j, 1] = remote(
                            "fsdp", sibling, first.at[a, j, k, 1, pl.ds((core ^ 1) * cap, cap)], target,
                            r_send.at[a, j, k, 1], r_recv.at[a, j, k, 1],
                        )
                    continue
                returns[a, k, j, c] = remote(
                    "fsdp", to * 2 + (core ^ c), first.at[a, j, k, 1, pl.ds((core ^ c) * cap, cap)], target,
                    r_send.at[a, j, k, c], r_recv.at[a, j, k, c],
                )

    staged = {}

    def weight_grads(j, which):
        left, right, out = ((R, I, dw_in), (A, G, dw_out))[which]
        for m in range(left.shape[2] // GRAD):
            slot = m % 2
            lanes = slice(m * GRAD, (m + 1) * GRAD)
            if slot in staged:
                staged.pop(slot).wait()

            @pl.loop(0, right.shape[2] // TILE)
            def _(t):
                cols = pl.ds(pl.multiple_of(t * TILE, TILE), TILE)
                stage[slot, :, cols] = transposed_times(left[j, :, lanes], right[j, :, cols])

            staged[slot] = local(stage.at[slot], out.at[j, lanes], store.at[slot])

    for j in range(2):
        loads.append(local(w_in.at[j], W1.at[j], load.at[j]))
        loads.append(local(w_out.at[j], W2.at[j], load.at[2 + j]))
    loads.append(local(route, RT, load.at[4]))
    loads.append(local(up_rows, U, load.at[5]))
    z_arrived(0)
    spread_out(0)
    for copy in loads:
        copy.wait()
    for k in range(chips):
        relay(k)
        if k + 1 < chips:
            z_arrived(k + 1)
            spread_out(k + 1)
        all_arrived(k)
        experts(k, 0)
        collect_one(k, 0)
        if k:
            collect_two(k - 1, 0)
            collect_two(k - 1, 1)
        experts(k, 1)
        collect_one(k, 1)
        if k:
            collect_three(k - 1, 0)
            collect_three(k - 1, 1)
    last = chips - 1
    weight_grads(0, 0)
    collect_two(last, 0)
    collect_two(last, 1)
    weight_grads(0, 1)
    weight_grads(1, 0)
    collect_three(last, 0)
    collect_three(last, 1)
    weight_grads(1, 1)
    for copy in staged.values():
        copy.wait()
    for copy in dispatched:
        copy.wait_send()
    for copy in sent.values():
        copy.wait_send()
    for copy in summed.values():
        copy.wait_send()
    for (a, k, j, c), copy in returns.items():
        copy.wait()


def moe(send_rows, up_rows, route, w_in, w_out, experts_all, number):
    S, low, dma = jax.ShapeDtypeStruct, jnp.bfloat16, pltpu.SemaphoreType.DMA
    owners, _, cap, width = send_rows.shape
    chips = owners // 2
    hidden_units = w_in.shape[2]
    count = owners * cap * 4
    part = 2 * cap

    def vmem(*shape, dtype=low):
        return pltpu.VMEM(shape, dtype)

    return pl.pallas_call(
        functools.partial(moe_kernel, chips, cap, experts_all),
        out_shape=(
            S((2, owners, 2, cap, width), low),
            S(w_in.shape, jnp.float32),
            S(w_out.shape, jnp.float32),
        ),
        in_specs=[ANY] * 5,
        out_specs=(ANY,) * 3,
        scratch_shapes=[
            vmem(2, count, width),
            vmem(2, count, width),
            vmem(2, count, width),
            vmem(2, count, hidden_units),
            vmem(2, count, hidden_units),
            vmem(2, 2, count, width),
            vmem(2, 2, chips, 2, part, width),
            vmem(2, 2, chips, part, width),
            vmem(*w_in.shape),
            vmem(*w_out.shape),
            vmem(*route.shape),
            vmem(2, GRAD, max(width, hidden_units), dtype=jnp.float32),
            dma((6,)),
            dma((5,)),
            dma((chips, 2)),
            dma((chips, 2)),
            dma((chips, 2, 2)),
            dma((chips, 2, 2)),
            dma((chips, 2)),
            dma((chips, 2)),
            dma((2, 2, chips, 2)),
            dma((2, 2, chips, 2)),
            dma((2, 2, chips)),
            dma((2, 2, chips)),
            dma((2, 2, chips, 2)),
            dma((2, 2, chips, 2)),
            dma((2,)),
        ],
        compiler_params=pltpu.CompilerParams(
            collective_id=number, has_side_effects=True, vmem_limit_bytes=58 * 2**20
        ),
        cost_estimate=pl.CostEstimate(
            flops=12 * 2 * count * width * hidden_units, bytes_accessed=2**25, transcendentals=0
        ),
    )(send_rows, up_rows, route, w_in, w_out)


def front_kernel(
    count, cap, experts_all, hidden, heads, mix, small, rows, length,
    normed_out, heads_out, mix_all, small_out, up, projected_out, attended_out, sums_out, mixed,
    staged, hid, heads_all, small_all, normed, proj, attended, sums, acc, stat,
    h_send, h_recv, q_send, q_recv, f_send, f_recv, n_send, n_recv, u_send, u_recv, m_send, m_recv,
    s_send, s_recv, x_send, x_recv, local,
):
    me, place = lax.axis_index("seq"), lax.axis_index("fsdp")
    one, two, both = me ^ 1, me ^ 2, me ^ 3
    others = (one, two, both)
    chips = count // 2
    chip, core = place // 2, lax.rem(place, 2)
    sibling = place ^ 1
    share = mix.shape[0]
    tokens = hidden.shape[0]
    group = attended.shape[1]
    part, chunk = 2 * cap, 8 * cap
    barrier = pltpu.get_barrier_semaphore()
    for peer in others:
        pl.semaphore_signal(barrier, inc=1, device_id={"seq": peer}, device_id_type=MESH)
    for step in range(1, count):
        pl.semaphore_signal(
            barrier, inc=1, device_id={"fsdp": lax.rem(place + step, count)}, device_id_type=MESH
        )
    pl.semaphore_wait(barrier, 3 + count - 1)
    finish = []

    def keep(source, target, number):
        copy = pltpu.make_async_copy(source, target, local.at[number])
        copy.start()
        return copy

    def far(k, sign):
        return lax.rem(chip + sign * k + chips, chips) * 2 + core

    def at_rows(ref, s, owner):
        return ref.at[pl.ds((s * count + owner) * share, share)]

    gathered = ((mix, mix_all), (small, small_all))
    away, near = {}, {}

    def block(a, owner):
        return heads_all.at[:, owner] if a == 2 else at_rows(gathered[a][1], me, owner)

    def send_own(a):
        source = staged if a == 2 else gathered[a][0]
        for k in range(1, chips):
            away[a, k] = remote(
                "fsdp", far(k, -1), source, block(a, place), f_send.at[a, k], f_recv.at[a, k]
            )
        near[a, 0] = remote("fsdp", sibling, source, block(a, place), n_send.at[a, 0], n_recv.at[a, 0])

    def pass_on(a):
        for k in range(1, chips):
            away[a, k].wait_recv()
            arrived = block(a, far(k, 1))
            near[a, k] = remote("fsdp", sibling, arrived, arrived, n_send.at[a, k], n_recv.at[a, k])

    direct = {}

    def both_ways(name, views, sources, send, receive):
        for side, peer in enumerate((one, two)):
            for order in range(2):
                p = (order + side) % 2
                direct[name, side, p] = remote(
                    "seq", peer, sources[p], views[p](me), send.at[side, p], receive.at[side, p]
                )

    def relay(name, views, send, receive):
        for side, (origin, peer) in enumerate(((one, two), (two, one))):
            direct[name, side, side].wait_recv()
            source = views[side](origin)
            direct[name, 2, side] = remote("seq", peer, source, source, send.at[2, side], receive.at[2, side])

    def arrived(name):
        for side in range(2):
            direct[name, side, 1 - side].wait_recv()
            direct[name, 2, side].wait_recv()

    send_own(1)
    exchanged = [
        remote("seq", peer, heads.at[peer], staged.at[me], q_send.at[i], q_recv.at[i])
        for i, peer in enumerate(others)
    ]
    own_heads = keep(heads.at[me], staged.at[me], 0)
    own_hidden = keep(hidden, hid.at[pl.ds(me * tokens, tokens)], 1)
    own_mix = keep(mix, block(0, place), 2)
    own_small = keep(small, block(1, place), 3)
    own_rows = keep(rows.at[place], up.at[:, pl.ds(me * part + core * cap, cap)], 4)
    half = tokens // 2
    hidden_views = [
        lambda origin, p=p: hid.at[pl.ds(origin * tokens + p * half, half)] for p in range(2)
    ]
    both_ways("hidden", hidden_views, [hidden.at[pl.ds(p * half, half)] for p in range(2)], h_send, h_recv)
    send_own(0)
    pass_on(1)
    own_heads.wait()
    for copy in exchanged:
        copy.wait_recv()
    own_block = keep(staged, heads_all.at[:, place], 5)
    send_own(2)
    own_small.wait()
    for k in range(chips):
        near[1, k].wait_recv()
    mine = small_all.at[pl.ds(me * count * share, count * share)]
    smalls = [remote("seq", peer, mine, mine, q_send.at[3 + i], q_recv.at[3 + i]) for i, peer in enumerate(others)]
    moved = {}
    for k in range(chips):
        for c in range(2):
            if k == 0 and c == 0:
                continue
            peer = lax.rem(chip - k + chips, chips) * 2 + (core ^ c)
            moved[k, c] = remote(
                "fsdp", peer, rows.at[peer], up.at[:, pl.ds(k * chunk + me * part + core * cap, cap)],
                u_send.at[k, c], u_recv.at[k, c],
            )

    def up_views(k):
        return [lambda origin, j=j: up.at[j, pl.ds(k * chunk + origin * part, part)] for j in range(2)]

    def up_out(k):
        if k == 0:
            own_rows.wait()
        for c in range(2):
            if (k, c) in moved:
                moved[k, c].wait_recv()
        views = up_views(k)
        both_ways(("up", k), views, [views[0](me), views[1](me)], s_send.at[k], s_recv.at[k])

    def up_relay(k):
        relay(("up", k), up_views(k), s_send.at[k], s_recv.at[k])

    relay("hidden", hidden_views, h_send, h_recv)
    pass_on(0)
    for copy in smalls:
        copy.wait_recv()
    small_kept = keep(small_all, small_out, 6)
    own_hidden.wait()
    arrived("hidden")
    up_out(0)
    own_mix.wait()
    for k in range(chips):
        near[0, k].wait_recv()
    length_rows = count // 2 * share
    mix_views = [
        lambda origin, p=p: mix_all.at[pl.ds(origin * count * share + p * length_rows, length_rows)] for p in range(2)
    ]
    both_ways("mix", mix_views, [mix_views[p](me) for p in range(2)], m_send, m_recv)
    gain = jnp.transpose(small_all[...].astype(jnp.float32))[experts_all : experts_all + 1]

    @pl.loop(0, hid.shape[0] // 128)
    def _(t):
        place_rows = pl.ds(pl.multiple_of(t * 128, 128), 128)
        value = hid[place_rows, :].astype(jnp.float32)
        scale = lax.rsqrt(jnp.mean(value * value, axis=-1, keepdims=True) + EPS)
        normed[place_rows, :] = (value * scale * gain).astype(normed.dtype)

    normed_kept = keep(normed, normed_out, 7)
    pass_on(2)
    own_block.wait()
    for k in range(chips):
        near[2, k].wait_recv()
    heads_kept = keep(heads_all, heads_out, 8)
    width = hid.shape[1]

    for p in range(3):

        @pl.loop(0, hid.shape[0] // TILE)
        def _(t):
            place_rows = pl.ds(pl.multiple_of(t * TILE, TILE), TILE)
            weights = heads_all[:, :, :, p * group : (p + 1) * group].reshape(width, group)
            proj[place_rows, p * group : (p + 1) * group] = times(normed[place_rows, :], weights).astype(proj.dtype)

    projected_kept = keep(proj, projected_out, 9)
    head_of = lax.broadcasted_iota(jnp.int32, (tokens, group), 1) // HEAD_DIM
    sent = []
    for i in range(4):
        own = slice(i * tokens, (i + 1) * tokens)
        reach = (i + 1) * tokens

        @pl.loop(0, group // HEAD_DIM)
        def _(h):
            query = jnp.where(head_of == h, proj[own, :group] * (HEAD_DIM**-0.5), 0).astype(proj.dtype)
            scores = times_transposed(query, proj[:reach, group : 2 * group])
            column = lax.broadcasted_iota(jnp.int32, scores.shape, 1)
            row = lax.broadcasted_iota(jnp.int32, scores.shape, 0) + i * tokens
            scores = jnp.where((column <= row) & (column < length[0]), scores, MASKED)
            top = jnp.max(scores, axis=1, keepdims=True)
            powers = jnp.exp(scores - top)
            total = jnp.sum(powers, axis=1, keepdims=True)
            probs = (powers * (1.0 / total)).astype(proj.dtype)
            out = times(probs, proj[:reach, 2 * group :])
            acc[...] = jnp.where(head_of == h, out, acc[...])
            lane = lax.broadcasted_iota(jnp.int32, stat.shape, 1)
            stat[...] = jnp.where(lane == h, top + jnp.log(total), stat[...])

        attended[own, :] = acc[...].astype(attended.dtype)
        sums[:, own] = jnp.transpose(stat[...])[:8]
        target = mixed.at[:, pl.ds(pl.multiple_of(me * group, group), group)]

        @pl.when(me != i)
        def _():
            remote("seq", i, attended.at[own], target, x_send.at[i], x_recv.at[me])

        @pl.when(me == i)
        def _():
            pltpu.make_async_copy(attended.at[own], target, local.at[10]).start()

        if i == 0:
            up_relay(0)
            relay("mix", mix_views, m_send, m_recv)
        elif i < chips:
            up_relay(i)
        if i + 1 < chips:
            up_out(i + 1)
    for k in range(4, chips):
        up_relay(k)
        if k + 1 < chips:
            up_out(k + 1)
    attended_kept = keep(attended, attended_out, 11)
    sums_kept = keep(sums, sums_out, 12)
    arrived("mix")
    for k in range(chips):
        arrived(("up", k))
    for i in range(4):
        target = mixed.at[:, pl.ds(i * group, group)]

        @pl.when(me != i)
        def _():
            copy = pltpu.make_async_remote_copy(
                attended.at[pl.ds(i * tokens, tokens)], target, x_send.at[i], x_recv.at[i],
                device_id={"seq": i}, device_id_type=MESH,
            )
            copy.wait()

        @pl.when(me == i)
        def _():
            pltpu.make_async_copy(attended.at[pl.ds(i * tokens, tokens)], target, local.at[10]).wait()

    for copy in (*direct.values(), *exchanged, *smalls, *away.values(), *near.values(), *moved.values()):
        copy.wait_send()
    for copy in (small_kept, normed_kept, heads_kept, projected_kept, attended_kept, sums_kept):
        copy.wait()


def front(hidden, heads, mix, small, rows, lengths, experts_all, number):
    S, dma, low = jax.ShapeDtypeStruct, pltpu.SemaphoreType.DMA, jnp.bfloat16
    count, _, cap, width = rows.shape
    chips = count // 2
    tokens = hidden.shape[0]
    group = heads.shape[2] // 3
    full = 4 * tokens
    all_heads = (4, count, *heads.shape[1:])
    return pl.pallas_call(
        functools.partial(front_kernel, count, cap, experts_all),
        out_shape=(
            S((full, width), low),
            S(all_heads, low),
            S((width, mix.shape[1]), low),
            S((width, small.shape[1]), low),
            S((2, 4 * count * cap, width), low),
            S((full, 3 * group), low),
            S((full, group), low),
            S((8, full), jnp.float32),
            S((tokens, width), low),
        ),
        in_specs=[ANY] * 5 + [pl.BlockSpec(memory_space=pltpu.SMEM)],
        out_specs=(ANY,) * 9,
        scratch_shapes=[
            pltpu.VMEM(heads.shape, low),
            pltpu.VMEM((full, width), low),
            pltpu.VMEM(all_heads, low),
            pltpu.VMEM((width, small.shape[1]), low),
            pltpu.VMEM((full, width), low),
            pltpu.VMEM((full, 3 * group), low),
            pltpu.VMEM((full, group), low),
            pltpu.VMEM((8, full), jnp.float32),
            pltpu.VMEM((tokens, group), jnp.float32),
            pltpu.VMEM((tokens, 128), jnp.float32),
            dma((3, 2)), dma((3, 2)), dma((6,)), dma((6,)),
            dma((3, chips)), dma((3, chips)), dma((3, chips)), dma((3, chips)),
            dma((chips, 2)), dma((chips, 2)), dma((3, 2)), dma((3, 2)),
            dma((chips, 3, 2)), dma((chips, 3, 2)), dma((4,)), dma((4,)), dma((13,)),
        ],
        compiler_params=pltpu.CompilerParams(
            collective_id=number, has_side_effects=True, vmem_limit_bytes=48 * 2**20
        ),
    )(hidden, heads, mix, small, rows, lengths)


def back_kernel(
    count, gain_row, grad_in, proj_in, attended_in, sums_in, normed_in, heads_in, mix_in, small_in, length,
    normed_out, heads_out, mix_out, small_out,
    grads, proj, attended, sums, normed, heads, mix, small, grad_heads, delta, masked_grad, masked_query,
    masked_key, masked_value, probs, slopes, grad_query, grad_key, grad_value, grad_proj, part, weights, weights_mix, gain_sum,
    sib_a, sib_b, sib_c, own_a, own_b, own_c, got_a, got_b, got_c, total_a, total_b, total_c, first, second,
    g_send, g_recv, b_send, b_recv, bb_send, bb_recv, z_send, z_recv, x_send, x_recv, c_send, c_recv, load, keep,
):
    me, place = lax.axis_index("seq"), lax.axis_index("fsdp")
    one, two, both = me ^ 1, me ^ 2, me ^ 3
    others = (one, two, both)
    chips = count // 2
    chip, core = place // 2, lax.rem(place, 2)
    sibling = place ^ 1
    tokens, width = grad_in.shape
    group = attended.shape[1]
    share = weights.shape[0] // (4 * count)
    heads_local = group // HEAD_DIM
    low = grads.dtype
    barrier = pltpu.get_barrier_semaphore()
    for peer in others:
        pl.semaphore_signal(barrier, inc=1, device_id={"seq": peer}, device_id_type=MESH)
    for k in range(1, chips):
        pl.semaphore_signal(
            barrier, inc=1, device_id={"fsdp": (chip ^ k) * 2 + core}, device_id_type=MESH
        )
    pl.semaphore_signal(barrier, inc=1, device_id={"fsdp": sibling}, device_id_type=MESH)
    pl.semaphore_wait(barrier, 3 + chips)

    def local(source, to, sem):
        copy = pltpu.make_async_copy(source, to, sem)
        copy.start()
        return copy

    own_grad = local(grad_in, grads.at[pl.ds(me * tokens, tokens)], load.at[0])
    half = tokens // 2
    direct = {}
    for side, peer in enumerate((one, two)):
        for order in range(2):
            p = (order + side) % 2
            direct[side, p] = remote(
                "seq", peer, grad_in.at[pl.ds(p * half, half)], grads.at[pl.ds(me * tokens + p * half, half)],
                g_send.at[side, p], g_recv.at[side, p],
            )
    loads = [
        local(source, to, load.at[1 + i])
        for i, (source, to) in enumerate(
            (
                (proj_in, proj),
                (attended_in, attended),
                (sums_in, sums),
                (mix_in, mix),
                (heads_in, heads),
                (normed_in, normed),
                (small_in, small),
            )
        )
    ]
    for side, (origin, peer) in enumerate(((one, two), (two, one))):
        direct[side, side].wait_recv()
        block = grads.at[pl.ds(origin * tokens + side * half, half)]
        direct[2, side] = remote("seq", peer, block, block, g_send.at[2, side], g_recv.at[2, side])
    for copy in loads:
        copy.wait()
    head_of = lax.broadcasted_iota(jnp.int32, (tokens, group), 1) // HEAD_DIM
    for i in range(4):
        rows = slice(i * tokens, (i + 1) * tokens)
        for h in range(heads_local):
            masked_query[i, h * tokens : (h + 1) * tokens, :] = jnp.where(head_of == h, proj[rows, :group], 0).astype(low)
    own_grad.wait()
    for side in range(2):
        direct[side, 1 - side].wait_recv()
        direct[2, side].wait_recv()

    for n in range(width // TILE):
        lanes = slice(n * TILE, (n + 1) * TILE)
        weights_mix[:, lanes] = transposed_times(attended[...], grads[:, lanes]).astype(low)
    order_of = [*range(1, chips), 0]
    to_sibling, away = {}, {}

    def rows_at(s, owner):
        return pl.ds(pl.multiple_of((s * count + owner) * share, share), share)

    def start_sibling(a, k, core_of):
        owner = (chip ^ k) * 2 + core_of
        if a == 1:
            return [
                remote(
                    "fsdp", sibling, weights_mix.at[pl.ds(pl.multiple_of(owner * share, share), share)], sib_b.at[k],
                    b_send.at[0, k], b_recv.at[0, k],
                )
            ]
        if a == 2:
            return [
                remote(
                    "fsdp", sibling, small.at[:, owner * share // 128], sib_c.at[k], b_send.at[1, k], b_recv.at[1, k]
                )
            ]
        return [
            remote(
                "fsdp", sibling, weights.at[rows_at(s, owner)], sib_a.at[k, pl.ds(s * share, share)],
                bb_send.at[s, k], bb_recv.at[s, k],
            )
            for s in range(4)
        ]

    sib, own, got = (sib_a, sib_b, sib_c), (own_a, own_b, own_c), (got_a, got_b, got_c)
    totals = (total_a, total_b, total_c)

    def pair_sum(a, k):
        owner = (chip ^ k) * 2 + core
        for copy in to_sibling[a, k]:
            copy.wait_recv()
        if a == 0:
            for s in range(4):
                rows = slice(s * share, (s + 1) * share)
                own_a[k, rows, :] = (
                    weights[rows_at(s, owner), :].astype(jnp.float32) + sib_a[k, rows, :].astype(jnp.float32)
                ).astype(low)
        elif a == 1:
            mine = weights_mix[pl.ds(pl.multiple_of(owner * share, share), share), :]
            own_b[k] = (mine.astype(jnp.float32) + sib_b[k].astype(jnp.float32)).astype(low)
        else:
            for s in range(4):
                own_c[k, s] = small[s, owner * share // 128] + sib_c[k, s]
        if k:
            away[a, k] = remote(
                "fsdp", (chip ^ k) * 2 + core, own[a].at[k], got[a].at[k], z_send.at[a, k], z_recv.at[a, k]
            )

    for k in order_of:
        to_sibling[1, k] = start_sibling(1, k, core ^ 1)
    for i in range(4):
        rows = slice(i * tokens, (i + 1) * tokens)
        out = times_transposed(grads[rows, :], mix[...])
        grad_heads[rows, :] = out.astype(low)
        out = grad_heads[rows, :].astype(jnp.float32)
        turned = jnp.transpose(out * attended[rows, :].astype(jnp.float32))
        for h in range(heads_local):
            delta[h : h + 1, rows] = jnp.sum(turned[h * HEAD_DIM : (h + 1) * HEAD_DIM], axis=0, keepdims=True)
            masked_grad[i, h * tokens : (h + 1) * tokens, :] = jnp.where(head_of == h, out, 0).astype(low)
    for k in order_of:
        pair_sum(1, k)

    grad_query[...] = jnp.zeros_like(grad_query)
    gain_sum[...] = jnp.zeros_like(gain_sum)
    for j in range(4):
        own_rows = slice(j * tokens, (j + 1) * tokens)
        for h in range(heads_local):
            key = proj[own_rows, group : 2 * group]
            masked_key[h] = jnp.where(head_of == h, key * (HEAD_DIM**-0.5), 0).astype(low)
            masked_value[h] = jnp.where(head_of == h, proj[own_rows, 2 * group :], 0).astype(low)
        grad_key[...] = jnp.zeros_like(grad_key)
        grad_value[...] = jnp.zeros_like(grad_value)
        key_at = lax.broadcasted_iota(jnp.int32, (tokens, tokens), 0)
        outside = j * tokens + key_at >= length[0]

        def block(i, masked):
            rows = pl.ds(pl.multiple_of(i * tokens, tokens), tokens)
            hidden = outside
            if masked:
                hidden = hidden | (key_at > lax.broadcasted_iota(jnp.int32, (tokens, tokens), 1))
            total = None
            for h in range(heads_local):
                lanes = slice(h * tokens, (h + 1) * tokens)
                scores = times_transposed(masked_key[h], proj[rows, :group])
                scores = jnp.where(hidden, MASKED, scores)
                p = jnp.exp(scores - sums[h : h + 1, rows])
                probs[:, lanes] = p.astype(low)
                grad = times_transposed(masked_value[h], grad_heads[rows, :])
                slopes[:, lanes] = (p * (grad - delta[h : h + 1, rows])).astype(low)
                term = transposed_times(slopes[:, lanes], masked_key[h])
                total = term if total is None else total + term
            grad_query[rows, :] += total
            grad_value[...] += times(probs[...], masked_grad[i])
            grad_key[...] += times(slopes[...], masked_query[i])

        block(j, True)
        if j < 3:

            @pl.loop(j + 1, 4)
            def _(i):
                block(i, False)

        grad_proj[own_rows, :group] = grad_query[own_rows, :].astype(low)
        grad_proj[own_rows, group : 2 * group] = (grad_key[...] * (HEAD_DIM**-0.5)).astype(low)
        grad_proj[own_rows, 2 * group :] = grad_value[...].astype(low)
        for n in range(width // TILE):
            lanes = slice(n * TILE, (n + 1) * TILE)
            back = times_transposed(grad_proj[own_rows, :], heads[lanes, :])
            gain_sum[:, lanes] += jnp.sum(back * normed[own_rows, lanes].astype(jnp.float32), axis=0, keepdims=True)
            part[j, :, lanes] = back.astype(low)
    summed = {}
    for side, (near, rest) in enumerate(((one, two), (two, one))):
        rows = pl.ds(side * half, half)
        for order, to in enumerate((both, near)):
            summed[side, order] = remote(
                "seq", near, part.at[to, rows], first.at[side, order], c_send.at[side, order], c_recv.at[side, order]
            )
    for b in range(width // 128):
        small[b // 2, b % 2, gain_row : gain_row + 1, :] = gain_sum[:, b * 128 : (b + 1) * 128]
    for s in range(4):
        lanes = slice(s * group, (s + 1) * group)
        weights[lanes, :] = transposed_times(normed[:, lanes], grad_proj[...]).astype(low)
    for k in order_of:
        to_sibling[0, k] = start_sibling(0, k, core ^ 1)
        to_sibling[2, k] = start_sibling(2, k, core ^ 1)
    for k in order_of:
        pair_sum(0, k)
        pair_sum(2, k)
    for side, rest in enumerate((two, one)):
        rows = slice(side * half, (side + 1) * half)
        summed[side, 0].wait_recv()
        first[side, 0] = (first[side, 0].astype(jnp.float32) + part[rest, rows, :].astype(jnp.float32)).astype(low)
        summed[side, 2] = remote("seq", rest, first.at[side, 0], second.at[side], c_send.at[2, side], c_recv.at[2, side])
    stored = []
    for side in range(2):
        rows = slice(side * half, (side + 1) * half)
        summed[side, 1].wait_recv()
        summed[side, 2].wait_recv()
        first[side, 1] = (
            part[me, rows, :].astype(jnp.float32)
            + first[side, 1].astype(jnp.float32)
            + second[side].astype(jnp.float32)
        ).astype(low)
        stored.append(local(first.at[side, 1], normed_out.at[pl.ds(side * half, half)], keep.at[side]))
    for a in (1, 0, 2):
        total = own[a][0].astype(jnp.float32)
        for k in range(1, chips):
            away[a, k].wait_recv()
            total = total + got[a][k].astype(jnp.float32)
        if a == 0:
            for s in range(4):
                total_a[s] = total[s * share : (s + 1) * share].astype(low)
        else:
            totals[a][...] = total
    crossed = []
    for a, out in ((0, heads_out), (2, small_out)):
        for i, peer in enumerate(others):
            crossed.append(remote("seq", peer, totals[a].at[peer], out.at[me], x_send.at[a, i], x_recv.at[a, i]))
        stored.append(local(totals[a].at[me], out.at[me], keep.at[3 + a // 2]))
    stored.append(local(total_b, mix_out, keep.at[2]))
    for copy in (*stored, *crossed):
        copy.wait()
    for copy in (*summed.values(), *away.values(), *direct.values()):
        copy.wait_send()
    for copies in to_sibling.values():
        for copy in copies:
            copy.wait_send()


def back(grad, proj, attended, sums, normed, heads, mix, small, lengths, count, gain_row, number):
    S, dma, f32, low = jax.ShapeDtypeStruct, pltpu.SemaphoreType.DMA, jnp.float32, jnp.bfloat16
    tokens, width = grad.shape
    group = attended.shape[1]
    chips = count // 2
    full = 4 * tokens
    share = width // (4 * count)
    local_heads = group // HEAD_DIM
    kinds = small.shape[2]

    def vmem(*shape, dtype=low):
        return pltpu.VMEM(shape, dtype)

    sets = [
        vmem(chips, 4 * share, 3 * group),
        vmem(chips, share, width),
        vmem(chips, 4, kinds, 128, dtype=f32),
    ]
    return pl.pallas_call(
        functools.partial(back_kernel, count, gain_row),
        out_shape=(
            S((tokens, width), low),
            S((4, share, 3 * group), low),
            S((share, width), f32),
            S((4, kinds, 128), f32),
        ),
        in_specs=[ANY] * 8 + [pl.BlockSpec(memory_space=pltpu.SMEM)],
        out_specs=(ANY,) * 4,
        scratch_shapes=[
            vmem(full, width),
            vmem(*proj.shape),
            vmem(*attended.shape),
            vmem(*sums.shape, dtype=f32),
            vmem(*normed.shape),
            vmem(*heads.shape),
            vmem(*mix.shape),
            vmem(*small.shape, dtype=f32),
            vmem(full, group),
            vmem(8, full, dtype=f32),
            vmem(4, local_heads * tokens, group),
            vmem(4, local_heads * tokens, group),
            vmem(local_heads, tokens, group),
            vmem(local_heads, tokens, group),
            vmem(tokens, local_heads * tokens),
            vmem(tokens, local_heads * tokens),
            vmem(full, group, dtype=f32),
            vmem(tokens, group, dtype=f32),
            vmem(tokens, group, dtype=f32),
            vmem(full, 3 * group),
            vmem(4, tokens, width),
            vmem(width, 3 * group),
            vmem(group, width),
            vmem(1, width, dtype=f32),
            *sets,
            *sets,
            *sets,
            vmem(4, share, 3 * group),
            vmem(share, width, dtype=f32),
            vmem(4, kinds, 128, dtype=f32),
            vmem(2, 2, tokens // 2, width),
            vmem(2, tokens // 2, width),
            dma((3, 2)), dma((3, 2)),
            dma((2, chips)), dma((2, chips)), dma((4, chips)), dma((4, chips)),
            dma((3, chips)), dma((3, chips)),
            dma((3, 3)), dma((3, 3)), dma((3, 2)), dma((3, 2)), dma((8,)), dma((5,)),
        ],
        compiler_params=pltpu.CompilerParams(
            collective_id=number, has_side_effects=True, vmem_limit_bytes=56 * 2**20
        ),
    )(grad, proj, attended, sums, normed, heads, mix, small, lengths)


def shards(
    hidden,
    lengths,
    expert_ids,
    attn_gain,
    qkv_weight,
    out_weight,
    moe_gain,
    router_weight,
    expert_in,
    expert_out,
    out_grad,
):
    S = jax.ShapeDtypeStruct
    low = jnp.bfloat16
    owners = lax.axis_size("fsdp")
    seq_place = lax.axis_index("seq")
    seq_count = lax.axis_size("seq")
    tokens, width = hidden.shape[1], hidden.shape[2]
    full_len = tokens * seq_count
    group_width = width // seq_count
    rows_own = qkv_weight.shape[0]
    length = lengths[0]
    experts_all = router_weight.shape[1]
    small = jnp.concatenate([router_weight, attn_gain[:, None], moe_gain[:, None]], axis=1)
    small = jnp.pad(small, ((0, 0), (0, -small.shape[1] % 128)))
    expert_local = expert_in.shape[0]
    capacity = -(-max(2, 2 * tokens // experts_all) // 16) * 16
    slots = experts_all * capacity

    position = seq_place * tokens + jnp.arange(tokens, dtype=jnp.int32)
    valid = (position < length).astype(jnp.float32)[:, None]
    chosen = expert_ids[0, :, 0]
    choose = chosen[:, None] == jnp.arange(experts_all, dtype=jnp.int32)[None, :]
    order = jnp.arange(tokens, dtype=jnp.int32)
    earlier = (order[None, :] < order[:, None]) & (chosen[None, :] == chosen[:, None])
    ranks = jnp.sum(earlier.astype(jnp.int32), axis=1)
    slot = chosen * capacity + ranks
    hit = jnp.arange(slots, dtype=jnp.int32)[:, None] == slot[None, :]
    dispatch = hit.astype(low)

    def to_owners(rows, number):
        return exchange(
            "fsdp",
            owners,
            (rows.reshape(owners, expert_local, capacity, width),),
            (S((expert_local, owners, capacity, width), low),),
            ((lead, second),),
            number,
        )[0].reshape(expert_local, owners * capacity, width)

    def to_sources(rows, number):
        return exchange(
            "fsdp",
            owners,
            (rows.reshape(expert_local, owners, capacity, width),),
            (S((owners, expert_local, capacity, width), low),),
            ((second, lead),),
            number,
        )[0].reshape(slots, width)

    upstream_low = jnp.where(valid > 0, out_grad[0], 0).astype(low)
    upstream = upstream_low.astype(jnp.float32)
    up_rows = times(dispatch, upstream_low).astype(low)
    normed, weight_qkv, weight_mix, small, up_all, projected, attended, totals, mixed = front(
        hidden[0],
        qkv_weight.reshape(rows_own, 3, seq_count, group_width)
        .transpose(2, 0, 1, 3)
        .reshape(seq_count, rows_own, 3 * group_width),
        out_weight,
        small,
        up_rows.reshape(owners, expert_local, capacity, width),
        lengths,
        experts_all,
        0,
    )
    weight_qkv = weight_qkv.reshape(width, 3 * group_width)
    weight_route = small[:, :experts_all]
    gain_one = small[:, experts_all].astype(jnp.float32)
    gain_two = small[:, experts_all + 1].astype(jnp.float32)
    mix_rows = lax.dynamic_slice_in_dim(weight_mix, seq_place * group_width, group_width, 0)
    fused = 4 * owners * capacity <= 1024
    if not fused:
        up_all = up_all.reshape(expert_local, owners // 2, seq_count, 2 * capacity, width)
        up_all = jnp.roll(up_all, lax.axis_index("fsdp") // 2, axis=1)
        up_all = up_all.transpose(0, 2, 1, 3, 4)
    inputs = hidden[0].astype(jnp.float32)
    middle = inputs + times(mixed, weight_mix)
    normed_two, norm_two_back = jax.vjp(scaled_norm, middle, gain_two)
    normed_two = normed_two.astype(low)
    logits = times(normed_two, weight_route)

    def gate_of(logit_rows):
        return jnp.sum(jnp.where(choose, jax.nn.softmax(logit_rows, axis=-1), 0.0), axis=-1)

    gate, gate_back = jax.vjp(gate_of, logits)
    sent = times(dispatch, normed_two).astype(low)
    if fused:
        (returned, grad_back), expert_in_grad, expert_out_grad = moe(
            sent.reshape(owners, expert_local, capacity, width),
            up_all,
            small,
            expert_in,
            expert_out,
            experts_all,
            5,
        )
        returned, grad_back = returned.reshape(slots, width), grad_back.reshape(slots, width)
    else:
        gate_rows = jnp.sum(jnp.where(hit, gate[None, :], 0.0), axis=1)
        gates = lax.all_to_all(
            gate_rows.reshape(owners, expert_local, capacity), "fsdp", split_axis=0, concat_axis=0, tiled=True
        )
        gates = lax.all_gather(gates, "seq", axis=0)
        gates = gates.transpose(2, 0, 1, 3).reshape(expert_local, seq_count * owners * capacity, 1)

        rows_all = spread(to_owners(sent, 5), 6)
        count = seq_count * owners * capacity
        rows_all = rows_all.reshape(expert_local, count, width)
        up_all = up_all.reshape(expert_local, count, width)
        grad_rows = (up_all.astype(jnp.float32) * gates).astype(low)

        def per_expert(form, left, right):
            return jnp.einsum(form, left, right, preferred_element_type=jnp.float32)

        inner = per_expert("jrd,jdf->jrf", rows_all, expert_in)
        active, active_back = jax.vjp(gelu_tanh, inner)
        active = active.astype(low)
        partial_out = per_expert("jrf,jfd->jrd", active, expert_out).astype(low)
        grad_active = per_expert("jrd,jfd->jrf", grad_rows, expert_out)
        grad_inner = active_back(grad_active)[0].astype(low)
        partial_back = per_expert("jrf,jdf->jrd", grad_inner, expert_in).astype(low)
        expert_out_grad = per_expert("jrf,jrd->jfd", active, grad_rows)
        expert_in_grad = per_expert("jrd,jrf->jdf", rows_all, grad_inner)

        shape = (expert_local, seq_count, owners * capacity, width)
        returned = to_sources(collect(partial_out.reshape(shape), 7), 8)
        grad_back = to_sources(collect(partial_back.reshape(shape), 9), 10)

    back_rows = transposed_times(dispatch, returned)
    output = valid * (middle + gate[:, None] * back_rows)
    grad_gate = jnp.sum(upstream * back_rows, axis=1)
    grad_logits = gate_back(grad_gate)[0].astype(low)
    grad_normed_two = times_transposed(grad_logits, weight_route) + transposed_times(dispatch, grad_back)
    grad_middle, grad_gain_two = norm_two_back(grad_normed_two)
    grad_middle = grad_middle + upstream
    grad_attn = grad_middle.astype(low)

    small_grad = jnp.concatenate([transposed_times(grad_logits, normed_two), jnp.zeros((1, width)), grad_gain_two[None]])
    small_grad = jnp.pad(small_grad, ((0, -small_grad.shape[0] % 8), (0, 0)))
    kinds = small_grad.shape[0]
    small_grad = small_grad.reshape(kinds, seq_count, group_width // 128, 128).transpose(1, 2, 0, 3)
    grad_normed, qkv_sum, mix_grad, small_sum = back(
        grad_attn,
        projected,
        attended,
        totals,
        normed,
        weight_qkv,
        mix_rows,
        small_grad,
        lengths,
        owners,
        experts_all,
        12,
    )
    qkv_weight_grad = (
        qkv_sum.astype(jnp.float32)
        .reshape(seq_count, rows_own, 3, group_width)
        .transpose(1, 2, 0, 3)
        .reshape(rows_own, 3 * width)
    )
    start = lax.axis_index("fsdp") * rows_own % 128
    small_sum = lax.dynamic_slice_in_dim(jnp.sum(small_sum, axis=0), start, rows_own, 1)
    _, norm_back = jax.vjp(scaled_norm, inputs, gain_one)
    grad_inputs = norm_back(grad_normed.astype(jnp.float32))[0] + grad_middle
    return (
        output.astype(low)[None],
        grad_inputs[None],
        small_sum[experts_all] / attn_gain.astype(jnp.float32),
        qkv_weight_grad,
        mix_grad,
        small_sum[experts_all + 1],
        small_sum[:experts_all].T,
        expert_in_grad,
        expert_out_grad,
    )


def solution(mesh):
    placed = (
        P("fsdp", "seq", None),
        P("fsdp"),
        P("fsdp", "seq", None),
        P(("seq", "fsdp")),
        P(("seq", "fsdp"), None),
        P(("seq", "fsdp"), None),
        P(("seq", "fsdp")),
        P(("seq", "fsdp"), None),
        P("fsdp", None, "seq"),
        P("fsdp", "seq", None),
        P("fsdp", "seq", None),
    )
    return jax.shard_map(
        shards,
        mesh=mesh,
        in_specs=placed,
        out_specs=(
            P("fsdp", "seq", None),
            P("fsdp", "seq", None),
            P(("seq", "fsdp")),
            P(("seq", "fsdp"), None),
            P(("seq", "fsdp"), None),
            P(("seq", "fsdp")),
            P(("seq", "fsdp"), None),
            P("fsdp", None, "seq"),
            P("fsdp", "seq", None),
        ),
        check_vma=False,
    )
```

```python
import functools

import jax
import jax.numpy as jnp
from jax import lax
from jax.experimental import pallas as pl
from jax.experimental.pallas import tpu as pltpu
from jax.sharding import PartitionSpec as P

HEAD_DIM = 64
EPS = 1e-05
MASKED = -1e30
ROOT = 0.7978845608028654
TILE = 256
SPREAD_FIRST = 3
GRAD = 256
MESH = pl.DeviceIdType.MESH
ANY = pl.BlockSpec(memory_space=pl.ANY)


def scaled_norm(value, gain):
    return value * lax.rsqrt(jnp.mean(value * value, axis=-1, keepdims=True) + EPS) * gain


def gelu_tanh(value):
    return jax.nn.gelu(value, approximate=True)


def times(left, right):
    return jnp.dot(left, right, preferred_element_type=jnp.float32)


def times_transposed(left, right):
    return lax.dot_general(
        left, right, (((1,), (1,)), ((), ())), preferred_element_type=jnp.float32
    )


def transposed_times(left, right):
    return lax.dot_general(
        left, right, (((0,), (0,)), ((), ())), preferred_element_type=jnp.float32
    )


def greet(axis, peers):
    barrier = pltpu.get_barrier_semaphore()
    for peer in peers:
        pl.semaphore_signal(barrier, inc=1, device_id={axis: peer}, device_id_type=MESH)
    pl.semaphore_wait(barrier, len(peers))


def remote(axis, peer, source, target, send, receive):
    copy = pltpu.make_async_remote_copy(
        source, target, send, receive, device_id={axis: peer}, device_id_type=MESH
    )
    copy.start()
    return copy


def call(kernel, inputs, outputs, scratch, number):
    return pl.pallas_call(
        kernel,
        out_shape=outputs,
        in_specs=[ANY] * len(inputs),
        out_specs=jax.tree.map(lambda _: ANY, outputs),
        scratch_shapes=scratch,
        compiler_params=pltpu.CompilerParams(
            collective_id=number, has_side_effects=True, vmem_limit_bytes=48 * 2**20
        ),
    )(*inputs)


def exchange_kernel(axis, count, views, *refs):
    arrays = len(views)
    sources, targets = refs[:arrays], refs[arrays : 2 * arrays]
    send, receive, local = refs[2 * arrays :]
    me = lax.axis_index(axis)
    peers = [lax.rem(me + step, count) for step in range(1, count)]
    greet(axis, peers)
    copies = []
    for step, peer in enumerate(peers):
        for a, (out_of, into) in enumerate(views):
            copies.append(
                remote(
                    axis,
                    peer,
                    out_of(sources[a], peer),
                    into(targets[a], me),
                    send.at[a, step],
                    receive.at[a, step],
                )
            )
    for a, (out_of, into) in enumerate(views):
        copy = pltpu.make_async_copy(out_of(sources[a], me), into(targets[a], me), local.at[a])
        copy.start()
        copies.append(copy)
    for copy in copies:
        copy.wait()


def exchange(axis, count, inputs, outputs, views, number):
    arrays = len(views)
    return call(
        functools.partial(exchange_kernel, axis, count, views),
        inputs,
        outputs,
        [
            pltpu.SemaphoreType.DMA((arrays, count - 1)),
            pltpu.SemaphoreType.DMA((arrays, count - 1)),
            pltpu.SemaphoreType.DMA((arrays,)),
        ],
        number,
    )


def lead(ref, place):
    return ref.at[place]


def second(ref, place):
    return ref.at[:, place]


def whole(ref, place):
    return ref


def spread_kernel(source, target, send, receive, local):
    me = lax.axis_index("seq")
    one, two, both = me ^ 1, me ^ 2, me ^ 3
    half = source.shape[1] // 2
    greet("seq", [one, two])
    parts = (pl.ds(0, half), pl.ds(half, half))
    own = pltpu.make_async_copy(source, target.at[:, me], local)
    own.start()
    copies = {}
    for side, peer in enumerate((one, two)):
        for order in range(2):
            part = (order + side) % 2
            copies[side, part] = remote(
                "seq",
                peer,
                source.at[:, parts[part]],
                target.at[:, me, parts[part]],
                send.at[side, part],
                receive.at[side, part],
            )
    relayed = []
    for side, (origin, peer) in enumerate(((one, two), (two, one))):
        copies[side, side].wait_recv()
        block = target.at[:, origin, parts[side]]
        relayed.append(remote("seq", peer, block, block, send.at[2, side], receive.at[2, side]))
    for side in range(2):
        copies[side, 1 - side].wait_recv()
        for part in range(2):
            copies[side, part].wait_send()
    for copy in relayed:
        copy.wait()
    own.wait()


def spread(source, number):
    return call(
        spread_kernel,
        (source,),
        jax.ShapeDtypeStruct((source.shape[0], 4, *source.shape[1:]), source.dtype),
        [
            pltpu.SemaphoreType.DMA((3, 2)),
            pltpu.SemaphoreType.DMA((3, 2)),
            pltpu.SemaphoreType.DMA,
        ],
        number,
    )


def collect_kernel(source, target, mine, first, second_in, outgoing, load, send, receive, store):
    me = lax.axis_index("seq")
    one, two, both = me ^ 1, me ^ 2, me ^ 3
    width = source.shape[3] // 2
    greet("seq", [one, two])
    copies = []
    for side, (near, rest) in enumerate(((one, two), (two, one))):
        lanes = pl.ds(side * width, width)
        for order, block in enumerate((both, near)):
            copies.append(
                remote(
                    "seq",
                    near,
                    source.at[:, block, :, lanes],
                    first.at[side, order],
                    send.at[side, order],
                    receive.at[side, order],
                )
            )
        for order, block in enumerate((rest, me)):
            pltpu.make_async_copy(
                source.at[:, block, :, lanes], mine.at[side, order], load.at[side, order]
            ).start()
    passed = []
    for side, rest in enumerate((two, one)):
        copies[side * 2].wait_recv()
        pltpu.make_async_copy(mine.at[side, 0], mine.at[side, 0], load.at[side, 0]).wait()
        outgoing[side] = (
            mine[side, 0].astype(jnp.float32) + first[side, 0].astype(jnp.float32)
        ).astype(outgoing.dtype)
        passed.append(
            remote("seq", rest, outgoing.at[side], second_in.at[side], send.at[2, side], receive.at[2, side])
        )
    for side in range(2):
        copies[side * 2 + 1].wait_recv()
        pltpu.make_async_copy(mine.at[side, 1], mine.at[side, 1], load.at[side, 1]).wait()
        passed[side].wait_recv()
        mine[side, 1] = (
            mine[side, 1].astype(jnp.float32)
            + first[side, 1].astype(jnp.float32)
            + second_in[side].astype(jnp.float32)
        ).astype(mine.dtype)
        out = pltpu.make_async_copy(
            mine.at[side, 1], target.at[:, :, pl.ds(side * width, width)], store.at[side]
        )
        out.start()
    for side in range(2):
        pltpu.make_async_copy(
            mine.at[side, 1], target.at[:, :, pl.ds(side * width, width)], store.at[side]
        ).wait()
    for copy in copies + passed:
        copy.wait_send()


def collect(source, number):
    a, _, rows, width = source.shape
    dma = pltpu.SemaphoreType.DMA
    block = (a, rows, width // 2)
    return call(
        collect_kernel,
        (source,),
        jax.ShapeDtypeStruct((a, rows, width), source.dtype),
        [
            pltpu.VMEM((2, 2, *block), source.dtype),
            pltpu.VMEM((2, 2, *block), source.dtype),
            pltpu.VMEM((2, *block), source.dtype),
            pltpu.VMEM((2, *block), source.dtype),
            dma((2, 2)),
            dma((3, 2)),
            dma((3, 2)),
            dma((2,)),
        ],
        number,
    )


def moe_kernel(
    chips, cap, experts_all, spread_first, send_rows, up_rows, route, w_in, w_out,
    ret, dw_in, dw_out,
    R, U, G, A, I, PB, first, second, W1, W2, RT, stage,
    load, own, z_send, z_recv, s_send, s_recv, y_send, y_recv,
    c_send, c_recv, d_send, d_recv, r_send, r_recv, store,
):
    me, place = lax.axis_index("seq"), lax.axis_index("fsdp")
    one, two, both = me ^ 1, me ^ 2, me ^ 3
    chip, core = place // 2, lax.rem(place, 2)
    sibling = place ^ 1
    count = chips * 2
    part = 2 * cap
    chunk = 4 * part
    barrier = pltpu.get_barrier_semaphore()
    for peer in (one, two):
        pl.semaphore_signal(barrier, inc=1, device_id={"seq": peer}, device_id_type=MESH)
    for step in range(1, count):
        pl.semaphore_signal(
            barrier, inc=1, device_id={"fsdp": lax.rem(place + step, count)}, device_id_type=MESH
        )
    pl.semaphore_wait(barrier, 2 + count - 1)

    def rows_of(k, s):
        return pl.ds(k * chunk + s * part, part)

    loads = []

    def local(source, target, sem):
        copy = pltpu.make_async_copy(source, target, sem)
        copy.start()
        return copy

    dispatched = {}
    own_rows = []

    def dispatch(k):
        target = R.at[:, pl.ds(k * chunk + me * part + core * cap, cap)]
        if k == 0:
            own_rows.append(local(send_rows.at[place], target, own.at[0]))
        for c in range(2):
            if k or c:
                peer = (chip ^ k) * 2 + (core ^ c)
                dispatched[k, c] = remote(
                    "fsdp", peer, send_rows.at[peer], target, z_send.at[k, c], z_recv.at[k, c]
                )

    def z_arrived(k):
        if k == 0:
            own_rows[0].wait()
        for c in range(2):
            if k or c:
                dispatched[k, c].wait_recv()

    sent = {}

    def spread_out(a, k):
        for side, peer in enumerate((one, two)):
            for order in range(2):
                j = (order + side) % 2
                target = (U, R)[a].at[j, rows_of(k, me)]
                source = target if a else up_rows.at[j, rows_of(k, me)]
                sent[a, k, side, j] = remote(
                    "seq", peer, source, target, s_send.at[a, k, side, j], s_recv.at[a, k, side, j]
                )

    def relay(a, k):
        for side, (origin, peer) in enumerate(((one, two), (two, one))):
            sent[a, k, side, side].wait_recv()
            block = (U, R)[a].at[side, rows_of(k, origin)]
            sent[a, k, 2, side] = remote("seq", peer, block, block, y_send.at[a, k, side], y_recv.at[a, k, side])

    def all_arrived(a, k):
        for side in range(2):
            sent[a, k, side, 1 - side].wait_recv()
            sent[a, k, 2, side].wait_recv()

    def experts(k, j):
        rows = pl.ds(k * chunk, chunk)
        logits = times(R[j, rows, :], RT[...])
        lane = lax.broadcasted_iota(jnp.int32, logits.shape, 1)
        logits = jnp.where(lane < experts_all, logits, MASKED)
        powers = jnp.exp(logits - jnp.max(logits, axis=1, keepdims=True))
        picked = jnp.sum(jnp.where(lane == place * 2 + j, powers, 0.0), axis=1, keepdims=True)
        gate = picked / jnp.sum(powers, axis=1, keepdims=True)
        G[j, rows, :] = (U[j, rows, :].astype(jnp.float32) * gate).astype(G.dtype)

        @pl.loop(0, W1.shape[2] // TILE)
        def _(t):
            cols = pl.ds(pl.multiple_of(t * TILE, TILE), TILE)
            v = times(R[j, rows, :], W1[j, :, cols])
            grad = times_transposed(G[j, rows, :], W2[j, cols, :])
            square = v * v
            t = jnp.tanh(ROOT * v * (1.0 + 0.044715 * square))
            half = 0.5 * (1.0 + t)
            A[j, rows, cols] = (v * half).astype(A.dtype)
            slope = half + 0.5 * v * (1.0 - t * t) * (ROOT * (1.0 + 0.134145 * square))
            I[j, rows, cols] = (grad * slope).astype(I.dtype)

        @pl.loop(0, W1.shape[1] // TILE)
        def _(t):
            cols = pl.ds(pl.multiple_of(t * TILE, TILE), TILE)
            PB[0, j, rows, cols] = times(A[j, rows, :], W2[j, :, cols]).astype(PB.dtype)
            PB[1, j, rows, cols] = times_transposed(I[j, rows, :], W1[j, cols, :]).astype(PB.dtype)

    summed = {}

    def near_of(j):
        return (one, two) if j == 0 else (two, one)

    def collect_one(k, j):
        near, rest = near_of(j)
        for a in range(2):
            for order, block in enumerate((both, near)):
                summed[a, k, j, order] = remote(
                    "seq", near, PB.at[a, j, rows_of(k, block)], first.at[a, j, k, order],
                    c_send.at[a, j, k, order], c_recv.at[a, j, k, order],
                )

    def collect_two(k, j):
        near, rest = near_of(j)
        for a in range(2):
            summed[a, k, j, 0].wait_recv()
            first[a, j, k, 0] = (
                first[a, j, k, 0].astype(jnp.float32) + PB[a, j, rows_of(k, rest), :].astype(jnp.float32)
            ).astype(first.dtype)
            summed[a, k, j, 2] = remote(
                "seq", rest, first.at[a, j, k, 0], second.at[a, j, k], d_send.at[a, j, k], d_recv.at[a, j, k]
            )

    returns = {}

    def collect_three(k, j):
        for a in range(2):
            summed[a, k, j, 1].wait_recv()
            summed[a, k, j, 2].wait_recv()
            first[a, j, k, 1] = (
                first[a, j, k, 1].astype(jnp.float32)
                + PB[a, j, rows_of(k, me), :].astype(jnp.float32)
                + second[a, j, k].astype(jnp.float32)
            ).astype(first.dtype)
            to = chip ^ k
            target = ret.at[a, place, j]
            for c in range(2):
                if k == 0:
                    if c == 0:
                        returns[a, k, j, 0] = local(
                            first.at[a, j, k, 1, pl.ds(core * cap, cap)], target, own.at[1 + a * 2 + j]
                        )
                        returns[a, k, j, 1] = remote(
                            "fsdp", sibling, first.at[a, j, k, 1, pl.ds((core ^ 1) * cap, cap)], target,
                            r_send.at[a, j, k, 1], r_recv.at[a, j, k, 1],
                        )
                    continue
                returns[a, k, j, c] = remote(
                    "fsdp", to * 2 + (core ^ c), first.at[a, j, k, 1, pl.ds((core ^ c) * cap, cap)], target,
                    r_send.at[a, j, k, c], r_recv.at[a, j, k, c],
                )

    staged = {}

    def weight_grads(j, which, tiles):
        left, right, out = ((R, I, dw_in), (A, G, dw_out))[which]
        for m in tiles:
            slot = m % 2
            lanes = slice(m * GRAD, (m + 1) * GRAD)
            if slot in staged:
                staged.pop(slot).wait()

            @pl.loop(0, right.shape[2] // TILE)
            def _(t):
                cols = pl.ds(pl.multiple_of(t * TILE, TILE), TILE)
                stage[slot, :, cols] = transposed_times(left[j, :, lanes], right[j, :, cols]).astype(stage.dtype)

            staged[slot] = local(stage.at[slot], out.at[j, lanes], store.at[slot])

    later = range(spread_first, chips)
    dispatch(0)
    dispatch(1)
    dispatch(2)
    for j in range(2):
        loads.append(local(w_in.at[j], W1.at[j], load.at[j]))
        loads.append(local(w_out.at[j], W2.at[j], load.at[2 + j]))
    loads.append(local(route, RT, load.at[4]))
    early = spread_first * chunk
    for j in range(2):
        loads.append(local(up_rows.at[j, pl.ds(0, early)], U.at[j, pl.ds(0, early)], load.at[5 + j]))
    for n, k in enumerate(later):
        for j in range(2):
            block = rows_of(k, me)
            loads.append(local(up_rows.at[j, block], U.at[j, block], load.at[7 + 2 * n + j]))
    z_arrived(0)
    spread_out(1, 0)
    for k in later:
        spread_out(0, k)
    z_arrived(1)
    spread_out(1, 1)
    dispatch(3)
    relay(1, 0)
    for copy in loads:
        copy.wait()
    for k in later:
        relay(0, k)
    z_arrived(2)
    spread_out(1, 2)
    all_arrived(1, 0)
    experts(0, 0)
    collect_one(0, 0)
    relay(1, 1)
    z_arrived(3)
    spread_out(1, 3)
    experts(0, 1)
    collect_one(0, 1)
    relay(1, 2)
    for k in range(1, chips):
        all_arrived(1, k)
        if k >= spread_first:
            all_arrived(0, k)
        experts(k, 0)
        collect_one(k, 0)
        if k == 1:
            relay(1, 3)
        collect_two(k - 1, 0)
        if k > 1:
            collect_three(k - 2, 0)
        experts(k, 1)
        collect_one(k, 1)
        collect_two(k - 1, 1)
        if k > 1:
            collect_three(k - 2, 1)
    last = chips - 1
    weight_grads(0, 0, range(4))
    collect_two(last, 0)
    collect_three(last - 1, 0)
    collect_two(last, 1)
    collect_three(last - 1, 1)
    weight_grads(0, 1, range(4))
    weight_grads(1, 0, range(2))
    collect_three(last, 0)
    weight_grads(1, 0, range(2, 4))
    collect_three(last, 1)
    weight_grads(1, 1, range(4))
    for copy in staged.values():
        copy.wait()
    for copy in dispatched.values():
        copy.wait_send()
    for copy in sent.values():
        copy.wait_send()
    for copy in summed.values():
        copy.wait_send()
    for (a, k, j, c), copy in returns.items():
        copy.wait()


def moe(send_rows, up_rows, route, w_in, w_out, experts_all, number):
    S, low, dma = jax.ShapeDtypeStruct, jnp.bfloat16, pltpu.SemaphoreType.DMA
    owners, _, cap, width = send_rows.shape
    chips = owners // 2
    hidden_units = w_in.shape[2]
    count = owners * cap * 4
    part = 2 * cap

    def vmem(*shape, dtype=low):
        return pltpu.VMEM(shape, dtype)

    return pl.pallas_call(
        functools.partial(moe_kernel, chips, cap, experts_all, SPREAD_FIRST),
        out_shape=(
            S((2, owners, 2, cap, width), low),
            S(w_in.shape, low),
            S(w_out.shape, low),
        ),
        in_specs=[ANY] * 5,
        out_specs=(ANY,) * 3,
        scratch_shapes=[
            vmem(2, count, width),
            vmem(2, count, width),
            vmem(2, count, width),
            vmem(2, count, hidden_units),
            vmem(2, count, hidden_units),
            vmem(2, 2, count, width),
            vmem(2, 2, chips, 2, part, width),
            vmem(2, 2, chips, part, width),
            vmem(*w_in.shape),
            vmem(*w_out.shape),
            vmem(*route.shape),
            vmem(2, GRAD, max(width, hidden_units)),
            dma((7 + 2 * (chips - SPREAD_FIRST),)),
            dma((5,)),
            dma((chips, 2)),
            dma((chips, 2)),
            dma((2, chips, 2, 2)),
            dma((2, chips, 2, 2)),
            dma((2, chips, 2)),
            dma((2, chips, 2)),
            dma((2, 2, chips, 2)),
            dma((2, 2, chips, 2)),
            dma((2, 2, chips)),
            dma((2, 2, chips)),
            dma((2, 2, chips, 2)),
            dma((2, 2, chips, 2)),
            dma((2,)),
        ],
        compiler_params=pltpu.CompilerParams(
            collective_id=number, has_side_effects=True, vmem_limit_bytes=58 * 2**20
        ),
        cost_estimate=pl.CostEstimate(
            flops=12 * 2 * count * width * hidden_units, bytes_accessed=2**25, transcendentals=0
        ),
    )(send_rows, up_rows, route, w_in, w_out)


def front_kernel(
    count, cap, experts_all, spread_here, hidden, heads, mix, small, rows, length,
    normed_out, heads_out, mix_all, small_out, up, projected_out, attended_out, sums_out, mixed,
    staged, hid, heads_all, small_all, normed, proj, attended, sums, acc, stat,
    h_send, h_recv, q_send, q_recv, f_send, f_recv, n_send, n_recv, u_send, u_recv, m_send, m_recv,
    s_send, s_recv, x_send, x_recv, y_send, y_recv, local,
):
    me, place = lax.axis_index("seq"), lax.axis_index("fsdp")
    one, two, both = me ^ 1, me ^ 2, me ^ 3
    others = (one, two, both)
    chips = count // 2
    chip, core = place // 2, lax.rem(place, 2)
    sibling = place ^ 1
    share = mix.shape[0]
    tokens = hidden.shape[0]
    group = attended.shape[1]
    part, chunk = 2 * cap, 8 * cap
    barrier = pltpu.get_barrier_semaphore()
    for peer in others:
        pl.semaphore_signal(barrier, inc=1, device_id={"seq": peer}, device_id_type=MESH)
    for step in range(1, count):
        pl.semaphore_signal(
            barrier, inc=1, device_id={"fsdp": lax.rem(place + step, count)}, device_id_type=MESH
        )
    pl.semaphore_wait(barrier, 3 + count - 1)

    def keep(source, target, number):
        copy = pltpu.make_async_copy(source, target, local.at[number])
        copy.start()
        return copy

    def far(k):
        return (chip ^ k) * 2 + core

    away, near = {}, {}

    def block(a, owner):
        if a == 0:
            return mix_all.at[me, owner // 2, core]
        if a == 1:
            return small_all.at[pl.ds(pl.multiple_of((me * count + owner) * share, share), share)]
        return heads_all.at[:, owner]

    own_of = (mix, small, staged)

    def send_far(a):
        for k in range(1, chips):
            away[a, k] = remote("fsdp", far(k), own_of[a], block(a, place), f_send.at[a, k], f_recv.at[a, k])

    def send_near(a):
        near[a, 0] = remote("fsdp", sibling, own_of[a], block(a, place), n_send.at[a, 0], n_recv.at[a, 0])

    def pass_on(a):
        for k in range(1, chips):
            away[a, k].wait_recv()
            arrived = block(a, far(k))
            near[a, k] = remote("fsdp", sibling, arrived, arrived, n_send.at[a, k], n_recv.at[a, k])

    direct = {}

    def both_ways(name, views, sources, send, receive):
        for side, peer in enumerate((one, two)):
            for order in range(2):
                p = (order + side) % 2
                direct[name, side, p] = remote(
                    "seq", peer, sources[p], views[p](me), send.at[side, p], receive.at[side, p]
                )

    def relay(name, views, send, receive):
        for side, (origin, peer) in enumerate(((one, two), (two, one))):
            direct[name, side, side].wait_recv()
            source = views[side](origin)
            direct[name, 2, side] = remote("seq", peer, source, source, send.at[2, side], receive.at[2, side])

    def arrived(name):
        for side in range(2):
            direct[name, side, 1 - side].wait_recv()
            direct[name, 2, side].wait_recv()

    moved = {}

    def send_rows(k):
        for c in range(2):
            if k == 0 and c == 0:
                continue
            peer = (chip ^ k) * 2 + (core ^ c)
            moved[k, c] = remote(
                "fsdp", peer, rows.at[peer], up.at[:, pl.ds(k * chunk + me * part + core * cap, cap)],
                u_send.at[k, c], u_recv.at[k, c],
            )

    send_far(1)
    send_near(1)
    exchanged = [
        remote("seq", peer, heads.at[peer], staged.at[me], q_send.at[i], q_recv.at[i])
        for i, peer in enumerate(others)
    ]
    own_heads = keep(heads.at[me], staged.at[me], 0)
    own_hidden = keep(hidden, hid.at[pl.ds(me * tokens, tokens)], 1)
    own_mix = keep(mix, block(0, place), 2)
    own_small = keep(small, block(1, place), 3)
    own_rows = keep(rows.at[place], up.at[:, pl.ds(me * part + core * cap, cap)], 4)
    half = tokens // 2
    hidden_views = [
        lambda origin, p=p: hid.at[pl.ds(origin * tokens + p * half, half)] for p in range(2)
    ]
    both_ways("hidden", hidden_views, [hidden.at[pl.ds(p * half, half)] for p in range(2)], h_send, h_recv)
    send_far(0)
    send_rows(0)
    pass_on(1)
    own_heads.wait()
    for copy in exchanged:
        copy.wait_recv()
    own_block = keep(staged, heads_all.at[:, place], 5)
    send_far(2)
    send_near(2)
    own_small.wait()
    for k in range(chips):
        near[1, k].wait_recv()
    mine = small_all.at[pl.ds(pl.multiple_of(me * count * share, share), count * share)]
    smalls = [remote("seq", peer, mine, mine, q_send.at[3 + i], q_recv.at[3 + i]) for i, peer in enumerate(others)]

    def up_views(k):
        return [lambda origin, j=j: up.at[j, pl.ds(k * chunk + origin * part, part)] for j in range(2)]

    def up_out(k):
        if k == 0:
            own_rows.wait()
        for c in range(2):
            if (k, c) in moved:
                moved[k, c].wait_recv()
        if k < spread_here:
            views = up_views(k)
            both_ways(("up", k), views, [views[0](me), views[1](me)], s_send.at[k], s_recv.at[k])

    def up_relay(k):
        if k < spread_here:
            relay(("up", k), up_views(k), s_send.at[k], s_recv.at[k])

    up_out(0)
    relay("hidden", hidden_views, h_send, h_recv)
    own_mix.wait()
    for k in range(1, chips):
        away[0, k].wait_recv()
    mix_views = [
        lambda origin, p=p: mix_all.at[origin, pl.ds(p * (chips // 2), chips // 2), core] for p in range(2)
    ]
    both_ways("mix", mix_views, [mix_views[p](me) for p in range(2)], m_send, m_recv)
    for copy in smalls:
        copy.wait_recv()
    small_kept = keep(small_all, small_out, 6)
    own_hidden.wait()
    arrived("hidden")
    gain = jnp.transpose(small_all[...].astype(jnp.float32))[experts_all : experts_all + 1]

    @pl.loop(0, hid.shape[0] // 128)
    def _(t):
        place_rows = pl.ds(pl.multiple_of(t * 128, 128), 128)
        value = hid[place_rows, :].astype(jnp.float32)
        scale = lax.rsqrt(jnp.mean(value * value, axis=-1, keepdims=True) + EPS)
        normed[place_rows, :] = (value * scale * gain).astype(normed.dtype)

    normed_kept = keep(normed, normed_out, 7)
    pass_on(2)
    for k in range(1, chips):
        send_rows(k)
    up_relay(0)
    relay("mix", mix_views, m_send, m_recv)
    own_block.wait()
    for k in range(chips):
        near[2, k].wait_recv()
    heads_kept = keep(heads_all, heads_out, 8)
    width = hid.shape[1]

    for p in range(3):

        @pl.loop(0, hid.shape[0] // TILE)
        def _(t):
            place_rows = pl.ds(pl.multiple_of(t * TILE, TILE), TILE)
            weights = heads_all[:, :, :, p * group : (p + 1) * group].reshape(width, group)
            proj[place_rows, p * group : (p + 1) * group] = times(normed[place_rows, :], weights).astype(proj.dtype)

    projected_kept = keep(proj, projected_out, 9)
    head_of = lax.broadcasted_iota(jnp.int32, (tokens, group), 1) // HEAD_DIM
    sent = []
    for i in range(4):
        own = slice(i * tokens, (i + 1) * tokens)
        reach = (i + 1) * tokens

        @pl.loop(0, group // HEAD_DIM)
        def _(h):
            query = jnp.where(head_of == h, proj[own, :group] * (HEAD_DIM**-0.5), 0).astype(proj.dtype)
            scores = times_transposed(query, proj[:reach, group : 2 * group])
            column = lax.broadcasted_iota(jnp.int32, scores.shape, 1)
            row = lax.broadcasted_iota(jnp.int32, scores.shape, 0) + i * tokens
            scores = jnp.where((column <= row) & (column < length[0]), scores, MASKED)
            top = jnp.max(scores, axis=1, keepdims=True)
            powers = jnp.exp(scores - top)
            total = jnp.sum(powers, axis=1, keepdims=True)
            probs = (powers * (1.0 / total)).astype(proj.dtype)
            out = times(probs, proj[:reach, 2 * group :])
            acc[...] = jnp.where(head_of == h, out, acc[...])
            lane = lax.broadcasted_iota(jnp.int32, stat.shape, 1)
            stat[...] = jnp.where(lane == h, top + jnp.log(total), stat[...])

        attended[own, :] = acc[...].astype(attended.dtype)
        sums[:, own] = jnp.transpose(stat[...])[:8]
        target = mixed.at[:, pl.ds(pl.multiple_of(me * group, group), group)]

        @pl.when(me != i)
        def _():
            remote("seq", i, attended.at[own], target, x_send.at[i], x_recv.at[me])

        @pl.when(me == i)
        def _():
            pltpu.make_async_copy(attended.at[own], target, local.at[10]).start()

        if i + 1 < chips:
            up_out(i + 1)
        if i:
            up_relay(i)
        if i == 0:
            arrived("mix")
            both_cores = [
                remote(
                    "fsdp", sibling, mix_all.at[s, :, core], mix_all.at[s, :, core], y_send.at[s], y_recv.at[s]
                )
                for s in range(4)
            ]
    for k in range(4, chips):
        up_relay(k)
        if k + 1 < chips:
            up_out(k + 1)
    attended_kept = keep(attended, attended_out, 11)
    sums_kept = keep(sums, sums_out, 12)
    for k in range(spread_here):
        arrived(("up", k))
    for copy in both_cores:
        copy.wait()
    for i in range(4):
        target = mixed.at[:, pl.ds(i * group, group)]

        @pl.when(me != i)
        def _():
            copy = pltpu.make_async_remote_copy(
                attended.at[pl.ds(i * tokens, tokens)], target, x_send.at[i], x_recv.at[i],
                device_id={"seq": i}, device_id_type=MESH,
            )
            copy.wait()

        @pl.when(me == i)
        def _():
            pltpu.make_async_copy(attended.at[pl.ds(i * tokens, tokens)], target, local.at[10]).wait()

    for copy in (*direct.values(), *exchanged, *smalls, *away.values(), *near.values(), *moved.values()):
        copy.wait_send()
    for copy in (small_kept, normed_kept, heads_kept, projected_kept, attended_kept, sums_kept):
        copy.wait()


def front(hidden, heads, mix, small, rows, lengths, experts_all, spread_here, number):
    S, dma, low = jax.ShapeDtypeStruct, pltpu.SemaphoreType.DMA, jnp.bfloat16
    count, _, cap, width = rows.shape
    chips = count // 2
    tokens = hidden.shape[0]
    group = heads.shape[2] // 3
    full = 4 * tokens
    all_heads = (4, count, *heads.shape[1:])
    return pl.pallas_call(
        functools.partial(front_kernel, count, cap, experts_all, spread_here),
        out_shape=(
            S((full, width), low),
            S(all_heads, low),
            S((4, chips, 2, *mix.shape), low),
            S((width, small.shape[1]), low),
            S((2, 4 * count * cap, width), low),
            S((full, 3 * group), low),
            S((full, group), low),
            S((8, full), jnp.float32),
            S((tokens, width), low),
        ),
        in_specs=[ANY] * 5 + [pl.BlockSpec(memory_space=pltpu.SMEM)],
        out_specs=(ANY,) * 9,
        scratch_shapes=[
            pltpu.VMEM(heads.shape, low),
            pltpu.VMEM((full, width), low),
            pltpu.VMEM(all_heads, low),
            pltpu.VMEM((width, small.shape[1]), low),
            pltpu.VMEM((full, width), low),
            pltpu.VMEM((full, 3 * group), low),
            pltpu.VMEM((full, group), low),
            pltpu.VMEM((8, full), jnp.float32),
            pltpu.VMEM((tokens, group), jnp.float32),
            pltpu.VMEM((tokens, 128), jnp.float32),
            dma((3, 2)), dma((3, 2)), dma((6,)), dma((6,)),
            dma((3, chips)), dma((3, chips)), dma((3, chips)), dma((3, chips)),
            dma((chips, 2)), dma((chips, 2)), dma((3, 2)), dma((3, 2)),
            dma((chips, 3, 2)), dma((chips, 3, 2)), dma((4,)), dma((4,)), dma((4,)), dma((4,)), dma((13,)),
        ],
        compiler_params=pltpu.CompilerParams(
            collective_id=number, has_side_effects=True, vmem_limit_bytes=48 * 2**20
        ),
    )(hidden, heads, mix, small, rows, lengths)


def back_kernel(
    count, gain_row, grad_in, proj_in, attended_in, sums_in, normed_in, heads_in, mix_in, small_in, length,
    normed_out, heads_out, mix_out, small_out,
    grads, proj, attended, sums, normed, heads, mix, small, grad_heads, delta, masked_grad, masked_query,
    masked_key, masked_value, probs, slopes, grad_query, grad_key, grad_value, grad_proj, part, weights, weights_mix, gain_sum,
    sib_a, sib_b, sib_c, own_a, own_b, own_c, got_a, got_b, got_c, total_a, total_b, total_c, first, second,
    g_send, g_recv, b_send, b_recv, bb_send, bb_recv, z_send, z_recv, x_send, x_recv, c_send, c_recv, load, keep,
):
    me, place = lax.axis_index("seq"), lax.axis_index("fsdp")
    one, two, both = me ^ 1, me ^ 2, me ^ 3
    others = (one, two, both)
    chips = count // 2
    chip, core = place // 2, lax.rem(place, 2)
    sibling = place ^ 1
    tokens, width = grad_in.shape
    group = attended.shape[1]
    share = weights.shape[0] // (4 * count)
    heads_local = group // HEAD_DIM
    low = grads.dtype
    barrier = pltpu.get_barrier_semaphore()
    for peer in others:
        pl.semaphore_signal(barrier, inc=1, device_id={"seq": peer}, device_id_type=MESH)
    for k in range(1, chips):
        pl.semaphore_signal(
            barrier, inc=1, device_id={"fsdp": (chip ^ k) * 2 + core}, device_id_type=MESH
        )
    pl.semaphore_signal(barrier, inc=1, device_id={"fsdp": sibling}, device_id_type=MESH)
    pl.semaphore_wait(barrier, 3 + chips)

    def local(source, to, sem):
        copy = pltpu.make_async_copy(source, to, sem)
        copy.start()
        return copy

    own_grad = local(grad_in, grads.at[pl.ds(me * tokens, tokens)], load.at[0])
    half = tokens // 2
    direct = {}
    for side, peer in enumerate((one, two)):
        for order in range(2):
            p = (order + side) % 2
            direct[side, p] = remote(
                "seq", peer, grad_in.at[pl.ds(p * half, half)], grads.at[pl.ds(me * tokens + p * half, half)],
                g_send.at[side, p], g_recv.at[side, p],
            )
    loads = [
        local(source, to, load.at[1 + i])
        for i, (source, to) in enumerate(
            (
                (proj_in, proj),
                (attended_in, attended),
                (sums_in, sums),
                (mix_in.at[pl.ds(pl.multiple_of(me * group, group), group)], mix),
                (heads_in, heads),
                (normed_in, normed),
                (small_in, small),
            )
        )
    ]
    for copy in loads:
        copy.wait()
    head_of = lax.broadcasted_iota(jnp.int32, (tokens, group), 1) // HEAD_DIM
    key_at = lax.broadcasted_iota(jnp.int32, (tokens, tokens), 0)
    for j in range(4):
        rows = slice(j * tokens, (j + 1) * tokens)
        for h in range(heads_local):
            key = proj[rows, group : 2 * group] * (HEAD_DIM**-0.5)
            masked_key[j * heads_local + h] = jnp.where(head_of == h, key, 0).astype(low)
            masked_value[j * heads_local + h] = jnp.where(head_of == h, proj[rows, 2 * group :], 0).astype(low)
    grad_key[...] = jnp.zeros_like(grad_key)
    grad_value[...] = jnp.zeros_like(grad_value)
    gain_sum[...] = jnp.zeros_like(gain_sum)

    def block(i, j, masked):
        rows = pl.ds(pl.multiple_of(i * tokens, tokens), tokens)
        keys = pl.ds(pl.multiple_of(j * tokens, tokens), tokens)
        hidden = j * tokens + key_at >= length[0]
        if masked:
            hidden = hidden | (key_at > lax.broadcasted_iota(jnp.int32, (tokens, tokens), 1))
        total = None
        for h in range(heads_local):
            lanes = slice(h * tokens, (h + 1) * tokens)
            key = masked_key[j * heads_local + h]
            scores = times_transposed(key, proj[rows, :group])
            scores = jnp.where(hidden, MASKED, scores)
            p = jnp.exp(scores - sums[h : h + 1, rows])
            probs[:, lanes] = p.astype(low)
            grad = times_transposed(masked_value[j * heads_local + h], grad_heads[...])
            slopes[:, lanes] = (p * (grad - delta[h : h + 1, :])).astype(low)
            term = transposed_times(slopes[:, lanes], key)
            total = term if total is None else total + term
        grad_query[...] += total
        grad_value[keys, :] += times(probs[...], masked_grad[...])
        grad_key[keys, :] += times(slopes[...], masked_query[...])

    def queries(i):
        rows = pl.ds(pl.multiple_of(i * tokens, tokens), tokens)
        grad_heads[...] = times_transposed(grads[rows, :], mix[...]).astype(low)
        out = grad_heads[...].astype(jnp.float32)
        turned = jnp.transpose(out * attended[rows, :].astype(jnp.float32))
        query = proj[rows, :group]
        for h in range(heads_local):
            delta[h : h + 1, :] = jnp.sum(turned[h * HEAD_DIM : (h + 1) * HEAD_DIM], axis=0, keepdims=True)
            masked_grad[h * tokens : (h + 1) * tokens, :] = jnp.where(head_of == h, out, 0).astype(low)
            masked_query[h * tokens : (h + 1) * tokens, :] = jnp.where(head_of == h, query, 0).astype(low)
        grad_query[...] = jnp.zeros_like(grad_query)

        @pl.loop(0, i)
        def _(j):
            block(i, j, False)

        block(i, i, True)
        grad_proj[rows, :group] = grad_query[...].astype(low)

    own_grad.wait()
    queries(me)
    for side, (origin, peer) in enumerate(((one, two), (two, one))):
        direct[side, side].wait_recv()
        source = grads.at[pl.ds(origin * tokens + side * half, half)]
        direct[2, side] = remote("seq", peer, source, source, g_send.at[2, side], g_recv.at[2, side])
    for side, origin in enumerate((one, two)):
        direct[side, 1 - side].wait_recv()
        queries(origin)
    for side in range(2):
        direct[2, side].wait_recv()
    for n in range(width // TILE):
        lanes = slice(n * TILE, (n + 1) * TILE)
        weights_mix[:, lanes] = transposed_times(attended[...], grads[:, lanes]).astype(low)
    order_of = [*range(1, chips), 0]
    to_sibling, away = {}, {}

    def rows_at(s, owner):
        return pl.ds(pl.multiple_of((s * count + owner) * share, share), share)

    def start_sibling(a, k, core_of):
        owner = (chip ^ k) * 2 + core_of
        if a == 1:
            return [
                remote(
                    "fsdp", sibling, weights_mix.at[pl.ds(pl.multiple_of(owner * share, share), share)], sib_b.at[k],
                    b_send.at[0, k], b_recv.at[0, k],
                )
            ]
        if a == 2:
            return [
                remote(
                    "fsdp", sibling, small.at[:, owner * share // 128], sib_c.at[k], b_send.at[1, k], b_recv.at[1, k]
                )
            ]
        raise ValueError(a)

    sib, own, got = (sib_a, sib_b, sib_c), (own_a, own_b, own_c), (got_a, got_b, got_c)
    totals = (total_a, total_b, total_c)

    def pair_sum(a, k):
        owner = (chip ^ k) * 2 + core
        for copy in to_sibling[a, k]:
            copy.wait_recv()
        if a == 1:
            mine = weights_mix[pl.ds(pl.multiple_of(owner * share, share), share), :]
            own_b[k] = (mine.astype(jnp.float32) + sib_b[k].astype(jnp.float32)).astype(low)
        else:
            for s in range(4):
                own_c[k, s] = small[s, owner * share // 128] + sib_c[k, s]
        if k:
            away[a, k] = remote(
                "fsdp", (chip ^ k) * 2 + core, own[a].at[k], got[a].at[k], z_send.at[a, k], z_recv.at[a, k]
            )

    for k in order_of:
        to_sibling[1, k] = start_sibling(1, k, core ^ 1)
    queries(both)
    for k in order_of:
        pair_sum(1, k)
    grad_proj[:, group : 2 * group] = (grad_key[...] * (HEAD_DIM**-0.5)).astype(low)
    grad_proj[:, 2 * group :] = grad_value[...].astype(low)
    for s in range(4):
        lanes = slice(s * group, (s + 1) * group)
        weights[lanes, :] = transposed_times(normed[:, lanes], grad_proj[...]).astype(low)
        for k in order_of:
            owner = (chip ^ k) * 2
            to_sibling[s + 3, k] = [
                remote(
                    "fsdp", sibling, weights.at[rows_at(s, owner + (core ^ 1))], sib_a.at[k, pl.ds(s * share, share)],
                    bb_send.at[s, k], bb_recv.at[s, k],
                )
            ]
    for s in range(4):
        rows = slice(s * share, (s + 1) * share)
        for k in order_of:
            owner = (chip ^ k) * 2 + core
            to_sibling[s + 3, k][0].wait_recv()
            own_a[k, rows, :] = (
                weights[rows_at(s, owner), :].astype(jnp.float32) + sib_a[k, rows, :].astype(jnp.float32)
            ).astype(low)
            if k:
                away[s + 3, k] = remote(
                    "fsdp", owner, own_a.at[k, pl.ds(s * share, share)], got_a.at[k, pl.ds(s * share, share)],
                    z_send.at[s + 3, k], z_recv.at[s + 3, k],
                )
    for j in range(4):
        own_rows = slice(j * tokens, (j + 1) * tokens)
        for n in range(width // TILE):
            lanes = slice(n * TILE, (n + 1) * TILE)
            back = times_transposed(grad_proj[own_rows, :], heads[lanes, :])
            gain_sum[:, lanes] += jnp.sum(back * normed[own_rows, lanes].astype(jnp.float32), axis=0, keepdims=True)
            part[j, :, lanes] = back.astype(low)
    summed = {}
    for side, (near, rest) in enumerate(((one, two), (two, one))):
        rows = pl.ds(side * half, half)
        for order, to in enumerate((both, near)):
            summed[side, order] = remote(
                "seq", near, part.at[to, rows], first.at[side, order], c_send.at[side, order], c_recv.at[side, order]
            )
    for b in range(width // 128):
        small[b // 2, b % 2, gain_row : gain_row + 1, :] = gain_sum[:, b * 128 : (b + 1) * 128]
    for k in order_of:
        to_sibling[2, k] = start_sibling(2, k, core ^ 1)
    for k in order_of:
        pair_sum(2, k)
    for side, rest in enumerate((two, one)):
        rows = slice(side * half, (side + 1) * half)
        summed[side, 0].wait_recv()
        first[side, 0] = (first[side, 0].astype(jnp.float32) + part[rest, rows, :].astype(jnp.float32)).astype(low)
        summed[side, 2] = remote("seq", rest, first.at[side, 0], second.at[side], c_send.at[2, side], c_recv.at[2, side])
    stored = []
    for side in range(2):
        rows = slice(side * half, (side + 1) * half)
        summed[side, 1].wait_recv()
        summed[side, 2].wait_recv()
        first[side, 1] = (
            part[me, rows, :].astype(jnp.float32)
            + first[side, 1].astype(jnp.float32)
            + second[side].astype(jnp.float32)
        ).astype(low)
        stored.append(local(first.at[side, 1], normed_out.at[pl.ds(side * half, half)], keep.at[side]))
    for a in (1, 0, 2):
        if a == 0:
            for s in range(4):
                rows = slice(s * share, (s + 1) * share)
                total = own_a[0, rows, :].astype(jnp.float32)
                for k in range(1, chips):
                    away[s + 3, k].wait_recv()
                    total = total + got_a[k, rows, :].astype(jnp.float32)
                total_a[s] = total.astype(low)
        else:
            total = own[a][0].astype(jnp.float32)
            for k in range(1, chips):
                away[a, k].wait_recv()
                total = total + got[a][k].astype(jnp.float32)
            totals[a][...] = total
    crossed = []
    for a, out in ((0, heads_out), (2, small_out)):
        for i, peer in enumerate(others):
            crossed.append(remote("seq", peer, totals[a].at[peer], out.at[me], x_send.at[a, i], x_recv.at[a, i]))
        stored.append(local(totals[a].at[me], out.at[me], keep.at[3 + a // 2]))
    stored.append(local(total_b, mix_out, keep.at[2]))
    for copy in (*stored, *crossed):
        copy.wait()
    for copy in (*summed.values(), *away.values(), *direct.values()):
        copy.wait_send()
    for copies in to_sibling.values():
        for copy in copies:
            copy.wait_send()


def back(grad, proj, attended, sums, normed, heads, mix, small, lengths, count, gain_row, number):
    S, dma, f32, low = jax.ShapeDtypeStruct, pltpu.SemaphoreType.DMA, jnp.float32, jnp.bfloat16
    tokens, width = grad.shape
    group = attended.shape[1]
    chips = count // 2
    full = 4 * tokens
    share = width // (4 * count)
    local_heads = group // HEAD_DIM
    kinds = small.shape[2]

    def vmem(*shape, dtype=low):
        return pltpu.VMEM(shape, dtype)

    sets = [
        vmem(chips, 4 * share, 3 * group),
        vmem(chips, share, width),
        vmem(chips, 4, kinds, 128, dtype=f32),
    ]
    return pl.pallas_call(
        functools.partial(back_kernel, count, gain_row),
        out_shape=(
            S((tokens, width), low),
            S((4, share, 3 * group), low),
            S((share, width), f32),
            S((4, kinds, 128), f32),
        ),
        in_specs=[ANY] * 8 + [pl.BlockSpec(memory_space=pltpu.SMEM)],
        out_specs=(ANY,) * 4,
        scratch_shapes=[
            vmem(full, width),
            vmem(*proj.shape),
            vmem(*attended.shape),
            vmem(*sums.shape, dtype=f32),
            vmem(*normed.shape),
            vmem(*heads.shape),
            vmem(group, width),
            vmem(*small.shape, dtype=f32),
            vmem(tokens, group),
            vmem(8, tokens, dtype=f32),
            vmem(local_heads * tokens, group),
            vmem(local_heads * tokens, group),
            vmem(4 * local_heads, tokens, group),
            vmem(4 * local_heads, tokens, group),
            vmem(tokens, local_heads * tokens),
            vmem(tokens, local_heads * tokens),
            vmem(tokens, group, dtype=f32),
            vmem(full, group, dtype=f32),
            vmem(full, group, dtype=f32),
            vmem(full, 3 * group),
            vmem(4, tokens, width),
            vmem(width, 3 * group),
            vmem(group, width),
            vmem(1, width, dtype=f32),
            *sets,
            *sets,
            *sets,
            vmem(4, share, 3 * group),
            vmem(share, width, dtype=f32),
            vmem(4, kinds, 128, dtype=f32),
            vmem(2, 2, tokens // 2, width),
            vmem(2, tokens // 2, width),
            dma((3, 2)), dma((3, 2)),
            dma((2, chips)), dma((2, chips)), dma((4, chips)), dma((4, chips)),
            dma((7, chips)), dma((7, chips)),
            dma((3, 3)), dma((3, 3)), dma((3, 2)), dma((3, 2)), dma((8,)), dma((5,)),
        ],
        compiler_params=pltpu.CompilerParams(
            collective_id=number, has_side_effects=True, vmem_limit_bytes=56 * 2**20
        ),
    )(grad, proj, attended, sums, normed, heads, mix, small, lengths)


def shards(
    hidden,
    lengths,
    expert_ids,
    attn_gain,
    qkv_weight,
    out_weight,
    moe_gain,
    router_weight,
    expert_in,
    expert_out,
    out_grad,
):
    S = jax.ShapeDtypeStruct
    low = jnp.bfloat16
    owners = lax.axis_size("fsdp")
    seq_place = lax.axis_index("seq")
    seq_count = lax.axis_size("seq")
    tokens, width = hidden.shape[1], hidden.shape[2]
    full_len = tokens * seq_count
    group_width = width // seq_count
    rows_own = qkv_weight.shape[0]
    length = lengths[0]
    experts_all = router_weight.shape[1]
    small = jnp.concatenate([router_weight, attn_gain[:, None], moe_gain[:, None]], axis=1)
    small = jnp.pad(small, ((0, 0), (0, -small.shape[1] % 128)))
    expert_local = expert_in.shape[0]
    capacity = -(-max(2, 2 * tokens // experts_all) // 16) * 16
    slots = experts_all * capacity

    position = seq_place * tokens + jnp.arange(tokens, dtype=jnp.int32)
    valid = (position < length).astype(jnp.float32)[:, None]
    chosen = expert_ids[0, :, 0]
    choose = chosen[:, None] == jnp.arange(experts_all, dtype=jnp.int32)[None, :]
    order = jnp.arange(tokens, dtype=jnp.int32)
    earlier = (order[None, :] < order[:, None]) & (chosen[None, :] == chosen[:, None])
    ranks = jnp.sum(earlier.astype(jnp.int32), axis=1)
    slot = chosen * capacity + ranks
    hit = jnp.arange(slots, dtype=jnp.int32)[:, None] == slot[None, :]
    dispatch = hit.astype(low)

    def to_owners(rows, number):
        return exchange(
            "fsdp",
            owners,
            (rows.reshape(owners, expert_local, capacity, width),),
            (S((expert_local, owners, capacity, width), low),),
            ((lead, second),),
            number,
        )[0].reshape(expert_local, owners * capacity, width)

    def to_sources(rows, number):
        return exchange(
            "fsdp",
            owners,
            (rows.reshape(expert_local, owners, capacity, width),),
            (S((owners, expert_local, capacity, width), low),),
            ((second, lead),),
            number,
        )[0].reshape(slots, width)

    upstream_low = jnp.where(valid > 0, out_grad[0], 0).astype(low)
    upstream = upstream_low.astype(jnp.float32)
    up_rows = times(dispatch, upstream_low).astype(low)
    chips = owners // 2
    fused = 4 * owners * capacity <= 1024
    normed, weight_qkv, weight_mix, small, up_all, projected, attended, totals, mixed = front(
        hidden[0],
        qkv_weight.reshape(rows_own, 3, seq_count, group_width)
        .transpose(2, 0, 1, 3)
        .reshape(seq_count, rows_own, 3 * group_width),
        out_weight,
        small,
        up_rows.reshape(owners, expert_local, capacity, width),
        lengths,
        experts_all,
        SPREAD_FIRST if fused else chips,
        0,
    )
    weight_qkv = weight_qkv.reshape(width, 3 * group_width)
    weight_mix = weight_mix.reshape(width, width)
    weight_route = small[:, :experts_all]
    gain_one = small[:, experts_all].astype(jnp.float32)
    gain_two = small[:, experts_all + 1].astype(jnp.float32)
    if not fused:
        up_all = up_all.reshape(expert_local, chips, seq_count, 2 * capacity, width)
        chip, bit = lax.axis_index("fsdp") // 2, 1
        while bit < chips:
            pairs = up_all.reshape(expert_local, chips // (2 * bit), 2, bit, seq_count, 2 * capacity, width)
            up_all = jnp.where((chip // bit) % 2 == 1, pairs[:, :, ::-1], pairs)
            bit *= 2
        up_all = up_all.reshape(expert_local, chips, seq_count, 2 * capacity, width)
        up_all = up_all.transpose(0, 2, 1, 3, 4)
    inputs = hidden[0].astype(jnp.float32)
    middle = inputs + times(mixed, weight_mix)
    normed_two, norm_two_back = jax.vjp(scaled_norm, middle, gain_two)
    normed_two = normed_two.astype(low)
    logits = times(normed_two, weight_route)

    def gate_of(logit_rows):
        return jnp.sum(jnp.where(choose, jax.nn.softmax(logit_rows, axis=-1), 0.0), axis=-1)

    gate, gate_back = jax.vjp(gate_of, logits)
    sent = times(dispatch, normed_two).astype(low)
    if fused:
        (returned, grad_back), expert_in_grad, expert_out_grad = moe(
            sent.reshape(owners, expert_local, capacity, width),
            up_all,
            small,
            expert_in,
            expert_out,
            experts_all,
            5,
        )
        returned, grad_back = returned.reshape(slots, width), grad_back.reshape(slots, width)
    else:
        gate_rows = jnp.sum(jnp.where(hit, gate[None, :], 0.0), axis=1)
        gates = lax.all_to_all(
            gate_rows.reshape(owners, expert_local, capacity), "fsdp", split_axis=0, concat_axis=0, tiled=True
        )
        gates = lax.all_gather(gates, "seq", axis=0)
        gates = gates.transpose(2, 0, 1, 3).reshape(expert_local, seq_count * owners * capacity, 1)

        rows_all = spread(to_owners(sent, 5), 6)
        count = seq_count * owners * capacity
        rows_all = rows_all.reshape(expert_local, count, width)
        up_all = up_all.reshape(expert_local, count, width)
        grad_rows = (up_all.astype(jnp.float32) * gates).astype(low)

        def per_expert(form, left, right):
            return jnp.einsum(form, left, right, preferred_element_type=jnp.float32)

        inner = per_expert("jrd,jdf->jrf", rows_all, expert_in)
        active, active_back = jax.vjp(gelu_tanh, inner)
        active = active.astype(low)
        partial_out = per_expert("jrf,jfd->jrd", active, expert_out).astype(low)
        grad_active = per_expert("jrd,jfd->jrf", grad_rows, expert_out)
        grad_inner = active_back(grad_active)[0].astype(low)
        partial_back = per_expert("jrf,jdf->jrd", grad_inner, expert_in).astype(low)
        expert_out_grad = per_expert("jrf,jrd->jfd", active, grad_rows)
        expert_in_grad = per_expert("jrd,jrf->jdf", rows_all, grad_inner)

        shape = (expert_local, seq_count, owners * capacity, width)
        returned = to_sources(collect(partial_out.reshape(shape), 7), 8)
        grad_back = to_sources(collect(partial_back.reshape(shape), 9), 10)

    back_rows = transposed_times(dispatch, returned)
    output = valid * (middle + gate[:, None] * back_rows)
    grad_gate = jnp.sum(upstream * back_rows, axis=1)
    grad_logits = gate_back(grad_gate)[0].astype(low)
    grad_normed_two = times_transposed(grad_logits, weight_route) + transposed_times(dispatch, grad_back)
    grad_middle, grad_gain_two = norm_two_back(grad_normed_two)
    grad_middle = grad_middle + upstream
    grad_attn = grad_middle.astype(low)

    small_grad = jnp.concatenate([transposed_times(grad_logits, normed_two), jnp.zeros((1, width)), grad_gain_two[None]])
    small_grad = jnp.pad(small_grad, ((0, -small_grad.shape[0] % 8), (0, 0)))
    kinds = small_grad.shape[0]
    small_grad = small_grad.reshape(kinds, seq_count, group_width // 128, 128).transpose(1, 2, 0, 3)
    grad_normed, qkv_sum, mix_grad, small_sum = back(
        grad_attn,
        projected,
        attended,
        totals,
        normed,
        weight_qkv,
        weight_mix,
        small_grad,
        lengths,
        owners,
        experts_all,
        12,
    )
    qkv_weight_grad = (
        qkv_sum.astype(jnp.float32)
        .reshape(seq_count, rows_own, 3, group_width)
        .transpose(1, 2, 0, 3)
        .reshape(rows_own, 3 * width)
    )
    start = lax.axis_index("fsdp") * rows_own % 128
    small_sum = lax.dynamic_slice_in_dim(jnp.sum(small_sum, axis=0), start, rows_own, 1)
    _, norm_back = jax.vjp(scaled_norm, inputs, gain_one)
    grad_inputs = norm_back(grad_normed.astype(jnp.float32))[0] + grad_middle
    return (
        output.astype(low)[None],
        grad_inputs[None],
        small_sum[experts_all] / attn_gain.astype(jnp.float32),
        qkv_weight_grad,
        mix_grad,
        small_sum[experts_all + 1],
        small_sum[:experts_all].T,
        expert_in_grad.astype(jnp.float32),
        expert_out_grad.astype(jnp.float32),
    )


def solution(mesh):
    placed = (
        P("fsdp", "seq", None),
        P("fsdp"),
        P("fsdp", "seq", None),
        P(("seq", "fsdp")),
        P(("seq", "fsdp"), None),
        P(("seq", "fsdp"), None),
        P(("seq", "fsdp")),
        P(("seq", "fsdp"), None),
        P("fsdp", None, "seq"),
        P("fsdp", "seq", None),
        P("fsdp", "seq", None),
    )
    return jax.shard_map(
        shards,
        mesh=mesh,
        in_specs=placed,
        out_specs=(
            P("fsdp", "seq", None),
            P("fsdp", "seq", None),
            P(("seq", "fsdp")),
            P(("seq", "fsdp"), None),
            P(("seq", "fsdp"), None),
            P(("seq", "fsdp")),
            P(("seq", "fsdp"), None),
            P("fsdp", None, "seq"),
            P("fsdp", "seq", None),
        ),
        check_vma=False,
    )
```

```python
import functools

import jax
import jax.numpy as jnp
from jax import lax
from jax.experimental import pallas as pl
from jax.experimental.pallas import tpu as pltpu
from jax.sharding import PartitionSpec as P

HEAD_DIM = 64
EPS = 1e-05
MASKED = -1e30
ROOT = 0.7978845608028654
TILE = 256
SPREAD_FIRST = 3
TURN = (1, 3, 2, 0)
GRAD = 256
MESH = pl.DeviceIdType.MESH
ANY = pl.BlockSpec(memory_space=pl.ANY)


def scaled_norm(value, gain):
    return value * lax.rsqrt(jnp.mean(value * value, axis=-1, keepdims=True) + EPS) * gain


def gelu_tanh(value):
    return jax.nn.gelu(value, approximate=True)


def times(left, right):
    return jnp.dot(left, right, preferred_element_type=jnp.float32)


def times_transposed(left, right):
    return lax.dot_general(
        left, right, (((1,), (1,)), ((), ())), preferred_element_type=jnp.float32
    )


def transposed_times(left, right):
    return lax.dot_general(
        left, right, (((0,), (0,)), ((), ())), preferred_element_type=jnp.float32
    )


def greet(axis, peers):
    barrier = pltpu.get_barrier_semaphore()
    for peer in peers:
        pl.semaphore_signal(barrier, inc=1, device_id={axis: peer}, device_id_type=MESH)
    pl.semaphore_wait(barrier, len(peers))


def remote(axis, peer, source, target, send, receive):
    copy = pltpu.make_async_remote_copy(
        source, target, send, receive, device_id={axis: peer}, device_id_type=MESH
    )
    copy.start()
    return copy


def call(kernel, inputs, outputs, scratch, number):
    return pl.pallas_call(
        kernel,
        out_shape=outputs,
        in_specs=[ANY] * len(inputs),
        out_specs=jax.tree.map(lambda _: ANY, outputs),
        scratch_shapes=scratch,
        compiler_params=pltpu.CompilerParams(
            collective_id=number, has_side_effects=True, vmem_limit_bytes=60 * 2**20
        ),
    )(*inputs)


def exchange_kernel(axis, count, views, *refs):
    arrays = len(views)
    sources, targets = refs[:arrays], refs[arrays : 2 * arrays]
    send, receive, local = refs[2 * arrays :]
    me = lax.axis_index(axis)
    peers = [lax.rem(me + step, count) for step in range(1, count)]
    greet(axis, peers)
    copies = []
    for step, peer in enumerate(peers):
        for a, (out_of, into) in enumerate(views):
            copies.append(
                remote(
                    axis,
                    peer,
                    out_of(sources[a], peer),
                    into(targets[a], me),
                    send.at[a, step],
                    receive.at[a, step],
                )
            )
    for a, (out_of, into) in enumerate(views):
        copy = pltpu.make_async_copy(out_of(sources[a], me), into(targets[a], me), local.at[a])
        copy.start()
        copies.append(copy)
    for copy in copies:
        copy.wait()


def exchange(axis, count, inputs, outputs, views, number):
    arrays = len(views)
    return call(
        functools.partial(exchange_kernel, axis, count, views),
        inputs,
        outputs,
        [
            pltpu.SemaphoreType.DMA((arrays, count - 1)),
            pltpu.SemaphoreType.DMA((arrays, count - 1)),
            pltpu.SemaphoreType.DMA((arrays,)),
        ],
        number,
    )


def lead(ref, place):
    return ref.at[place]


def second(ref, place):
    return ref.at[:, place]


def whole(ref, place):
    return ref


def spread_kernel(source, target, send, receive, local):
    me = lax.axis_index("seq")
    one, two, both = me ^ 1, me ^ 2, me ^ 3
    half = source.shape[1] // 2
    greet("seq", [one, two])
    parts = (pl.ds(0, half), pl.ds(half, half))
    own = pltpu.make_async_copy(source, target.at[:, me], local)
    own.start()
    copies = {}
    for side, peer in enumerate((one, two)):
        for order in range(2):
            part = (order + side) % 2
            copies[side, part] = remote(
                "seq",
                peer,
                source.at[:, parts[part]],
                target.at[:, me, parts[part]],
                send.at[side, part],
                receive.at[side, part],
            )
    relayed = []
    for side, (origin, peer) in enumerate(((one, two), (two, one))):
        copies[side, side].wait_recv()
        block = target.at[:, origin, parts[side]]
        relayed.append(remote("seq", peer, block, block, send.at[2, side], receive.at[2, side]))
    for side in range(2):
        copies[side, 1 - side].wait_recv()
        for part in range(2):
            copies[side, part].wait_send()
    for copy in relayed:
        copy.wait()
    own.wait()


def spread(source, number):
    return call(
        spread_kernel,
        (source,),
        jax.ShapeDtypeStruct((source.shape[0], 4, *source.shape[1:]), source.dtype),
        [
            pltpu.SemaphoreType.DMA((3, 2)),
            pltpu.SemaphoreType.DMA((3, 2)),
            pltpu.SemaphoreType.DMA,
        ],
        number,
    )


def collect_kernel(source, target, mine, first, second_in, outgoing, load, send, receive, store):
    me = lax.axis_index("seq")
    one, two, both = me ^ 1, me ^ 2, me ^ 3
    width = source.shape[3] // 2
    greet("seq", [one, two])
    copies = []
    for side, (near, rest) in enumerate(((one, two), (two, one))):
        lanes = pl.ds(side * width, width)
        for order, block in enumerate((both, near)):
            copies.append(
                remote(
                    "seq",
                    near,
                    source.at[:, block, :, lanes],
                    first.at[side, order],
                    send.at[side, order],
                    receive.at[side, order],
                )
            )
        for order, block in enumerate((rest, me)):
            pltpu.make_async_copy(
                source.at[:, block, :, lanes], mine.at[side, order], load.at[side, order]
            ).start()
    passed = []
    for side, rest in enumerate((two, one)):
        copies[side * 2].wait_recv()
        pltpu.make_async_copy(mine.at[side, 0], mine.at[side, 0], load.at[side, 0]).wait()
        outgoing[side] = (
            mine[side, 0].astype(jnp.float32) + first[side, 0].astype(jnp.float32)
        ).astype(outgoing.dtype)
        passed.append(
            remote("seq", rest, outgoing.at[side], second_in.at[side], send.at[2, side], receive.at[2, side])
        )
    for side in range(2):
        copies[side * 2 + 1].wait_recv()
        pltpu.make_async_copy(mine.at[side, 1], mine.at[side, 1], load.at[side, 1]).wait()
        passed[side].wait_recv()
        mine[side, 1] = (
            mine[side, 1].astype(jnp.float32)
            + first[side, 1].astype(jnp.float32)
            + second_in[side].astype(jnp.float32)
        ).astype(mine.dtype)
        out = pltpu.make_async_copy(
            mine.at[side, 1], target.at[:, :, pl.ds(side * width, width)], store.at[side]
        )
        out.start()
    for side in range(2):
        pltpu.make_async_copy(
            mine.at[side, 1], target.at[:, :, pl.ds(side * width, width)], store.at[side]
        ).wait()
    for copy in copies + passed:
        copy.wait_send()


def collect(source, number):
    a, _, rows, width = source.shape
    dma = pltpu.SemaphoreType.DMA
    block = (a, rows, width // 2)
    return call(
        collect_kernel,
        (source,),
        jax.ShapeDtypeStruct((a, rows, width), source.dtype),
        [
            pltpu.VMEM((2, 2, *block), source.dtype),
            pltpu.VMEM((2, 2, *block), source.dtype),
            pltpu.VMEM((2, *block), source.dtype),
            pltpu.VMEM((2, *block), source.dtype),
            dma((2, 2)),
            dma((3, 2)),
            dma((3, 2)),
            dma((2,)),
        ],
        number,
    )


def moe_kernel(
    chips, cap, experts_all, spread_first, send_rows, up_rows, route, w_in, w_out,
    ret, dw_in, dw_out,
    R, U, G, A, I, PB, first, second, W1, W2, RT, stage,
    load, own, z_send, z_recv, s_send, s_recv, y_send, y_recv,
    c_send, c_recv, d_send, d_recv, r_send, r_recv, store,
):
    me, place = lax.axis_index("seq"), lax.axis_index("fsdp")
    one, two, both = me ^ 1, me ^ 2, me ^ 3
    chip, core = place // 2, lax.rem(place, 2)
    sibling = place ^ 1
    count = chips * 2
    part = 2 * cap
    chunk = 4 * part
    barrier = pltpu.get_barrier_semaphore()
    for peer in (one, two):
        pl.semaphore_signal(barrier, inc=1, device_id={"seq": peer}, device_id_type=MESH)
    for step in range(1, count):
        pl.semaphore_signal(
            barrier, inc=1, device_id={"fsdp": lax.rem(place + step, count)}, device_id_type=MESH
        )
    pl.semaphore_wait(barrier, 2 + count - 1)

    def rows_of(k, s):
        return pl.ds(k * chunk + s * part, part)

    loads = []

    def local(source, target, sem):
        copy = pltpu.make_async_copy(source, target, sem)
        copy.start()
        return copy

    dispatched = {}
    own_rows = []

    def dispatch(k):
        target = R.at[:, pl.ds(k * chunk + me * part + core * cap, cap)]
        if k == 0:
            own_rows.append(local(send_rows.at[place], target, own.at[0]))
        for c in range(2):
            if k or c:
                peer = (chip ^ k) * 2 + (core ^ c)
                dispatched[k, c] = remote(
                    "fsdp", peer, send_rows.at[peer], target, z_send.at[k, c], z_recv.at[k, c]
                )

    def z_arrived(k):
        if k == 0:
            own_rows[0].wait()
        for c in range(2):
            if k or c:
                dispatched[k, c].wait_recv()

    sent = {}

    def spread_out(a, k):
        for side, peer in enumerate((one, two)):
            for order in range(2):
                j = (order + side) % 2
                target = (U, R)[a].at[j, rows_of(k, me)]
                source = target if a else up_rows.at[j, rows_of(k, me)]
                sent[a, k, side, j] = remote(
                    "seq", peer, source, target, s_send.at[a, k, side, j], s_recv.at[a, k, side, j]
                )

    def relay(a, k):
        for side, (origin, peer) in enumerate(((one, two), (two, one))):
            sent[a, k, side, side].wait_recv()
            block = (U, R)[a].at[side, rows_of(k, origin)]
            sent[a, k, 2, side] = remote("seq", peer, block, block, y_send.at[a, k, side], y_recv.at[a, k, side])

    def all_arrived(a, k):
        for side in range(2):
            sent[a, k, side, 1 - side].wait_recv()
            sent[a, k, 2, side].wait_recv()

    def experts(k, j):
        rows = pl.ds(k * chunk, chunk)
        logits = times(R[j, rows, :], RT[...])
        lane = lax.broadcasted_iota(jnp.int32, logits.shape, 1)
        logits = jnp.where(lane < experts_all, logits, MASKED)
        powers = jnp.exp(logits - jnp.max(logits, axis=1, keepdims=True))
        picked = jnp.sum(jnp.where(lane == place * 2 + j, powers, 0.0), axis=1, keepdims=True)
        gate = picked / jnp.sum(powers, axis=1, keepdims=True)
        G[j, rows, :] = (U[j, rows, :].astype(jnp.float32) * gate).astype(G.dtype)

        @pl.loop(0, W1.shape[2] // TILE)
        def _(t):
            cols = pl.ds(pl.multiple_of(t * TILE, TILE), TILE)
            v = times(R[j, rows, :], W1[j, :, cols])
            grad = times_transposed(G[j, rows, :], W2[j, cols, :])
            square = v * v
            t = jnp.tanh(ROOT * v * (1.0 + 0.044715 * square))
            half = 0.5 * (1.0 + t)
            A[j, rows, cols] = (v * half).astype(A.dtype)
            slope = half + 0.5 * v * (1.0 - t * t) * (ROOT * (1.0 + 0.134145 * square))
            I[j, rows, cols] = (grad * slope).astype(I.dtype)

        @pl.loop(0, W1.shape[1] // TILE)
        def _(t):
            cols = pl.ds(pl.multiple_of(t * TILE, TILE), TILE)
            PB[0, j, rows, cols] = times(A[j, rows, :], W2[j, :, cols]).astype(PB.dtype)
            PB[1, j, rows, cols] = times_transposed(I[j, rows, :], W1[j, cols, :]).astype(PB.dtype)

    summed = {}

    def near_of(j):
        return (one, two) if j == 0 else (two, one)

    def collect_one(k, j):
        near, rest = near_of(j)
        for a in range(2):
            for order, block in enumerate((both, near)):
                summed[a, k, j, order] = remote(
                    "seq", near, PB.at[a, j, rows_of(k, block)], first.at[a, j, k, order],
                    c_send.at[a, j, k, order], c_recv.at[a, j, k, order],
                )

    def collect_two(k, j):
        near, rest = near_of(j)
        for a in range(2):
            summed[a, k, j, 0].wait_recv()
            first[a, j, k, 0] = (
                first[a, j, k, 0].astype(jnp.float32) + PB[a, j, rows_of(k, rest), :].astype(jnp.float32)
            ).astype(first.dtype)
            summed[a, k, j, 2] = remote(
                "seq", rest, first.at[a, j, k, 0], second.at[a, j, k], d_send.at[a, j, k], d_recv.at[a, j, k]
            )

    returns = {}

    def collect_three(k, j):
        for a in range(2):
            summed[a, k, j, 1].wait_recv()
            summed[a, k, j, 2].wait_recv()
            first[a, j, k, 1] = (
                first[a, j, k, 1].astype(jnp.float32)
                + PB[a, j, rows_of(k, me), :].astype(jnp.float32)
                + second[a, j, k].astype(jnp.float32)
            ).astype(first.dtype)
            to = chip ^ k
            target = ret.at[a, place, j]
            for c in range(2):
                if k == 0:
                    if c == 0:
                        returns[a, k, j, 0] = local(
                            first.at[a, j, k, 1, pl.ds(core * cap, cap)], target, own.at[1 + a * 2 + j]
                        )
                        returns[a, k, j, 1] = remote(
                            "fsdp", sibling, first.at[a, j, k, 1, pl.ds((core ^ 1) * cap, cap)], target,
                            r_send.at[a, j, k, 1], r_recv.at[a, j, k, 1],
                        )
                    continue
                returns[a, k, j, c] = remote(
                    "fsdp", to * 2 + (core ^ c), first.at[a, j, k, 1, pl.ds((core ^ c) * cap, cap)], target,
                    r_send.at[a, j, k, c], r_recv.at[a, j, k, c],
                )

    staged = {}

    def weight_grads(j, which, tiles):
        left, right, out = ((R, I, dw_in), (A, G, dw_out))[which]
        for m in tiles:
            slot = m % 2
            lanes = slice(m * GRAD, (m + 1) * GRAD)
            if slot in staged:
                staged.pop(slot).wait()

            @pl.loop(0, right.shape[2] // TILE)
            def _(t):
                cols = pl.ds(pl.multiple_of(t * TILE, TILE), TILE)
                stage[slot, :, cols] = transposed_times(left[j, :, lanes], right[j, :, cols]).astype(stage.dtype)

            staged[slot] = local(stage.at[slot], out.at[j, lanes], store.at[slot])

    later = range(spread_first, chips)
    turn = TURN
    away = [k for k in turn if k]
    dispatch(0)
    dispatch(away[0])
    dispatch(away[1])
    for j in range(2):
        loads.append(local(w_in.at[j], W1.at[j], load.at[j]))
        loads.append(local(w_out.at[j], W2.at[j], load.at[2 + j]))
    loads.append(local(route, RT, load.at[4]))
    early = spread_first * chunk
    for j in range(2):
        loads.append(local(up_rows.at[j, pl.ds(0, early)], U.at[j, pl.ds(0, early)], load.at[5 + j]))
    for n, k in enumerate(later):
        for j in range(2):
            block = rows_of(k, me)
            loads.append(local(up_rows.at[j, block], U.at[j, block], load.at[7 + 2 * n + j]))
    if turn[0]:
        for k in later:
            spread_out(0, k)
    z_arrived(turn[0])
    spread_out(1, turn[0])
    if not turn[0]:
        for k in later:
            spread_out(0, k)
    z_arrived(turn[1])
    spread_out(1, turn[1])
    dispatch(away[2])
    relay(1, turn[0])
    for copy in loads:
        copy.wait()
    for k in later:
        relay(0, k)
    z_arrived(turn[2])
    spread_out(1, turn[2])
    for n in range(chips):
        k = turn[n]
        all_arrived(1, k)
        if k >= spread_first:
            all_arrived(0, k)
        experts(k, 0)
        collect_one(k, 0)
        if n < 2:
            relay(1, turn[n + 1 + (n > 0)])
        if n == 0:
            z_arrived(turn[3])
            spread_out(1, turn[3])
        else:
            collect_two(turn[n - 1], 0)
        if n > 1:
            collect_three(turn[n - 2], 0)
        experts(k, 1)
        collect_one(k, 1)
        if n == 0:
            relay(1, turn[2])
        else:
            collect_two(turn[n - 1], 1)
        if n > 1:
            collect_three(turn[n - 2], 1)
    weight_grads(0, 0, range(4))
    collect_two(turn[3], 0)
    collect_three(turn[2], 0)
    collect_two(turn[3], 1)
    collect_three(turn[2], 1)
    weight_grads(0, 1, range(4))
    weight_grads(1, 0, range(2))
    collect_three(turn[3], 0)
    weight_grads(1, 0, range(2, 4))
    collect_three(turn[3], 1)
    weight_grads(1, 1, range(4))
    for copy in staged.values():
        copy.wait()
    for copy in dispatched.values():
        copy.wait_send()
    for copy in sent.values():
        copy.wait_send()
    for copy in summed.values():
        copy.wait_send()
    for (a, k, j, c), copy in returns.items():
        copy.wait()


def moe(send_rows, up_rows, route, w_in, w_out, experts_all, number):
    S, low, dma = jax.ShapeDtypeStruct, jnp.bfloat16, pltpu.SemaphoreType.DMA
    owners, _, cap, width = send_rows.shape
    chips = owners // 2
    hidden_units = w_in.shape[2]
    count = owners * cap * 4
    part = 2 * cap

    def vmem(*shape, dtype=low):
        return pltpu.VMEM(shape, dtype)

    return pl.pallas_call(
        functools.partial(moe_kernel, chips, cap, experts_all, SPREAD_FIRST),
        out_shape=(
            S((2, owners, 2, cap, width), low),
            S(w_in.shape, low),
            S(w_out.shape, low),
        ),
        in_specs=[ANY] * 5,
        out_specs=(ANY,) * 3,
        scratch_shapes=[
            vmem(2, count, width),
            vmem(2, count, width),
            vmem(2, count, width),
            vmem(2, count, hidden_units),
            vmem(2, count, hidden_units),
            vmem(2, 2, count, width),
            vmem(2, 2, chips, 2, part, width),
            vmem(2, 2, chips, part, width),
            vmem(*w_in.shape),
            vmem(*w_out.shape),
            vmem(*route.shape),
            vmem(2, GRAD, max(width, hidden_units)),
            dma((7 + 2 * (chips - SPREAD_FIRST),)),
            dma((5,)),
            dma((chips, 2)),
            dma((chips, 2)),
            dma((2, chips, 2, 2)),
            dma((2, chips, 2, 2)),
            dma((2, chips, 2)),
            dma((2, chips, 2)),
            dma((2, 2, chips, 2)),
            dma((2, 2, chips, 2)),
            dma((2, 2, chips)),
            dma((2, 2, chips)),
            dma((2, 2, chips, 2)),
            dma((2, 2, chips, 2)),
            dma((2,)),
        ],
        compiler_params=pltpu.CompilerParams(
            collective_id=number, has_side_effects=True, vmem_limit_bytes=60 * 2**20
        ),
        cost_estimate=pl.CostEstimate(
            flops=12 * 2 * count * width * hidden_units, bytes_accessed=2**25, transcendentals=0
        ),
    )(send_rows, up_rows, route, w_in, w_out)


def front_kernel(
    count, cap, experts_all, spread_here, hidden, qkv_weight, mix, out_grad, router, gain_a, gain_b, ids, length,
    normed_out, heads_out, mix_out, small_out, gains_out, up, projected_out, attended_out, sums_out,
    middle_out, low_out, logits_out, sent_out, hit_out,
    staged, hid, heads_all, small_own, small_all, gains, normed, proj, attended, sums, acc, stat,
    mix_all, up_low, rows, hit, mixed, middle, normed_low, logits, sent_rows,
    h_send, h_recv, q_send, q_recv, f_send, f_recv, n_send, n_recv, u_send, u_recv, m_send, m_recv,
    s_send, s_recv, x_send, x_recv, y_send, y_recv, local,
):
    me, place = lax.axis_index("seq"), lax.axis_index("fsdp")
    one, two, both = me ^ 1, me ^ 2, me ^ 3
    others = (one, two, both)
    chips = count // 2
    chip, core = place // 2, lax.rem(place, 2)
    sibling = place ^ 1
    share = mix.shape[0]
    tokens = hidden.shape[0]
    group = attended.shape[1]
    part, chunk = 2 * cap, 8 * cap
    barrier = pltpu.get_barrier_semaphore()
    for peer in others:
        pl.semaphore_signal(barrier, inc=1, device_id={"seq": peer}, device_id_type=MESH)
    for step in range(1, count):
        pl.semaphore_signal(
            barrier, inc=1, device_id={"fsdp": lax.rem(place + step, count)}, device_id_type=MESH
        )
    pl.semaphore_wait(barrier, 3 + count - 1)

    def keep(source, target, number):
        copy = pltpu.make_async_copy(source, target, local.at[number])
        copy.start()
        return copy

    def far(k):
        return (chip ^ k) * 2 + core

    away, near = {}, {}

    def block(a, owner):
        if a == 0:
            return mix_all.at[me, owner // 2, core]
        if a == 1:
            return small_all.at[pl.ds(pl.multiple_of((me * count + owner) * share, share), share)]
        return heads_all.at[:, owner]

    own_of = (mix, small_own, staged)

    def send_far(a):
        for k in range(1, chips):
            away[a, k] = remote("fsdp", far(k), own_of[a], block(a, place), f_send.at[a, k], f_recv.at[a, k])

    def send_near(a):
        near[a, 0] = remote("fsdp", sibling, own_of[a], block(a, place), n_send.at[a, 0], n_recv.at[a, 0])

    def pass_on(a):
        for k in range(1, chips):
            away[a, k].wait_recv()
            arrived = block(a, far(k))
            near[a, k] = remote("fsdp", sibling, arrived, arrived, n_send.at[a, k], n_recv.at[a, k])

    direct = {}

    def both_ways(name, views, sources, send, receive):
        for side, peer in enumerate((one, two)):
            for order in range(2):
                p = (order + side) % 2
                direct[name, side, p] = remote(
                    "seq", peer, sources[p], views[p](me), send.at[side, p], receive.at[side, p]
                )

    def relay(name, views, send, receive):
        for side, (origin, peer) in enumerate(((one, two), (two, one))):
            direct[name, side, side].wait_recv()
            source = views[side](origin)
            direct[name, 2, side] = remote("seq", peer, source, source, send.at[2, side], receive.at[2, side])

    def arrived(name):
        for side in range(2):
            direct[name, side, 1 - side].wait_recv()
            direct[name, 2, side].wait_recv()

    moved = {}

    def send_rows(k):
        for c in range(2):
            if k == 0 and c == 0:
                continue
            peer = (chip ^ k) * 2 + (core ^ c)
            moved[k, c] = remote(
                "fsdp", peer, rows.at[peer], up.at[:, pl.ds(k * chunk + me * part + core * cap, cap)],
                u_send.at[k, c], u_recv.at[k, c],
            )

    columns = [
        (pl.ds(p * group, group), lambda to, p=p: pl.ds(pl.multiple_of((p * 4 + to) * group, group), group))
        for p in range(3)
    ]
    exchanged = [
        remote(
            "seq", peer, qkv_weight.at[:, view(peer)], staged.at[me, :, into], q_send.at[i, p], q_recv.at[i, p]
        )
        for i, peer in enumerate(others)
        for p, (into, view) in enumerate(columns)
    ]
    half = tokens // 2
    hidden_views = [
        lambda origin, p=p: hid.at[pl.ds(origin * tokens + p * half, half)] for p in range(2)
    ]
    both_ways("hidden", hidden_views, [hidden.at[pl.ds(p * half, half)] for p in range(2)], h_send, h_recv)
    send_far(0)
    own_heads = [
        keep(qkv_weight.at[:, view(me)], staged.at[me, :, into], 14 + p) for p, (into, view) in enumerate(columns)
    ]
    own_hidden = keep(hidden, hid.at[pl.ds(me * tokens, tokens)], 1)
    own_mix = keep(mix, block(0, place), 2)
    own_grad = keep(out_grad, up_low, 13)
    at_lane = lax.broadcasted_iota(jnp.int32, small_own.shape, 1)
    square = lax.broadcasted_iota(jnp.int32, (share, share), 0) == lax.broadcasted_iota(jnp.int32, (share, share), 1)
    stat[:share, :] = jnp.zeros((share, 128), jnp.float32)
    stat[:share, :experts_all] = router[...].astype(jnp.float32)
    packed = stat[:share, :]
    for n, gain in enumerate((gain_a, gain_b)):
        column = jnp.sum(jnp.where(square, gain[...].astype(jnp.float32), 0.0), axis=1, keepdims=True)
        packed = jnp.where(at_lane == experts_all + n, column, packed)
    small_own[...] = packed.astype(small_own.dtype)
    send_far(1)
    send_near(1)
    own_small = keep(small_own, block(1, place), 3)
    chosen = ids[...].astype(jnp.float32)
    across = jnp.transpose(jnp.broadcast_to(chosen, (tokens, 128)))[:1]
    first = lax.broadcasted_iota(jnp.int32, (tokens, tokens), 0)
    second = lax.broadcasted_iota(jnp.int32, (tokens, tokens), 1)
    ranks = jnp.sum(jnp.where((chosen == across) & (first < second), 1.0, 0.0), axis=0, keepdims=True)
    slot = (across * cap + ranks).astype(jnp.int32)
    hit[...] = jnp.where(lax.broadcasted_iota(jnp.int32, hit.shape, 0) == slot, 1.0, 0.0).astype(hit.dtype)
    own_grad.wait()
    position = me * tokens + lax.broadcasted_iota(jnp.int32, (tokens, 1), 0)
    up_low[...] = jnp.where(position < length[0], up_low[...].astype(jnp.float32), 0.0).astype(up_low.dtype)

    def to_slots(values, target):
        @pl.loop(0, count)
        def _(owner):
            picked = hit[pl.ds(pl.multiple_of(owner * 2 * cap, 2 * cap), 2 * cap), :]
            target[owner] = times(picked, values[...]).astype(target.dtype).reshape(target.shape[1:])

    to_slots(up_low, rows)
    own_rows = keep(rows.at[place], up.at[:, pl.ds(me * part + core * cap, cap)], 4)
    send_rows(0)
    hit_kept = keep(hit, hit_out, 0)
    pass_on(1)
    for copy in own_heads:
        copy.wait()
    for copy in exchanged:
        copy.wait_recv()
    own_block = keep(staged, heads_all.at[:, place], 5)
    send_far(2)
    send_near(2)
    own_small.wait()
    for k in range(chips):
        near[1, k].wait_recv()
    mine = small_all.at[pl.ds(pl.multiple_of(me * count * share, share), count * share)]
    smalls = [remote("seq", peer, mine, mine, q_send.at[3, i], q_recv.at[3, i]) for i, peer in enumerate(others)]

    def up_views(k):
        return [lambda origin, j=j: up.at[j, pl.ds(k * chunk + origin * part, part)] for j in range(2)]

    def up_out(k):
        if k == 0:
            own_rows.wait()
        for c in range(2):
            if (k, c) in moved:
                moved[k, c].wait_recv()
        if k < spread_here:
            views = up_views(k)
            both_ways(("up", k), views, [views[0](me), views[1](me)], s_send.at[k], s_recv.at[k])

    def up_relay(k):
        if k < spread_here:
            relay(("up", k), up_views(k), s_send.at[k], s_recv.at[k])

    up_out(0)
    relay("hidden", hidden_views, h_send, h_recv)
    own_mix.wait()
    for k in range(1, chips):
        away[0, k].wait_recv()
    mix_views = [
        lambda origin, p=p: mix_all.at[origin, pl.ds(p * (chips // 2), chips // 2), core] for p in range(2)
    ]
    both_ways("mix", mix_views, [mix_views[p](me) for p in range(2)], m_send, m_recv)
    for copy in smalls:
        copy.wait_recv()
    small_kept = keep(small_all, small_out, 6)
    own_hidden.wait()
    arrived("hidden")
    turned = jnp.transpose(small_all[...].astype(jnp.float32))
    gains[0:1, :] = turned[experts_all : experts_all + 1]
    gains[1:2, :] = turned[experts_all + 1 : experts_all + 2]
    gains_kept = keep(gains, gains_out, 17)
    gain = gains[0:1, :]

    @pl.loop(0, hid.shape[0] // 128)
    def _(t):
        place_rows = pl.ds(pl.multiple_of(t * 128, 128), 128)
        value = hid[place_rows, :].astype(jnp.float32)
        scale = lax.rsqrt(jnp.mean(value * value, axis=-1, keepdims=True) + EPS)
        normed[place_rows, :] = (value * scale * gain).astype(normed.dtype)

    normed_kept = keep(normed, normed_out, 7)
    pass_on(2)
    for k in range(1, chips):
        send_rows(k)
    up_relay(0)
    relay("mix", mix_views, m_send, m_recv)
    own_block.wait()
    for k in range(chips):
        near[2, k].wait_recv()
    heads_kept = keep(heads_all, heads_out, 8)
    width = hid.shape[1]

    for p in range(3):

        @pl.loop(0, hid.shape[0] // TILE)
        def _(t):
            place_rows = pl.ds(pl.multiple_of(t * TILE, TILE), TILE)
            weights = heads_all[:, :, :, p * group : (p + 1) * group].reshape(width, group)
            proj[place_rows, p * group : (p + 1) * group] = times(normed[place_rows, :], weights).astype(proj.dtype)

    projected_kept = keep(proj, projected_out, 9)
    head_of = lax.broadcasted_iota(jnp.int32, (tokens, group), 1) // HEAD_DIM
    sent = []
    for i in range(4):
        own = slice(i * tokens, (i + 1) * tokens)
        reach = (i + 1) * tokens

        @pl.loop(0, group // HEAD_DIM)
        def _(h):
            query = jnp.where(head_of == h, proj[own, :group] * (HEAD_DIM**-0.5), 0).astype(proj.dtype)
            scores = times_transposed(query, proj[:reach, group : 2 * group])
            column = lax.broadcasted_iota(jnp.int32, scores.shape, 1)
            row = lax.broadcasted_iota(jnp.int32, scores.shape, 0) + i * tokens
            scores = jnp.where((column <= row) & (column < length[0]), scores, MASKED)
            top = jnp.max(scores, axis=1, keepdims=True)
            powers = jnp.exp(scores - top)
            total = jnp.sum(powers, axis=1, keepdims=True)
            probs = (powers * (1.0 / total)).astype(proj.dtype)
            out = times(probs, proj[:reach, 2 * group :])
            acc[...] = jnp.where(head_of == h, out, acc[...])
            lane = lax.broadcasted_iota(jnp.int32, stat.shape, 1)
            stat[...] = jnp.where(lane == h, top + jnp.log(total), stat[...])

        attended[own, :] = acc[...].astype(attended.dtype)
        sums[:, own] = jnp.transpose(stat[...])[:8]
        target = mixed.at[:, pl.ds(pl.multiple_of(me * group, group), group)]

        @pl.when(me != i)
        def _():
            remote("seq", i, attended.at[own], target, x_send.at[i], x_recv.at[me])

        @pl.when(me == i)
        def _():
            pltpu.make_async_copy(attended.at[own], target, local.at[10]).start()

        if i == 1:
            up_relay(1)
        if i == 0:
            up_out(1)
            arrived("mix")
            both_cores = [
                remote(
                    "fsdp", sibling, mix_all.at[s, :, core], mix_all.at[s, :, core], y_send.at[s], y_recv.at[s]
                )
                for s in range(4)
            ]
    up_out(2)
    attended_kept = keep(attended, attended_out, 11)
    sums_kept = keep(sums, sums_out, 12)
    for i in range(4):
        target = mixed.at[:, pl.ds(i * group, group)]

        @pl.when(me != i)
        def _():
            copy = pltpu.make_async_remote_copy(
                attended.at[pl.ds(i * tokens, tokens)], target, x_send.at[i], x_recv.at[i],
                device_id={"seq": i}, device_id_type=MESH,
            )
            copy.wait()

        @pl.when(me == i)
        def _():
            pltpu.make_async_copy(attended.at[pl.ds(i * tokens, tokens)], target, local.at[10]).wait()

    up_relay(2)
    for copy in both_cores:
        copy.wait()
    mix_kept = keep(mix_all.at[me], mix_out, 18)
    for n in range(width // TILE):
        lanes = slice(n * TILE, (n + 1) * TILE)
        total = hid[pl.ds(pl.multiple_of(me * tokens, tokens), tokens), lanes].astype(jnp.float32)
        for s in range(4):
            weights = mix_all[s, :, :, :, lanes].reshape(group, TILE)
            total = total + times(mixed[:, s * group : (s + 1) * group], weights)
        middle[:, lanes] = total
    middle_kept = keep(middle, middle_out, 19)
    for t in range(tokens // 128):
        span = slice(t * 128, (t + 1) * 128)
        value = middle[span, :]
        scale = lax.rsqrt(jnp.mean(value * value, axis=-1, keepdims=True) + EPS)
        normed_low[span, :] = (value * scale * gains[1:2, :]).astype(normed_low.dtype)
    logits[...] = times(normed_low[...], small_all[...])
    to_slots(normed_low, sent_rows)
    last = [
        keep(normed_low, low_out, 20),
        keep(logits, logits_out, 21),
        keep(sent_rows, sent_out, 22),
    ]
    for k in range(3, chips):
        up_out(k)
        up_relay(k)
    for k in range(spread_here):
        arrived(("up", k))
    for copy in (*direct.values(), *exchanged, *smalls, *away.values(), *near.values(), *moved.values()):
        copy.wait_send()
    for copy in (
        small_kept, normed_kept, heads_kept, projected_kept, attended_kept, sums_kept,
        hit_kept, gains_kept, mix_kept, middle_kept, *last,
    ):
        copy.wait()


def front(hidden, qkv_weight, mix, out_grad, router, gain_a, gain_b, ids, lengths, count, cap, spread_here, number):
    S, dma, low, f32 = jax.ShapeDtypeStruct, pltpu.SemaphoreType.DMA, jnp.bfloat16, jnp.float32
    chips = count // 2
    tokens, width = hidden.shape
    experts_all = router.shape[1]
    group = qkv_weight.shape[1] // 12
    share = qkv_weight.shape[0]
    full = 4 * tokens
    lanes = -(-(experts_all + 2) // 128) * 128
    all_heads = (4, count, share, 3 * group)
    slots = experts_all * cap

    def vmem(*shape, dtype=low):
        return pltpu.VMEM(shape, dtype)

    near = pl.BlockSpec(memory_space=pltpu.VMEM)
    return pl.pallas_call(
        functools.partial(front_kernel, count, cap, experts_all, spread_here),
        out_shape=(
            S((full, width), low),
            S(all_heads, low),
            S((chips, 2, share, width), low),
            S((width, lanes), low),
            S((8, width), f32),
            S((2, 4 * count * cap, width), low),
            S((full, 3 * group), low),
            S((full, group), low),
            S((8, full), f32),
            S((tokens, width), f32),
            S((tokens, width), low),
            S((tokens, lanes), f32),
            S((count, 2, cap, width), low),
            S((slots, tokens), low),
        ),
        in_specs=[ANY] * 4 + [near] * 4 + [pl.BlockSpec(memory_space=pltpu.SMEM)],
        out_specs=(ANY,) * 14,
        scratch_shapes=[
            vmem(4, share, 3 * group),
            vmem(full, width),
            vmem(*all_heads),
            vmem(share, lanes),
            vmem(width, lanes),
            vmem(8, width, dtype=f32),
            vmem(full, width),
            vmem(full, 3 * group),
            vmem(full, group),
            vmem(8, full, dtype=f32),
            vmem(tokens, group, dtype=f32),
            vmem(tokens, 128, dtype=f32),
            vmem(4, chips, 2, share, width),
            vmem(tokens, width),
            vmem(count, 2, cap, width),
            vmem(slots, tokens),
            vmem(tokens, width),
            vmem(tokens, width, dtype=f32),
            vmem(tokens, width),
            vmem(tokens, lanes, dtype=f32),
            vmem(count, 2, cap, width),
            dma((3, 2)), dma((3, 2)), dma((4, 3)), dma((4, 3)),
            dma((3, chips)), dma((3, chips)), dma((3, chips)), dma((3, chips)),
            dma((chips, 2)), dma((chips, 2)), dma((3, 2)), dma((3, 2)),
            dma((chips, 3, 2)), dma((chips, 3, 2)), dma((4,)), dma((4,)), dma((4,)), dma((4,)), dma((23,)),
        ],
        compiler_params=pltpu.CompilerParams(
            collective_id=number, has_side_effects=True, vmem_limit_bytes=60 * 2**20
        ),
    )(hidden, qkv_weight, mix, out_grad, router, gain_a, gain_b, ids, lengths)


def back_kernel(
    count, gain_row, grad_in, proj_in, attended_in, sums_in, normed_in, heads_in, mix_in, small_in, length,
    normed_out, heads_out, mix_out, small_out,
    grads, proj, attended, sums, normed, heads, mix, small, grad_heads, delta, masked_grad, masked_query,
    masked_key, masked_value, probs, slopes, grad_query, grad_key, grad_value, grad_proj, part, weights, weights_mix, gain_sum,
    sib_a, sib_b, sib_c, own_a, own_b, own_c, got_a, got_b, got_c, total_a, total_b, total_c, first, second,
    g_send, g_recv, b_send, b_recv, bb_send, bb_recv, z_send, z_recv, x_send, x_recv, c_send, c_recv, load, keep,
):
    me, place = lax.axis_index("seq"), lax.axis_index("fsdp")
    one, two, both = me ^ 1, me ^ 2, me ^ 3
    others = (one, two, both)
    chips = count // 2
    chip, core = place // 2, lax.rem(place, 2)
    sibling = place ^ 1
    tokens, width = grad_in.shape
    group = attended.shape[1]
    share = weights.shape[0] // (4 * count)
    heads_local = group // HEAD_DIM
    low = grads.dtype
    barrier = pltpu.get_barrier_semaphore()
    for peer in others:
        pl.semaphore_signal(barrier, inc=1, device_id={"seq": peer}, device_id_type=MESH)
    for k in range(1, chips):
        pl.semaphore_signal(
            barrier, inc=1, device_id={"fsdp": (chip ^ k) * 2 + core}, device_id_type=MESH
        )
    pl.semaphore_signal(barrier, inc=1, device_id={"fsdp": sibling}, device_id_type=MESH)
    pl.semaphore_wait(barrier, 3 + chips)

    def local(source, to, sem):
        copy = pltpu.make_async_copy(source, to, sem)
        copy.start()
        return copy

    own_grad = local(grad_in, grads.at[pl.ds(me * tokens, tokens)], load.at[0])
    half = tokens // 2
    direct = {}
    for side, peer in enumerate((one, two)):
        for order in range(2):
            p = (order + side) % 2
            direct[side, p] = remote(
                "seq", peer, grad_in.at[pl.ds(p * half, half)], grads.at[pl.ds(me * tokens + p * half, half)],
                g_send.at[side, p], g_recv.at[side, p],
            )
    loads = [
        local(source, to, load.at[1 + i])
        for i, (source, to) in enumerate(
            (
                (proj_in, proj),
                (attended_in, attended),
                (sums_in, sums),
                (mix_in, mix),
                (heads_in, heads),
                (normed_in, normed),
                (small_in, small),
            )
        )
    ]
    for copy in loads:
        copy.wait()
    head_of = lax.broadcasted_iota(jnp.int32, (tokens, group), 1) // HEAD_DIM
    key_at = lax.broadcasted_iota(jnp.int32, (tokens, tokens), 0)
    for j in range(4):
        rows = slice(j * tokens, (j + 1) * tokens)
        for h in range(heads_local):
            key = proj[rows, group : 2 * group] * (HEAD_DIM**-0.5)
            masked_key[j * heads_local + h] = jnp.where(head_of == h, key, 0).astype(low)
            masked_value[j * heads_local + h] = jnp.where(head_of == h, proj[rows, 2 * group :], 0).astype(low)
    grad_key[...] = jnp.zeros_like(grad_key)
    grad_value[...] = jnp.zeros_like(grad_value)
    gain_sum[...] = jnp.zeros_like(gain_sum)

    def block(i, j, masked):
        rows = pl.ds(pl.multiple_of(i * tokens, tokens), tokens)
        keys = pl.ds(pl.multiple_of(j * tokens, tokens), tokens)
        hidden = j * tokens + key_at >= length[0]
        if masked:
            hidden = hidden | (key_at > lax.broadcasted_iota(jnp.int32, (tokens, tokens), 1))
        total = None
        for h in range(heads_local):
            lanes = slice(h * tokens, (h + 1) * tokens)
            key = masked_key[j * heads_local + h]
            scores = times_transposed(key, proj[rows, :group])
            scores = jnp.where(hidden, MASKED, scores)
            p = jnp.exp(scores - sums[h : h + 1, rows])
            probs[:, lanes] = p.astype(low)
            grad = times_transposed(masked_value[j * heads_local + h], grad_heads[...])
            slopes[:, lanes] = (p * (grad - delta[h : h + 1, :])).astype(low)
            term = transposed_times(slopes[:, lanes], key)
            total = term if total is None else total + term
        grad_query[...] += total
        grad_value[keys, :] += times(probs[...], masked_grad[...])
        grad_key[keys, :] += times(slopes[...], masked_query[...])

    def queries(i):
        rows = pl.ds(pl.multiple_of(i * tokens, tokens), tokens)
        grad_heads[...] = times_transposed(grads[rows, :], mix[...]).astype(low)
        out = grad_heads[...].astype(jnp.float32)
        turned = jnp.transpose(out * attended[rows, :].astype(jnp.float32))
        query = proj[rows, :group]
        for h in range(heads_local):
            delta[h : h + 1, :] = jnp.sum(turned[h * HEAD_DIM : (h + 1) * HEAD_DIM], axis=0, keepdims=True)
            masked_grad[h * tokens : (h + 1) * tokens, :] = jnp.where(head_of == h, out, 0).astype(low)
            masked_query[h * tokens : (h + 1) * tokens, :] = jnp.where(head_of == h, query, 0).astype(low)
        grad_query[...] = jnp.zeros_like(grad_query)

        @pl.loop(0, i)
        def _(j):
            block(i, j, False)

        block(i, i, True)
        grad_proj[rows, :group] = grad_query[...].astype(low)

    own_grad.wait()
    queries(me)
    for side, (origin, peer) in enumerate(((one, two), (two, one))):
        direct[side, side].wait_recv()
        source = grads.at[pl.ds(origin * tokens + side * half, half)]
        direct[2, side] = remote("seq", peer, source, source, g_send.at[2, side], g_recv.at[2, side])
    for side, origin in enumerate((one, two)):
        direct[side, 1 - side].wait_recv()
        queries(origin)
    for side in range(2):
        direct[2, side].wait_recv()
    for n in range(width // TILE):
        lanes = slice(n * TILE, (n + 1) * TILE)
        weights_mix[:, lanes] = transposed_times(attended[...], grads[:, lanes]).astype(low)
    order_of = [*range(1, chips), 0]
    to_sibling, away = {}, {}

    def rows_at(s, owner):
        return pl.ds(pl.multiple_of((s * count + owner) * share, share), share)

    def start_sibling(a, k, core_of):
        owner = (chip ^ k) * 2 + core_of
        if a == 1:
            return [
                remote(
                    "fsdp", sibling, weights_mix.at[pl.ds(pl.multiple_of(owner * share, share), share)], sib_b.at[k],
                    b_send.at[0, k], b_recv.at[0, k],
                )
            ]
        if a == 2:
            return [
                remote(
                    "fsdp", sibling, small.at[:, owner * share // 128], sib_c.at[k], b_send.at[1, k], b_recv.at[1, k]
                )
            ]
        raise ValueError(a)

    sib, own, got = (sib_a, sib_b, sib_c), (own_a, own_b, own_c), (got_a, got_b, got_c)
    totals = (total_a, total_b, total_c)

    def pair_sum(a, k):
        owner = (chip ^ k) * 2 + core
        for copy in to_sibling[a, k]:
            copy.wait_recv()
        if a == 1:
            mine = weights_mix[pl.ds(pl.multiple_of(owner * share, share), share), :]
            own_b[k] = (mine.astype(jnp.float32) + sib_b[k].astype(jnp.float32)).astype(low)
        else:
            for s in range(4):
                own_c[k, s] = small[s, owner * share // 128] + sib_c[k, s]
        if k:
            away[a, k] = remote(
                "fsdp", (chip ^ k) * 2 + core, own[a].at[k], got[a].at[k], z_send.at[a, k], z_recv.at[a, k]
            )

    for k in order_of:
        to_sibling[1, k] = start_sibling(1, k, core ^ 1)
    queries(both)
    for k in order_of:
        pair_sum(1, k)
    grad_proj[:, group : 2 * group] = (grad_key[...] * (HEAD_DIM**-0.5)).astype(low)
    grad_proj[:, 2 * group :] = grad_value[...].astype(low)
    for s in range(4):
        lanes = slice(s * group, (s + 1) * group)
        weights[lanes, :] = transposed_times(normed[:, lanes], grad_proj[...]).astype(low)
        for k in order_of:
            owner = (chip ^ k) * 2
            to_sibling[s + 3, k] = [
                remote(
                    "fsdp", sibling, weights.at[rows_at(s, owner + (core ^ 1))], sib_a.at[k, pl.ds(s * share, share)],
                    bb_send.at[s, k], bb_recv.at[s, k],
                )
            ]
    for s in range(4):
        rows = slice(s * share, (s + 1) * share)
        for k in order_of:
            owner = (chip ^ k) * 2 + core
            to_sibling[s + 3, k][0].wait_recv()
            own_a[k, rows, :] = (
                weights[rows_at(s, owner), :].astype(jnp.float32) + sib_a[k, rows, :].astype(jnp.float32)
            ).astype(low)
            if k:
                away[s + 3, k] = remote(
                    "fsdp", owner, own_a.at[k, pl.ds(s * share, share)], got_a.at[k, pl.ds(s * share, share)],
                    z_send.at[s + 3, k], z_recv.at[s + 3, k],
                )
    for j in range(4):
        own_rows = slice(j * tokens, (j + 1) * tokens)
        for n in range(width // TILE):
            lanes = slice(n * TILE, (n + 1) * TILE)
            back = times_transposed(grad_proj[own_rows, :], heads[lanes, :])
            gain_sum[:, lanes] += jnp.sum(back * normed[own_rows, lanes].astype(jnp.float32), axis=0, keepdims=True)
            part[j, :, lanes] = back.astype(low)
    summed = {}
    for side, (near, rest) in enumerate(((one, two), (two, one))):
        rows = pl.ds(side * half, half)
        for order, to in enumerate((both, near)):
            summed[side, order] = remote(
                "seq", near, part.at[to, rows], first.at[side, order], c_send.at[side, order], c_recv.at[side, order]
            )
    for b in range(width // 128):
        small[b // 2, b % 2, gain_row : gain_row + 1, :] = gain_sum[:, b * 128 : (b + 1) * 128]
    for k in order_of:
        to_sibling[2, k] = start_sibling(2, k, core ^ 1)
    for k in order_of:
        pair_sum(2, k)
    for side, rest in enumerate((two, one)):
        rows = slice(side * half, (side + 1) * half)
        summed[side, 0].wait_recv()
        first[side, 0] = (first[side, 0].astype(jnp.float32) + part[rest, rows, :].astype(jnp.float32)).astype(low)
        summed[side, 2] = remote("seq", rest, first.at[side, 0], second.at[side], c_send.at[2, side], c_recv.at[2, side])
    stored = []
    for side in range(2):
        rows = slice(side * half, (side + 1) * half)
        summed[side, 1].wait_recv()
        summed[side, 2].wait_recv()
        first[side, 1] = (
            part[me, rows, :].astype(jnp.float32)
            + first[side, 1].astype(jnp.float32)
            + second[side].astype(jnp.float32)
        ).astype(low)
        stored.append(local(first.at[side, 1], normed_out.at[pl.ds(side * half, half)], keep.at[side]))
    for a in (1, 0, 2):
        if a == 0:
            for s in range(4):
                rows = slice(s * share, (s + 1) * share)
                total = own_a[0, rows, :].astype(jnp.float32)
                for k in range(1, chips):
                    away[s + 3, k].wait_recv()
                    total = total + got_a[k, rows, :].astype(jnp.float32)
                total_a[s] = total.astype(low)
        else:
            total = own[a][0].astype(jnp.float32)
            for k in range(1, chips):
                away[a, k].wait_recv()
                total = total + got[a][k].astype(jnp.float32)
            totals[a][...] = total
    crossed = []
    for a, out in ((0, heads_out), (2, small_out)):
        for i, peer in enumerate(others):
            crossed.append(remote("seq", peer, totals[a].at[peer], out.at[me], x_send.at[a, i], x_recv.at[a, i]))
        stored.append(local(totals[a].at[me], out.at[me], keep.at[3 + a // 2]))
    stored.append(local(total_b, mix_out, keep.at[2]))
    for copy in (*stored, *crossed):
        copy.wait()
    for copy in (*summed.values(), *away.values(), *direct.values()):
        copy.wait_send()
    for copies in to_sibling.values():
        for copy in copies:
            copy.wait_send()


def back(grad, proj, attended, sums, normed, heads, mix, small, lengths, count, gain_row, number):
    S, dma, f32, low = jax.ShapeDtypeStruct, pltpu.SemaphoreType.DMA, jnp.float32, jnp.bfloat16
    tokens, width = grad.shape
    group = attended.shape[1]
    chips = count // 2
    full = 4 * tokens
    share = width // (4 * count)
    local_heads = group // HEAD_DIM
    kinds = small.shape[2]

    def vmem(*shape, dtype=low):
        return pltpu.VMEM(shape, dtype)

    sets = [
        vmem(chips, 4 * share, 3 * group),
        vmem(chips, share, width),
        vmem(chips, 4, kinds, 128, dtype=f32),
    ]
    return pl.pallas_call(
        functools.partial(back_kernel, count, gain_row),
        out_shape=(
            S((tokens, width), low),
            S((4, share, 3 * group), low),
            S((share, width), f32),
            S((4, kinds, 128), f32),
        ),
        in_specs=[ANY] * 8 + [pl.BlockSpec(memory_space=pltpu.SMEM)],
        out_specs=(ANY,) * 4,
        scratch_shapes=[
            vmem(full, width),
            vmem(*proj.shape),
            vmem(*attended.shape),
            vmem(*sums.shape, dtype=f32),
            vmem(*normed.shape),
            vmem(*heads.shape),
            vmem(group, width),
            vmem(*small.shape, dtype=f32),
            vmem(tokens, group),
            vmem(8, tokens, dtype=f32),
            vmem(local_heads * tokens, group),
            vmem(local_heads * tokens, group),
            vmem(4 * local_heads, tokens, group),
            vmem(4 * local_heads, tokens, group),
            vmem(tokens, local_heads * tokens),
            vmem(tokens, local_heads * tokens),
            vmem(tokens, group, dtype=f32),
            vmem(full, group, dtype=f32),
            vmem(full, group, dtype=f32),
            vmem(full, 3 * group),
            vmem(4, tokens, width),
            vmem(width, 3 * group),
            vmem(group, width),
            vmem(1, width, dtype=f32),
            *sets,
            *sets,
            *sets,
            vmem(4, share, 3 * group),
            vmem(share, width, dtype=f32),
            vmem(4, kinds, 128, dtype=f32),
            vmem(2, 2, tokens // 2, width),
            vmem(2, tokens // 2, width),
            dma((3, 2)), dma((3, 2)),
            dma((2, chips)), dma((2, chips)), dma((4, chips)), dma((4, chips)),
            dma((7, chips)), dma((7, chips)),
            dma((3, 3)), dma((3, 3)), dma((3, 2)), dma((3, 2)), dma((8,)), dma((5,)),
        ],
        compiler_params=pltpu.CompilerParams(
            collective_id=number, has_side_effects=True, vmem_limit_bytes=60 * 2**20
        ),
    )(grad, proj, attended, sums, normed, heads, mix, small, lengths)


def shards(
    hidden,
    lengths,
    expert_ids,
    attn_gain,
    qkv_weight,
    out_weight,
    moe_gain,
    router_weight,
    expert_in,
    expert_out,
    out_grad,
):
    S = jax.ShapeDtypeStruct
    low = jnp.bfloat16
    owners = lax.axis_size("fsdp")
    seq_place = lax.axis_index("seq")
    seq_count = lax.axis_size("seq")
    tokens, width = hidden.shape[1], hidden.shape[2]
    full_len = tokens * seq_count
    group_width = width // seq_count
    rows_own = qkv_weight.shape[0]
    length = lengths[0]
    experts_all = router_weight.shape[1]
    expert_local = expert_in.shape[0]
    capacity = -(-max(2, 2 * tokens // experts_all) // 16) * 16
    slots = experts_all * capacity

    position = seq_place * tokens + jnp.arange(tokens, dtype=jnp.int32)
    valid = (position < length).astype(jnp.float32)[:, None]
    chosen = expert_ids[0, :, 0]
    choose = chosen[:, None] == jnp.arange(experts_all, dtype=jnp.int32)[None, :]
    def to_owners(rows, number):
        return exchange(
            "fsdp",
            owners,
            (rows.reshape(owners, expert_local, capacity, width),),
            (S((expert_local, owners, capacity, width), low),),
            ((lead, second),),
            number,
        )[0].reshape(expert_local, owners * capacity, width)

    def to_sources(rows, number):
        return exchange(
            "fsdp",
            owners,
            (rows.reshape(expert_local, owners, capacity, width),),
            (S((owners, expert_local, capacity, width), low),),
            ((second, lead),),
            number,
        )[0].reshape(slots, width)

    upstream_low = jnp.where(valid > 0, out_grad[0], 0).astype(low)
    upstream = upstream_low.astype(jnp.float32)
    chips = owners // 2
    fused = 4 * owners * capacity <= 1024
    (
        normed,
        weight_qkv,
        mix_rows,
        small,
        gains,
        up_all,
        projected,
        attended,
        totals,
        middle,
        normed_two,
        logits,
        sent,
        dispatch,
    ) = front(
        hidden[0],
        qkv_weight,
        out_weight,
        out_grad[0],
        router_weight,
        attn_gain[None],
        moe_gain[None],
        expert_ids[0],
        lengths,
        owners,
        capacity,
        SPREAD_FIRST if fused else chips,
        0,
    )
    weight_qkv = weight_qkv.reshape(width, 3 * group_width)
    mix_rows = mix_rows.reshape(group_width, width)
    weight_route = small[:, :experts_all]
    gain_one, gain_two = gains[0], gains[1]
    if not fused:
        up_all = up_all.reshape(expert_local, chips, seq_count, 2 * capacity, width)
        chip, bit = lax.axis_index("fsdp") // 2, 1
        while bit < chips:
            pairs = up_all.reshape(expert_local, chips // (2 * bit), 2, bit, seq_count, 2 * capacity, width)
            up_all = jnp.where((chip // bit) % 2 == 1, pairs[:, :, ::-1], pairs)
            bit *= 2
        up_all = up_all.reshape(expert_local, chips, seq_count, 2 * capacity, width)
        up_all = up_all.transpose(0, 2, 1, 3, 4)
    inputs = hidden[0].astype(jnp.float32)
    _, norm_two_back = jax.vjp(scaled_norm, middle, gain_two)
    logits = logits[:, :experts_all]

    def gate_of(logit_rows):
        return jnp.sum(jnp.where(choose, jax.nn.softmax(logit_rows, axis=-1), 0.0), axis=-1)

    gate, gate_back = jax.vjp(gate_of, logits)
    if fused:
        (returned, grad_back), expert_in_grad, expert_out_grad = moe(
            sent,
            up_all,
            small,
            expert_in,
            expert_out,
            experts_all,
            5,
        )
        returned, grad_back = returned.reshape(slots, width), grad_back.reshape(slots, width)
    else:
        gate_rows = jnp.sum(jnp.where(dispatch > 0, gate[None, :], 0.0), axis=1)
        gates = lax.all_to_all(
            gate_rows.reshape(owners, expert_local, capacity), "fsdp", split_axis=0, concat_axis=0, tiled=True
        )
        gates = lax.all_gather(gates, "seq", axis=0)
        gates = gates.transpose(2, 0, 1, 3).reshape(expert_local, seq_count * owners * capacity, 1)

        rows_all = spread(to_owners(sent, 5), 6)
        count = seq_count * owners * capacity
        rows_all = rows_all.reshape(expert_local, count, width)
        up_all = up_all.reshape(expert_local, count, width)
        grad_rows = (up_all.astype(jnp.float32) * gates).astype(low)

        def per_expert(form, left, right):
            return jnp.einsum(form, left, right, preferred_element_type=jnp.float32)

        inner = per_expert("jrd,jdf->jrf", rows_all, expert_in)
        active, active_back = jax.vjp(gelu_tanh, inner)
        active = active.astype(low)
        partial_out = per_expert("jrf,jfd->jrd", active, expert_out).astype(low)
        grad_active = per_expert("jrd,jfd->jrf", grad_rows, expert_out)
        grad_inner = active_back(grad_active)[0].astype(low)
        partial_back = per_expert("jrf,jdf->jrd", grad_inner, expert_in).astype(low)
        expert_out_grad = per_expert("jrf,jrd->jfd", active, grad_rows)
        expert_in_grad = per_expert("jrd,jrf->jdf", rows_all, grad_inner)

        shape = (expert_local, seq_count, owners * capacity, width)
        returned = to_sources(collect(partial_out.reshape(shape), 7), 8)
        grad_back = to_sources(collect(partial_back.reshape(shape), 9), 10)

    back_rows = transposed_times(dispatch, returned)
    output = valid * (middle + gate[:, None] * back_rows)
    grad_gate = jnp.sum(upstream * back_rows, axis=1)
    grad_logits = gate_back(grad_gate)[0].astype(low)
    grad_normed_two = times_transposed(grad_logits, weight_route) + transposed_times(dispatch, grad_back)
    grad_middle, grad_gain_two = norm_two_back(grad_normed_two)
    grad_middle = grad_middle + upstream
    grad_attn = grad_middle.astype(low)

    small_grad = jnp.concatenate([transposed_times(grad_logits, normed_two), jnp.zeros((1, width)), grad_gain_two[None]])
    small_grad = jnp.pad(small_grad, ((0, -small_grad.shape[0] % 8), (0, 0)))
    kinds = small_grad.shape[0]
    small_grad = small_grad.reshape(kinds, seq_count, group_width // 128, 128).transpose(1, 2, 0, 3)
    grad_normed, qkv_sum, mix_grad, small_sum = back(
        grad_attn,
        projected,
        attended,
        totals,
        normed,
        weight_qkv,
        mix_rows,
        small_grad,
        lengths,
        owners,
        experts_all,
        12,
    )
    qkv_weight_grad = (
        qkv_sum.astype(jnp.float32)
        .reshape(seq_count, rows_own, 3, group_width)
        .transpose(1, 2, 0, 3)
        .reshape(rows_own, 3 * width)
    )
    start = lax.axis_index("fsdp") * rows_own % 128
    small_sum = lax.dynamic_slice_in_dim(jnp.sum(small_sum, axis=0), start, rows_own, 1)
    _, norm_back = jax.vjp(scaled_norm, inputs, gain_one)
    grad_inputs = norm_back(grad_normed.astype(jnp.float32))[0] + grad_middle
    return (
        output.astype(low)[None],
        grad_inputs[None],
        small_sum[experts_all] / attn_gain.astype(jnp.float32),
        qkv_weight_grad,
        mix_grad,
        small_sum[experts_all + 1],
        small_sum[:experts_all].T,
        expert_in_grad.astype(jnp.float32),
        expert_out_grad.astype(jnp.float32),
    )


def solution(mesh):
    placed = (
        P("fsdp", "seq", None),
        P("fsdp"),
        P("fsdp", "seq", None),
        P(("seq", "fsdp")),
        P(("seq", "fsdp"), None),
        P(("seq", "fsdp"), None),
        P(("seq", "fsdp")),
        P(("seq", "fsdp"), None),
        P("fsdp", None, "seq"),
        P("fsdp", "seq", None),
        P("fsdp", "seq", None),
    )
    return jax.shard_map(
        shards,
        mesh=mesh,
        in_specs=placed,
        out_specs=(
            P("fsdp", "seq", None),
            P("fsdp", "seq", None),
            P(("seq", "fsdp")),
            P(("seq", "fsdp"), None),
            P(("seq", "fsdp"), None),
            P(("seq", "fsdp")),
            P(("seq", "fsdp"), None),
            P("fsdp", None, "seq"),
            P("fsdp", "seq", None),
        ),
        check_vma=False,
    )
```

```python
import functools

import jax
import jax.numpy as jnp
from jax import lax
from jax.experimental import pallas as pl
from jax.experimental.pallas import tpu as pltpu
from jax.sharding import PartitionSpec as P

HEAD_DIM = 64
EPS = 1e-05
MASKED = -1e30
ROOT = 0.7978845608028654
TILE = 256
WIDEN = 512
STEP = 128
SPREAD_FIRST = 3
TURN = (1, 3, 2, 0)
GRAD = 256
MESH = pl.DeviceIdType.MESH
ANY = pl.BlockSpec(memory_space=pl.ANY)


def scaled_norm(value, gain):
    return value * lax.rsqrt(jnp.mean(value * value, axis=-1, keepdims=True) + EPS) * gain


def gelu_tanh(value):
    return jax.nn.gelu(value, approximate=True)


def times(left, right):
    return jnp.dot(left, right, preferred_element_type=jnp.float32)


def times_transposed(left, right):
    return lax.dot_general(
        left, right, (((1,), (1,)), ((), ())), preferred_element_type=jnp.float32
    )


def transposed_times(left, right):
    return lax.dot_general(
        left, right, (((0,), (0,)), ((), ())), preferred_element_type=jnp.float32
    )


def greet(axis, peers):
    barrier = pltpu.get_barrier_semaphore()
    for peer in peers:
        pl.semaphore_signal(barrier, inc=1, device_id={axis: peer}, device_id_type=MESH)
    pl.semaphore_wait(barrier, len(peers))


def remote(axis, peer, source, target, send, receive):
    copy = pltpu.make_async_remote_copy(
        source, target, send, receive, device_id={axis: peer}, device_id_type=MESH
    )
    copy.start()
    return copy


def call(kernel, inputs, outputs, scratch, number):
    return pl.pallas_call(
        kernel,
        out_shape=outputs,
        in_specs=[ANY] * len(inputs),
        out_specs=jax.tree.map(lambda _: ANY, outputs),
        scratch_shapes=scratch,
        compiler_params=pltpu.CompilerParams(
            collective_id=number, has_side_effects=True, vmem_limit_bytes=60 * 2**20
        ),
    )(*inputs)


def exchange_kernel(axis, count, views, *refs):
    arrays = len(views)
    sources, targets = refs[:arrays], refs[arrays : 2 * arrays]
    send, receive, local = refs[2 * arrays :]
    me = lax.axis_index(axis)
    peers = [lax.rem(me + step, count) for step in range(1, count)]
    greet(axis, peers)
    copies = []
    for step, peer in enumerate(peers):
        for a, (out_of, into) in enumerate(views):
            copies.append(
                remote(
                    axis,
                    peer,
                    out_of(sources[a], peer),
                    into(targets[a], me),
                    send.at[a, step],
                    receive.at[a, step],
                )
            )
    for a, (out_of, into) in enumerate(views):
        copy = pltpu.make_async_copy(out_of(sources[a], me), into(targets[a], me), local.at[a])
        copy.start()
        copies.append(copy)
    for copy in copies:
        copy.wait()


def exchange(axis, count, inputs, outputs, views, number):
    arrays = len(views)
    return call(
        functools.partial(exchange_kernel, axis, count, views),
        inputs,
        outputs,
        [
            pltpu.SemaphoreType.DMA((arrays, count - 1)),
            pltpu.SemaphoreType.DMA((arrays, count - 1)),
            pltpu.SemaphoreType.DMA((arrays,)),
        ],
        number,
    )


def lead(ref, place):
    return ref.at[place]


def second(ref, place):
    return ref.at[:, place]


def whole(ref, place):
    return ref


def spread_kernel(source, target, send, receive, local):
    me = lax.axis_index("seq")
    one, two, both = me ^ 1, me ^ 2, me ^ 3
    half = source.shape[1] // 2
    greet("seq", [one, two])
    parts = (pl.ds(0, half), pl.ds(half, half))
    own = pltpu.make_async_copy(source, target.at[:, me], local)
    own.start()
    copies = {}
    for side, peer in enumerate((one, two)):
        for order in range(2):
            part = (order + side) % 2
            copies[side, part] = remote(
                "seq",
                peer,
                source.at[:, parts[part]],
                target.at[:, me, parts[part]],
                send.at[side, part],
                receive.at[side, part],
            )
    relayed = []
    for side, (origin, peer) in enumerate(((one, two), (two, one))):
        copies[side, side].wait_recv()
        block = target.at[:, origin, parts[side]]
        relayed.append(remote("seq", peer, block, block, send.at[2, side], receive.at[2, side]))
    for side in range(2):
        copies[side, 1 - side].wait_recv()
        for part in range(2):
            copies[side, part].wait_send()
    for copy in relayed:
        copy.wait()
    own.wait()


def spread(source, number):
    return call(
        spread_kernel,
        (source,),
        jax.ShapeDtypeStruct((source.shape[0], 4, *source.shape[1:]), source.dtype),
        [
            pltpu.SemaphoreType.DMA((3, 2)),
            pltpu.SemaphoreType.DMA((3, 2)),
            pltpu.SemaphoreType.DMA,
        ],
        number,
    )


def collect_kernel(source, target, mine, first, second_in, outgoing, load, send, receive, store):
    me = lax.axis_index("seq")
    one, two, both = me ^ 1, me ^ 2, me ^ 3
    width = source.shape[3] // 2
    greet("seq", [one, two])
    copies = []
    for side, (near, rest) in enumerate(((one, two), (two, one))):
        lanes = pl.ds(side * width, width)
        for order, block in enumerate((both, near)):
            copies.append(
                remote(
                    "seq",
                    near,
                    source.at[:, block, :, lanes],
                    first.at[side, order],
                    send.at[side, order],
                    receive.at[side, order],
                )
            )
        for order, block in enumerate((rest, me)):
            pltpu.make_async_copy(
                source.at[:, block, :, lanes], mine.at[side, order], load.at[side, order]
            ).start()
    passed = []
    for side, rest in enumerate((two, one)):
        copies[side * 2].wait_recv()
        pltpu.make_async_copy(mine.at[side, 0], mine.at[side, 0], load.at[side, 0]).wait()
        outgoing[side] = (
            mine[side, 0].astype(jnp.float32) + first[side, 0].astype(jnp.float32)
        ).astype(outgoing.dtype)
        passed.append(
            remote("seq", rest, outgoing.at[side], second_in.at[side], send.at[2, side], receive.at[2, side])
        )
    for side in range(2):
        copies[side * 2 + 1].wait_recv()
        pltpu.make_async_copy(mine.at[side, 1], mine.at[side, 1], load.at[side, 1]).wait()
        passed[side].wait_recv()
        mine[side, 1] = (
            mine[side, 1].astype(jnp.float32)
            + first[side, 1].astype(jnp.float32)
            + second_in[side].astype(jnp.float32)
        ).astype(mine.dtype)
        out = pltpu.make_async_copy(
            mine.at[side, 1], target.at[:, :, pl.ds(side * width, width)], store.at[side]
        )
        out.start()
    for side in range(2):
        pltpu.make_async_copy(
            mine.at[side, 1], target.at[:, :, pl.ds(side * width, width)], store.at[side]
        ).wait()
    for copy in copies + passed:
        copy.wait_send()


def collect(source, number):
    a, _, rows, width = source.shape
    dma = pltpu.SemaphoreType.DMA
    block = (a, rows, width // 2)
    return call(
        collect_kernel,
        (source,),
        jax.ShapeDtypeStruct((a, rows, width), source.dtype),
        [
            pltpu.VMEM((2, 2, *block), source.dtype),
            pltpu.VMEM((2, 2, *block), source.dtype),
            pltpu.VMEM((2, *block), source.dtype),
            pltpu.VMEM((2, *block), source.dtype),
            dma((2, 2)),
            dma((3, 2)),
            dma((3, 2)),
            dma((2,)),
        ],
        number,
    )


def moe_kernel(
    chips, cap, experts_all, spread_first, send_rows, up_rows, route, w_in, w_out,
    ret, dw_in, dw_out,
    R, U, G, A, I, PB, first, second, W1, W2, RT, stage,
    load, own, z_send, z_recv, s_send, s_recv, y_send, y_recv,
    c_send, c_recv, d_send, d_recv, r_send, r_recv, store,
):
    me, place = lax.axis_index("seq"), lax.axis_index("fsdp")
    one, two, both = me ^ 1, me ^ 2, me ^ 3
    chip, core = place // 2, lax.rem(place, 2)
    sibling = place ^ 1
    count = chips * 2
    part = 2 * cap
    chunk = 4 * part
    barrier = pltpu.get_barrier_semaphore()
    for peer in (one, two):
        pl.semaphore_signal(barrier, inc=1, device_id={"seq": peer}, device_id_type=MESH)
    for step in range(1, count):
        pl.semaphore_signal(
            barrier, inc=1, device_id={"fsdp": lax.rem(place + step, count)}, device_id_type=MESH
        )
    pl.semaphore_wait(barrier, 2 + count - 1)

    def rows_of(k, s):
        return pl.ds(k * chunk + s * part, part)

    loads = []

    def local(source, target, sem):
        copy = pltpu.make_async_copy(source, target, sem)
        copy.start()
        return copy

    dispatched = {}
    own_rows = []

    def dispatch(k):
        target = R.at[:, pl.ds(k * chunk + me * part + core * cap, cap)]
        if k == 0:
            own_rows.append(local(send_rows.at[place], target, own.at[0]))
        for c in range(2):
            if k or c:
                peer = (chip ^ k) * 2 + (core ^ c)
                dispatched[k, c] = remote(
                    "fsdp", peer, send_rows.at[peer], target, z_send.at[k, c], z_recv.at[k, c]
                )

    def z_arrived(k):
        if k == 0:
            own_rows[0].wait()
        for c in range(2):
            if k or c:
                dispatched[k, c].wait_recv()

    sent = {}

    def spread_out(a, k):
        for side, peer in enumerate((one, two)):
            for order in range(2):
                j = (order + side) % 2
                target = (U, R)[a].at[j, rows_of(k, me)]
                source = target if a else up_rows.at[j, rows_of(k, me)]
                sent[a, k, side, j] = remote(
                    "seq", peer, source, target, s_send.at[a, k, side, j], s_recv.at[a, k, side, j]
                )

    def relay(a, k):
        for side, (origin, peer) in enumerate(((one, two), (two, one))):
            sent[a, k, side, side].wait_recv()
            block = (U, R)[a].at[side, rows_of(k, origin)]
            sent[a, k, 2, side] = remote("seq", peer, block, block, y_send.at[a, k, side], y_recv.at[a, k, side])

    def all_arrived(a, k):
        for side in range(2):
            sent[a, k, side, 1 - side].wait_recv()
            sent[a, k, 2, side].wait_recv()

    def experts(k, j):
        rows = pl.ds(k * chunk, chunk)
        logits = times(R[j, rows, :], RT[...])
        lane = lax.broadcasted_iota(jnp.int32, logits.shape, 1)
        logits = jnp.where(lane < experts_all, logits, MASKED)
        powers = jnp.exp(logits - jnp.max(logits, axis=1, keepdims=True))
        picked = jnp.sum(jnp.where(lane == place * 2 + j, powers, 0.0), axis=1, keepdims=True)
        gate = picked / jnp.sum(powers, axis=1, keepdims=True)
        G[j, rows, :] = (U[j, rows, :].astype(jnp.float32) * gate).astype(G.dtype)

        @pl.loop(0, W1.shape[2] // TILE)
        def _(t):
            cols = pl.ds(pl.multiple_of(t * TILE, TILE), TILE)
            v = times(R[j, rows, :], W1[j, :, cols])
            grad = times_transposed(G[j, rows, :], W2[j, cols, :])
            square = v * v
            t = jnp.tanh(ROOT * v * (1.0 + 0.044715 * square))
            half = 0.5 * (1.0 + t)
            A[j, rows, cols] = (v * half).astype(A.dtype)
            slope = half + 0.5 * v * (1.0 - t * t) * (ROOT * (1.0 + 0.134145 * square))
            I[j, rows, cols] = (grad * slope).astype(I.dtype)

        @pl.loop(0, W1.shape[1] // TILE)
        def _(t):
            cols = pl.ds(pl.multiple_of(t * TILE, TILE), TILE)
            PB[0, j, rows, cols] = times(A[j, rows, :], W2[j, :, cols]).astype(PB.dtype)
            PB[1, j, rows, cols] = times_transposed(I[j, rows, :], W1[j, cols, :]).astype(PB.dtype)

    summed = {}

    def near_of(j):
        return (one, two) if j == 0 else (two, one)

    def collect_one(k, j):
        near, rest = near_of(j)
        for a in range(2):
            for order, block in enumerate((both, near)):
                summed[a, k, j, order] = remote(
                    "seq", near, PB.at[a, j, rows_of(k, block)], first.at[a, j, k, order],
                    c_send.at[a, j, k, order], c_recv.at[a, j, k, order],
                )

    def collect_two(k, j):
        near, rest = near_of(j)
        for a in range(2):
            summed[a, k, j, 0].wait_recv()
            first[a, j, k, 0] = (
                first[a, j, k, 0].astype(jnp.float32) + PB[a, j, rows_of(k, rest), :].astype(jnp.float32)
            ).astype(first.dtype)
            summed[a, k, j, 2] = remote(
                "seq", rest, first.at[a, j, k, 0], second.at[a, j, k], d_send.at[a, j, k], d_recv.at[a, j, k]
            )

    returns = {}

    def collect_three(k, j):
        for a in range(2):
            summed[a, k, j, 1].wait_recv()
            summed[a, k, j, 2].wait_recv()
            first[a, j, k, 1] = (
                first[a, j, k, 1].astype(jnp.float32)
                + PB[a, j, rows_of(k, me), :].astype(jnp.float32)
                + second[a, j, k].astype(jnp.float32)
            ).astype(first.dtype)
            to = chip ^ k
            target = ret.at[a, place, j]
            for c in range(2):
                if k == 0:
                    if c == 0:
                        returns[a, k, j, 0] = local(
                            first.at[a, j, k, 1, pl.ds(core * cap, cap)], target, own.at[1 + a * 2 + j]
                        )
                        returns[a, k, j, 1] = remote(
                            "fsdp", sibling, first.at[a, j, k, 1, pl.ds((core ^ 1) * cap, cap)], target,
                            r_send.at[a, j, k, 1], r_recv.at[a, j, k, 1],
                        )
                    continue
                returns[a, k, j, c] = remote(
                    "fsdp", to * 2 + (core ^ c), first.at[a, j, k, 1, pl.ds((core ^ c) * cap, cap)], target,
                    r_send.at[a, j, k, c], r_recv.at[a, j, k, c],
                )

    staged = {}

    def weight_grads(j, which, tiles):
        left, right, out = ((R, I, dw_in), (A, G, dw_out))[which]
        for m in tiles:
            slot = m % 2
            lanes = slice(m * GRAD, (m + 1) * GRAD)
            if slot in staged:
                staged.pop(slot).wait()

            @pl.loop(0, right.shape[2] // TILE)
            def _(t):
                cols = pl.ds(pl.multiple_of(t * TILE, TILE), TILE)
                stage[slot, :, cols] = transposed_times(left[j, :, lanes], right[j, :, cols]).astype(stage.dtype)

            staged[slot] = local(stage.at[slot], out.at[j, lanes], store.at[slot])

    later = range(spread_first, chips)
    turn = TURN
    away = [k for k in turn if k]
    dispatch(0)
    dispatch(away[0])
    dispatch(away[1])
    for j in range(2):
        loads.append(local(w_in.at[j], W1.at[j], load.at[j]))
        loads.append(local(w_out.at[j], W2.at[j], load.at[2 + j]))
    loads.append(local(route, RT, load.at[4]))
    early = spread_first * chunk
    for j in range(2):
        loads.append(local(up_rows.at[j, pl.ds(0, early)], U.at[j, pl.ds(0, early)], load.at[5 + j]))
    for n, k in enumerate(later):
        for j in range(2):
            block = rows_of(k, me)
            loads.append(local(up_rows.at[j, block], U.at[j, block], load.at[7 + 2 * n + j]))
    if turn[0]:
        for k in later:
            spread_out(0, k)
    z_arrived(turn[0])
    spread_out(1, turn[0])
    if not turn[0]:
        for k in later:
            spread_out(0, k)
    z_arrived(turn[1])
    spread_out(1, turn[1])
    dispatch(away[2])
    relay(1, turn[0])
    for copy in loads:
        copy.wait()
    for k in later:
        relay(0, k)
    z_arrived(turn[2])
    spread_out(1, turn[2])
    for n in range(chips):
        k = turn[n]
        all_arrived(1, k)
        if k >= spread_first:
            all_arrived(0, k)
        experts(k, 0)
        collect_one(k, 0)
        if n < 2:
            relay(1, turn[n + 1 + (n > 0)])
        if n == 0:
            z_arrived(turn[3])
            spread_out(1, turn[3])
        else:
            collect_two(turn[n - 1], 0)
        if n > 1:
            collect_three(turn[n - 2], 0)
        experts(k, 1)
        collect_one(k, 1)
        if n == 0:
            relay(1, turn[2])
        else:
            collect_two(turn[n - 1], 1)
        if n > 1:
            collect_three(turn[n - 2], 1)
    weight_grads(0, 0, range(4))
    collect_two(turn[3], 0)
    collect_three(turn[2], 0)
    collect_two(turn[3], 1)
    collect_three(turn[2], 1)
    weight_grads(0, 1, range(4))
    weight_grads(1, 0, range(2))
    collect_three(turn[3], 0)
    weight_grads(1, 0, range(2, 4))
    collect_three(turn[3], 1)
    weight_grads(1, 1, range(4))
    for copy in staged.values():
        copy.wait()
    for copy in dispatched.values():
        copy.wait_send()
    for copy in sent.values():
        copy.wait_send()
    for copy in summed.values():
        copy.wait_send()
    for (a, k, j, c), copy in returns.items():
        copy.wait()


def moe(send_rows, up_rows, route, w_in, w_out, experts_all, number):
    S, low, dma = jax.ShapeDtypeStruct, jnp.bfloat16, pltpu.SemaphoreType.DMA
    owners, _, cap, width = send_rows.shape
    chips = owners // 2
    hidden_units = w_in.shape[2]
    count = owners * cap * 4
    part = 2 * cap

    def vmem(*shape, dtype=low):
        return pltpu.VMEM(shape, dtype)

    return pl.pallas_call(
        functools.partial(moe_kernel, chips, cap, experts_all, SPREAD_FIRST),
        out_shape=(
            S((2, owners, 2, cap, width), low),
            S(w_in.shape, low),
            S(w_out.shape, low),
        ),
        in_specs=[ANY] * 5,
        out_specs=(ANY,) * 3,
        scratch_shapes=[
            vmem(2, count, width),
            vmem(2, count, width),
            vmem(2, count, width),
            vmem(2, count, hidden_units),
            vmem(2, count, hidden_units),
            vmem(2, 2, count, width),
            vmem(2, 2, chips, 2, part, width),
            vmem(2, 2, chips, part, width),
            vmem(*w_in.shape),
            vmem(*w_out.shape),
            vmem(*route.shape),
            vmem(2, GRAD, max(width, hidden_units)),
            dma((7 + 2 * (chips - SPREAD_FIRST),)),
            dma((5,)),
            dma((chips, 2)),
            dma((chips, 2)),
            dma((2, chips, 2, 2)),
            dma((2, chips, 2, 2)),
            dma((2, chips, 2)),
            dma((2, chips, 2)),
            dma((2, 2, chips, 2)),
            dma((2, 2, chips, 2)),
            dma((2, 2, chips)),
            dma((2, 2, chips)),
            dma((2, 2, chips, 2)),
            dma((2, 2, chips, 2)),
            dma((2,)),
        ],
        compiler_params=pltpu.CompilerParams(
            collective_id=number, has_side_effects=True, vmem_limit_bytes=60 * 2**20
        ),
        cost_estimate=pl.CostEstimate(
            flops=12 * 2 * count * width * hidden_units, bytes_accessed=2**25, transcendentals=0
        ),
    )(send_rows, up_rows, route, w_in, w_out)


def front_kernel(
    count, cap, experts_all, spread_here, hidden, qkv_weight, mix, out_grad, router, gain_a, gain_b, ids, length,
    normed_out, heads_out, mix_out, small_out, gains_out, up, projected_out, attended_out, sums_out,
    middle_out, low_out, logits_out, sent_out, hit_out,
    staged, hid, heads_all, small_own, small_all, gains, normed, proj, attended, sums, acc, stat,
    mix_all, up_low, rows, hit, mixed, middle, normed_low, logits, sent_rows, pile,
    h_send, h_recv, q_send, q_recv, f_send, f_recv, n_send, n_recv, u_send, u_recv, m_send, m_recv,
    s_send, s_recv, x_send, x_recv, y_send, y_recv, local,
):
    me, place = lax.axis_index("seq"), lax.axis_index("fsdp")
    one, two, both = me ^ 1, me ^ 2, me ^ 3
    others = (one, two, both)
    chips = count // 2
    chip, core = place // 2, lax.rem(place, 2)
    sibling = place ^ 1
    share = mix.shape[0]
    tokens = hidden.shape[0]
    group = attended.shape[1]
    part, chunk = 2 * cap, 8 * cap
    barrier = pltpu.get_barrier_semaphore()
    for peer in others:
        pl.semaphore_signal(barrier, inc=1, device_id={"seq": peer}, device_id_type=MESH)
    for step in range(1, count):
        pl.semaphore_signal(
            barrier, inc=1, device_id={"fsdp": lax.rem(place + step, count)}, device_id_type=MESH
        )
    pl.semaphore_wait(barrier, 3 + count - 1)

    def keep(source, target, number):
        copy = pltpu.make_async_copy(source, target, local.at[number])
        copy.start()
        return copy

    def far(k):
        return (chip ^ k) * 2 + core

    away, near = {}, {}

    def block(a, owner):
        if a == 0:
            return mix_all.at[me, owner // 2, core]
        if a == 1:
            return small_all.at[pl.ds(pl.multiple_of((me * count + owner) * share, share), share)]
        return heads_all.at[:, owner]

    own_of = (mix, small_own, staged)

    def send_far(a):
        for k in range(1, chips):
            away[a, k] = remote("fsdp", far(k), own_of[a], block(a, place), f_send.at[a, k], f_recv.at[a, k])

    def send_near(a):
        near[a, 0] = remote("fsdp", sibling, own_of[a], block(a, place), n_send.at[a, 0], n_recv.at[a, 0])

    def pass_on(a):
        for k in range(1, chips):
            away[a, k].wait_recv()
            arrived = block(a, far(k))
            near[a, k] = remote("fsdp", sibling, arrived, arrived, n_send.at[a, k], n_recv.at[a, k])

    direct = {}

    def both_ways(name, views, sources, send, receive):
        for side, peer in enumerate((one, two)):
            for order in range(2):
                p = (order + side) % 2
                direct[name, side, p] = remote(
                    "seq", peer, sources[p], views[p](me), send.at[side, p], receive.at[side, p]
                )

    def relay(name, views, send, receive):
        for side, (origin, peer) in enumerate(((one, two), (two, one))):
            direct[name, side, side].wait_recv()
            source = views[side](origin)
            direct[name, 2, side] = remote("seq", peer, source, source, send.at[2, side], receive.at[2, side])

    def arrived(name):
        for side in range(2):
            direct[name, side, 1 - side].wait_recv()
            direct[name, 2, side].wait_recv()

    moved = {}

    def send_rows(k):
        for c in range(2):
            if k == 0 and c == 0:
                continue
            peer = (chip ^ k) * 2 + (core ^ c)
            moved[k, c] = remote(
                "fsdp", peer, rows.at[peer], up.at[:, pl.ds(k * chunk + me * part + core * cap, cap)],
                u_send.at[k, c], u_recv.at[k, c],
            )

    columns = [
        (pl.ds(p * group, group), lambda to, p=p: pl.ds(pl.multiple_of((p * 4 + to) * group, group), group))
        for p in range(3)
    ]
    exchanged = [
        remote(
            "seq", peer, qkv_weight.at[:, view(peer)], staged.at[me, :, into], q_send.at[i, p], q_recv.at[i, p]
        )
        for i, peer in enumerate(others)
        for p, (into, view) in enumerate(columns)
    ]
    half = tokens // 2
    hidden_views = [
        lambda origin, p=p: hid.at[pl.ds(origin * tokens + p * half, half)] for p in range(2)
    ]
    both_ways("hidden", hidden_views, [hidden.at[pl.ds(p * half, half)] for p in range(2)], h_send, h_recv)
    send_far(0)
    own_heads = [
        keep(qkv_weight.at[:, view(me)], staged.at[me, :, into], 14 + p) for p, (into, view) in enumerate(columns)
    ]
    own_hidden = keep(hidden, hid.at[pl.ds(me * tokens, tokens)], 1)
    own_mix = keep(mix, block(0, place), 2)
    own_grad = keep(out_grad, up_low, 13)
    pile[...] = jnp.zeros_like(pile)
    pile[:experts_all, :share] = router[...].astype(jnp.float32)
    for n, gain in enumerate((gain_a, gain_b)):
        pile[experts_all + n : experts_all + n + 1, :share] = gain[...].astype(jnp.float32)
    small_own[...] = jnp.transpose(pile[...])[:share].astype(small_own.dtype)
    send_far(1)
    send_near(1)
    own_small = keep(small_own, block(1, place), 3)
    across = ids[...].astype(jnp.float32)
    chosen = jnp.transpose(jnp.broadcast_to(across, (128, tokens)))[:, :1]
    first = lax.broadcasted_iota(jnp.int32, (tokens, tokens), 0)
    second = lax.broadcasted_iota(jnp.int32, (tokens, tokens), 1)
    ranks = jnp.sum(jnp.where((chosen == across) & (first < second), 1.0, 0.0), axis=0, keepdims=True)
    slot = (across * cap + ranks).astype(jnp.int32)
    hit[...] = jnp.where(lax.broadcasted_iota(jnp.int32, hit.shape, 0) == slot, 1.0, 0.0).astype(hit.dtype)
    own_grad.wait()
    position = me * tokens + lax.broadcasted_iota(jnp.int32, (tokens, 1), 0)
    up_low[...] = jnp.where(position < length[0], up_low[...].astype(jnp.float32), 0.0).astype(up_low.dtype)

    def to_slots(values, target):
        @pl.loop(0, count)
        def _(owner):
            picked = hit[pl.ds(pl.multiple_of(owner * 2 * cap, 2 * cap), 2 * cap), :]
            target[owner] = times(picked, values[...]).astype(target.dtype).reshape(target.shape[1:])

    to_slots(up_low, rows)
    own_rows = keep(rows.at[place], up.at[:, pl.ds(me * part + core * cap, cap)], 4)
    send_rows(0)
    hit_kept = keep(hit, hit_out, 0)
    pass_on(1)
    for copy in own_heads:
        copy.wait()
    for copy in exchanged:
        copy.wait_recv()
    own_block = keep(staged, heads_all.at[:, place], 5)
    send_far(2)
    send_near(2)
    own_small.wait()
    for k in range(chips):
        near[1, k].wait_recv()
    mine = small_all.at[pl.ds(pl.multiple_of(me * count * share, share), count * share)]
    smalls = [remote("seq", peer, mine, mine, q_send.at[3, i], q_recv.at[3, i]) for i, peer in enumerate(others)]

    def up_views(k):
        return [lambda origin, j=j: up.at[j, pl.ds(k * chunk + origin * part, part)] for j in range(2)]

    def up_out(k):
        if k == 0:
            own_rows.wait()
        for c in range(2):
            if (k, c) in moved:
                moved[k, c].wait_recv()
        if k < spread_here:
            views = up_views(k)
            both_ways(("up", k), views, [views[0](me), views[1](me)], s_send.at[k], s_recv.at[k])

    def up_relay(k):
        if k < spread_here:
            relay(("up", k), up_views(k), s_send.at[k], s_recv.at[k])

    up_out(0)
    relay("hidden", hidden_views, h_send, h_recv)
    own_mix.wait()
    for k in range(1, chips):
        away[0, k].wait_recv()
    mix_views = [
        lambda origin, p=p: mix_all.at[origin, pl.ds(p * (chips // 2), chips // 2), core] for p in range(2)
    ]
    both_ways("mix", mix_views, [mix_views[p](me) for p in range(2)], m_send, m_recv)
    for copy in smalls:
        copy.wait_recv()
    small_kept = keep(small_all, small_out, 6)
    own_hidden.wait()
    arrived("hidden")
    turned = jnp.transpose(small_all[...].astype(jnp.float32))
    gains[0:1, :] = turned[experts_all : experts_all + 1]
    gains[1:2, :] = turned[experts_all + 1 : experts_all + 2]
    gains_kept = keep(gains, gains_out, 17)
    gain = gains[0:1, :]

    @pl.loop(0, hid.shape[0] // 128)
    def _(t):
        place_rows = pl.ds(pl.multiple_of(t * 128, 128), 128)
        value = hid[place_rows, :].astype(jnp.float32)
        scale = lax.rsqrt(jnp.mean(value * value, axis=-1, keepdims=True) + EPS)
        normed[place_rows, :] = (value * scale * gain).astype(normed.dtype)

    normed_kept = keep(normed, normed_out, 7)
    pass_on(2)
    for k in range(1, chips):
        send_rows(k)
    up_relay(0)
    relay("mix", mix_views, m_send, m_recv)
    own_block.wait()
    for k in range(chips):
        near[2, k].wait_recv()
    heads_kept = keep(heads_all, heads_out, 8)
    width = hid.shape[1]

    for p in range(3):

        @pl.loop(0, hid.shape[0] // TILE)
        def _(t):
            place_rows = pl.ds(pl.multiple_of(t * TILE, TILE), TILE)
            weights = heads_all[:, :, :, p * group : (p + 1) * group].reshape(width, group)
            proj[place_rows, p * group : (p + 1) * group] = times(normed[place_rows, :], weights).astype(proj.dtype)

    projected_kept = keep(proj, projected_out, 9)
    head_of = lax.broadcasted_iota(jnp.int32, (tokens, group), 1) // HEAD_DIM
    sent = []
    for i in range(4):
        own = slice(i * tokens, (i + 1) * tokens)
        reach = (i + 1) * tokens

        @pl.loop(0, group // HEAD_DIM)
        def _(h):
            query = jnp.where(head_of == h, proj[own, :group] * (HEAD_DIM**-0.5), 0).astype(proj.dtype)
            scores = times_transposed(query, proj[:reach, group : 2 * group])
            column = lax.broadcasted_iota(jnp.int32, scores.shape, 1)
            row = lax.broadcasted_iota(jnp.int32, scores.shape, 0) + i * tokens
            scores = jnp.where((column <= row) & (column < length[0]), scores, MASKED)
            top = jnp.max(scores, axis=1, keepdims=True)
            powers = jnp.exp(scores - top)
            total = jnp.sum(powers, axis=1, keepdims=True)
            probs = (powers * (1.0 / total)).astype(proj.dtype)
            out = times(probs, proj[:reach, 2 * group :])
            acc[...] = jnp.where(head_of == h, out, acc[...])
            lane = lax.broadcasted_iota(jnp.int32, stat.shape, 1)
            stat[...] = jnp.where(lane == h, top + jnp.log(total), stat[...])

        attended[own, :] = acc[...].astype(attended.dtype)
        sums[:, own] = jnp.transpose(stat[...])[:8]
        target = mixed.at[:, pl.ds(pl.multiple_of(me * group, group), group)]

        @pl.when(me != i)
        def _():
            remote("seq", i, attended.at[own], target, x_send.at[i], x_recv.at[me])

        @pl.when(me == i)
        def _():
            pltpu.make_async_copy(attended.at[own], target, local.at[10]).start()

        if i == 1:
            up_relay(1)
        if i == 0:
            up_out(1)
            arrived("mix")
            both_cores = [
                remote(
                    "fsdp", sibling, mix_all.at[s, :, core], mix_all.at[s, :, core], y_send.at[s], y_recv.at[s]
                )
                for s in range(4)
            ]
    up_out(2)
    attended_kept = keep(attended, attended_out, 11)
    sums_kept = keep(sums, sums_out, 12)
    for i in range(4):
        target = mixed.at[:, pl.ds(i * group, group)]

        @pl.when(me != i)
        def _():
            copy = pltpu.make_async_remote_copy(
                attended.at[pl.ds(i * tokens, tokens)], target, x_send.at[i], x_recv.at[i],
                device_id={"seq": i}, device_id_type=MESH,
            )
            copy.wait()

        @pl.when(me == i)
        def _():
            pltpu.make_async_copy(attended.at[pl.ds(i * tokens, tokens)], target, local.at[10]).wait()

    up_relay(2)
    for copy in both_cores:
        copy.wait()
    mix_kept = keep(mix_all.at[me], mix_out, 18)
    for n in range(width // TILE):
        lanes = slice(n * TILE, (n + 1) * TILE)
        total = hid[pl.ds(pl.multiple_of(me * tokens, tokens), tokens), lanes].astype(jnp.float32)
        for s in range(4):
            weights = mix_all[s, :, :, :, lanes].reshape(group, TILE)
            total = total + times(mixed[:, s * group : (s + 1) * group], weights)
        middle[:, lanes] = total
    middle_kept = keep(middle, middle_out, 19)
    for t in range(tokens // 128):
        span = slice(t * 128, (t + 1) * 128)
        value = middle[span, :]
        scale = lax.rsqrt(jnp.mean(value * value, axis=-1, keepdims=True) + EPS)
        normed_low[span, :] = (value * scale * gains[1:2, :]).astype(normed_low.dtype)
    logits[...] = times(normed_low[...], small_all[...])
    to_slots(normed_low, sent_rows)
    last = [
        keep(normed_low, low_out, 20),
        keep(logits, logits_out, 21),
        keep(sent_rows, sent_out, 22),
    ]
    for k in range(3, chips):
        up_out(k)
        up_relay(k)
    for k in range(spread_here):
        arrived(("up", k))
    for copy in (*direct.values(), *exchanged, *smalls, *away.values(), *near.values(), *moved.values()):
        copy.wait_send()
    for copy in (
        small_kept, normed_kept, heads_kept, projected_kept, attended_kept, sums_kept,
        hit_kept, gains_kept, mix_kept, middle_kept, *last,
    ):
        copy.wait()


def front(hidden, qkv_weight, mix, out_grad, router, gain_a, gain_b, ids, lengths, count, cap, spread_here, number):
    S, dma, low, f32 = jax.ShapeDtypeStruct, pltpu.SemaphoreType.DMA, jnp.bfloat16, jnp.float32
    chips = count // 2
    tokens, width = hidden.shape
    experts_all = router.shape[0]
    group = qkv_weight.shape[1] // 12
    share = qkv_weight.shape[0]
    full = 4 * tokens
    lanes = -(-(experts_all + 2) // 128) * 128
    all_heads = (4, count, share, 3 * group)
    slots = experts_all * cap

    def vmem(*shape, dtype=low):
        return pltpu.VMEM(shape, dtype)

    near = pl.BlockSpec(memory_space=pltpu.VMEM)
    return pl.pallas_call(
        functools.partial(front_kernel, count, cap, experts_all, spread_here),
        out_shape=(
            S((full, width), low),
            S(all_heads, low),
            S((chips, 2, share, width), low),
            S((width, lanes), low),
            S((8, width), f32),
            S((2, 4 * count * cap, width), low),
            S((full, 3 * group), low),
            S((full, group), low),
            S((8, full), f32),
            S((tokens, width), f32),
            S((tokens, width), low),
            S((tokens, lanes), f32),
            S((count, 2, cap, width), low),
            S((slots, tokens), low),
        ),
        in_specs=[ANY] * 4 + [near] * 4 + [pl.BlockSpec(memory_space=pltpu.SMEM)],
        out_specs=(ANY,) * 14,
        scratch_shapes=[
            vmem(4, share, 3 * group),
            vmem(full, width),
            vmem(*all_heads),
            vmem(share, lanes),
            vmem(width, lanes),
            vmem(8, width, dtype=f32),
            vmem(full, width),
            vmem(full, 3 * group),
            vmem(full, group),
            vmem(8, full, dtype=f32),
            vmem(tokens, group, dtype=f32),
            vmem(tokens, 128, dtype=f32),
            vmem(4, chips, 2, share, width),
            vmem(tokens, width),
            vmem(count, 2, cap, width),
            vmem(slots, tokens),
            vmem(tokens, width),
            vmem(tokens, width, dtype=f32),
            vmem(tokens, width),
            vmem(tokens, lanes, dtype=f32),
            vmem(count, 2, cap, width),
            vmem(lanes, 128, dtype=f32),
            dma((3, 2)), dma((3, 2)), dma((4, 3)), dma((4, 3)),
            dma((3, chips)), dma((3, chips)), dma((3, chips)), dma((3, chips)),
            dma((chips, 2)), dma((chips, 2)), dma((3, 2)), dma((3, 2)),
            dma((chips, 3, 2)), dma((chips, 3, 2)), dma((4,)), dma((4,)), dma((4,)), dma((4,)), dma((23,)),
        ],
        compiler_params=pltpu.CompilerParams(
            collective_id=number, has_side_effects=True, vmem_limit_bytes=60 * 2**20
        ),
    )(hidden, qkv_weight, mix, out_grad, router, gain_a, gain_b, ids, lengths)


def widen_kernel(one, two, one_out, two_out):
    one_out[...] = one[...].astype(one_out.dtype)
    two_out[...] = two[...].astype(two_out.dtype)


def widen(one, two):
    steps = one.shape[1] // WIDEN
    blocks = [pl.BlockSpec((1, WIDEN, x.shape[2]), lambda a, b: (a, b, 0)) for x in (one, two)]
    return pl.pallas_call(
        widen_kernel,
        out_shape=tuple(jax.ShapeDtypeStruct(x.shape, jnp.float32) for x in (one, two)),
        grid=(one.shape[0], steps),
        in_specs=blocks,
        out_specs=blocks,
        compiler_params=pltpu.CompilerParams(vmem_limit_bytes=48 * 2**20),
    )(one, two)


def back_kernel(
    count, experts_all, ret_in, hit_in, middle_in, logits_in, low_in, out_grad, small_all, gains_in, hidden_in,
    proj_in, attended_in, sums_in, normed_in, heads_in, mix_in, ids, length,
    output_out, input_out, heads_out, mix_out, small_out,
    ret, hit, middle, logits, normed_two, up_low, route, gains, hid, output, grad_middle, grad_in, grad_logits, grad_two,
    grads, proj, attended, sums, normed, heads, mix, small, grad_heads, delta, masked_grad, masked_query,
    masked_key, masked_value, probs, slopes, grad_query, grad_key, grad_value, grad_proj, part, weights, weights_mix, gain_sum,
    sib_a, sib_b, sib_c, own_a, own_b, own_c, got_a, got_b, got_c, total_a, total_b, total_c, first, second,
    g_send, g_recv, b_send, b_recv, bb_send, bb_recv, z_send, z_recv, x_send, x_recv, c_send, c_recv, load, keep,
):
    me, place = lax.axis_index("seq"), lax.axis_index("fsdp")
    one, two, both = me ^ 1, me ^ 2, me ^ 3
    others = (one, two, both)
    chips = count // 2
    chip, core = place // 2, lax.rem(place, 2)
    sibling = place ^ 1
    tokens, width = grad_in.shape
    gain_row = experts_all
    group = attended.shape[1]
    share = weights.shape[0] // (4 * count)
    heads_local = group // HEAD_DIM
    low = grads.dtype
    barrier = pltpu.get_barrier_semaphore()
    for peer in others:
        pl.semaphore_signal(barrier, inc=1, device_id={"seq": peer}, device_id_type=MESH)
    for k in range(1, chips):
        pl.semaphore_signal(
            barrier, inc=1, device_id={"fsdp": (chip ^ k) * 2 + core}, device_id_type=MESH
        )
    pl.semaphore_signal(barrier, inc=1, device_id={"fsdp": sibling}, device_id_type=MESH)
    pl.semaphore_wait(barrier, 3 + chips)

    def local(source, to, sem):
        copy = pltpu.make_async_copy(source, to, sem)
        copy.start()
        return copy

    heads_of = [
        local(source, to, load.at[9 + i])
        for i, (source, to) in enumerate(
            (
                (hit_in, hit),
                (ret_in, ret),
                (middle_in, middle),
                (logits_in, logits),
                (low_in, normed_two),
                (out_grad, up_low),
                (small_all, route),
                (gains_in, gains),
                (hidden_in, hid),
            )
        )
    ]
    loads = [
        local(source, to, load.at[1 + i])
        for i, (source, to) in enumerate(
            (
                (proj_in, proj),
                (attended_in, attended),
                (sums_in, sums),
                (mix_in, mix),
                (heads_in, heads),
                (normed_in, normed),
            )
        )
    ]
    for copy in heads_of:
        copy.wait()
    small[...] = jnp.zeros_like(small)
    grad_two[...] = jnp.zeros_like(grad_two)
    lane = lax.broadcasted_iota(jnp.int32, (STEP, route.shape[1]), 1)
    chosen = jnp.transpose(jnp.broadcast_to(ids[...].astype(jnp.float32), (128, tokens)))[:, :1].astype(jnp.int32)
    for t in range(tokens // STEP):
        span = slice(t * STEP, (t + 1) * STEP)
        position = me * tokens + t * STEP + lax.broadcasted_iota(jnp.int32, (STEP, 1), 0)
        valid = jnp.where(position < length[0], 1.0, 0.0)
        scores = jnp.where(lane < experts_all, logits[span, :], MASKED)
        powers = jnp.exp(scores - jnp.max(scores, axis=1, keepdims=True))
        share_of = powers / jnp.sum(powers, axis=1, keepdims=True)
        choose = lane == chosen[span]
        gate = jnp.sum(jnp.where(choose, share_of, 0.0), axis=1, keepdims=True)
        back_rows = transposed_times(hit[:, span], ret[0])
        value = middle[span, :]
        output[span, :] = (valid * (value + gate * back_rows)).astype(low)
        upstream = valid * up_low[span, :].astype(jnp.float32)
        grad_gate = jnp.sum(upstream * back_rows, axis=1, keepdims=True)
        slope = grad_gate * gate * (jnp.where(choose, 1.0, 0.0) - share_of)
        grad_logits[span, :] = slope.astype(low)
        incoming = times_transposed(grad_logits[span, :], route[...]) + transposed_times(hit[:, span], ret[1])
        scale = lax.rsqrt(jnp.mean(value * value, axis=-1, keepdims=True) + EPS)
        shrunk = value * scale
        grad_two[...] += jnp.sum(incoming * shrunk, axis=0, keepdims=True)
        scaled = incoming * gains[1:2, :]
        total = upstream + scale * (scaled - shrunk * jnp.mean(scaled * shrunk, axis=-1, keepdims=True))
        grad_middle[span, :] = total
        grad_in[span, :] = total.astype(low)
    output_kept = local(output, output_out, load.at[8])
    own_grad = local(grad_in, grads.at[pl.ds(me * tokens, tokens)], load.at[0])
    half = tokens // 2
    direct = {}
    for side, peer in enumerate((one, two)):
        for order in range(2):
            p = (order + side) % 2
            direct[side, p] = remote(
                "seq", peer, grad_in.at[pl.ds(p * half, half)], grads.at[pl.ds(me * tokens + p * half, half)],
                g_send.at[side, p], g_recv.at[side, p],
            )
    for n in range(width // 128):
        lanes = slice(n * 128, (n + 1) * 128)
        kinds = transposed_times(grad_logits[...], normed_two[:, lanes])
        small[n // 2, n % 2, :experts_all, :] = kinds[:experts_all]
        small[n // 2, n % 2, gain_row + 1 : gain_row + 2, :] = grad_two[:, lanes]
    for copy in loads:
        copy.wait()
    head_of = lax.broadcasted_iota(jnp.int32, (tokens, group), 1) // HEAD_DIM
    key_at = lax.broadcasted_iota(jnp.int32, (tokens, tokens), 0)
    for j in range(4):
        rows = slice(j * tokens, (j + 1) * tokens)
        for h in range(heads_local):
            key = proj[rows, group : 2 * group] * (HEAD_DIM**-0.5)
            masked_key[j * heads_local + h] = jnp.where(head_of == h, key, 0).astype(low)
            masked_value[j * heads_local + h] = jnp.where(head_of == h, proj[rows, 2 * group :], 0).astype(low)
    grad_key[...] = jnp.zeros_like(grad_key)
    grad_value[...] = jnp.zeros_like(grad_value)
    gain_sum[...] = jnp.zeros_like(gain_sum)

    def block(i, j, masked):
        rows = pl.ds(pl.multiple_of(i * tokens, tokens), tokens)
        keys = pl.ds(pl.multiple_of(j * tokens, tokens), tokens)
        hidden = j * tokens + key_at >= length[0]
        if masked:
            hidden = hidden | (key_at > lax.broadcasted_iota(jnp.int32, (tokens, tokens), 1))
        total = None
        for h in range(heads_local):
            lanes = slice(h * tokens, (h + 1) * tokens)
            key = masked_key[j * heads_local + h]
            scores = times_transposed(key, proj[rows, :group])
            scores = jnp.where(hidden, MASKED, scores)
            p = jnp.exp(scores - sums[h : h + 1, rows])
            probs[:, lanes] = p.astype(low)
            grad = times_transposed(masked_value[j * heads_local + h], grad_heads[...])
            slopes[:, lanes] = (p * (grad - delta[h : h + 1, :])).astype(low)
            term = transposed_times(slopes[:, lanes], key)
            total = term if total is None else total + term
        grad_query[...] += total
        grad_value[keys, :] += times(probs[...], masked_grad[...])
        grad_key[keys, :] += times(slopes[...], masked_query[...])

    def queries(i):
        rows = pl.ds(pl.multiple_of(i * tokens, tokens), tokens)
        grad_heads[...] = times_transposed(grads[rows, :], mix[...]).astype(low)
        out = grad_heads[...].astype(jnp.float32)
        turned = jnp.transpose(out * attended[rows, :].astype(jnp.float32))
        query = proj[rows, :group]
        for h in range(heads_local):
            delta[h : h + 1, :] = jnp.sum(turned[h * HEAD_DIM : (h + 1) * HEAD_DIM], axis=0, keepdims=True)
            masked_grad[h * tokens : (h + 1) * tokens, :] = jnp.where(head_of == h, out, 0).astype(low)
            masked_query[h * tokens : (h + 1) * tokens, :] = jnp.where(head_of == h, query, 0).astype(low)
        grad_query[...] = jnp.zeros_like(grad_query)

        @pl.loop(0, i)
        def _(j):
            block(i, j, False)

        block(i, i, True)
        grad_proj[rows, :group] = grad_query[...].astype(low)

    own_grad.wait()
    queries(me)
    for side, (origin, peer) in enumerate(((one, two), (two, one))):
        direct[side, side].wait_recv()
        source = grads.at[pl.ds(origin * tokens + side * half, half)]
        direct[2, side] = remote("seq", peer, source, source, g_send.at[2, side], g_recv.at[2, side])
    for side, origin in enumerate((one, two)):
        direct[side, 1 - side].wait_recv()
        queries(origin)
    for side in range(2):
        direct[2, side].wait_recv()
    for n in range(width // TILE):
        lanes = slice(n * TILE, (n + 1) * TILE)
        weights_mix[:, lanes] = transposed_times(attended[...], grads[:, lanes]).astype(low)
    order_of = [*range(1, chips), 0]
    to_sibling, away = {}, {}

    def rows_at(s, owner):
        return pl.ds(pl.multiple_of((s * count + owner) * share, share), share)

    def start_sibling(a, k, core_of):
        owner = (chip ^ k) * 2 + core_of
        if a == 1:
            return [
                remote(
                    "fsdp", sibling, weights_mix.at[pl.ds(pl.multiple_of(owner * share, share), share)], sib_b.at[k],
                    b_send.at[0, k], b_recv.at[0, k],
                )
            ]
        if a == 2:
            return [
                remote(
                    "fsdp", sibling, small.at[:, owner * share // 128], sib_c.at[k], b_send.at[1, k], b_recv.at[1, k]
                )
            ]
        raise ValueError(a)

    sib, own, got = (sib_a, sib_b, sib_c), (own_a, own_b, own_c), (got_a, got_b, got_c)
    totals = (total_a, total_b, total_c)

    def pair_sum(a, k):
        owner = (chip ^ k) * 2 + core
        for copy in to_sibling[a, k]:
            copy.wait_recv()
        if a == 1:
            mine = weights_mix[pl.ds(pl.multiple_of(owner * share, share), share), :]
            own_b[k] = (mine.astype(jnp.float32) + sib_b[k].astype(jnp.float32)).astype(low)
        else:
            for s in range(4):
                own_c[k, s] = small[s, owner * share // 128] + sib_c[k, s]
        if k:
            away[a, k] = remote(
                "fsdp", (chip ^ k) * 2 + core, own[a].at[k], got[a].at[k], z_send.at[a, k], z_recv.at[a, k]
            )

    for k in order_of:
        to_sibling[1, k] = start_sibling(1, k, core ^ 1)
    queries(both)
    for k in order_of:
        pair_sum(1, k)
    grad_proj[:, group : 2 * group] = (grad_key[...] * (HEAD_DIM**-0.5)).astype(low)
    grad_proj[:, 2 * group :] = grad_value[...].astype(low)
    for s in range(4):
        lanes = slice(s * group, (s + 1) * group)
        weights[lanes, :] = transposed_times(normed[:, lanes], grad_proj[...]).astype(low)
        for k in order_of:
            owner = (chip ^ k) * 2
            to_sibling[s + 3, k] = [
                remote(
                    "fsdp", sibling, weights.at[rows_at(s, owner + (core ^ 1))], sib_a.at[k, pl.ds(s * share, share)],
                    bb_send.at[s, k], bb_recv.at[s, k],
                )
            ]
    for s in range(4):
        rows = slice(s * share, (s + 1) * share)
        for k in order_of:
            owner = (chip ^ k) * 2 + core
            to_sibling[s + 3, k][0].wait_recv()
            own_a[k, rows, :] = (
                weights[rows_at(s, owner), :].astype(jnp.float32) + sib_a[k, rows, :].astype(jnp.float32)
            ).astype(low)
            if k:
                away[s + 3, k] = remote(
                    "fsdp", owner, own_a.at[k, pl.ds(s * share, share)], got_a.at[k, pl.ds(s * share, share)],
                    z_send.at[s + 3, k], z_recv.at[s + 3, k],
                )
    for j in range(4):
        own_rows = slice(j * tokens, (j + 1) * tokens)
        for n in range(width // TILE):
            lanes = slice(n * TILE, (n + 1) * TILE)
            back = times_transposed(grad_proj[own_rows, :], heads[lanes, :])
            gain_sum[:, lanes] += jnp.sum(back * normed[own_rows, lanes].astype(jnp.float32), axis=0, keepdims=True)
            part[j, :, lanes] = back.astype(low)
    summed = {}
    for side, (near, rest) in enumerate(((one, two), (two, one))):
        rows = pl.ds(side * half, half)
        for order, to in enumerate((both, near)):
            summed[side, order] = remote(
                "seq", near, part.at[to, rows], first.at[side, order], c_send.at[side, order], c_recv.at[side, order]
            )
    for b in range(width // 128):
        small[b // 2, b % 2, gain_row : gain_row + 1, :] = gain_sum[:, b * 128 : (b + 1) * 128]
    for k in order_of:
        to_sibling[2, k] = start_sibling(2, k, core ^ 1)
    for k in order_of:
        pair_sum(2, k)
    for side, rest in enumerate((two, one)):
        rows = slice(side * half, (side + 1) * half)
        summed[side, 0].wait_recv()
        first[side, 0] = (first[side, 0].astype(jnp.float32) + part[rest, rows, :].astype(jnp.float32)).astype(low)
        summed[side, 2] = remote("seq", rest, first.at[side, 0], second.at[side], c_send.at[2, side], c_recv.at[2, side])
    stored = []
    for side in range(2):
        rows = slice(side * half, (side + 1) * half)
        summed[side, 1].wait_recv()
        summed[side, 2].wait_recv()
        incoming = (
            part[me, rows, :].astype(jnp.float32)
            + first[side, 1].astype(jnp.float32)
            + second[side].astype(jnp.float32)
        )
        value = hid[rows, :].astype(jnp.float32)
        scale = lax.rsqrt(jnp.mean(value * value, axis=-1, keepdims=True) + EPS)
        shrunk = value * scale
        scaled = incoming * gains[0:1, :]
        grad_middle[rows, :] += scale * (scaled - shrunk * jnp.mean(scaled * shrunk, axis=-1, keepdims=True))
        stored.append(
            local(grad_middle.at[pl.ds(side * half, half)], input_out.at[pl.ds(side * half, half)], keep.at[side])
        )
    for a in (1, 0, 2):
        if a == 0:
            for s in range(4):
                rows = slice(s * share, (s + 1) * share)
                total = own_a[0, rows, :].astype(jnp.float32)
                for k in range(1, chips):
                    away[s + 3, k].wait_recv()
                    total = total + got_a[k, rows, :].astype(jnp.float32)
                total_a[s] = total.astype(low)
        else:
            total = own[a][0].astype(jnp.float32)
            for k in range(1, chips):
                away[a, k].wait_recv()
                total = total + got[a][k].astype(jnp.float32)
            totals[a][...] = total
    crossed = []
    for a, out in ((0, heads_out), (2, small_out)):
        for i, peer in enumerate(others):
            crossed.append(remote("seq", peer, totals[a].at[peer], out.at[me], x_send.at[a, i], x_recv.at[a, i]))
        stored.append(local(totals[a].at[me], out.at[me], keep.at[3 + a // 2]))
    stored.append(local(total_b, mix_out, keep.at[2]))
    for copy in (*stored, *crossed, output_kept):
        copy.wait()
    for copy in (*summed.values(), *away.values(), *direct.values()):
        copy.wait_send()
    for copies in to_sibling.values():
        for copy in copies:
            copy.wait_send()


def back(
    ret, hit, middle, logits, normed_two, out_grad, route, gains, hidden,
    proj, attended, sums, normed, heads, mix, ids, lengths, count, experts_all, number,
):
    S, dma, f32, low = jax.ShapeDtypeStruct, pltpu.SemaphoreType.DMA, jnp.float32, jnp.bfloat16
    tokens, width = out_grad.shape
    group = attended.shape[1]
    chips = count // 2
    full = 4 * tokens
    share = width // (4 * count)
    local_heads = group // HEAD_DIM
    kinds = -(-(experts_all + 2) // 8) * 8

    def vmem(*shape, dtype=low):
        return pltpu.VMEM(shape, dtype)

    sets = [
        vmem(chips, 4 * share, 3 * group),
        vmem(chips, share, width),
        vmem(chips, 4, kinds, 128, dtype=f32),
    ]
    return pl.pallas_call(
        functools.partial(back_kernel, count, experts_all),
        out_shape=(
            S((tokens, width), low),
            S((tokens, width), f32),
            S((4, share, 3 * group), low),
            S((share, width), f32),
            S((4, kinds, 128), f32),
        ),
        in_specs=[ANY] * 15 + [pl.BlockSpec(memory_space=pltpu.VMEM), pl.BlockSpec(memory_space=pltpu.SMEM)],
        out_specs=(ANY,) * 5,
        scratch_shapes=[
            vmem(*ret.shape),
            vmem(*hit.shape),
            vmem(tokens, width, dtype=f32),
            vmem(*logits.shape, dtype=f32),
            vmem(tokens, width),
            vmem(tokens, width),
            vmem(*route.shape),
            vmem(*gains.shape, dtype=f32),
            vmem(tokens, width),
            vmem(tokens, width),
            vmem(tokens, width, dtype=f32),
            vmem(tokens, width),
            vmem(*logits.shape),
            vmem(1, width, dtype=f32),
            vmem(full, width),
            vmem(*proj.shape),
            vmem(*attended.shape),
            vmem(*sums.shape, dtype=f32),
            vmem(*normed.shape),
            vmem(*heads.shape),
            vmem(group, width),
            vmem(4, group // 128, kinds, 128, dtype=f32),
            vmem(tokens, group),
            vmem(8, tokens, dtype=f32),
            vmem(local_heads * tokens, group),
            vmem(local_heads * tokens, group),
            vmem(4 * local_heads, tokens, group),
            vmem(4 * local_heads, tokens, group),
            vmem(tokens, local_heads * tokens),
            vmem(tokens, local_heads * tokens),
            vmem(tokens, group, dtype=f32),
            vmem(full, group, dtype=f32),
            vmem(full, group, dtype=f32),
            vmem(full, 3 * group),
            vmem(4, tokens, width),
            vmem(width, 3 * group),
            vmem(group, width),
            vmem(1, width, dtype=f32),
            *sets,
            *sets,
            *sets,
            vmem(4, share, 3 * group),
            vmem(share, width, dtype=f32),
            vmem(4, kinds, 128, dtype=f32),
            vmem(2, 2, tokens // 2, width),
            vmem(2, tokens // 2, width),
            dma((3, 2)), dma((3, 2)),
            dma((2, chips)), dma((2, chips)), dma((4, chips)), dma((4, chips)),
            dma((7, chips)), dma((7, chips)),
            dma((3, 3)), dma((3, 3)), dma((3, 2)), dma((3, 2)), dma((18,)), dma((5,)),
        ],
        compiler_params=pltpu.CompilerParams(
            collective_id=number, has_side_effects=True, vmem_limit_bytes=60 * 2**20
        ),
    )(
        ret, hit, middle, logits, normed_two, out_grad, route, gains, hidden,
        proj, attended, sums, normed, heads, mix, ids, lengths,
    )


def shards(
    hidden,
    lengths,
    expert_ids,
    attn_gain,
    qkv_weight,
    out_weight,
    moe_gain,
    router_weight,
    expert_in,
    expert_out,
    out_grad,
):
    S = jax.ShapeDtypeStruct
    low = jnp.bfloat16
    owners = lax.axis_size("fsdp")
    seq_count = lax.axis_size("seq")
    tokens, width = hidden.shape[1], hidden.shape[2]
    full_len = tokens * seq_count
    group_width = width // seq_count
    rows_own = qkv_weight.shape[0]
    experts_all = router_weight.shape[1]
    expert_local = expert_in.shape[0]
    capacity = -(-max(2, 2 * tokens // experts_all) // 16) * 16
    slots = experts_all * capacity

    chosen = expert_ids[0, :, 0]

    def to_owners(rows, number):
        return exchange(
            "fsdp",
            owners,
            (rows.reshape(owners, expert_local, capacity, width),),
            (S((expert_local, owners, capacity, width), low),),
            ((lead, second),),
            number,
        )[0].reshape(expert_local, owners * capacity, width)

    def to_sources(rows, number):
        return exchange(
            "fsdp",
            owners,
            (rows.reshape(expert_local, owners, capacity, width),),
            (S((owners, expert_local, capacity, width), low),),
            ((second, lead),),
            number,
        )[0].reshape(slots, width)

    chips = owners // 2
    fused = 4 * owners * capacity <= 1024
    (
        normed,
        weight_qkv,
        mix_rows,
        small,
        gains,
        up_all,
        projected,
        attended,
        totals,
        middle,
        normed_two,
        logits,
        sent,
        dispatch,
    ) = front(
        hidden[0],
        qkv_weight,
        out_weight,
        out_grad[0],
        router_weight.T,
        attn_gain[None],
        moe_gain[None],
        expert_ids[0].T,
        lengths,
        owners,
        capacity,
        SPREAD_FIRST if fused else chips,
        0,
    )
    weight_qkv = weight_qkv.reshape(width, 3 * group_width)
    mix_rows = mix_rows.reshape(group_width, width)
    if not fused:
        up_all = up_all.reshape(expert_local, chips, seq_count, 2 * capacity, width)
        chip, bit = lax.axis_index("fsdp") // 2, 1
        while bit < chips:
            pairs = up_all.reshape(expert_local, chips // (2 * bit), 2, bit, seq_count, 2 * capacity, width)
            up_all = jnp.where((chip // bit) % 2 == 1, pairs[:, :, ::-1], pairs)
            bit *= 2
        up_all = up_all.reshape(expert_local, chips, seq_count, 2 * capacity, width)
        up_all = up_all.transpose(0, 2, 1, 3, 4)
    if fused:
        returned, *expert_grads = moe(
            sent,
            up_all,
            small,
            expert_in,
            expert_out,
            experts_all,
            5,
        )
        expert_in_grad, expert_out_grad = widen(*expert_grads)
        returned = returned.reshape(2, slots, width)
    else:
        choose = chosen[:, None] == jnp.arange(experts_all, dtype=jnp.int32)[None, :]
        weights = jax.nn.softmax(logits[:, :experts_all], axis=-1)
        gate = jnp.sum(jnp.where(choose, weights, 0.0), axis=-1)
        gate_rows = jnp.sum(jnp.where(dispatch > 0, gate[None, :], 0.0), axis=1)
        gates = lax.all_to_all(
            gate_rows.reshape(owners, expert_local, capacity), "fsdp", split_axis=0, concat_axis=0, tiled=True
        )
        gates = lax.all_gather(gates, "seq", axis=0)
        gates = gates.transpose(2, 0, 1, 3).reshape(expert_local, seq_count * owners * capacity, 1)

        rows_all = spread(to_owners(sent, 5), 6)
        count = seq_count * owners * capacity
        rows_all = rows_all.reshape(expert_local, count, width)
        up_all = up_all.reshape(expert_local, count, width)
        grad_rows = (up_all.astype(jnp.float32) * gates).astype(low)

        def per_expert(form, left, right):
            return jnp.einsum(form, left, right, preferred_element_type=jnp.float32)

        inner = per_expert("jrd,jdf->jrf", rows_all, expert_in)
        active, active_back = jax.vjp(gelu_tanh, inner)
        active = active.astype(low)
        partial_out = per_expert("jrf,jfd->jrd", active, expert_out).astype(low)
        grad_active = per_expert("jrd,jfd->jrf", grad_rows, expert_out)
        grad_inner = active_back(grad_active)[0].astype(low)
        partial_back = per_expert("jrf,jdf->jrd", grad_inner, expert_in).astype(low)
        expert_out_grad = per_expert("jrf,jrd->jfd", active, grad_rows)
        expert_in_grad = per_expert("jrd,jrf->jdf", rows_all, grad_inner)

        shape = (expert_local, seq_count, owners * capacity, width)
        returned = to_sources(collect(partial_out.reshape(shape), 7), 8)
        grad_back = to_sources(collect(partial_back.reshape(shape), 9), 10)
        returned = jnp.stack([returned, grad_back])
    output, grad_inputs, qkv_sum, mix_grad, small_sum = back(
        returned,
        dispatch,
        middle,
        logits,
        normed_two,
        out_grad[0],
        small,
        gains,
        hidden[0],
        projected,
        attended,
        totals,
        normed,
        weight_qkv,
        mix_rows,
        expert_ids[0].T,
        lengths,
        owners,
        experts_all,
        12,
    )
    qkv_weight_grad = (
        qkv_sum.astype(jnp.float32)
        .reshape(seq_count, rows_own, 3, group_width)
        .transpose(1, 2, 0, 3)
        .reshape(rows_own, 3 * width)
    )
    start = lax.axis_index("fsdp") * rows_own % 128
    small_sum = lax.dynamic_slice_in_dim(jnp.sum(small_sum, axis=0), start, rows_own, 1)
    return (
        output[None],
        grad_inputs[None],
        small_sum[experts_all] / attn_gain.astype(jnp.float32),
        qkv_weight_grad,
        mix_grad,
        small_sum[experts_all + 1],
        small_sum[:experts_all].T,
        expert_in_grad,
        expert_out_grad,
    )


def solution(mesh):
    placed = (
        P("fsdp", "seq", None),
        P("fsdp"),
        P("fsdp", "seq", None),
        P(("seq", "fsdp")),
        P(("seq", "fsdp"), None),
        P(("seq", "fsdp"), None),
        P(("seq", "fsdp")),
        P(("seq", "fsdp"), None),
        P("fsdp", None, "seq"),
        P("fsdp", "seq", None),
        P("fsdp", "seq", None),
    )
    return jax.shard_map(
        shards,
        mesh=mesh,
        in_specs=placed,
        out_specs=(
            P("fsdp", "seq", None),
            P("fsdp", "seq", None),
            P(("seq", "fsdp")),
            P(("seq", "fsdp"), None),
            P(("seq", "fsdp"), None),
            P(("seq", "fsdp")),
            P(("seq", "fsdp"), None),
            P("fsdp", None, "seq"),
            P("fsdp", "seq", None),
        ),
        check_vma=False,
    )
```

```python
import functools

import jax
import jax.numpy as jnp
from jax import lax
from jax.experimental import pallas as pl
from jax.experimental.pallas import tpu as pltpu
from jax.sharding import PartitionSpec as P

HEAD_DIM = 64
EPS = 1e-05
MASKED = -1e30
ROOT = 0.7978845608028654
TILE = 256
STEP = 128
SPREAD_FIRST = 3
TURN = (1, 3, 2, 0)
GRAD = 256
MESH = pl.DeviceIdType.MESH
ANY = pl.BlockSpec(memory_space=pl.ANY)


def scaled_norm(value, gain):
    return value * lax.rsqrt(jnp.mean(value * value, axis=-1, keepdims=True) + EPS) * gain


def gelu_tanh(value):
    return jax.nn.gelu(value, approximate=True)


def times(left, right):
    return jnp.dot(left, right, preferred_element_type=jnp.float32)


def times_transposed(left, right):
    return lax.dot_general(
        left, right, (((1,), (1,)), ((), ())), preferred_element_type=jnp.float32
    )


def transposed_times(left, right):
    return lax.dot_general(
        left, right, (((0,), (0,)), ((), ())), preferred_element_type=jnp.float32
    )


def greet(axis, peers):
    barrier = pltpu.get_barrier_semaphore()
    for peer in peers:
        pl.semaphore_signal(barrier, inc=1, device_id={axis: peer}, device_id_type=MESH)
    pl.semaphore_wait(barrier, len(peers))


def remote(axis, peer, source, target, send, receive):
    copy = pltpu.make_async_remote_copy(
        source, target, send, receive, device_id={axis: peer}, device_id_type=MESH
    )
    copy.start()
    return copy


def call(kernel, inputs, outputs, scratch, number):
    return pl.pallas_call(
        kernel,
        out_shape=outputs,
        in_specs=[ANY] * len(inputs),
        out_specs=jax.tree.map(lambda _: ANY, outputs),
        scratch_shapes=scratch,
        compiler_params=pltpu.CompilerParams(
            collective_id=number, has_side_effects=True, vmem_limit_bytes=60 * 2**20
        ),
    )(*inputs)


def exchange_kernel(axis, count, views, *refs):
    arrays = len(views)
    sources, targets = refs[:arrays], refs[arrays : 2 * arrays]
    send, receive, local = refs[2 * arrays :]
    me = lax.axis_index(axis)
    peers = [lax.rem(me + step, count) for step in range(1, count)]
    greet(axis, peers)
    copies = []
    for step, peer in enumerate(peers):
        for a, (out_of, into) in enumerate(views):
            copies.append(
                remote(
                    axis,
                    peer,
                    out_of(sources[a], peer),
                    into(targets[a], me),
                    send.at[a, step],
                    receive.at[a, step],
                )
            )
    for a, (out_of, into) in enumerate(views):
        copy = pltpu.make_async_copy(out_of(sources[a], me), into(targets[a], me), local.at[a])
        copy.start()
        copies.append(copy)
    for copy in copies:
        copy.wait()


def exchange(axis, count, inputs, outputs, views, number):
    arrays = len(views)
    return call(
        functools.partial(exchange_kernel, axis, count, views),
        inputs,
        outputs,
        [
            pltpu.SemaphoreType.DMA((arrays, count - 1)),
            pltpu.SemaphoreType.DMA((arrays, count - 1)),
            pltpu.SemaphoreType.DMA((arrays,)),
        ],
        number,
    )


def lead(ref, place):
    return ref.at[place]


def second(ref, place):
    return ref.at[:, place]


def whole(ref, place):
    return ref


def spread_kernel(source, target, send, receive, local):
    me = lax.axis_index("seq")
    one, two, both = me ^ 1, me ^ 2, me ^ 3
    half = source.shape[1] // 2
    greet("seq", [one, two])
    parts = (pl.ds(0, half), pl.ds(half, half))
    own = pltpu.make_async_copy(source, target.at[:, me], local)
    own.start()
    copies = {}
    for side, peer in enumerate((one, two)):
        for order in range(2):
            part = (order + side) % 2
            copies[side, part] = remote(
                "seq",
                peer,
                source.at[:, parts[part]],
                target.at[:, me, parts[part]],
                send.at[side, part],
                receive.at[side, part],
            )
    relayed = []
    for side, (origin, peer) in enumerate(((one, two), (two, one))):
        copies[side, side].wait_recv()
        block = target.at[:, origin, parts[side]]
        relayed.append(remote("seq", peer, block, block, send.at[2, side], receive.at[2, side]))
    for side in range(2):
        copies[side, 1 - side].wait_recv()
        for part in range(2):
            copies[side, part].wait_send()
    for copy in relayed:
        copy.wait()
    own.wait()


def spread(source, number):
    return call(
        spread_kernel,
        (source,),
        jax.ShapeDtypeStruct((source.shape[0], 4, *source.shape[1:]), source.dtype),
        [
            pltpu.SemaphoreType.DMA((3, 2)),
            pltpu.SemaphoreType.DMA((3, 2)),
            pltpu.SemaphoreType.DMA,
        ],
        number,
    )


def collect_kernel(source, target, mine, first, second_in, outgoing, load, send, receive, store):
    me = lax.axis_index("seq")
    one, two, both = me ^ 1, me ^ 2, me ^ 3
    width = source.shape[3] // 2
    greet("seq", [one, two])
    copies = []
    for side, (near, rest) in enumerate(((one, two), (two, one))):
        lanes = pl.ds(side * width, width)
        for order, block in enumerate((both, near)):
            copies.append(
                remote(
                    "seq",
                    near,
                    source.at[:, block, :, lanes],
                    first.at[side, order],
                    send.at[side, order],
                    receive.at[side, order],
                )
            )
        for order, block in enumerate((rest, me)):
            pltpu.make_async_copy(
                source.at[:, block, :, lanes], mine.at[side, order], load.at[side, order]
            ).start()
    passed = []
    for side, rest in enumerate((two, one)):
        copies[side * 2].wait_recv()
        pltpu.make_async_copy(mine.at[side, 0], mine.at[side, 0], load.at[side, 0]).wait()
        outgoing[side] = (
            mine[side, 0].astype(jnp.float32) + first[side, 0].astype(jnp.float32)
        ).astype(outgoing.dtype)
        passed.append(
            remote("seq", rest, outgoing.at[side], second_in.at[side], send.at[2, side], receive.at[2, side])
        )
    for side in range(2):
        copies[side * 2 + 1].wait_recv()
        pltpu.make_async_copy(mine.at[side, 1], mine.at[side, 1], load.at[side, 1]).wait()
        passed[side].wait_recv()
        mine[side, 1] = (
            mine[side, 1].astype(jnp.float32)
            + first[side, 1].astype(jnp.float32)
            + second_in[side].astype(jnp.float32)
        ).astype(mine.dtype)
        out = pltpu.make_async_copy(
            mine.at[side, 1], target.at[:, :, pl.ds(side * width, width)], store.at[side]
        )
        out.start()
    for side in range(2):
        pltpu.make_async_copy(
            mine.at[side, 1], target.at[:, :, pl.ds(side * width, width)], store.at[side]
        ).wait()
    for copy in copies + passed:
        copy.wait_send()


def collect(source, number):
    a, _, rows, width = source.shape
    dma = pltpu.SemaphoreType.DMA
    block = (a, rows, width // 2)
    return call(
        collect_kernel,
        (source,),
        jax.ShapeDtypeStruct((a, rows, width), source.dtype),
        [
            pltpu.VMEM((2, 2, *block), source.dtype),
            pltpu.VMEM((2, 2, *block), source.dtype),
            pltpu.VMEM((2, *block), source.dtype),
            pltpu.VMEM((2, *block), source.dtype),
            dma((2, 2)),
            dma((3, 2)),
            dma((3, 2)),
            dma((2,)),
        ],
        number,
    )


def moe_kernel(
    chips, cap, experts_all, spread_first, send_rows, up_rows, route, w_in, w_out,
    ret, dw_in, dw_out,
    R, U, G, A, I, PB, first, second, W1, W2, RT, stage,
    load, own, z_send, z_recv, s_send, s_recv, y_send, y_recv,
    c_send, c_recv, d_send, d_recv, r_send, r_recv, store,
):
    me, place = lax.axis_index("seq"), lax.axis_index("fsdp")
    one, two, both = me ^ 1, me ^ 2, me ^ 3
    chip, core = place // 2, lax.rem(place, 2)
    sibling = place ^ 1
    count = chips * 2
    part = 2 * cap
    chunk = 4 * part
    barrier = pltpu.get_barrier_semaphore()
    for peer in (one, two):
        pl.semaphore_signal(barrier, inc=1, device_id={"seq": peer}, device_id_type=MESH)
    for step in range(1, count):
        pl.semaphore_signal(
            barrier, inc=1, device_id={"fsdp": lax.rem(place + step, count)}, device_id_type=MESH
        )
    pl.semaphore_wait(barrier, 2 + count - 1)

    def rows_of(k, s):
        return pl.ds(k * chunk + s * part, part)

    loads = []

    def local(source, target, sem):
        copy = pltpu.make_async_copy(source, target, sem)
        copy.start()
        return copy

    dispatched = {}
    own_rows = []

    def dispatch(k):
        target = R.at[:, pl.ds(k * chunk + me * part + core * cap, cap)]
        if k == 0:
            own_rows.append(local(send_rows.at[place], target, own.at[0]))
        for c in range(2):
            if k or c:
                peer = (chip ^ k) * 2 + (core ^ c)
                dispatched[k, c] = remote(
                    "fsdp", peer, send_rows.at[peer], target, z_send.at[k, c], z_recv.at[k, c]
                )

    def z_arrived(k):
        if k == 0:
            own_rows[0].wait()
        for c in range(2):
            if k or c:
                dispatched[k, c].wait_recv()

    sent = {}

    def spread_out(a, k):
        for side, peer in enumerate((one, two)):
            for order in range(2):
                j = (order + side) % 2
                target = (U, R)[a].at[j, rows_of(k, me)]
                source = target if a else up_rows.at[j, rows_of(k, me)]
                sent[a, k, side, j] = remote(
                    "seq", peer, source, target, s_send.at[a, k, side, j], s_recv.at[a, k, side, j]
                )

    def relay(a, k):
        for side, (origin, peer) in enumerate(((one, two), (two, one))):
            sent[a, k, side, side].wait_recv()
            block = (U, R)[a].at[side, rows_of(k, origin)]
            sent[a, k, 2, side] = remote("seq", peer, block, block, y_send.at[a, k, side], y_recv.at[a, k, side])

    def all_arrived(a, k):
        for side in range(2):
            sent[a, k, side, 1 - side].wait_recv()
            sent[a, k, 2, side].wait_recv()

    def experts(k, j):
        rows = pl.ds(k * chunk, chunk)
        logits = times(R[j, rows, :], RT[...])
        lane = lax.broadcasted_iota(jnp.int32, logits.shape, 1)
        logits = jnp.where(lane < experts_all, logits, MASKED)
        powers = jnp.exp(logits - jnp.max(logits, axis=1, keepdims=True))
        picked = jnp.sum(jnp.where(lane == place * 2 + j, powers, 0.0), axis=1, keepdims=True)
        gate = picked / jnp.sum(powers, axis=1, keepdims=True)
        G[j, rows, :] = (U[j, rows, :].astype(jnp.float32) * gate).astype(G.dtype)

        @pl.loop(0, W1.shape[2] // TILE)
        def _(t):
            cols = pl.ds(pl.multiple_of(t * TILE, TILE), TILE)
            v = times(R[j, rows, :], W1[j, :, cols])
            grad = times_transposed(G[j, rows, :], W2[j, cols, :])
            square = v * v
            t = jnp.tanh(ROOT * v * (1.0 + 0.044715 * square))
            half = 0.5 * (1.0 + t)
            A[j, rows, cols] = (v * half).astype(A.dtype)
            slope = half + 0.5 * v * (1.0 - t * t) * (ROOT * (1.0 + 0.134145 * square))
            I[j, rows, cols] = (grad * slope).astype(I.dtype)

        @pl.loop(0, W1.shape[1] // TILE)
        def _(t):
            cols = pl.ds(pl.multiple_of(t * TILE, TILE), TILE)
            PB[0, j, rows, cols] = times(A[j, rows, :], W2[j, :, cols]).astype(PB.dtype)
            PB[1, j, rows, cols] = times_transposed(I[j, rows, :], W1[j, cols, :]).astype(PB.dtype)

    summed = {}

    def near_of(j):
        return (one, two) if j == 0 else (two, one)

    def collect_one(k, j):
        near, rest = near_of(j)
        for a in range(2):
            for order, block in enumerate((both, near)):
                summed[a, k, j, order] = remote(
                    "seq", near, PB.at[a, j, rows_of(k, block)], first.at[a, j, k, order],
                    c_send.at[a, j, k, order], c_recv.at[a, j, k, order],
                )

    def collect_two(k, j):
        near, rest = near_of(j)
        for a in range(2):
            summed[a, k, j, 0].wait_recv()
            first[a, j, k, 0] = (
                first[a, j, k, 0].astype(jnp.float32) + PB[a, j, rows_of(k, rest), :].astype(jnp.float32)
            ).astype(first.dtype)
            summed[a, k, j, 2] = remote(
                "seq", rest, first.at[a, j, k, 0], second.at[a, j, k], d_send.at[a, j, k], d_recv.at[a, j, k]
            )

    returns = {}

    def collect_three(k, j):
        for a in range(2):
            summed[a, k, j, 1].wait_recv()
            summed[a, k, j, 2].wait_recv()
            first[a, j, k, 1] = (
                first[a, j, k, 1].astype(jnp.float32)
                + PB[a, j, rows_of(k, me), :].astype(jnp.float32)
                + second[a, j, k].astype(jnp.float32)
            ).astype(first.dtype)
            to = chip ^ k
            target = ret.at[a, place, j]
            for c in range(2):
                if k == 0:
                    if c == 0:
                        returns[a, k, j, 0] = local(
                            first.at[a, j, k, 1, pl.ds(core * cap, cap)], target, own.at[1 + a * 2 + j]
                        )
                        returns[a, k, j, 1] = remote(
                            "fsdp", sibling, first.at[a, j, k, 1, pl.ds((core ^ 1) * cap, cap)], target,
                            r_send.at[a, j, k, 1], r_recv.at[a, j, k, 1],
                        )
                    continue
                returns[a, k, j, c] = remote(
                    "fsdp", to * 2 + (core ^ c), first.at[a, j, k, 1, pl.ds((core ^ c) * cap, cap)], target,
                    r_send.at[a, j, k, c], r_recv.at[a, j, k, c],
                )

    staged = {}

    def weight_grads(j, which, tiles):
        left, right, out = ((R, I, dw_in), (A, G, dw_out))[which]
        for m in tiles:
            slot = m % 2
            lanes = slice(m * GRAD, (m + 1) * GRAD)
            if slot in staged:
                staged.pop(slot).wait()

            @pl.loop(0, right.shape[2] // TILE)
            def _(t):
                cols = pl.ds(pl.multiple_of(t * TILE, TILE), TILE)
                stage[slot, :, cols] = transposed_times(left[j, :, lanes], right[j, :, cols]).astype(stage.dtype)

            staged[slot] = local(stage.at[slot], out.at[j, lanes], store.at[slot])

    later = range(spread_first, chips)
    turn = TURN
    away = [k for k in turn if k]
    dispatch(0)
    dispatch(away[0])
    dispatch(away[1])
    for j in range(2):
        loads.append(local(w_in.at[j], W1.at[j], load.at[j]))
        loads.append(local(w_out.at[j], W2.at[j], load.at[2 + j]))
    loads.append(local(route, RT, load.at[4]))
    early = spread_first * chunk
    for j in range(2):
        loads.append(local(up_rows.at[j, pl.ds(0, early)], U.at[j, pl.ds(0, early)], load.at[5 + j]))
    for n, k in enumerate(later):
        for j in range(2):
            block = rows_of(k, me)
            loads.append(local(up_rows.at[j, block], U.at[j, block], load.at[7 + 2 * n + j]))
    if turn[0]:
        for k in later:
            spread_out(0, k)
    z_arrived(turn[0])
    spread_out(1, turn[0])
    if not turn[0]:
        for k in later:
            spread_out(0, k)
    z_arrived(turn[1])
    spread_out(1, turn[1])
    dispatch(away[2])
    relay(1, turn[0])
    for copy in loads:
        copy.wait()
    for k in later:
        relay(0, k)
    z_arrived(turn[2])
    spread_out(1, turn[2])
    for n in range(chips):
        k = turn[n]
        all_arrived(1, k)
        if k >= spread_first:
            all_arrived(0, k)
        experts(k, 0)
        collect_one(k, 0)
        if n < 2:
            relay(1, turn[n + 1 + (n > 0)])
        if n == 0:
            z_arrived(turn[3])
            spread_out(1, turn[3])
        else:
            collect_two(turn[n - 1], 0)
        if n > 1:
            collect_three(turn[n - 2], 0)
        experts(k, 1)
        collect_one(k, 1)
        if n == 0:
            relay(1, turn[2])
        else:
            collect_two(turn[n - 1], 1)
        if n > 1:
            collect_three(turn[n - 2], 1)
    weight_grads(0, 0, range(4))
    collect_two(turn[3], 0)
    collect_three(turn[2], 0)
    collect_two(turn[3], 1)
    collect_three(turn[2], 1)
    weight_grads(0, 1, range(4))
    weight_grads(1, 0, range(2))
    collect_three(turn[3], 0)
    weight_grads(1, 0, range(2, 4))
    collect_three(turn[3], 1)
    weight_grads(1, 1, range(4))
    for copy in staged.values():
        copy.wait()
    for copy in dispatched.values():
        copy.wait_send()
    for copy in sent.values():
        copy.wait_send()
    for copy in summed.values():
        copy.wait_send()
    for (a, k, j, c), copy in returns.items():
        copy.wait()


def moe(send_rows, up_rows, route, w_in, w_out, experts_all, number):
    S, low, dma = jax.ShapeDtypeStruct, jnp.bfloat16, pltpu.SemaphoreType.DMA
    owners, _, cap, width = send_rows.shape
    chips = owners // 2
    hidden_units = w_in.shape[2]
    count = owners * cap * 4
    part = 2 * cap

    def vmem(*shape, dtype=low):
        return pltpu.VMEM(shape, dtype)

    return pl.pallas_call(
        functools.partial(moe_kernel, chips, cap, experts_all, SPREAD_FIRST),
        out_shape=(
            S((2, owners, 2, cap, width), low),
            S(w_in.shape, low),
            S(w_out.shape, low),
        ),
        in_specs=[ANY] * 5,
        out_specs=(ANY,) * 3,
        scratch_shapes=[
            vmem(2, count, width),
            vmem(2, count, width),
            vmem(2, count, width),
            vmem(2, count, hidden_units),
            vmem(2, count, hidden_units),
            vmem(2, 2, count, width),
            vmem(2, 2, chips, 2, part, width),
            vmem(2, 2, chips, part, width),
            vmem(*w_in.shape),
            vmem(*w_out.shape),
            vmem(*route.shape),
            vmem(2, GRAD, max(width, hidden_units)),
            dma((7 + 2 * (chips - SPREAD_FIRST),)),
            dma((5,)),
            dma((chips, 2)),
            dma((chips, 2)),
            dma((2, chips, 2, 2)),
            dma((2, chips, 2, 2)),
            dma((2, chips, 2)),
            dma((2, chips, 2)),
            dma((2, 2, chips, 2)),
            dma((2, 2, chips, 2)),
            dma((2, 2, chips)),
            dma((2, 2, chips)),
            dma((2, 2, chips, 2)),
            dma((2, 2, chips, 2)),
            dma((2,)),
        ],
        compiler_params=pltpu.CompilerParams(
            collective_id=number, has_side_effects=True, vmem_limit_bytes=60 * 2**20
        ),
        cost_estimate=pl.CostEstimate(
            flops=12 * 2 * count * width * hidden_units, bytes_accessed=2**25, transcendentals=0
        ),
    )(send_rows, up_rows, route, w_in, w_out)


def front_kernel(
    count, cap, experts_all, spread_here, hidden, qkv_weight, mix, out_grad, router, gain_a, gain_b, ids, length,
    normed_out, heads_out, mix_out, small_out, gains_out, up, projected_out, attended_out, sums_out,
    middle_out, low_out, logits_out, sent_out, hit_out,
    staged, hid, heads_all, small_own, small_all, gains, normed, proj, attended, sums, acc, stat,
    mix_all, up_low, rows, hit, mixed, middle, normed_low, logits, sent_rows, pile,
    h_send, h_recv, q_send, q_recv, f_send, f_recv, n_send, n_recv, u_send, u_recv, m_send, m_recv,
    s_send, s_recv, x_send, x_recv, y_send, y_recv, local,
):
    me, place = lax.axis_index("seq"), lax.axis_index("fsdp")
    one, two, both = me ^ 1, me ^ 2, me ^ 3
    others = (one, two, both)
    chips = count // 2
    chip, core = place // 2, lax.rem(place, 2)
    sibling = place ^ 1
    share = mix.shape[0]
    tokens = hidden.shape[0]
    group = attended.shape[1]
    part, chunk = 2 * cap, 8 * cap
    barrier = pltpu.get_barrier_semaphore()
    for peer in others:
        pl.semaphore_signal(barrier, inc=1, device_id={"seq": peer}, device_id_type=MESH)
    for step in range(1, count):
        pl.semaphore_signal(
            barrier, inc=1, device_id={"fsdp": lax.rem(place + step, count)}, device_id_type=MESH
        )
    pl.semaphore_wait(barrier, 3 + count - 1)

    def keep(source, target, number):
        copy = pltpu.make_async_copy(source, target, local.at[number])
        copy.start()
        return copy

    def far(k):
        return (chip ^ k) * 2 + core

    away, near = {}, {}

    def block(a, owner):
        if a == 0:
            return mix_all.at[me, owner // 2, core]
        if a == 1:
            return small_all.at[pl.ds(pl.multiple_of((me * count + owner) * share, share), share)]
        return heads_all.at[:, owner]

    own_of = (mix, small_own, staged)

    def send_far(a):
        for k in range(1, chips):
            away[a, k] = remote("fsdp", far(k), own_of[a], block(a, place), f_send.at[a, k], f_recv.at[a, k])

    def send_near(a):
        near[a, 0] = remote("fsdp", sibling, own_of[a], block(a, place), n_send.at[a, 0], n_recv.at[a, 0])

    def pass_on(a):
        for k in range(1, chips):
            away[a, k].wait_recv()
            arrived = block(a, far(k))
            near[a, k] = remote("fsdp", sibling, arrived, arrived, n_send.at[a, k], n_recv.at[a, k])

    direct = {}

    def both_ways(name, views, sources, send, receive):
        for side, peer in enumerate((one, two)):
            for order in range(2):
                p = (order + side) % 2
                direct[name, side, p] = remote(
                    "seq", peer, sources[p], views[p](me), send.at[side, p], receive.at[side, p]
                )

    def relay(name, views, send, receive):
        for side, (origin, peer) in enumerate(((one, two), (two, one))):
            direct[name, side, side].wait_recv()
            source = views[side](origin)
            direct[name, 2, side] = remote("seq", peer, source, source, send.at[2, side], receive.at[2, side])

    def arrived(name):
        for side in range(2):
            direct[name, side, 1 - side].wait_recv()
            direct[name, 2, side].wait_recv()

    moved = {}

    def send_rows(k):
        for c in range(2):
            if k == 0 and c == 0:
                continue
            peer = (chip ^ k) * 2 + (core ^ c)
            moved[k, c] = remote(
                "fsdp", peer, rows.at[peer], up.at[:, pl.ds(k * chunk + me * part + core * cap, cap)],
                u_send.at[k, c], u_recv.at[k, c],
            )

    columns = [
        (pl.ds(p * group, group), lambda to, p=p: pl.ds(pl.multiple_of((p * 4 + to) * group, group), group))
        for p in range(3)
    ]
    exchanged = [
        remote(
            "seq", peer, qkv_weight.at[:, view(peer)], staged.at[me, :, into], q_send.at[i, p], q_recv.at[i, p]
        )
        for i, peer in enumerate(others)
        for p, (into, view) in enumerate(columns)
    ]
    half = tokens // 2
    hidden_views = [
        lambda origin, p=p: hid.at[pl.ds(origin * tokens + p * half, half)] for p in range(2)
    ]
    both_ways("hidden", hidden_views, [hidden.at[pl.ds(p * half, half)] for p in range(2)], h_send, h_recv)
    send_far(0)
    own_heads = [
        keep(qkv_weight.at[:, view(me)], staged.at[me, :, into], 14 + p) for p, (into, view) in enumerate(columns)
    ]
    own_hidden = keep(hidden, hid.at[pl.ds(me * tokens, tokens)], 1)
    own_mix = keep(mix, block(0, place), 2)
    own_grad = keep(out_grad, up_low, 13)
    pile[...] = jnp.zeros_like(pile)
    pile[:experts_all, :share] = router[...].astype(jnp.float32)
    for n, gain in enumerate((gain_a, gain_b)):
        pile[experts_all + n : experts_all + n + 1, :share] = gain[...].astype(jnp.float32)
    small_own[...] = jnp.transpose(pile[...])[:share].astype(small_own.dtype)
    send_far(1)
    send_near(1)
    own_small = keep(small_own, block(1, place), 3)
    across = ids[...].astype(jnp.float32)
    chosen = jnp.transpose(jnp.broadcast_to(across, (128, tokens)))[:, :1]
    first = lax.broadcasted_iota(jnp.int32, (tokens, tokens), 0)
    second = lax.broadcasted_iota(jnp.int32, (tokens, tokens), 1)
    ranks = jnp.sum(jnp.where((chosen == across) & (first < second), 1.0, 0.0), axis=0, keepdims=True)
    slot = (across * cap + ranks).astype(jnp.int32)
    hit[...] = jnp.where(lax.broadcasted_iota(jnp.int32, hit.shape, 0) == slot, 1.0, 0.0).astype(hit.dtype)
    own_grad.wait()
    position = me * tokens + lax.broadcasted_iota(jnp.int32, (tokens, 1), 0)
    up_low[...] = jnp.where(position < length[0], up_low[...].astype(jnp.float32), 0.0).astype(up_low.dtype)

    def to_slots(values, target):
        @pl.loop(0, count)
        def _(owner):
            picked = hit[pl.ds(pl.multiple_of(owner * 2 * cap, 2 * cap), 2 * cap), :]
            target[owner] = times(picked, values[...]).astype(target.dtype).reshape(target.shape[1:])

    to_slots(up_low, rows)
    own_rows = keep(rows.at[place], up.at[:, pl.ds(me * part + core * cap, cap)], 4)
    send_rows(0)
    hit_kept = keep(hit, hit_out, 0)
    pass_on(1)
    for copy in own_heads:
        copy.wait()
    for copy in exchanged:
        copy.wait_recv()
    own_block = keep(staged, heads_all.at[:, place], 5)
    send_far(2)
    send_near(2)
    own_small.wait()
    for k in range(chips):
        near[1, k].wait_recv()
    mine = small_all.at[pl.ds(pl.multiple_of(me * count * share, share), count * share)]
    smalls = [remote("seq", peer, mine, mine, q_send.at[3, i], q_recv.at[3, i]) for i, peer in enumerate(others)]

    def up_views(k):
        return [lambda origin, j=j: up.at[j, pl.ds(k * chunk + origin * part, part)] for j in range(2)]

    def up_out(k):
        if k == 0:
            own_rows.wait()
        for c in range(2):
            if (k, c) in moved:
                moved[k, c].wait_recv()
        if k < spread_here:
            views = up_views(k)
            both_ways(("up", k), views, [views[0](me), views[1](me)], s_send.at[k], s_recv.at[k])

    def up_relay(k):
        if k < spread_here:
            relay(("up", k), up_views(k), s_send.at[k], s_recv.at[k])

    up_out(0)
    relay("hidden", hidden_views, h_send, h_recv)
    own_mix.wait()
    for k in range(1, chips):
        away[0, k].wait_recv()
    mix_views = [
        lambda origin, p=p: mix_all.at[origin, pl.ds(p * (chips // 2), chips // 2), core] for p in range(2)
    ]
    both_ways("mix", mix_views, [mix_views[p](me) for p in range(2)], m_send, m_recv)
    for copy in smalls:
        copy.wait_recv()
    small_kept = keep(small_all, small_out, 6)
    own_hidden.wait()
    arrived("hidden")
    turned = jnp.transpose(small_all[...].astype(jnp.float32))
    gains[0:1, :] = turned[experts_all : experts_all + 1]
    gains[1:2, :] = turned[experts_all + 1 : experts_all + 2]
    gains_kept = keep(gains, gains_out, 17)
    gain = gains[0:1, :]

    @pl.loop(0, hid.shape[0] // 128)
    def _(t):
        place_rows = pl.ds(pl.multiple_of(t * 128, 128), 128)
        value = hid[place_rows, :].astype(jnp.float32)
        scale = lax.rsqrt(jnp.mean(value * value, axis=-1, keepdims=True) + EPS)
        normed[place_rows, :] = (value * scale * gain).astype(normed.dtype)

    normed_kept = keep(normed, normed_out, 7)
    pass_on(2)
    for k in range(1, chips):
        send_rows(k)
    up_relay(0)
    relay("mix", mix_views, m_send, m_recv)
    own_block.wait()
    for k in range(chips):
        near[2, k].wait_recv()
    heads_kept = keep(heads_all, heads_out, 8)
    width = hid.shape[1]

    for p in range(3):

        @pl.loop(0, hid.shape[0] // TILE)
        def _(t):
            place_rows = pl.ds(pl.multiple_of(t * TILE, TILE), TILE)
            weights = heads_all[:, :, :, p * group : (p + 1) * group].reshape(width, group)
            proj[place_rows, p * group : (p + 1) * group] = times(normed[place_rows, :], weights).astype(proj.dtype)

    projected_kept = keep(proj, projected_out, 9)
    head_of = lax.broadcasted_iota(jnp.int32, (tokens, group), 1) // HEAD_DIM
    sent = []
    for i in range(4):
        own = slice(i * tokens, (i + 1) * tokens)
        reach = (i + 1) * tokens

        @pl.loop(0, group // HEAD_DIM)
        def _(h):
            query = jnp.where(head_of == h, proj[own, :group] * (HEAD_DIM**-0.5), 0).astype(proj.dtype)
            scores = times_transposed(query, proj[:reach, group : 2 * group])
            column = lax.broadcasted_iota(jnp.int32, scores.shape, 1)
            row = lax.broadcasted_iota(jnp.int32, scores.shape, 0) + i * tokens
            scores = jnp.where((column <= row) & (column < length[0]), scores, MASKED)
            top = jnp.max(scores, axis=1, keepdims=True)
            powers = jnp.exp(scores - top)
            total = jnp.sum(powers, axis=1, keepdims=True)
            probs = (powers * (1.0 / total)).astype(proj.dtype)
            out = times(probs, proj[:reach, 2 * group :])
            acc[...] = jnp.where(head_of == h, out, acc[...])
            lane = lax.broadcasted_iota(jnp.int32, stat.shape, 1)
            stat[...] = jnp.where(lane == h, top + jnp.log(total), stat[...])

        attended[own, :] = acc[...].astype(attended.dtype)
        sums[:, own] = jnp.transpose(stat[...])[:8]
        target = mixed.at[:, pl.ds(pl.multiple_of(me * group, group), group)]

        @pl.when(me != i)
        def _():
            remote("seq", i, attended.at[own], target, x_send.at[i], x_recv.at[me])

        @pl.when(me == i)
        def _():
            pltpu.make_async_copy(attended.at[own], target, local.at[10]).start()

        if i == 1:
            up_relay(1)
        if i == 0:
            up_out(1)
            arrived("mix")
            both_cores = [
                remote(
                    "fsdp", sibling, mix_all.at[s, :, core], mix_all.at[s, :, core], y_send.at[s], y_recv.at[s]
                )
                for s in range(4)
            ]
    up_out(2)
    attended_kept = keep(attended, attended_out, 11)
    sums_kept = keep(sums, sums_out, 12)
    for i in range(4):
        target = mixed.at[:, pl.ds(i * group, group)]

        @pl.when(me != i)
        def _():
            copy = pltpu.make_async_remote_copy(
                attended.at[pl.ds(i * tokens, tokens)], target, x_send.at[i], x_recv.at[i],
                device_id={"seq": i}, device_id_type=MESH,
            )
            copy.wait()

        @pl.when(me == i)
        def _():
            pltpu.make_async_copy(attended.at[pl.ds(i * tokens, tokens)], target, local.at[10]).wait()

    up_relay(2)
    for copy in both_cores:
        copy.wait()
    mix_kept = keep(mix_all.at[me], mix_out, 18)
    for n in range(width // TILE):
        lanes = slice(n * TILE, (n + 1) * TILE)
        total = hid[pl.ds(pl.multiple_of(me * tokens, tokens), tokens), lanes].astype(jnp.float32)
        for s in range(4):
            weights = mix_all[s, :, :, :, lanes].reshape(group, TILE)
            total = total + times(mixed[:, s * group : (s + 1) * group], weights)
        middle[:, lanes] = total
    middle_kept = keep(middle, middle_out, 19)
    for t in range(tokens // 128):
        span = slice(t * 128, (t + 1) * 128)
        value = middle[span, :]
        scale = lax.rsqrt(jnp.mean(value * value, axis=-1, keepdims=True) + EPS)
        normed_low[span, :] = (value * scale * gains[1:2, :]).astype(normed_low.dtype)
    logits[...] = times(normed_low[...], small_all[...])
    to_slots(normed_low, sent_rows)
    last = [
        keep(normed_low, low_out, 20),
        keep(logits, logits_out, 21),
        keep(sent_rows, sent_out, 22),
    ]
    for k in range(3, chips):
        up_out(k)
        up_relay(k)
    for k in range(spread_here):
        arrived(("up", k))
    for copy in (*direct.values(), *exchanged, *smalls, *away.values(), *near.values(), *moved.values()):
        copy.wait_send()
    for copy in (
        small_kept, normed_kept, heads_kept, projected_kept, attended_kept, sums_kept,
        hit_kept, gains_kept, mix_kept, middle_kept, *last,
    ):
        copy.wait()


def front(hidden, qkv_weight, mix, out_grad, router, gain_a, gain_b, ids, lengths, count, cap, spread_here, number):
    S, dma, low, f32 = jax.ShapeDtypeStruct, pltpu.SemaphoreType.DMA, jnp.bfloat16, jnp.float32
    chips = count // 2
    tokens, width = hidden.shape
    experts_all = router.shape[0]
    group = qkv_weight.shape[1] // 12
    share = qkv_weight.shape[0]
    full = 4 * tokens
    lanes = -(-(experts_all + 2) // 128) * 128
    all_heads = (4, count, share, 3 * group)
    slots = experts_all * cap

    def vmem(*shape, dtype=low):
        return pltpu.VMEM(shape, dtype)

    near = pl.BlockSpec(memory_space=pltpu.VMEM)
    return pl.pallas_call(
        functools.partial(front_kernel, count, cap, experts_all, spread_here),
        out_shape=(
            S((full, width), low),
            S(all_heads, low),
            S((chips, 2, share, width), low),
            S((width, lanes), low),
            S((8, width), f32),
            S((2, 4 * count * cap, width), low),
            S((full, 3 * group), low),
            S((full, group), low),
            S((8, full), f32),
            S((tokens, width), f32),
            S((tokens, width), low),
            S((tokens, lanes), f32),
            S((count, 2, cap, width), low),
            S((slots, tokens), low),
        ),
        in_specs=[ANY] * 4 + [near] * 4 + [pl.BlockSpec(memory_space=pltpu.SMEM)],
        out_specs=(ANY,) * 14,
        scratch_shapes=[
            vmem(4, share, 3 * group),
            vmem(full, width),
            vmem(*all_heads),
            vmem(share, lanes),
            vmem(width, lanes),
            vmem(8, width, dtype=f32),
            vmem(full, width),
            vmem(full, 3 * group),
            vmem(full, group),
            vmem(8, full, dtype=f32),
            vmem(tokens, group, dtype=f32),
            vmem(tokens, 128, dtype=f32),
            vmem(4, chips, 2, share, width),
            vmem(tokens, width),
            vmem(count, 2, cap, width),
            vmem(slots, tokens),
            vmem(tokens, width),
            vmem(tokens, width, dtype=f32),
            vmem(tokens, width),
            vmem(tokens, lanes, dtype=f32),
            vmem(count, 2, cap, width),
            vmem(lanes, 128, dtype=f32),
            dma((3, 2)), dma((3, 2)), dma((4, 3)), dma((4, 3)),
            dma((3, chips)), dma((3, chips)), dma((3, chips)), dma((3, chips)),
            dma((chips, 2)), dma((chips, 2)), dma((3, 2)), dma((3, 2)),
            dma((chips, 3, 2)), dma((chips, 3, 2)), dma((4,)), dma((4,)), dma((4,)), dma((4,)), dma((23,)),
        ],
        compiler_params=pltpu.CompilerParams(
            collective_id=number, has_side_effects=True, vmem_limit_bytes=60 * 2**20
        ),
    )(hidden, qkv_weight, mix, out_grad, router, gain_a, gain_b, ids, lengths)


def finish_kernel(
    experts_all, experts, output, input_grad, heads, mix, small, gain, *refs
):
    wide, refs = refs[:experts], refs[experts:]
    output_out, input_out, heads_out, mix_out, route_out, gain_a, gain_b = refs[:7]
    wide_out, kinds = refs[7 : 7 + experts], refs[7 + experts]
    for source, target in zip(wide, wide_out):
        target[...] = source[...].astype(target.dtype)
    output_out[...] = output[...]
    input_out[...] = input_grad[...]
    heads_out[...] = heads[...].astype(heads_out.dtype)
    mix_out[...] = mix[...]

    @pl.when(pl.program_id(0) == 0)
    def _():
        share = route_out.shape[1]
        start = lax.rem(lax.axis_index("fsdp") * share, 128)
        total = small[0] + small[1] + small[2] + small[3]
        own = jnp.zeros((total.shape[0], share), jnp.float32)
        for place in range(0, 128, share):
            own = own + jnp.where(start == place, total[:, place : place + share], 0.0)
        kinds[...] = own
        route_out[...] = kinds[:experts_all]
        gain_a[...] = kinds[experts_all : experts_all + 1] / gain[...].astype(jnp.float32)
        gain_b[...] = kinds[experts_all + 1 : experts_all + 2]


def finish(output, input_grad, heads, mix, small, gain, experts_all, wide):
    S, f32 = jax.ShapeDtypeStruct, jnp.float32
    steps = 8
    share = heads.shape[0]

    def part(x, dim):
        shape = tuple(size // steps if d == dim else size for d, size in enumerate(x.shape))
        return pl.BlockSpec(shape, lambda n: tuple(n if d == dim else 0 for d in range(len(shape))))

    def same(*shape):
        return pl.BlockSpec(shape, lambda n: (0,) * len(shape))

    halves = [pl.BlockSpec((1, x.shape[1] * 2 // steps, x.shape[2]), lambda n: (n // (steps // 2), n % (steps // 2), 0)) for x in wide]
    return pl.pallas_call(
        functools.partial(finish_kernel, experts_all, len(wide)),
        grid=(steps,),
        out_shape=(
            S(output.shape, output.dtype),
            S(input_grad.shape, f32),
            S(heads.shape, f32),
            S(mix.shape, f32),
            S((experts_all, share), f32),
            S((1, share), f32),
            S((1, share), f32),
            *(S(x.shape, f32) for x in wide),
        ),
        in_specs=[
            part(output, 0), part(input_grad, 0), part(heads, 1), part(mix, 1), same(*small.shape), same(1, share), *halves
        ],
        out_specs=(
            part(output, 0), part(input_grad, 0), part(heads, 1), part(mix, 1),
            same(experts_all, share), same(1, share), same(1, share), *halves,
        ),
        scratch_shapes=[pltpu.VMEM((small.shape[1], share), f32)],
        compiler_params=pltpu.CompilerParams(vmem_limit_bytes=60 * 2**20),
    )(output, input_grad, heads, mix, small, gain, *wide)


def back_kernel(
    count, experts_all, ret_in, hit_in, middle_in, logits_in, low_in, out_grad, small_all, gains_in, hidden_in,
    proj_in, attended_in, sums_in, normed_in, heads_in, mix_in, ids, length,
    output_out, input_out, heads_out, mix_out, small_out,
    ret, hit, middle, logits, normed_two, up_low, route, gains, hid, output, grad_middle, grad_in, grad_logits, grad_two,
    grads, proj, attended, sums, normed, heads, mix, small, grad_heads, delta, masked_grad, masked_query,
    masked_key, masked_value, probs, slopes, grad_query, grad_key, grad_value, grad_proj, part, weights, weights_mix, gain_sum,
    sib_a, sib_b, sib_c, own_a, own_b, own_c, got_a, got_b, got_c, total_a, total_b, total_c, first, second,
    g_send, g_recv, b_send, b_recv, bb_send, bb_recv, z_send, z_recv, x_send, x_recv, w_send, w_recv, c_send, c_recv, load, keep,
):
    me, place = lax.axis_index("seq"), lax.axis_index("fsdp")
    one, two, both = me ^ 1, me ^ 2, me ^ 3
    others = (one, two, both)
    chips = count // 2
    chip, core = place // 2, lax.rem(place, 2)
    sibling = place ^ 1
    tokens, width = grad_in.shape
    gain_row = experts_all
    group = attended.shape[1]
    share = weights.shape[0] // (4 * count)
    heads_local = group // HEAD_DIM
    low = grads.dtype
    barrier = pltpu.get_barrier_semaphore()
    for peer in others:
        pl.semaphore_signal(barrier, inc=1, device_id={"seq": peer}, device_id_type=MESH)
    for k in range(1, chips):
        pl.semaphore_signal(
            barrier, inc=1, device_id={"fsdp": (chip ^ k) * 2 + core}, device_id_type=MESH
        )
    pl.semaphore_signal(barrier, inc=1, device_id={"fsdp": sibling}, device_id_type=MESH)
    pl.semaphore_wait(barrier, 3 + chips)

    def local(source, to, sem):
        copy = pltpu.make_async_copy(source, to, sem)
        copy.start()
        return copy

    heads_of = [
        local(source, to, load.at[9 + i])
        for i, (source, to) in enumerate(
            (
                (hit_in, hit),
                (ret_in, ret),
                (middle_in, middle),
                (logits_in, logits),
                (low_in, normed_two),
                (out_grad, up_low),
                (small_all, route),
                (gains_in, gains),
                (hidden_in, hid),
            )
        )
    ]
    loads = [
        local(source, to, load.at[1 + i])
        for i, (source, to) in enumerate(
            (
                (proj_in, proj),
                (attended_in, attended),
                (sums_in, sums),
                (mix_in, mix),
                (heads_in, heads),
                (normed_in, normed),
            )
        )
    ]
    for copy in heads_of:
        copy.wait()
    small[...] = jnp.zeros_like(small)
    grad_two[...] = jnp.zeros_like(grad_two)
    lane = lax.broadcasted_iota(jnp.int32, (STEP, route.shape[1]), 1)
    chosen = jnp.transpose(jnp.broadcast_to(ids[...].astype(jnp.float32), (128, tokens)))[:, :1].astype(jnp.int32)
    for t in range(tokens // STEP):
        span = slice(t * STEP, (t + 1) * STEP)
        position = me * tokens + t * STEP + lax.broadcasted_iota(jnp.int32, (STEP, 1), 0)
        valid = jnp.where(position < length[0], 1.0, 0.0)
        scores = jnp.where(lane < experts_all, logits[span, :], MASKED)
        powers = jnp.exp(scores - jnp.max(scores, axis=1, keepdims=True))
        share_of = powers / jnp.sum(powers, axis=1, keepdims=True)
        choose = lane == chosen[span]
        gate = jnp.sum(jnp.where(choose, share_of, 0.0), axis=1, keepdims=True)
        back_rows = transposed_times(hit[:, span], ret[0])
        value = middle[span, :]
        output[span, :] = (valid * (value + gate * back_rows)).astype(low)
        upstream = valid * up_low[span, :].astype(jnp.float32)
        grad_gate = jnp.sum(upstream * back_rows, axis=1, keepdims=True)
        slope = grad_gate * gate * (jnp.where(choose, 1.0, 0.0) - share_of)
        grad_logits[span, :] = slope.astype(low)
        incoming = times_transposed(grad_logits[span, :], route[...]) + transposed_times(hit[:, span], ret[1])
        scale = lax.rsqrt(jnp.mean(value * value, axis=-1, keepdims=True) + EPS)
        shrunk = value * scale
        grad_two[...] += jnp.sum(incoming * shrunk, axis=0, keepdims=True)
        scaled = incoming * gains[1:2, :]
        total = upstream + scale * (scaled - shrunk * jnp.mean(scaled * shrunk, axis=-1, keepdims=True))
        grad_middle[span, :] = total
        grad_in[span, :] = total.astype(low)
    output_kept = local(output, output_out, load.at[8])
    own_grad = local(grad_in, grads.at[pl.ds(me * tokens, tokens)], load.at[0])
    half = tokens // 2
    direct = {}
    for side, peer in enumerate((one, two)):
        for order in range(2):
            p = (order + side) % 2
            direct[side, p] = remote(
                "seq", peer, grad_in.at[pl.ds(p * half, half)], grads.at[pl.ds(me * tokens + p * half, half)],
                g_send.at[side, p], g_recv.at[side, p],
            )
    for n in range(width // 128):
        lanes = slice(n * 128, (n + 1) * 128)
        kinds = transposed_times(grad_logits[...], normed_two[:, lanes])
        small[n // 2, n % 2, :experts_all, :] = kinds[:experts_all]
        small[n // 2, n % 2, gain_row + 1 : gain_row + 2, :] = grad_two[:, lanes]
    for copy in loads:
        copy.wait()
    head_of = lax.broadcasted_iota(jnp.int32, (tokens, group), 1) // HEAD_DIM
    key_at = lax.broadcasted_iota(jnp.int32, (tokens, tokens), 0)
    for j in range(4):
        rows = slice(j * tokens, (j + 1) * tokens)
        for h in range(heads_local):
            key = proj[rows, group : 2 * group] * (HEAD_DIM**-0.5)
            masked_key[j * heads_local + h] = jnp.where(head_of == h, key, 0).astype(low)
            masked_value[j * heads_local + h] = jnp.where(head_of == h, proj[rows, 2 * group :], 0).astype(low)
    grad_key[...] = jnp.zeros_like(grad_key)
    grad_value[...] = jnp.zeros_like(grad_value)
    gain_sum[...] = jnp.zeros_like(gain_sum)

    def block(i, j, masked):
        rows = pl.ds(pl.multiple_of(i * tokens, tokens), tokens)
        keys = pl.ds(pl.multiple_of(j * tokens, tokens), tokens)
        hidden = j * tokens + key_at >= length[0]
        if masked:
            hidden = hidden | (key_at > lax.broadcasted_iota(jnp.int32, (tokens, tokens), 1))
        total = None
        for h in range(heads_local):
            lanes = slice(h * tokens, (h + 1) * tokens)
            key = masked_key[j * heads_local + h]
            scores = times_transposed(key, proj[rows, :group])
            scores = jnp.where(hidden, MASKED, scores)
            p = jnp.exp(scores - sums[h : h + 1, rows])
            probs[:, lanes] = p.astype(low)
            grad = times_transposed(masked_value[j * heads_local + h], grad_heads[...])
            slopes[:, lanes] = (p * (grad - delta[h : h + 1, :])).astype(low)
            term = transposed_times(slopes[:, lanes], key)
            total = term if total is None else total + term
        grad_query[...] += total
        grad_value[keys, :] += times(probs[...], masked_grad[...])
        grad_key[keys, :] += times(slopes[...], masked_query[...])

    def queries(i):
        rows = pl.ds(pl.multiple_of(i * tokens, tokens), tokens)
        grad_heads[...] = times_transposed(grads[rows, :], mix[...]).astype(low)
        out = grad_heads[...].astype(jnp.float32)
        turned = jnp.transpose(out * attended[rows, :].astype(jnp.float32))
        query = proj[rows, :group]
        for h in range(heads_local):
            delta[h : h + 1, :] = jnp.sum(turned[h * HEAD_DIM : (h + 1) * HEAD_DIM], axis=0, keepdims=True)
            masked_grad[h * tokens : (h + 1) * tokens, :] = jnp.where(head_of == h, out, 0).astype(low)
            masked_query[h * tokens : (h + 1) * tokens, :] = jnp.where(head_of == h, query, 0).astype(low)
        grad_query[...] = jnp.zeros_like(grad_query)

        @pl.loop(0, i)
        def _(j):
            block(i, j, False)

        block(i, i, True)
        grad_proj[rows, :group] = grad_query[...].astype(low)

    own_grad.wait()
    queries(me)
    for side, (origin, peer) in enumerate(((one, two), (two, one))):
        direct[side, side].wait_recv()
        source = grads.at[pl.ds(origin * tokens + side * half, half)]
        direct[2, side] = remote("seq", peer, source, source, g_send.at[2, side], g_recv.at[2, side])
    for side, origin in enumerate((one, two)):
        direct[side, 1 - side].wait_recv()
        queries(origin)
    for side in range(2):
        direct[2, side].wait_recv()
    for n in range(width // TILE):
        lanes = slice(n * TILE, (n + 1) * TILE)
        weights_mix[:, lanes] = transposed_times(attended[...], grads[:, lanes]).astype(low)
    order_of = [*range(1, chips), 0]
    to_sibling, away = {}, {}

    def rows_at(s, owner):
        return pl.ds(pl.multiple_of((s * count + owner) * share, share), share)

    def start_sibling(a, k, core_of):
        owner = (chip ^ k) * 2 + core_of
        if a == 1:
            return [
                remote(
                    "fsdp", sibling, weights_mix.at[pl.ds(pl.multiple_of(owner * share, share), share)], sib_b.at[k],
                    b_send.at[0, k], b_recv.at[0, k],
                )
            ]
        if a == 2:
            return [
                remote(
                    "fsdp", sibling, small.at[:, owner * share // 128], sib_c.at[k], b_send.at[1, k], b_recv.at[1, k]
                )
            ]
        raise ValueError(a)

    sib, own, got = (sib_a, sib_b, sib_c), (own_a, own_b, own_c), (got_a, got_b, got_c)
    totals = (total_a, total_b, total_c)

    def pair_sum(a, k):
        owner = (chip ^ k) * 2 + core
        for copy in to_sibling[a, k]:
            copy.wait_recv()
        if a == 1:
            mine = weights_mix[pl.ds(pl.multiple_of(owner * share, share), share), :]
            own_b[k] = (mine.astype(jnp.float32) + sib_b[k].astype(jnp.float32)).astype(low)
        else:
            for s in range(4):
                own_c[k, s] = small[s, owner * share // 128] + sib_c[k, s]
        if k:
            away[a, k] = remote(
                "fsdp", (chip ^ k) * 2 + core, own[a].at[k], got[a].at[k], z_send.at[a, k], z_recv.at[a, k]
            )

    for k in order_of:
        to_sibling[1, k] = start_sibling(1, k, core ^ 1)
    queries(both)
    for k in order_of:
        pair_sum(1, k)
    grad_proj[:, group : 2 * group] = (grad_key[...] * (HEAD_DIM**-0.5)).astype(low)
    grad_proj[:, 2 * group :] = grad_value[...].astype(low)
    for s in range(4):
        lanes = slice(s * group, (s + 1) * group)
        weights[lanes, :] = transposed_times(normed[:, lanes], grad_proj[...]).astype(low)
        for k in order_of:
            owner = (chip ^ k) * 2
            to_sibling[s + 3, k] = [
                remote(
                    "fsdp", sibling, weights.at[rows_at(s, owner + (core ^ 1))], sib_a.at[k, pl.ds(s * share, share)],
                    bb_send.at[s, k], bb_recv.at[s, k],
                )
            ]
    for s in range(4):
        rows = slice(s * share, (s + 1) * share)
        for k in order_of:
            owner = (chip ^ k) * 2 + core
            to_sibling[s + 3, k][0].wait_recv()
            own_a[k, rows, :] = (
                weights[rows_at(s, owner), :].astype(jnp.float32) + sib_a[k, rows, :].astype(jnp.float32)
            ).astype(low)
            if k:
                away[s + 3, k] = remote(
                    "fsdp", owner, own_a.at[k, pl.ds(s * share, share)], got_a.at[k, pl.ds(s * share, share)],
                    z_send.at[s + 3, k], z_recv.at[s + 3, k],
                )
    for j in range(4):
        own_rows = slice(j * tokens, (j + 1) * tokens)
        for n in range(width // TILE):
            lanes = slice(n * TILE, (n + 1) * TILE)
            back = times_transposed(grad_proj[own_rows, :], heads[lanes, :])
            gain_sum[:, lanes] += jnp.sum(back * normed[own_rows, lanes].astype(jnp.float32), axis=0, keepdims=True)
            part[j, :, lanes] = back.astype(low)
    summed = {}
    for side, (near, rest) in enumerate(((one, two), (two, one))):
        rows = pl.ds(side * half, half)
        for order, to in enumerate((both, near)):
            summed[side, order] = remote(
                "seq", near, part.at[to, rows], first.at[side, order], c_send.at[side, order], c_recv.at[side, order]
            )
    for b in range(width // 128):
        small[b // 2, b % 2, gain_row : gain_row + 1, :] = gain_sum[:, b * 128 : (b + 1) * 128]
    for k in order_of:
        to_sibling[2, k] = start_sibling(2, k, core ^ 1)
    for k in order_of:
        pair_sum(2, k)
    for side, rest in enumerate((two, one)):
        rows = slice(side * half, (side + 1) * half)
        summed[side, 0].wait_recv()
        first[side, 0] = (first[side, 0].astype(jnp.float32) + part[rest, rows, :].astype(jnp.float32)).astype(low)
        summed[side, 2] = remote("seq", rest, first.at[side, 0], second.at[side], c_send.at[2, side], c_recv.at[2, side])
    stored = []
    for side in range(2):
        rows = slice(side * half, (side + 1) * half)
        summed[side, 1].wait_recv()
        summed[side, 2].wait_recv()
        incoming = (
            part[me, rows, :].astype(jnp.float32)
            + first[side, 1].astype(jnp.float32)
            + second[side].astype(jnp.float32)
        )
        value = hid[rows, :].astype(jnp.float32)
        scale = lax.rsqrt(jnp.mean(value * value, axis=-1, keepdims=True) + EPS)
        shrunk = value * scale
        scaled = incoming * gains[0:1, :]
        grad_middle[rows, :] += scale * (scaled - shrunk * jnp.mean(scaled * shrunk, axis=-1, keepdims=True))
        stored.append(
            local(grad_middle.at[pl.ds(side * half, half)], input_out.at[pl.ds(side * half, half)], keep.at[side])
        )
    for a in (1, 0, 2):
        if a == 0:
            for s in range(4):
                rows = slice(s * share, (s + 1) * share)
                total = own_a[0, rows, :].astype(jnp.float32)
                for k in range(1, chips):
                    away[s + 3, k].wait_recv()
                    total = total + got_a[k, rows, :].astype(jnp.float32)
                total_a[s] = total.astype(low)
        else:
            total = own[a][0].astype(jnp.float32)
            for k in range(1, chips):
                away[a, k].wait_recv()
                total = total + got[a][k].astype(jnp.float32)
            totals[a][...] = total
    crossed = []
    for p in range(3):
        lanes = pl.ds(p * group, group)
        target = heads_out.at[:, pl.ds(pl.multiple_of((p * 4 + me) * group, group), group)]
        for i, peer in enumerate(others):
            crossed.append(
                remote("seq", peer, total_a.at[peer, :, lanes], target, w_send.at[p, i], w_recv.at[p, i])
            )
        stored.append(local(total_a.at[me, :, lanes], target, load.at[18 + p]))
    for i, peer in enumerate(others):
        crossed.append(remote("seq", peer, total_c.at[peer], small_out.at[me], x_send.at[i], x_recv.at[i]))
    stored.append(local(total_c.at[me], small_out.at[me], keep.at[3]))
    stored.append(local(total_b, mix_out, keep.at[2]))
    for copy in (*stored, *crossed, output_kept):
        copy.wait()
    for copy in (*summed.values(), *away.values(), *direct.values()):
        copy.wait_send()
    for copies in to_sibling.values():
        for copy in copies:
            copy.wait_send()


def back(
    ret, hit, middle, logits, normed_two, out_grad, route, gains, hidden,
    proj, attended, sums, normed, heads, mix, ids, lengths, count, experts_all, number,
):
    S, dma, f32, low = jax.ShapeDtypeStruct, pltpu.SemaphoreType.DMA, jnp.float32, jnp.bfloat16
    tokens, width = out_grad.shape
    group = attended.shape[1]
    chips = count // 2
    full = 4 * tokens
    share = width // (4 * count)
    local_heads = group // HEAD_DIM
    kinds = -(-(experts_all + 2) // 8) * 8

    def vmem(*shape, dtype=low):
        return pltpu.VMEM(shape, dtype)

    sets = [
        vmem(chips, 4 * share, 3 * group),
        vmem(chips, share, width),
        vmem(chips, 4, kinds, 128, dtype=f32),
    ]
    return pl.pallas_call(
        functools.partial(back_kernel, count, experts_all),
        out_shape=(
            S((tokens, width), low),
            S((tokens, width), f32),
            S((share, 12 * group), low),
            S((share, width), f32),
            S((4, kinds, 128), f32),
        ),
        in_specs=[ANY] * 15 + [pl.BlockSpec(memory_space=pltpu.VMEM), pl.BlockSpec(memory_space=pltpu.SMEM)],
        out_specs=(ANY,) * 5,
        scratch_shapes=[
            vmem(*ret.shape),
            vmem(*hit.shape),
            vmem(tokens, width, dtype=f32),
            vmem(*logits.shape, dtype=f32),
            vmem(tokens, width),
            vmem(tokens, width),
            vmem(*route.shape),
            vmem(*gains.shape, dtype=f32),
            vmem(tokens, width),
            vmem(tokens, width),
            vmem(tokens, width, dtype=f32),
            vmem(tokens, width),
            vmem(*logits.shape),
            vmem(1, width, dtype=f32),
            vmem(full, width),
            vmem(*proj.shape),
            vmem(*attended.shape),
            vmem(*sums.shape, dtype=f32),
            vmem(*normed.shape),
            vmem(*heads.shape),
            vmem(group, width),
            vmem(4, group // 128, kinds, 128, dtype=f32),
            vmem(tokens, group),
            vmem(8, tokens, dtype=f32),
            vmem(local_heads * tokens, group),
            vmem(local_heads * tokens, group),
            vmem(4 * local_heads, tokens, group),
            vmem(4 * local_heads, tokens, group),
            vmem(tokens, local_heads * tokens),
            vmem(tokens, local_heads * tokens),
            vmem(tokens, group, dtype=f32),
            vmem(full, group, dtype=f32),
            vmem(full, group, dtype=f32),
            vmem(full, 3 * group),
            vmem(4, tokens, width),
            vmem(width, 3 * group),
            vmem(group, width),
            vmem(1, width, dtype=f32),
            *sets,
            *sets,
            *sets,
            vmem(4, share, 3 * group),
            vmem(share, width, dtype=f32),
            vmem(4, kinds, 128, dtype=f32),
            vmem(2, 2, tokens // 2, width),
            vmem(2, tokens // 2, width),
            dma((3, 2)), dma((3, 2)),
            dma((2, chips)), dma((2, chips)), dma((4, chips)), dma((4, chips)),
            dma((7, chips)), dma((7, chips)),
            dma((3,)), dma((3,)), dma((3, 3)), dma((3, 3)), dma((3, 2)), dma((3, 2)), dma((21,)), dma((5,)),
        ],
        compiler_params=pltpu.CompilerParams(
            collective_id=number, has_side_effects=True, vmem_limit_bytes=60 * 2**20
        ),
    )(
        ret, hit, middle, logits, normed_two, out_grad, route, gains, hidden,
        proj, attended, sums, normed, heads, mix, ids, lengths,
    )


def shards(
    hidden,
    lengths,
    expert_ids,
    attn_gain,
    qkv_weight,
    out_weight,
    moe_gain,
    router_weight,
    expert_in,
    expert_out,
    out_grad,
):
    S = jax.ShapeDtypeStruct
    low = jnp.bfloat16
    owners = lax.axis_size("fsdp")
    seq_count = lax.axis_size("seq")
    tokens, width = hidden.shape[1], hidden.shape[2]
    full_len = tokens * seq_count
    group_width = width // seq_count
    experts_all = router_weight.shape[1]
    expert_local = expert_in.shape[0]
    capacity = -(-max(2, 2 * tokens // experts_all) // 16) * 16
    slots = experts_all * capacity

    chosen = expert_ids[0, :, 0]

    def to_owners(rows, number):
        return exchange(
            "fsdp",
            owners,
            (rows.reshape(owners, expert_local, capacity, width),),
            (S((expert_local, owners, capacity, width), low),),
            ((lead, second),),
            number,
        )[0].reshape(expert_local, owners * capacity, width)

    def to_sources(rows, number):
        return exchange(
            "fsdp",
            owners,
            (rows.reshape(expert_local, owners, capacity, width),),
            (S((owners, expert_local, capacity, width), low),),
            ((second, lead),),
            number,
        )[0].reshape(slots, width)

    chips = owners // 2
    fused = 4 * owners * capacity <= 1024
    (
        normed,
        weight_qkv,
        mix_rows,
        small,
        gains,
        up_all,
        projected,
        attended,
        totals,
        middle,
        normed_two,
        logits,
        sent,
        dispatch,
    ) = front(
        hidden[0],
        qkv_weight,
        out_weight,
        out_grad[0],
        router_weight.T,
        attn_gain[None],
        moe_gain[None],
        expert_ids[0].T,
        lengths,
        owners,
        capacity,
        SPREAD_FIRST if fused else chips,
        0,
    )
    weight_qkv = weight_qkv.reshape(width, 3 * group_width)
    mix_rows = mix_rows.reshape(group_width, width)
    if not fused:
        up_all = up_all.reshape(expert_local, chips, seq_count, 2 * capacity, width)
        chip, bit = lax.axis_index("fsdp") // 2, 1
        while bit < chips:
            pairs = up_all.reshape(expert_local, chips // (2 * bit), 2, bit, seq_count, 2 * capacity, width)
            up_all = jnp.where((chip // bit) % 2 == 1, pairs[:, :, ::-1], pairs)
            bit *= 2
        up_all = up_all.reshape(expert_local, chips, seq_count, 2 * capacity, width)
        up_all = up_all.transpose(0, 2, 1, 3, 4)
    if fused:
        returned, *expert_grads = moe(
            sent,
            up_all,
            small,
            expert_in,
            expert_out,
            experts_all,
            5,
        )
        returned = returned.reshape(2, slots, width)
    else:
        choose = chosen[:, None] == jnp.arange(experts_all, dtype=jnp.int32)[None, :]
        weights = jax.nn.softmax(logits[:, :experts_all], axis=-1)
        gate = jnp.sum(jnp.where(choose, weights, 0.0), axis=-1)
        gate_rows = jnp.sum(jnp.where(dispatch > 0, gate[None, :], 0.0), axis=1)
        gates = lax.all_to_all(
            gate_rows.reshape(owners, expert_local, capacity), "fsdp", split_axis=0, concat_axis=0, tiled=True
        )
        gates = lax.all_gather(gates, "seq", axis=0)
        gates = gates.transpose(2, 0, 1, 3).reshape(expert_local, seq_count * owners * capacity, 1)

        rows_all = spread(to_owners(sent, 5), 6)
        count = seq_count * owners * capacity
        rows_all = rows_all.reshape(expert_local, count, width)
        up_all = up_all.reshape(expert_local, count, width)
        grad_rows = (up_all.astype(jnp.float32) * gates).astype(low)

        def per_expert(form, left, right):
            return jnp.einsum(form, left, right, preferred_element_type=jnp.float32)

        inner = per_expert("jrd,jdf->jrf", rows_all, expert_in)
        active, active_back = jax.vjp(gelu_tanh, inner)
        active = active.astype(low)
        partial_out = per_expert("jrf,jfd->jrd", active, expert_out).astype(low)
        grad_active = per_expert("jrd,jfd->jrf", grad_rows, expert_out)
        grad_inner = active_back(grad_active)[0].astype(low)
        partial_back = per_expert("jrf,jdf->jrd", grad_inner, expert_in).astype(low)
        expert_out_grad = per_expert("jrf,jrd->jfd", active, grad_rows)
        expert_in_grad = per_expert("jrd,jrf->jdf", rows_all, grad_inner)

        shape = (expert_local, seq_count, owners * capacity, width)
        returned = to_sources(collect(partial_out.reshape(shape), 7), 8)
        grad_back = to_sources(collect(partial_back.reshape(shape), 9), 10)
        returned, expert_grads = jnp.stack([returned, grad_back]), ()
    output, grad_inputs, qkv_sum, mix_grad, small_sum = back(
        returned,
        dispatch,
        middle,
        logits,
        normed_two,
        out_grad[0],
        small,
        gains,
        hidden[0],
        projected,
        attended,
        totals,
        normed,
        weight_qkv,
        mix_rows,
        expert_ids[0].T,
        lengths,
        owners,
        experts_all,
        12,
    )
    output, grad_inputs, qkv_grad, mix_grad, route_grad, gain_one_grad, gain_two_grad, *wide = finish(
        output, grad_inputs, qkv_sum, mix_grad, small_sum, attn_gain[None], experts_all, expert_grads
    )
    if fused:
        expert_in_grad, expert_out_grad = wide
    return (
        output[None],
        grad_inputs[None],
        gain_one_grad[0],
        qkv_grad,
        mix_grad,
        gain_two_grad[0],
        route_grad.T,
        expert_in_grad,
        expert_out_grad,
    )


def solution(mesh):
    placed = (
        P("fsdp", "seq", None),
        P("fsdp"),
        P("fsdp", "seq", None),
        P(("seq", "fsdp")),
        P(("seq", "fsdp"), None),
        P(("seq", "fsdp"), None),
        P(("seq", "fsdp")),
        P(("seq", "fsdp"), None),
        P("fsdp", None, "seq"),
        P("fsdp", "seq", None),
        P("fsdp", "seq", None),
    )
    return jax.shard_map(
        shards,
        mesh=mesh,
        in_specs=placed,
        out_specs=(
            P("fsdp", "seq", None),
            P("fsdp", "seq", None),
            P(("seq", "fsdp")),
            P(("seq", "fsdp"), None),
            P(("seq", "fsdp"), None),
            P(("seq", "fsdp")),
            P(("seq", "fsdp"), None),
            P("fsdp", None, "seq"),
            P("fsdp", "seq", None),
        ),
        check_vma=False,
    )
```

```python
import functools

import jax
import jax.numpy as jnp
from jax import lax
from jax.experimental import pallas as pl
from jax.experimental.pallas import tpu as pltpu
from jax.sharding import PartitionSpec as P

HEAD_DIM = 64
EPS = 1e-05
MASKED = -1e30
ROOT = 0.7978845608028654
TILE = 256
SPREAD_FIRST = 3
TURN = (1, 3, 2, 0)
GRAD = 256
MESH = pl.DeviceIdType.MESH
ANY = pl.BlockSpec(memory_space=pl.ANY)


def scaled_norm(value, gain):
    return value * lax.rsqrt(jnp.mean(value * value, axis=-1, keepdims=True) + EPS) * gain


def gelu_tanh(value):
    return jax.nn.gelu(value, approximate=True)


def times(left, right):
    return jnp.dot(left, right, preferred_element_type=jnp.float32)


def times_transposed(left, right):
    return lax.dot_general(
        left, right, (((1,), (1,)), ((), ())), preferred_element_type=jnp.float32
    )


def transposed_times(left, right):
    return lax.dot_general(
        left, right, (((0,), (0,)), ((), ())), preferred_element_type=jnp.float32
    )


def greet(axis, peers):
    barrier = pltpu.get_barrier_semaphore()
    for peer in peers:
        pl.semaphore_signal(barrier, inc=1, device_id={axis: peer}, device_id_type=MESH)
    pl.semaphore_wait(barrier, len(peers))


def remote(axis, peer, source, target, send, receive):
    copy = pltpu.make_async_remote_copy(
        source, target, send, receive, device_id={axis: peer}, device_id_type=MESH
    )
    copy.start()
    return copy


def call(kernel, inputs, outputs, scratch, number):
    return pl.pallas_call(
        kernel,
        out_shape=outputs,
        in_specs=[ANY] * len(inputs),
        out_specs=jax.tree.map(lambda _: ANY, outputs),
        scratch_shapes=scratch,
        compiler_params=pltpu.CompilerParams(
            collective_id=number, has_side_effects=True, vmem_limit_bytes=60 * 2**20
        ),
    )(*inputs)


def exchange_kernel(axis, count, views, *refs):
    arrays = len(views)
    sources, targets = refs[:arrays], refs[arrays : 2 * arrays]
    send, receive, local = refs[2 * arrays :]
    me = lax.axis_index(axis)
    peers = [lax.rem(me + step, count) for step in range(1, count)]
    greet(axis, peers)
    copies = []
    for step, peer in enumerate(peers):
        for a, (out_of, into) in enumerate(views):
            copies.append(
                remote(
                    axis,
                    peer,
                    out_of(sources[a], peer),
                    into(targets[a], me),
                    send.at[a, step],
                    receive.at[a, step],
                )
            )
    for a, (out_of, into) in enumerate(views):
        copy = pltpu.make_async_copy(out_of(sources[a], me), into(targets[a], me), local.at[a])
        copy.start()
        copies.append(copy)
    for copy in copies:
        copy.wait()


def exchange(axis, count, inputs, outputs, views, number):
    arrays = len(views)
    return call(
        functools.partial(exchange_kernel, axis, count, views),
        inputs,
        outputs,
        [
            pltpu.SemaphoreType.DMA((arrays, count - 1)),
            pltpu.SemaphoreType.DMA((arrays, count - 1)),
            pltpu.SemaphoreType.DMA((arrays,)),
        ],
        number,
    )


def lead(ref, place):
    return ref.at[place]


def second(ref, place):
    return ref.at[:, place]


def whole(ref, place):
    return ref


def spread_kernel(source, target, send, receive, local):
    me = lax.axis_index("seq")
    one, two, both = me ^ 1, me ^ 2, me ^ 3
    half = source.shape[1] // 2
    greet("seq", [one, two])
    parts = (pl.ds(0, half), pl.ds(half, half))
    own = pltpu.make_async_copy(source, target.at[:, me], local)
    own.start()
    copies = {}
    for side, peer in enumerate((one, two)):
        for order in range(2):
            part = (order + side) % 2
            copies[side, part] = remote(
                "seq",
                peer,
                source.at[:, parts[part]],
                target.at[:, me, parts[part]],
                send.at[side, part],
                receive.at[side, part],
            )
    relayed = []
    for side, (origin, peer) in enumerate(((one, two), (two, one))):
        copies[side, side].wait_recv()
        block = target.at[:, origin, parts[side]]
        relayed.append(remote("seq", peer, block, block, send.at[2, side], receive.at[2, side]))
    for side in range(2):
        copies[side, 1 - side].wait_recv()
        for part in range(2):
            copies[side, part].wait_send()
    for copy in relayed:
        copy.wait()
    own.wait()


def spread(source, number):
    return call(
        spread_kernel,
        (source,),
        jax.ShapeDtypeStruct((source.shape[0], 4, *source.shape[1:]), source.dtype),
        [
            pltpu.SemaphoreType.DMA((3, 2)),
            pltpu.SemaphoreType.DMA((3, 2)),
            pltpu.SemaphoreType.DMA,
        ],
        number,
    )


def collect_kernel(source, target, mine, first, second_in, outgoing, load, send, receive, store):
    me = lax.axis_index("seq")
    one, two, both = me ^ 1, me ^ 2, me ^ 3
    width = source.shape[3] // 2
    greet("seq", [one, two])
    copies = []
    for side, (near, rest) in enumerate(((one, two), (two, one))):
        lanes = pl.ds(side * width, width)
        for order, block in enumerate((both, near)):
            copies.append(
                remote(
                    "seq",
                    near,
                    source.at[:, block, :, lanes],
                    first.at[side, order],
                    send.at[side, order],
                    receive.at[side, order],
                )
            )
        for order, block in enumerate((rest, me)):
            pltpu.make_async_copy(
                source.at[:, block, :, lanes], mine.at[side, order], load.at[side, order]
            ).start()
    passed = []
    for side, rest in enumerate((two, one)):
        copies[side * 2].wait_recv()
        pltpu.make_async_copy(mine.at[side, 0], mine.at[side, 0], load.at[side, 0]).wait()
        outgoing[side] = (
            mine[side, 0].astype(jnp.float32) + first[side, 0].astype(jnp.float32)
        ).astype(outgoing.dtype)
        passed.append(
            remote("seq", rest, outgoing.at[side], second_in.at[side], send.at[2, side], receive.at[2, side])
        )
    for side in range(2):
        copies[side * 2 + 1].wait_recv()
        pltpu.make_async_copy(mine.at[side, 1], mine.at[side, 1], load.at[side, 1]).wait()
        passed[side].wait_recv()
        mine[side, 1] = (
            mine[side, 1].astype(jnp.float32)
            + first[side, 1].astype(jnp.float32)
            + second_in[side].astype(jnp.float32)
        ).astype(mine.dtype)
        out = pltpu.make_async_copy(
            mine.at[side, 1], target.at[:, :, pl.ds(side * width, width)], store.at[side]
        )
        out.start()
    for side in range(2):
        pltpu.make_async_copy(
            mine.at[side, 1], target.at[:, :, pl.ds(side * width, width)], store.at[side]
        ).wait()
    for copy in copies + passed:
        copy.wait_send()


def collect(source, number):
    a, _, rows, width = source.shape
    dma = pltpu.SemaphoreType.DMA
    block = (a, rows, width // 2)
    return call(
        collect_kernel,
        (source,),
        jax.ShapeDtypeStruct((a, rows, width), source.dtype),
        [
            pltpu.VMEM((2, 2, *block), source.dtype),
            pltpu.VMEM((2, 2, *block), source.dtype),
            pltpu.VMEM((2, *block), source.dtype),
            pltpu.VMEM((2, *block), source.dtype),
            dma((2, 2)),
            dma((3, 2)),
            dma((3, 2)),
            dma((2,)),
        ],
        number,
    )


def moe_kernel(
    chips, cap, experts_all, spread_first, send_rows, up_rows, route, w_in, w_out,
    ret, dw_in, dw_out,
    R, U, G, A, I, PB, first, second, W1, W2, RT, stage,
    load, own, z_send, z_recv, s_send, s_recv, y_send, y_recv,
    c_send, c_recv, d_send, d_recv, r_send, r_recv, store,
):
    me, place = lax.axis_index("seq"), lax.axis_index("fsdp")
    one, two, both = me ^ 1, me ^ 2, me ^ 3
    chip, core = place // 2, lax.rem(place, 2)
    sibling = place ^ 1
    count = chips * 2
    part = 2 * cap
    chunk = 4 * part
    barrier = pltpu.get_barrier_semaphore()
    for peer in (one, two):
        pl.semaphore_signal(barrier, inc=1, device_id={"seq": peer}, device_id_type=MESH)
    for step in range(1, count):
        pl.semaphore_signal(
            barrier, inc=1, device_id={"fsdp": lax.rem(place + step, count)}, device_id_type=MESH
        )
    pl.semaphore_wait(barrier, 2 + count - 1)

    def rows_of(k, s):
        return pl.ds(k * chunk + s * part, part)

    loads = []

    def local(source, target, sem):
        copy = pltpu.make_async_copy(source, target, sem)
        copy.start()
        return copy

    dispatched = {}
    own_rows = []

    def dispatch(k):
        target = R.at[:, pl.ds(k * chunk + me * part + core * cap, cap)]
        if k == 0:
            own_rows.append(local(send_rows.at[place], target, own.at[0]))
        for c in range(2):
            if k or c:
                peer = (chip ^ k) * 2 + (core ^ c)
                dispatched[k, c] = remote(
                    "fsdp", peer, send_rows.at[peer], target, z_send.at[k, c], z_recv.at[k, c]
                )

    def z_arrived(k):
        if k == 0:
            own_rows[0].wait()
        for c in range(2):
            if k or c:
                dispatched[k, c].wait_recv()

    sent = {}

    def spread_out(a, k):
        for side, peer in enumerate((one, two)):
            for order in range(2):
                j = (order + side) % 2
                target = (U, R)[a].at[j, rows_of(k, me)]
                source = target if a else up_rows.at[j, rows_of(k, me)]
                sent[a, k, side, j] = remote(
                    "seq", peer, source, target, s_send.at[a, k, side, j], s_recv.at[a, k, side, j]
                )

    def relay(a, k):
        for side, (origin, peer) in enumerate(((one, two), (two, one))):
            sent[a, k, side, side].wait_recv()
            block = (U, R)[a].at[side, rows_of(k, origin)]
            sent[a, k, 2, side] = remote("seq", peer, block, block, y_send.at[a, k, side], y_recv.at[a, k, side])

    def all_arrived(a, k):
        for side in range(2):
            sent[a, k, side, 1 - side].wait_recv()
            sent[a, k, 2, side].wait_recv()

    def experts(k, j):
        rows = pl.ds(k * chunk, chunk)
        logits = times(R[j, rows, :], RT[...])
        lane = lax.broadcasted_iota(jnp.int32, logits.shape, 1)
        logits = jnp.where(lane < experts_all, logits, MASKED)
        powers = jnp.exp(logits - jnp.max(logits, axis=1, keepdims=True))
        picked = jnp.sum(jnp.where(lane == place * 2 + j, powers, 0.0), axis=1, keepdims=True)
        gate = picked / jnp.sum(powers, axis=1, keepdims=True)
        G[j, rows, :] = (U[j, rows, :].astype(jnp.float32) * gate).astype(G.dtype)

        @pl.loop(0, W1.shape[2] // TILE)
        def _(t):
            cols = pl.ds(pl.multiple_of(t * TILE, TILE), TILE)
            v = times(R[j, rows, :], W1[j, :, cols])
            grad = times_transposed(G[j, rows, :], W2[j, cols, :])
            square = v * v
            t = jnp.tanh(ROOT * v * (1.0 + 0.044715 * square))
            half = 0.5 * (1.0 + t)
            A[j, rows, cols] = (v * half).astype(A.dtype)
            slope = half + 0.5 * v * (1.0 - t * t) * (ROOT * (1.0 + 0.134145 * square))
            I[j, rows, cols] = (grad * slope).astype(I.dtype)

        @pl.loop(0, W1.shape[1] // TILE)
        def _(t):
            cols = pl.ds(pl.multiple_of(t * TILE, TILE), TILE)
            PB[0, j, rows, cols] = times(A[j, rows, :], W2[j, :, cols]).astype(PB.dtype)
            PB[1, j, rows, cols] = times_transposed(I[j, rows, :], W1[j, cols, :]).astype(PB.dtype)

    summed = {}

    def near_of(j):
        return (one, two) if j == 0 else (two, one)

    def collect_one(k, j):
        near, rest = near_of(j)
        for a in range(2):
            for order, block in enumerate((both, near)):
                summed[a, k, j, order] = remote(
                    "seq", near, PB.at[a, j, rows_of(k, block)], first.at[a, j, k, order],
                    c_send.at[a, j, k, order], c_recv.at[a, j, k, order],
                )

    def collect_two(k, j):
        near, rest = near_of(j)
        for a in range(2):
            summed[a, k, j, 0].wait_recv()
            first[a, j, k, 0] = (
                first[a, j, k, 0].astype(jnp.float32) + PB[a, j, rows_of(k, rest), :].astype(jnp.float32)
            ).astype(first.dtype)
            summed[a, k, j, 2] = remote(
                "seq", rest, first.at[a, j, k, 0], second.at[a, j, k], d_send.at[a, j, k], d_recv.at[a, j, k]
            )

    returns = {}

    def collect_three(k, j):
        for a in range(2):
            summed[a, k, j, 1].wait_recv()
            summed[a, k, j, 2].wait_recv()
            first[a, j, k, 1] = (
                first[a, j, k, 1].astype(jnp.float32)
                + PB[a, j, rows_of(k, me), :].astype(jnp.float32)
                + second[a, j, k].astype(jnp.float32)
            ).astype(first.dtype)
            to = chip ^ k
            target = ret.at[a, place, j]
            for c in range(2):
                if k == 0:
                    if c == 0:
                        returns[a, k, j, 0] = local(
                            first.at[a, j, k, 1, pl.ds(core * cap, cap)], target, own.at[1 + a * 2 + j]
                        )
                        returns[a, k, j, 1] = remote(
                            "fsdp", sibling, first.at[a, j, k, 1, pl.ds((core ^ 1) * cap, cap)], target,
                            r_send.at[a, j, k, 1], r_recv.at[a, j, k, 1],
                        )
                    continue
                returns[a, k, j, c] = remote(
                    "fsdp", to * 2 + (core ^ c), first.at[a, j, k, 1, pl.ds((core ^ c) * cap, cap)], target,
                    r_send.at[a, j, k, c], r_recv.at[a, j, k, c],
                )

    staged = {}

    def weight_grads(j, which, tiles):
        left, right, out = ((R, I, dw_in), (A, G, dw_out))[which]
        for m in tiles:
            slot = m % 2
            lanes = slice(m * GRAD, (m + 1) * GRAD)
            if slot in staged:
                staged.pop(slot).wait()

            @pl.loop(0, right.shape[2] // TILE)
            def _(t):
                cols = pl.ds(pl.multiple_of(t * TILE, TILE), TILE)
                stage[slot, :, cols] = transposed_times(left[j, :, lanes], right[j, :, cols]).astype(stage.dtype)

            staged[slot] = local(stage.at[slot], out.at[j, lanes], store.at[slot])

    later = range(spread_first, chips)
    turn = TURN
    away = [k for k in turn if k]
    dispatch(0)
    dispatch(away[0])
    dispatch(away[1])
    for j in range(2):
        loads.append(local(w_in.at[j], W1.at[j], load.at[j]))
        loads.append(local(w_out.at[j], W2.at[j], load.at[2 + j]))
    loads.append(local(route, RT, load.at[4]))
    early = spread_first * chunk
    for j in range(2):
        loads.append(local(up_rows.at[j, pl.ds(0, early)], U.at[j, pl.ds(0, early)], load.at[5 + j]))
    for n, k in enumerate(later):
        for j in range(2):
            block = rows_of(k, me)
            loads.append(local(up_rows.at[j, block], U.at[j, block], load.at[7 + 2 * n + j]))
    if turn[0]:
        for k in later:
            spread_out(0, k)
    z_arrived(turn[0])
    spread_out(1, turn[0])
    if not turn[0]:
        for k in later:
            spread_out(0, k)
    z_arrived(turn[1])
    spread_out(1, turn[1])
    dispatch(away[2])
    relay(1, turn[0])
    for copy in loads:
        copy.wait()
    for k in later:
        relay(0, k)
    z_arrived(turn[2])
    spread_out(1, turn[2])
    for n in range(chips):
        k = turn[n]
        all_arrived(1, k)
        if k >= spread_first:
            all_arrived(0, k)
        experts(k, 0)
        collect_one(k, 0)
        if n < 2:
            relay(1, turn[n + 1 + (n > 0)])
        if n == 0:
            z_arrived(turn[3])
            spread_out(1, turn[3])
        else:
            collect_two(turn[n - 1], 0)
        if n > 1:
            collect_three(turn[n - 2], 0)
        experts(k, 1)
        collect_one(k, 1)
        if n == 0:
            relay(1, turn[2])
        else:
            collect_two(turn[n - 1], 1)
        if n > 1:
            collect_three(turn[n - 2], 1)
    weight_grads(0, 0, range(4))
    collect_two(turn[3], 0)
    collect_three(turn[2], 0)
    collect_two(turn[3], 1)
    collect_three(turn[2], 1)
    weight_grads(0, 1, range(4))
    weight_grads(1, 0, range(2))
    collect_three(turn[3], 0)
    weight_grads(1, 0, range(2, 4))
    collect_three(turn[3], 1)
    weight_grads(1, 1, range(4))
    for copy in staged.values():
        copy.wait()
    for copy in dispatched.values():
        copy.wait_send()
    for copy in sent.values():
        copy.wait_send()
    for copy in summed.values():
        copy.wait_send()
    for (a, k, j, c), copy in returns.items():
        copy.wait()


def moe(send_rows, up_rows, route, w_in, w_out, experts_all, number):
    S, low, dma = jax.ShapeDtypeStruct, jnp.bfloat16, pltpu.SemaphoreType.DMA
    owners, _, cap, width = send_rows.shape
    chips = owners // 2
    hidden_units = w_in.shape[2]
    count = owners * cap * 4
    part = 2 * cap

    def vmem(*shape, dtype=low):
        return pltpu.VMEM(shape, dtype)

    return pl.pallas_call(
        functools.partial(moe_kernel, chips, cap, experts_all, SPREAD_FIRST),
        out_shape=(
            S((2, owners, 2, cap, width), low),
            S(w_in.shape, low),
            S(w_out.shape, low),
        ),
        in_specs=[ANY] * 5,
        out_specs=(ANY,) * 3,
        scratch_shapes=[
            vmem(2, count, width),
            vmem(2, count, width),
            vmem(2, count, width),
            vmem(2, count, hidden_units),
            vmem(2, count, hidden_units),
            vmem(2, 2, count, width),
            vmem(2, 2, chips, 2, part, width),
            vmem(2, 2, chips, part, width),
            vmem(*w_in.shape),
            vmem(*w_out.shape),
            vmem(*route.shape),
            vmem(2, GRAD, max(width, hidden_units)),
            dma((7 + 2 * (chips - SPREAD_FIRST),)),
            dma((5,)),
            dma((chips, 2)),
            dma((chips, 2)),
            dma((2, chips, 2, 2)),
            dma((2, chips, 2, 2)),
            dma((2, chips, 2)),
            dma((2, chips, 2)),
            dma((2, 2, chips, 2)),
            dma((2, 2, chips, 2)),
            dma((2, 2, chips)),
            dma((2, 2, chips)),
            dma((2, 2, chips, 2)),
            dma((2, 2, chips, 2)),
            dma((2,)),
        ],
        compiler_params=pltpu.CompilerParams(
            collective_id=number, has_side_effects=True, vmem_limit_bytes=60 * 2**20
        ),
        cost_estimate=pl.CostEstimate(
            flops=12 * 2 * count * width * hidden_units, bytes_accessed=2**25, transcendentals=0
        ),
    )(send_rows, up_rows, route, w_in, w_out)


def front_kernel(
    count, cap, experts_all, spread_here, hidden, qkv_weight, mix, out_grad, router, gain_a, gain_b, ids, length,
    normed_out, heads_out, mix_out, small_out, gains_out, up, projected_out, attended_out, sums_out,
    middle_out, low_out, logits_out, sent_out, hit_out,
    staged, hid, heads_all, small_own, small_all, gains, normed, proj, attended, sums, acc, stat,
    mix_all, up_low, rows, hit, mixed, middle, normed_low, logits, sent_rows, pile,
    h_send, h_recv, q_send, q_recv, f_send, f_recv, n_send, n_recv, u_send, u_recv, m_send, m_recv,
    s_send, s_recv, x_send, x_recv, y_send, y_recv, local,
):
    me, place = lax.axis_index("seq"), lax.axis_index("fsdp")
    one, two, both = me ^ 1, me ^ 2, me ^ 3
    others = (one, two, both)
    chips = count // 2
    chip, core = place // 2, lax.rem(place, 2)
    sibling = place ^ 1
    share = mix.shape[0]
    tokens = hidden.shape[0]
    group = attended.shape[1]
    part, chunk = 2 * cap, 8 * cap
    barrier = pltpu.get_barrier_semaphore()
    for peer in others:
        pl.semaphore_signal(barrier, inc=1, device_id={"seq": peer}, device_id_type=MESH)
    for step in range(1, count):
        pl.semaphore_signal(
            barrier, inc=1, device_id={"fsdp": lax.rem(place + step, count)}, device_id_type=MESH
        )
    pl.semaphore_wait(barrier, 3 + count - 1)

    def keep(source, target, number):
        copy = pltpu.make_async_copy(source, target, local.at[number])
        copy.start()
        return copy

    def far(k):
        return (chip ^ k) * 2 + core

    away, near = {}, {}

    def block(a, owner):
        if a == 0:
            return mix_all.at[me, owner // 2, core]
        if a == 1:
            return small_all.at[pl.ds(pl.multiple_of((me * count + owner) * share, share), share)]
        return heads_all.at[:, owner]

    own_of = (mix, small_own, staged)

    def send_far(a):
        for k in range(1, chips):
            away[a, k] = remote("fsdp", far(k), own_of[a], block(a, place), f_send.at[a, k], f_recv.at[a, k])

    def send_near(a):
        near[a, 0] = remote("fsdp", sibling, own_of[a], block(a, place), n_send.at[a, 0], n_recv.at[a, 0])

    def pass_on(a):
        for k in range(1, chips):
            away[a, k].wait_recv()
            arrived = block(a, far(k))
            near[a, k] = remote("fsdp", sibling, arrived, arrived, n_send.at[a, k], n_recv.at[a, k])

    direct = {}

    def both_ways(name, views, sources, send, receive):
        for side, peer in enumerate((one, two)):
            for order in range(2):
                p = (order + side) % 2
                direct[name, side, p] = remote(
                    "seq", peer, sources[p], views[p](me), send.at[side, p], receive.at[side, p]
                )

    def relay(name, views, send, receive):
        for side, (origin, peer) in enumerate(((one, two), (two, one))):
            direct[name, side, side].wait_recv()
            source = views[side](origin)
            direct[name, 2, side] = remote("seq", peer, source, source, send.at[2, side], receive.at[2, side])

    def arrived(name):
        for side in range(2):
            direct[name, side, 1 - side].wait_recv()
            direct[name, 2, side].wait_recv()

    moved = {}

    def send_rows(k):
        for c in range(2):
            if k == 0 and c == 0:
                continue
            peer = (chip ^ k) * 2 + (core ^ c)
            moved[k, c] = remote(
                "fsdp", peer, rows.at[peer], up.at[:, pl.ds(k * chunk + me * part + core * cap, cap)],
                u_send.at[k, c], u_recv.at[k, c],
            )

    columns = [
        (pl.ds(p * group, group), lambda to, p=p: pl.ds(pl.multiple_of((p * 4 + to) * group, group), group))
        for p in range(3)
    ]
    exchanged = [
        remote(
            "seq", peer, qkv_weight.at[:, view(peer)], staged.at[me, :, into], q_send.at[i, p], q_recv.at[i, p]
        )
        for i, peer in enumerate(others)
        for p, (into, view) in enumerate(columns)
    ]
    half = tokens // 2
    hidden_views = [
        lambda origin, p=p: hid.at[pl.ds(origin * tokens + p * half, half)] for p in range(2)
    ]
    both_ways("hidden", hidden_views, [hidden.at[pl.ds(p * half, half)] for p in range(2)], h_send, h_recv)
    send_far(0)
    own_heads = [
        keep(qkv_weight.at[:, view(me)], staged.at[me, :, into], 14 + p) for p, (into, view) in enumerate(columns)
    ]
    own_hidden = keep(hidden, hid.at[pl.ds(me * tokens, tokens)], 1)
    own_mix = keep(mix, block(0, place), 2)
    own_grad = keep(out_grad, up_low, 13)
    pile[...] = jnp.zeros_like(pile)
    pile[:experts_all, :share] = router[...].astype(jnp.float32)
    for n, gain in enumerate((gain_a, gain_b)):
        pile[experts_all + n : experts_all + n + 1, :share] = gain[...].astype(jnp.float32)
    small_own[...] = jnp.transpose(pile[...])[:share].astype(small_own.dtype)
    send_far(1)
    send_near(1)
    own_small = keep(small_own, block(1, place), 3)
    across = ids[...].astype(jnp.float32)
    chosen = jnp.transpose(jnp.broadcast_to(across, (128, tokens)))[:, :1]
    first = lax.broadcasted_iota(jnp.int32, (tokens, tokens), 0)
    second = lax.broadcasted_iota(jnp.int32, (tokens, tokens), 1)
    ranks = jnp.sum(jnp.where((chosen == across) & (first < second), 1.0, 0.0), axis=0, keepdims=True)
    slot = (across * cap + ranks).astype(jnp.int32)
    hit[...] = jnp.where(lax.broadcasted_iota(jnp.int32, hit.shape, 0) == slot, 1.0, 0.0).astype(hit.dtype)
    own_grad.wait()
    position = me * tokens + lax.broadcasted_iota(jnp.int32, (tokens, 1), 0)
    up_low[...] = jnp.where(position < length[0], up_low[...].astype(jnp.float32), 0.0).astype(up_low.dtype)

    def to_slots(values, target):
        @pl.loop(0, count)
        def _(owner):
            picked = hit[pl.ds(pl.multiple_of(owner * 2 * cap, 2 * cap), 2 * cap), :]
            target[owner] = times(picked, values[...]).astype(target.dtype).reshape(target.shape[1:])

    to_slots(up_low, rows)
    own_rows = keep(rows.at[place], up.at[:, pl.ds(me * part + core * cap, cap)], 4)
    send_rows(0)
    hit_kept = keep(hit, hit_out, 0)
    pass_on(1)
    for copy in own_heads:
        copy.wait()
    for copy in exchanged:
        copy.wait_recv()
    own_block = keep(staged, heads_all.at[:, place], 5)
    send_far(2)
    send_near(2)
    own_small.wait()
    for k in range(chips):
        near[1, k].wait_recv()
    mine = small_all.at[pl.ds(pl.multiple_of(me * count * share, share), count * share)]
    smalls = [remote("seq", peer, mine, mine, q_send.at[3, i], q_recv.at[3, i]) for i, peer in enumerate(others)]

    def up_views(k):
        return [lambda origin, j=j: up.at[j, pl.ds(k * chunk + origin * part, part)] for j in range(2)]

    def up_out(k):
        if k == 0:
            own_rows.wait()
        for c in range(2):
            if (k, c) in moved:
                moved[k, c].wait_recv()
        if k < spread_here:
            views = up_views(k)
            both_ways(("up", k), views, [views[0](me), views[1](me)], s_send.at[k], s_recv.at[k])

    def up_relay(k):
        if k < spread_here:
            relay(("up", k), up_views(k), s_send.at[k], s_recv.at[k])

    up_out(0)
    relay("hidden", hidden_views, h_send, h_recv)
    own_mix.wait()
    for k in range(1, chips):
        away[0, k].wait_recv()
    mix_views = [
        lambda origin, p=p: mix_all.at[origin, pl.ds(p * (chips // 2), chips // 2), core] for p in range(2)
    ]
    both_ways("mix", mix_views, [mix_views[p](me) for p in range(2)], m_send, m_recv)
    for copy in smalls:
        copy.wait_recv()
    small_kept = keep(small_all, small_out, 6)
    own_hidden.wait()
    arrived("hidden")
    turned = jnp.transpose(small_all[...].astype(jnp.float32))
    gains[0:1, :] = turned[experts_all : experts_all + 1]
    gains[1:2, :] = turned[experts_all + 1 : experts_all + 2]
    gains_kept = keep(gains, gains_out, 17)
    gain = gains[0:1, :]

    @pl.loop(0, hid.shape[0] // 128)
    def _(t):
        place_rows = pl.ds(pl.multiple_of(t * 128, 128), 128)
        value = hid[place_rows, :].astype(jnp.float32)
        scale = lax.rsqrt(jnp.mean(value * value, axis=-1, keepdims=True) + EPS)
        normed[place_rows, :] = (value * scale * gain).astype(normed.dtype)

    normed_kept = keep(normed, normed_out, 7)
    pass_on(2)
    for k in range(1, chips):
        send_rows(k)
    up_relay(0)
    relay("mix", mix_views, m_send, m_recv)
    own_block.wait()
    for k in range(chips):
        near[2, k].wait_recv()
    heads_kept = keep(heads_all, heads_out, 8)
    width = hid.shape[1]

    for p in range(3):

        @pl.loop(0, hid.shape[0] // TILE)
        def _(t):
            place_rows = pl.ds(pl.multiple_of(t * TILE, TILE), TILE)
            weights = heads_all[:, :, :, p * group : (p + 1) * group].reshape(width, group)
            proj[place_rows, p * group : (p + 1) * group] = times(normed[place_rows, :], weights).astype(proj.dtype)

    projected_kept = keep(proj, projected_out, 9)
    head_of = lax.broadcasted_iota(jnp.int32, (tokens, group), 1) // HEAD_DIM
    sent = []
    for i in range(4):
        own = slice(i * tokens, (i + 1) * tokens)
        reach = (i + 1) * tokens

        @pl.loop(0, group // HEAD_DIM)
        def _(h):
            query = jnp.where(head_of == h, proj[own, :group] * (HEAD_DIM**-0.5), 0).astype(proj.dtype)
            scores = times_transposed(query, proj[:reach, group : 2 * group])
            column = lax.broadcasted_iota(jnp.int32, scores.shape, 1)
            row = lax.broadcasted_iota(jnp.int32, scores.shape, 0) + i * tokens
            scores = jnp.where((column <= row) & (column < length[0]), scores, MASKED)
            top = jnp.max(scores, axis=1, keepdims=True)
            powers = jnp.exp(scores - top)
            total = jnp.sum(powers, axis=1, keepdims=True)
            probs = (powers * (1.0 / total)).astype(proj.dtype)
            out = times(probs, proj[:reach, 2 * group :])
            acc[...] = jnp.where(head_of == h, out, acc[...])
            lane = lax.broadcasted_iota(jnp.int32, stat.shape, 1)
            stat[...] = jnp.where(lane == h, top + jnp.log(total), stat[...])

        attended[own, :] = acc[...].astype(attended.dtype)
        sums[:, own] = jnp.transpose(stat[...])[:8]
        target = mixed.at[:, pl.ds(pl.multiple_of(me * group, group), group)]

        @pl.when(me != i)
        def _():
            remote("seq", i, attended.at[own], target, x_send.at[i], x_recv.at[me])

        @pl.when(me == i)
        def _():
            pltpu.make_async_copy(attended.at[own], target, local.at[10]).start()

        if i == 1:
            up_relay(1)
        if i == 0:
            up_out(1)
            arrived("mix")
            both_cores = [
                remote(
                    "fsdp", sibling, mix_all.at[s, :, core], mix_all.at[s, :, core], y_send.at[s], y_recv.at[s]
                )
                for s in range(4)
            ]
    up_out(2)
    attended_kept = keep(attended, attended_out, 11)
    sums_kept = keep(sums, sums_out, 12)
    for i in range(4):
        target = mixed.at[:, pl.ds(i * group, group)]

        @pl.when(me != i)
        def _():
            copy = pltpu.make_async_remote_copy(
                attended.at[pl.ds(i * tokens, tokens)], target, x_send.at[i], x_recv.at[i],
                device_id={"seq": i}, device_id_type=MESH,
            )
            copy.wait()

        @pl.when(me == i)
        def _():
            pltpu.make_async_copy(attended.at[pl.ds(i * tokens, tokens)], target, local.at[10]).wait()

    up_relay(2)
    for copy in both_cores:
        copy.wait()
    mix_kept = keep(mix_all.at[me], mix_out, 18)
    for n in range(width // TILE):
        lanes = slice(n * TILE, (n + 1) * TILE)
        total = hid[pl.ds(pl.multiple_of(me * tokens, tokens), tokens), lanes].astype(jnp.float32)
        for s in range(4):
            weights = mix_all[s, :, :, :, lanes].reshape(group, TILE)
            total = total + times(mixed[:, s * group : (s + 1) * group], weights)
        middle[:, lanes] = total
    middle_kept = keep(middle, middle_out, 19)
    for t in range(tokens // 128):
        span = slice(t * 128, (t + 1) * 128)
        value = middle[span, :]
        scale = lax.rsqrt(jnp.mean(value * value, axis=-1, keepdims=True) + EPS)
        normed_low[span, :] = (value * scale * gains[1:2, :]).astype(normed_low.dtype)
    logits[...] = times(normed_low[...], small_all[...])
    to_slots(normed_low, sent_rows)
    last = [
        keep(normed_low, low_out, 20),
        keep(logits, logits_out, 21),
        keep(sent_rows, sent_out, 22),
    ]
    for k in range(3, chips):
        up_out(k)
        up_relay(k)
    for k in range(spread_here):
        arrived(("up", k))
    for copy in (*direct.values(), *exchanged, *smalls, *away.values(), *near.values(), *moved.values()):
        copy.wait_send()
    for copy in (
        small_kept, normed_kept, heads_kept, projected_kept, attended_kept, sums_kept,
        hit_kept, gains_kept, mix_kept, middle_kept, *last,
    ):
        copy.wait()


def front(hidden, qkv_weight, mix, out_grad, router, gain_a, gain_b, ids, lengths, count, cap, spread_here, number):
    S, dma, low, f32 = jax.ShapeDtypeStruct, pltpu.SemaphoreType.DMA, jnp.bfloat16, jnp.float32
    chips = count // 2
    tokens, width = hidden.shape
    experts_all = router.shape[0]
    group = qkv_weight.shape[1] // 12
    share = qkv_weight.shape[0]
    full = 4 * tokens
    lanes = -(-(experts_all + 2) // 128) * 128
    all_heads = (4, count, share, 3 * group)
    slots = experts_all * cap

    def vmem(*shape, dtype=low):
        return pltpu.VMEM(shape, dtype)

    near = pl.BlockSpec(memory_space=pltpu.VMEM)
    return pl.pallas_call(
        functools.partial(front_kernel, count, cap, experts_all, spread_here),
        out_shape=(
            S((full, width), low),
            S(all_heads, low),
            S((chips, 2, share, width), low),
            S((width, lanes), low),
            S((8, width), f32),
            S((2, 4 * count * cap, width), low),
            S((full, 3 * group), low),
            S((full, group), low),
            S((8, full), f32),
            S((tokens, width), f32),
            S((tokens, width), low),
            S((tokens, lanes), f32),
            S((count, 2, cap, width), low),
            S((slots, tokens), low),
        ),
        in_specs=[ANY] * 4 + [near] * 4 + [pl.BlockSpec(memory_space=pltpu.SMEM)],
        out_specs=(ANY,) * 14,
        scratch_shapes=[
            vmem(4, share, 3 * group),
            vmem(full, width),
            vmem(*all_heads),
            vmem(share, lanes),
            vmem(width, lanes),
            vmem(8, width, dtype=f32),
            vmem(full, width),
            vmem(full, 3 * group),
            vmem(full, group),
            vmem(8, full, dtype=f32),
            vmem(tokens, group, dtype=f32),
            vmem(tokens, 128, dtype=f32),
            vmem(4, chips, 2, share, width),
            vmem(tokens, width),
            vmem(count, 2, cap, width),
            vmem(slots, tokens),
            vmem(tokens, width),
            vmem(tokens, width, dtype=f32),
            vmem(tokens, width),
            vmem(tokens, lanes, dtype=f32),
            vmem(count, 2, cap, width),
            vmem(lanes, 128, dtype=f32),
            dma((3, 2)), dma((3, 2)), dma((4, 3)), dma((4, 3)),
            dma((3, chips)), dma((3, chips)), dma((3, chips)), dma((3, chips)),
            dma((chips, 2)), dma((chips, 2)), dma((3, 2)), dma((3, 2)),
            dma((chips, 3, 2)), dma((chips, 3, 2)), dma((4,)), dma((4,)), dma((4,)), dma((4,)), dma((23,)),
        ],
        compiler_params=pltpu.CompilerParams(
            collective_id=number, has_side_effects=True, vmem_limit_bytes=60 * 2**20
        ),
    )(hidden, qkv_weight, mix, out_grad, router, gain_a, gain_b, ids, lengths)


def finish_kernel(
    experts_all, experts, output, input_grad, heads, mix, small, gain, *refs
):
    wide, refs = refs[:experts], refs[experts:]
    output_out, input_out, heads_out, mix_out, route_out, gain_a, gain_b = refs[:7]
    wide_out, kinds = refs[7 : 7 + experts], refs[7 + experts]
    for source, target in zip(wide, wide_out):
        target[...] = source[...].astype(target.dtype)
    output_out[...] = output[...]
    input_out[...] = input_grad[...]
    heads_out[...] = heads[...].astype(heads_out.dtype)
    mix_out[...] = mix[...]

    @pl.when(pl.program_id(0) == 0)
    def _():
        share = route_out.shape[1]
        start = lax.rem(lax.axis_index("fsdp") * share, 128)
        total = small[0] + small[1] + small[2] + small[3]
        own = jnp.zeros((total.shape[0], share), jnp.float32)
        for place in range(0, 128, share):
            own = own + jnp.where(start == place, total[:, place : place + share], 0.0)
        kinds[...] = own
        route_out[...] = kinds[:experts_all]
        gain_a[...] = kinds[experts_all : experts_all + 1] / gain[...].astype(jnp.float32)
        gain_b[...] = kinds[experts_all + 1 : experts_all + 2]


def finish(output, input_grad, heads, mix, small, gain, experts_all, wide):
    S, f32 = jax.ShapeDtypeStruct, jnp.float32
    steps = 8
    share = heads.shape[0]

    def part(x, dim):
        shape = tuple(size // steps if d == dim else size for d, size in enumerate(x.shape))
        return pl.BlockSpec(shape, lambda n: tuple(n if d == dim else 0 for d in range(len(shape))))

    def same(*shape):
        return pl.BlockSpec(shape, lambda n: (0,) * len(shape))

    halves = [pl.BlockSpec((1, x.shape[1] * 2 // steps, x.shape[2]), lambda n: (n // (steps // 2), n % (steps // 2), 0)) for x in wide]
    return pl.pallas_call(
        functools.partial(finish_kernel, experts_all, len(wide)),
        grid=(steps,),
        out_shape=(
            S(output.shape, output.dtype),
            S(input_grad.shape, f32),
            S(heads.shape, f32),
            S(mix.shape, f32),
            S((experts_all, share), f32),
            S((1, share), f32),
            S((1, share), f32),
            *(S(x.shape, f32) for x in wide),
        ),
        in_specs=[
            part(output, 0), part(input_grad, 0), part(heads, 1), part(mix, 1), same(*small.shape), same(1, share), *halves
        ],
        out_specs=(
            part(output, 0), part(input_grad, 0), part(heads, 1), part(mix, 1),
            same(experts_all, share), same(1, share), same(1, share), *halves,
        ),
        scratch_shapes=[pltpu.VMEM((small.shape[1], share), f32)],
        compiler_params=pltpu.CompilerParams(vmem_limit_bytes=60 * 2**20),
    )(output, input_grad, heads, mix, small, gain, *wide)


def back_kernel(
    count, experts_all, ret_in, hit_in, middle_in, logits_in, low_in, out_grad, small_all, gains_in, hidden_in,
    proj_in, attended_in, sums_in, normed_in, heads_in, mix_in, ids, length,
    output_out, input_out, heads_out, mix_out, small_out,
    ret, hit, middle, logits, normed_two, up_low, route, gains, hid, output, grad_middle, grad_in, grad_logits, grad_two,
    grads, proj, attended, sums, normed, heads, mix, small, grad_heads, delta, masked_grad, masked_query,
    masked_key, masked_value, probs, slopes, grad_query, grad_key, grad_value, grad_proj, part, weights, weights_mix, gain_sum,
    sib_a, sib_b, sib_c, own_a, own_b, own_c, got_a, got_b, got_c, total_a, total_b, total_c, first, second,
    g_send, g_recv, b_send, b_recv, bb_send, bb_recv, z_send, z_recv, x_send, x_recv, w_send, w_recv, c_send, c_recv, load, keep,
):
    me, place = lax.axis_index("seq"), lax.axis_index("fsdp")
    one, two, both = me ^ 1, me ^ 2, me ^ 3
    others = (one, two, both)
    chips = count // 2
    chip, core = place // 2, lax.rem(place, 2)
    sibling = place ^ 1
    tokens, width = grad_in.shape
    gain_row = experts_all
    group = attended.shape[1]
    share = weights.shape[0] // (4 * count)
    heads_local = group // HEAD_DIM
    low = grads.dtype
    barrier = pltpu.get_barrier_semaphore()
    for peer in others:
        pl.semaphore_signal(barrier, inc=1, device_id={"seq": peer}, device_id_type=MESH)
    for k in range(1, chips):
        pl.semaphore_signal(
            barrier, inc=1, device_id={"fsdp": (chip ^ k) * 2 + core}, device_id_type=MESH
        )
    pl.semaphore_signal(barrier, inc=1, device_id={"fsdp": sibling}, device_id_type=MESH)

    def local(source, to, sem):
        copy = pltpu.make_async_copy(source, to, sem)
        copy.start()
        return copy

    heads_of = [
        local(source, to, load.at[9 + i])
        for i, (source, to) in enumerate(
            (
                (hit_in, hit),
                (ret_in, ret),
                (middle_in, middle),
                (logits_in, logits),
                (low_in, normed_two),
                (out_grad, up_low),
                (small_all, route),
                (gains_in, gains),
                (hidden_in, hid),
            )
        )
    ]
    loads = [
        local(source, to, load.at[1 + i])
        for i, (source, to) in enumerate(
            (
                (proj_in, proj),
                (attended_in, attended),
                (sums_in, sums),
                (mix_in, mix),
                (heads_in, heads),
                (normed_in, normed),
            )
        )
    ]
    for copy in heads_of:
        copy.wait()
    small[...] = jnp.zeros_like(small)
    grad_two[...] = jnp.zeros_like(grad_two)
    lane = lax.broadcasted_iota(jnp.int32, (tokens // 2, route.shape[1]), 1)
    chosen = jnp.transpose(jnp.broadcast_to(ids[...].astype(jnp.float32), (128, tokens)))[:, :1].astype(jnp.int32)
    half = tokens // 2
    direct = {}
    for t in range(2):
        span = slice(t * half, (t + 1) * half)
        position = me * tokens + t * half + lax.broadcasted_iota(jnp.int32, (half, 1), 0)
        valid = jnp.where(position < length[0], 1.0, 0.0)
        scores = jnp.where(lane < experts_all, logits[span, :], MASKED)
        powers = jnp.exp(scores - jnp.max(scores, axis=1, keepdims=True))
        share_of = powers / jnp.sum(powers, axis=1, keepdims=True)
        choose = lane == chosen[span]
        gate = jnp.sum(jnp.where(choose, share_of, 0.0), axis=1, keepdims=True)
        back_rows = transposed_times(hit[:, span], ret[0])
        value = middle[span, :]
        output[span, :] = (valid * (value + gate * back_rows)).astype(low)
        upstream = valid * up_low[span, :].astype(jnp.float32)
        grad_gate = jnp.sum(upstream * back_rows, axis=1, keepdims=True)
        slope = grad_gate * gate * (jnp.where(choose, 1.0, 0.0) - share_of)
        grad_logits[span, :] = slope.astype(low)
        incoming = times_transposed(grad_logits[span, :], route[...]) + transposed_times(hit[:, span], ret[1])
        scale = lax.rsqrt(jnp.mean(value * value, axis=-1, keepdims=True) + EPS)
        shrunk = value * scale
        grad_two[...] += jnp.sum(incoming * shrunk, axis=0, keepdims=True)
        scaled = incoming * gains[1:2, :]
        total = upstream + scale * (scaled - shrunk * jnp.mean(scaled * shrunk, axis=-1, keepdims=True))
        grad_middle[span, :] = total
        grad_in[span, :] = total.astype(low)
        if t == 0:
            pl.semaphore_wait(barrier, 3 + chips)
        for side, peer in enumerate((one, two)):
            direct[side, t] = remote(
                "seq", peer, grad_in.at[pl.ds(t * half, half)], grads.at[pl.ds(me * tokens + t * half, half)],
                g_send.at[side, t], g_recv.at[side, t],
            )
    output_kept = local(output, output_out, load.at[8])
    own_grad = local(grad_in, grads.at[pl.ds(me * tokens, tokens)], load.at[0])
    for n in range(width // 128):
        lanes = slice(n * 128, (n + 1) * 128)
        kinds = transposed_times(grad_logits[...], normed_two[:, lanes])
        small[n // 2, n % 2, :experts_all, :] = kinds[:experts_all]
        small[n // 2, n % 2, gain_row + 1 : gain_row + 2, :] = grad_two[:, lanes]
    for copy in loads:
        copy.wait()
    head_of = lax.broadcasted_iota(jnp.int32, (tokens, group), 1) // HEAD_DIM
    key_at = lax.broadcasted_iota(jnp.int32, (tokens, tokens), 0)
    for j in range(4):
        rows = slice(j * tokens, (j + 1) * tokens)
        for h in range(heads_local):
            key = proj[rows, group : 2 * group] * (HEAD_DIM**-0.5)
            masked_key[j * heads_local + h] = jnp.where(head_of == h, key, 0).astype(low)
            masked_value[j * heads_local + h] = jnp.where(head_of == h, proj[rows, 2 * group :], 0).astype(low)
    grad_key[...] = jnp.zeros_like(grad_key)
    grad_value[...] = jnp.zeros_like(grad_value)
    gain_sum[...] = jnp.zeros_like(gain_sum)

    def block(i, j, masked):
        rows = pl.ds(pl.multiple_of(i * tokens, tokens), tokens)
        keys = pl.ds(pl.multiple_of(j * tokens, tokens), tokens)
        hidden = j * tokens + key_at >= length[0]
        if masked:
            hidden = hidden | (key_at > lax.broadcasted_iota(jnp.int32, (tokens, tokens), 1))
        total = None
        for h in range(heads_local):
            lanes = slice(h * tokens, (h + 1) * tokens)
            key = masked_key[j * heads_local + h]
            scores = times_transposed(key, proj[rows, :group])
            scores = jnp.where(hidden, MASKED, scores)
            p = jnp.exp(scores - sums[h : h + 1, rows])
            probs[:, lanes] = p.astype(low)
            grad = times_transposed(masked_value[j * heads_local + h], grad_heads[...])
            slopes[:, lanes] = (p * (grad - delta[h : h + 1, :])).astype(low)
            term = transposed_times(slopes[:, lanes], key)
            total = term if total is None else total + term
        grad_query[...] += total
        grad_value[keys, :] += times(probs[...], masked_grad[...])
        grad_key[keys, :] += times(slopes[...], masked_query[...])

    def queries(i):
        rows = pl.ds(pl.multiple_of(i * tokens, tokens), tokens)
        grad_heads[...] = times_transposed(grads[rows, :], mix[...]).astype(low)
        out = grad_heads[...].astype(jnp.float32)
        turned = jnp.transpose(out * attended[rows, :].astype(jnp.float32))
        query = proj[rows, :group]
        for h in range(heads_local):
            delta[h : h + 1, :] = jnp.sum(turned[h * HEAD_DIM : (h + 1) * HEAD_DIM], axis=0, keepdims=True)
            masked_grad[h * tokens : (h + 1) * tokens, :] = jnp.where(head_of == h, out, 0).astype(low)
            masked_query[h * tokens : (h + 1) * tokens, :] = jnp.where(head_of == h, query, 0).astype(low)
        grad_query[...] = jnp.zeros_like(grad_query)

        @pl.loop(0, i)
        def _(j):
            block(i, j, False)

        block(i, i, True)
        grad_proj[rows, :group] = grad_query[...].astype(low)

    own_grad.wait()
    queries(me)
    for side, (origin, peer) in enumerate(((one, two), (two, one))):
        direct[side, side].wait_recv()
        source = grads.at[pl.ds(origin * tokens + side * half, half)]
        direct[2, side] = remote("seq", peer, source, source, g_send.at[2, side], g_recv.at[2, side])
    for side, origin in enumerate((one, two)):
        direct[side, 1 - side].wait_recv()
        queries(origin)
    for side in range(2):
        direct[2, side].wait_recv()
    for n in range(width // TILE):
        lanes = slice(n * TILE, (n + 1) * TILE)
        weights_mix[:, lanes] = transposed_times(attended[...], grads[:, lanes]).astype(low)
    order_of = [*range(1, chips), 0]
    to_sibling, away = {}, {}

    def rows_at(s, owner):
        return pl.ds(pl.multiple_of((s * count + owner) * share, share), share)

    def start_sibling(a, k, core_of):
        owner = (chip ^ k) * 2 + core_of
        if a == 1:
            return [
                remote(
                    "fsdp", sibling, weights_mix.at[pl.ds(pl.multiple_of(owner * share, share), share)], sib_b.at[k],
                    b_send.at[0, k], b_recv.at[0, k],
                )
            ]
        if a == 2:
            return [
                remote(
                    "fsdp", sibling, small.at[:, owner * share // 128], sib_c.at[k], b_send.at[1, k], b_recv.at[1, k]
                )
            ]
        raise ValueError(a)

    sib, own, got = (sib_a, sib_b, sib_c), (own_a, own_b, own_c), (got_a, got_b, got_c)
    totals = (total_a, total_b, total_c)

    def pair_sum(a, k):
        owner = (chip ^ k) * 2 + core
        for copy in to_sibling[a, k]:
            copy.wait_recv()
        if a == 1:
            mine = weights_mix[pl.ds(pl.multiple_of(owner * share, share), share), :]
            own_b[k] = (mine.astype(jnp.float32) + sib_b[k].astype(jnp.float32)).astype(low)
        else:
            for s in range(4):
                own_c[k, s] = small[s, owner * share // 128] + sib_c[k, s]
        if k:
            away[a, k] = remote(
                "fsdp", (chip ^ k) * 2 + core, own[a].at[k], got[a].at[k], z_send.at[a, k], z_recv.at[a, k]
            )

    for k in order_of:
        to_sibling[1, k] = start_sibling(1, k, core ^ 1)
    queries(both)
    for k in order_of:
        pair_sum(1, k)
    grad_proj[:, group : 2 * group] = (grad_key[...] * (HEAD_DIM**-0.5)).astype(low)
    grad_proj[:, 2 * group :] = grad_value[...].astype(low)

    def partial(j):
        own_rows = pl.ds(pl.multiple_of(j * tokens, tokens), tokens)
        for n in range(width // TILE):
            lanes = slice(n * TILE, (n + 1) * TILE)
            back = times_transposed(grad_proj[own_rows, :], heads[lanes, :])
            gain_sum[:, lanes] += jnp.sum(back * normed[own_rows, lanes].astype(jnp.float32), axis=0, keepdims=True)
            part[j, :, lanes] = back.astype(low)

    summed = {}

    def send_part(side, order):
        near = (one, two)[side]
        block_of = near if order else both
        summed[side, order] = remote(
            "seq", near, part.at[block_of, pl.ds(side * half, half)], first.at[side, order],
            c_send.at[side, order], c_recv.at[side, order],
        )

    partial(both)
    send_part(0, 0)
    send_part(1, 0)
    partial(one)
    send_part(0, 1)
    partial(two)
    send_part(1, 1)
    for s in range(4):
        lanes = slice(s * group, (s + 1) * group)
        weights[lanes, :] = transposed_times(normed[:, lanes], grad_proj[...]).astype(low)
        for k in order_of:
            owner = (chip ^ k) * 2
            to_sibling[s + 3, k] = [
                remote(
                    "fsdp", sibling, weights.at[rows_at(s, owner + (core ^ 1))], sib_a.at[k, pl.ds(s * share, share)],
                    bb_send.at[s, k], bb_recv.at[s, k],
                )
            ]
    for s in range(4):
        rows = slice(s * share, (s + 1) * share)
        for k in order_of:
            owner = (chip ^ k) * 2 + core
            to_sibling[s + 3, k][0].wait_recv()
            own_a[k, rows, :] = (
                weights[rows_at(s, owner), :].astype(jnp.float32) + sib_a[k, rows, :].astype(jnp.float32)
            ).astype(low)
            if k:
                away[s + 3, k] = remote(
                    "fsdp", owner, own_a.at[k, pl.ds(s * share, share)], got_a.at[k, pl.ds(s * share, share)],
                    z_send.at[s + 3, k], z_recv.at[s + 3, k],
                )
    partial(me)
    for b in range(width // 128):
        small[b // 2, b % 2, gain_row : gain_row + 1, :] = gain_sum[:, b * 128 : (b + 1) * 128]
    for k in order_of:
        to_sibling[2, k] = start_sibling(2, k, core ^ 1)
    for k in order_of:
        pair_sum(2, k)
    for side, rest in enumerate((two, one)):
        rows = slice(side * half, (side + 1) * half)
        summed[side, 0].wait_recv()
        first[side, 0] = (first[side, 0].astype(jnp.float32) + part[rest, rows, :].astype(jnp.float32)).astype(low)
        summed[side, 2] = remote("seq", rest, first.at[side, 0], second.at[side], c_send.at[2, side], c_recv.at[2, side])
    stored = []
    for side in range(2):
        rows = slice(side * half, (side + 1) * half)
        summed[side, 1].wait_recv()
        summed[side, 2].wait_recv()
        incoming = (
            part[me, rows, :].astype(jnp.float32)
            + first[side, 1].astype(jnp.float32)
            + second[side].astype(jnp.float32)
        )
        value = hid[rows, :].astype(jnp.float32)
        scale = lax.rsqrt(jnp.mean(value * value, axis=-1, keepdims=True) + EPS)
        shrunk = value * scale
        scaled = incoming * gains[0:1, :]
        grad_middle[rows, :] += scale * (scaled - shrunk * jnp.mean(scaled * shrunk, axis=-1, keepdims=True))
        stored.append(
            local(grad_middle.at[pl.ds(side * half, half)], input_out.at[pl.ds(side * half, half)], keep.at[side])
        )
    for a in (1, 0, 2):
        if a == 0:
            for s in range(4):
                rows = slice(s * share, (s + 1) * share)
                total = own_a[0, rows, :].astype(jnp.float32)
                for k in range(1, chips):
                    away[s + 3, k].wait_recv()
                    total = total + got_a[k, rows, :].astype(jnp.float32)
                total_a[s] = total.astype(low)
        else:
            total = own[a][0].astype(jnp.float32)
            for k in range(1, chips):
                away[a, k].wait_recv()
                total = total + got[a][k].astype(jnp.float32)
            totals[a][...] = total
    crossed = []
    for p in range(3):
        lanes = pl.ds(p * group, group)
        target = heads_out.at[:, pl.ds(pl.multiple_of((p * 4 + me) * group, group), group)]
        for i, peer in enumerate(others):
            crossed.append(
                remote("seq", peer, total_a.at[peer, :, lanes], target, w_send.at[p, i], w_recv.at[p, i])
            )
        stored.append(local(total_a.at[me, :, lanes], target, load.at[18 + p]))
    for i, peer in enumerate(others):
        crossed.append(remote("seq", peer, total_c.at[peer], small_out.at[me], x_send.at[i], x_recv.at[i]))
    stored.append(local(total_c.at[me], small_out.at[me], keep.at[3]))
    stored.append(local(total_b, mix_out, keep.at[2]))
    for copy in (*stored, *crossed, output_kept):
        copy.wait()
    for copy in (*summed.values(), *away.values(), *direct.values()):
        copy.wait_send()
    for copies in to_sibling.values():
        for copy in copies:
            copy.wait_send()


def back(
    ret, hit, middle, logits, normed_two, out_grad, route, gains, hidden,
    proj, attended, sums, normed, heads, mix, ids, lengths, count, experts_all, number,
):
    S, dma, f32, low = jax.ShapeDtypeStruct, pltpu.SemaphoreType.DMA, jnp.float32, jnp.bfloat16
    tokens, width = out_grad.shape
    group = attended.shape[1]
    chips = count // 2
    full = 4 * tokens
    share = width // (4 * count)
    local_heads = group // HEAD_DIM
    kinds = -(-(experts_all + 2) // 8) * 8

    def vmem(*shape, dtype=low):
        return pltpu.VMEM(shape, dtype)

    sets = [
        vmem(chips, 4 * share, 3 * group),
        vmem(chips, share, width),
        vmem(chips, 4, kinds, 128, dtype=f32),
    ]
    return pl.pallas_call(
        functools.partial(back_kernel, count, experts_all),
        out_shape=(
            S((tokens, width), low),
            S((tokens, width), f32),
            S((share, 12 * group), low),
            S((share, width), f32),
            S((4, kinds, 128), f32),
        ),
        in_specs=[ANY] * 15 + [pl.BlockSpec(memory_space=pltpu.VMEM), pl.BlockSpec(memory_space=pltpu.SMEM)],
        out_specs=(ANY,) * 5,
        scratch_shapes=[
            vmem(*ret.shape),
            vmem(*hit.shape),
            vmem(tokens, width, dtype=f32),
            vmem(*logits.shape, dtype=f32),
            vmem(tokens, width),
            vmem(tokens, width),
            vmem(*route.shape),
            vmem(*gains.shape, dtype=f32),
            vmem(tokens, width),
            vmem(tokens, width),
            vmem(tokens, width, dtype=f32),
            vmem(tokens, width),
            vmem(*logits.shape),
            vmem(1, width, dtype=f32),
            vmem(full, width),
            vmem(*proj.shape),
            vmem(*attended.shape),
            vmem(*sums.shape, dtype=f32),
            vmem(*normed.shape),
            vmem(*heads.shape),
            vmem(group, width),
            vmem(4, group // 128, kinds, 128, dtype=f32),
            vmem(tokens, group),
            vmem(8, tokens, dtype=f32),
            vmem(local_heads * tokens, group),
            vmem(local_heads * tokens, group),
            vmem(4 * local_heads, tokens, group),
            vmem(4 * local_heads, tokens, group),
            vmem(tokens, local_heads * tokens),
            vmem(tokens, local_heads * tokens),
            vmem(tokens, group, dtype=f32),
            vmem(full, group, dtype=f32),
            vmem(full, group, dtype=f32),
            vmem(full, 3 * group),
            vmem(4, tokens, width),
            vmem(width, 3 * group),
            vmem(group, width),
            vmem(1, width, dtype=f32),
            *sets,
            *sets,
            *sets,
            vmem(4, share, 3 * group),
            vmem(share, width, dtype=f32),
            vmem(4, kinds, 128, dtype=f32),
            vmem(2, 2, tokens // 2, width),
            vmem(2, tokens // 2, width),
            dma((3, 2)), dma((3, 2)),
            dma((2, chips)), dma((2, chips)), dma((4, chips)), dma((4, chips)),
            dma((7, chips)), dma((7, chips)),
            dma((3,)), dma((3,)), dma((3, 3)), dma((3, 3)), dma((3, 2)), dma((3, 2)), dma((21,)), dma((5,)),
        ],
        compiler_params=pltpu.CompilerParams(
            collective_id=number, has_side_effects=True, vmem_limit_bytes=60 * 2**20
        ),
    )(
        ret, hit, middle, logits, normed_two, out_grad, route, gains, hidden,
        proj, attended, sums, normed, heads, mix, ids, lengths,
    )


def shards(
    hidden,
    lengths,
    expert_ids,
    attn_gain,
    qkv_weight,
    out_weight,
    moe_gain,
    router_weight,
    expert_in,
    expert_out,
    out_grad,
):
    S = jax.ShapeDtypeStruct
    low = jnp.bfloat16
    owners = lax.axis_size("fsdp")
    seq_count = lax.axis_size("seq")
    tokens, width = hidden.shape[1], hidden.shape[2]
    full_len = tokens * seq_count
    group_width = width // seq_count
    experts_all = router_weight.shape[1]
    expert_local = expert_in.shape[0]
    capacity = -(-max(2, 2 * tokens // experts_all) // 16) * 16
    slots = experts_all * capacity

    chosen = expert_ids[0, :, 0]

    def to_owners(rows, number):
        return exchange(
            "fsdp",
            owners,
            (rows.reshape(owners, expert_local, capacity, width),),
            (S((expert_local, owners, capacity, width), low),),
            ((lead, second),),
            number,
        )[0].reshape(expert_local, owners * capacity, width)

    def to_sources(rows, number):
        return exchange(
            "fsdp",
            owners,
            (rows.reshape(expert_local, owners, capacity, width),),
            (S((owners, expert_local, capacity, width), low),),
            ((second, lead),),
            number,
        )[0].reshape(slots, width)

    chips = owners // 2
    fused = 4 * owners * capacity <= 1024
    (
        normed,
        weight_qkv,
        mix_rows,
        small,
        gains,
        up_all,
        projected,
        attended,
        totals,
        middle,
        normed_two,
        logits,
        sent,
        dispatch,
    ) = front(
        hidden[0],
        qkv_weight,
        out_weight,
        out_grad[0],
        router_weight.T,
        attn_gain[None],
        moe_gain[None],
        expert_ids[0].T,
        lengths,
        owners,
        capacity,
        SPREAD_FIRST if fused else chips,
        0,
    )
    weight_qkv = weight_qkv.reshape(width, 3 * group_width)
    mix_rows = mix_rows.reshape(group_width, width)
    if not fused:
        up_all = up_all.reshape(expert_local, chips, seq_count, 2 * capacity, width)
        chip, bit = lax.axis_index("fsdp") // 2, 1
        while bit < chips:
            pairs = up_all.reshape(expert_local, chips // (2 * bit), 2, bit, seq_count, 2 * capacity, width)
            up_all = jnp.where((chip // bit) % 2 == 1, pairs[:, :, ::-1], pairs)
            bit *= 2
        up_all = up_all.reshape(expert_local, chips, seq_count, 2 * capacity, width)
        up_all = up_all.transpose(0, 2, 1, 3, 4)
    if fused:
        returned, *expert_grads = moe(
            sent,
            up_all,
            small,
            expert_in,
            expert_out,
            experts_all,
            5,
        )
        returned = returned.reshape(2, slots, width)
    else:
        choose = chosen[:, None] == jnp.arange(experts_all, dtype=jnp.int32)[None, :]
        weights = jax.nn.softmax(logits[:, :experts_all], axis=-1)
        gate = jnp.sum(jnp.where(choose, weights, 0.0), axis=-1)
        gate_rows = jnp.sum(jnp.where(dispatch > 0, gate[None, :], 0.0), axis=1)
        gates = lax.all_to_all(
            gate_rows.reshape(owners, expert_local, capacity), "fsdp", split_axis=0, concat_axis=0, tiled=True
        )
        gates = lax.all_gather(gates, "seq", axis=0)
        gates = gates.transpose(2, 0, 1, 3).reshape(expert_local, seq_count * owners * capacity, 1)

        rows_all = spread(to_owners(sent, 5), 6)
        count = seq_count * owners * capacity
        rows_all = rows_all.reshape(expert_local, count, width)
        up_all = up_all.reshape(expert_local, count, width)
        grad_rows = (up_all.astype(jnp.float32) * gates).astype(low)

        def per_expert(form, left, right):
            return jnp.einsum(form, left, right, preferred_element_type=jnp.float32)

        inner = per_expert("jrd,jdf->jrf", rows_all, expert_in)
        active, active_back = jax.vjp(gelu_tanh, inner)
        active = active.astype(low)
        partial_out = per_expert("jrf,jfd->jrd", active, expert_out).astype(low)
        grad_active = per_expert("jrd,jfd->jrf", grad_rows, expert_out)
        grad_inner = active_back(grad_active)[0].astype(low)
        partial_back = per_expert("jrf,jdf->jrd", grad_inner, expert_in).astype(low)
        expert_out_grad = per_expert("jrf,jrd->jfd", active, grad_rows)
        expert_in_grad = per_expert("jrd,jrf->jdf", rows_all, grad_inner)

        shape = (expert_local, seq_count, owners * capacity, width)
        returned = to_sources(collect(partial_out.reshape(shape), 7), 8)
        grad_back = to_sources(collect(partial_back.reshape(shape), 9), 10)
        returned, expert_grads = jnp.stack([returned, grad_back]), ()
    output, grad_inputs, qkv_sum, mix_grad, small_sum = back(
        returned,
        dispatch,
        middle,
        logits,
        normed_two,
        out_grad[0],
        small,
        gains,
        hidden[0],
        projected,
        attended,
        totals,
        normed,
        weight_qkv,
        mix_rows,
        expert_ids[0].T,
        lengths,
        owners,
        experts_all,
        12,
    )
    output, grad_inputs, qkv_grad, mix_grad, route_grad, gain_one_grad, gain_two_grad, *wide = finish(
        output, grad_inputs, qkv_sum, mix_grad, small_sum, attn_gain[None], experts_all, expert_grads
    )
    if fused:
        expert_in_grad, expert_out_grad = wide
    return (
        output[None],
        grad_inputs[None],
        gain_one_grad[0],
        qkv_grad,
        mix_grad,
        gain_two_grad[0],
        route_grad.T,
        expert_in_grad,
        expert_out_grad,
    )


def solution(mesh):
    placed = (
        P("fsdp", "seq", None),
        P("fsdp"),
        P("fsdp", "seq", None),
        P(("seq", "fsdp")),
        P(("seq", "fsdp"), None),
        P(("seq", "fsdp"), None),
        P(("seq", "fsdp")),
        P(("seq", "fsdp"), None),
        P("fsdp", None, "seq"),
        P("fsdp", "seq", None),
        P("fsdp", "seq", None),
    )
    return jax.shard_map(
        shards,
        mesh=mesh,
        in_specs=placed,
        out_specs=(
            P("fsdp", "seq", None),
            P("fsdp", "seq", None),
            P(("seq", "fsdp")),
            P(("seq", "fsdp"), None),
            P(("seq", "fsdp"), None),
            P(("seq", "fsdp")),
            P(("seq", "fsdp"), None),
            P("fsdp", None, "seq"),
            P("fsdp", "seq", None),
        ),
        check_vma=False,
    )
```

```python
import functools

import jax
import jax.numpy as jnp
from jax import lax
from jax.experimental import pallas as pl
from jax.experimental.pallas import tpu as pltpu
from jax.sharding import PartitionSpec as P

HEAD_DIM = 64
EPS = 1e-05
MASKED = -1e30
ROOT = 0.7978845608028654
TILE = 256
SPREAD_FIRST = 3
TURN = (1, 3, 2, 0)
GRAD = 256
MESH = pl.DeviceIdType.MESH
ANY = pl.BlockSpec(memory_space=pl.ANY)


def scaled_norm(value, gain):
    return value * lax.rsqrt(jnp.mean(value * value, axis=-1, keepdims=True) + EPS) * gain


def gelu_tanh(value):
    return jax.nn.gelu(value, approximate=True)


def times(left, right):
    return jnp.dot(left, right, preferred_element_type=jnp.float32)


def times_transposed(left, right):
    return lax.dot_general(
        left, right, (((1,), (1,)), ((), ())), preferred_element_type=jnp.float32
    )


def transposed_times(left, right):
    return lax.dot_general(
        left, right, (((0,), (0,)), ((), ())), preferred_element_type=jnp.float32
    )


def greet(axis, peers):
    barrier = pltpu.get_barrier_semaphore()
    for peer in peers:
        pl.semaphore_signal(barrier, inc=1, device_id={axis: peer}, device_id_type=MESH)
    pl.semaphore_wait(barrier, len(peers))


def remote(axis, peer, source, target, send, receive):
    copy = pltpu.make_async_remote_copy(
        source, target, send, receive, device_id={axis: peer}, device_id_type=MESH
    )
    copy.start()
    return copy


def call(kernel, inputs, outputs, scratch, number):
    return pl.pallas_call(
        kernel,
        out_shape=outputs,
        in_specs=[ANY] * len(inputs),
        out_specs=jax.tree.map(lambda _: ANY, outputs),
        scratch_shapes=scratch,
        compiler_params=pltpu.CompilerParams(
            collective_id=number, has_side_effects=True, vmem_limit_bytes=60 * 2**20
        ),
    )(*inputs)


def exchange_kernel(axis, count, views, *refs):
    arrays = len(views)
    sources, targets = refs[:arrays], refs[arrays : 2 * arrays]
    send, receive, local = refs[2 * arrays :]
    me = lax.axis_index(axis)
    peers = [lax.rem(me + step, count) for step in range(1, count)]
    greet(axis, peers)
    copies = []
    for step, peer in enumerate(peers):
        for a, (out_of, into) in enumerate(views):
            copies.append(
                remote(
                    axis,
                    peer,
                    out_of(sources[a], peer),
                    into(targets[a], me),
                    send.at[a, step],
                    receive.at[a, step],
                )
            )
    for a, (out_of, into) in enumerate(views):
        copy = pltpu.make_async_copy(out_of(sources[a], me), into(targets[a], me), local.at[a])
        copy.start()
        copies.append(copy)
    for copy in copies:
        copy.wait()


def exchange(axis, count, inputs, outputs, views, number):
    arrays = len(views)
    return call(
        functools.partial(exchange_kernel, axis, count, views),
        inputs,
        outputs,
        [
            pltpu.SemaphoreType.DMA((arrays, count - 1)),
            pltpu.SemaphoreType.DMA((arrays, count - 1)),
            pltpu.SemaphoreType.DMA((arrays,)),
        ],
        number,
    )


def lead(ref, place):
    return ref.at[place]


def second(ref, place):
    return ref.at[:, place]


def whole(ref, place):
    return ref


def spread_kernel(source, target, send, receive, local):
    me = lax.axis_index("seq")
    one, two, both = me ^ 1, me ^ 2, me ^ 3
    half = source.shape[1] // 2
    greet("seq", [one, two])
    parts = (pl.ds(0, half), pl.ds(half, half))
    own = pltpu.make_async_copy(source, target.at[:, me], local)
    own.start()
    copies = {}
    for side, peer in enumerate((one, two)):
        for order in range(2):
            part = (order + side) % 2
            copies[side, part] = remote(
                "seq",
                peer,
                source.at[:, parts[part]],
                target.at[:, me, parts[part]],
                send.at[side, part],
                receive.at[side, part],
            )
    relayed = []
    for side, (origin, peer) in enumerate(((one, two), (two, one))):
        copies[side, side].wait_recv()
        block = target.at[:, origin, parts[side]]
        relayed.append(remote("seq", peer, block, block, send.at[2, side], receive.at[2, side]))
    for side in range(2):
        copies[side, 1 - side].wait_recv()
        for part in range(2):
            copies[side, part].wait_send()
    for copy in relayed:
        copy.wait()
    own.wait()


def spread(source, number):
    return call(
        spread_kernel,
        (source,),
        jax.ShapeDtypeStruct((source.shape[0], 4, *source.shape[1:]), source.dtype),
        [
            pltpu.SemaphoreType.DMA((3, 2)),
            pltpu.SemaphoreType.DMA((3, 2)),
            pltpu.SemaphoreType.DMA,
        ],
        number,
    )


def collect_kernel(source, target, mine, first, second_in, outgoing, load, send, receive, store):
    me = lax.axis_index("seq")
    one, two, both = me ^ 1, me ^ 2, me ^ 3
    width = source.shape[3] // 2
    greet("seq", [one, two])
    copies = []
    for side, (near, rest) in enumerate(((one, two), (two, one))):
        lanes = pl.ds(side * width, width)
        for order, block in enumerate((both, near)):
            copies.append(
                remote(
                    "seq",
                    near,
                    source.at[:, block, :, lanes],
                    first.at[side, order],
                    send.at[side, order],
                    receive.at[side, order],
                )
            )
        for order, block in enumerate((rest, me)):
            pltpu.make_async_copy(
                source.at[:, block, :, lanes], mine.at[side, order], load.at[side, order]
            ).start()
    passed = []
    for side, rest in enumerate((two, one)):
        copies[side * 2].wait_recv()
        pltpu.make_async_copy(mine.at[side, 0], mine.at[side, 0], load.at[side, 0]).wait()
        outgoing[side] = (
            mine[side, 0].astype(jnp.float32) + first[side, 0].astype(jnp.float32)
        ).astype(outgoing.dtype)
        passed.append(
            remote("seq", rest, outgoing.at[side], second_in.at[side], send.at[2, side], receive.at[2, side])
        )
    for side in range(2):
        copies[side * 2 + 1].wait_recv()
        pltpu.make_async_copy(mine.at[side, 1], mine.at[side, 1], load.at[side, 1]).wait()
        passed[side].wait_recv()
        mine[side, 1] = (
            mine[side, 1].astype(jnp.float32)
            + first[side, 1].astype(jnp.float32)
            + second_in[side].astype(jnp.float32)
        ).astype(mine.dtype)
        out = pltpu.make_async_copy(
            mine.at[side, 1], target.at[:, :, pl.ds(side * width, width)], store.at[side]
        )
        out.start()
    for side in range(2):
        pltpu.make_async_copy(
            mine.at[side, 1], target.at[:, :, pl.ds(side * width, width)], store.at[side]
        ).wait()
    for copy in copies + passed:
        copy.wait_send()


def collect(source, number):
    a, _, rows, width = source.shape
    dma = pltpu.SemaphoreType.DMA
    block = (a, rows, width // 2)
    return call(
        collect_kernel,
        (source,),
        jax.ShapeDtypeStruct((a, rows, width), source.dtype),
        [
            pltpu.VMEM((2, 2, *block), source.dtype),
            pltpu.VMEM((2, 2, *block), source.dtype),
            pltpu.VMEM((2, *block), source.dtype),
            pltpu.VMEM((2, *block), source.dtype),
            dma((2, 2)),
            dma((3, 2)),
            dma((3, 2)),
            dma((2,)),
        ],
        number,
    )


def moe_kernel(
    chips, cap, experts_all, spread_first, send_rows, up_rows, route, w_in, w_out,
    ret, dw_in, dw_out,
    R, U, G, A, I, PB, first, second, W1, W2, RT, stage,
    load, own, z_send, z_recv, s_send, s_recv, y_send, y_recv,
    c_send, c_recv, d_send, d_recv, r_send, r_recv, store,
):
    me, place = lax.axis_index("seq"), lax.axis_index("fsdp")
    one, two, both = me ^ 1, me ^ 2, me ^ 3
    chip, core = place // 2, lax.rem(place, 2)
    sibling = place ^ 1
    count = chips * 2
    part = 2 * cap
    chunk = 4 * part
    barrier = pltpu.get_barrier_semaphore()
    for peer in (one, two):
        pl.semaphore_signal(barrier, inc=1, device_id={"seq": peer}, device_id_type=MESH)
    for step in range(1, count):
        pl.semaphore_signal(
            barrier, inc=1, device_id={"fsdp": lax.rem(place + step, count)}, device_id_type=MESH
        )
    pl.semaphore_wait(barrier, 2 + count - 1)

    def rows_of(k, s):
        return pl.ds(k * chunk + s * part, part)

    loads = []

    def local(source, target, sem):
        copy = pltpu.make_async_copy(source, target, sem)
        copy.start()
        return copy

    dispatched = {}
    own_rows = []

    def dispatch(k):
        target = R.at[:, pl.ds(k * chunk + me * part + core * cap, cap)]
        if k == 0:
            own_rows.append(local(send_rows.at[place], target, own.at[0]))
        for c in range(2):
            if k or c:
                peer = (chip ^ k) * 2 + (core ^ c)
                dispatched[k, c] = remote(
                    "fsdp", peer, send_rows.at[peer], target, z_send.at[k, c], z_recv.at[k, c]
                )

    def z_arrived(k):
        if k == 0:
            own_rows[0].wait()
        for c in range(2):
            if k or c:
                dispatched[k, c].wait_recv()

    sent = {}

    def spread_out(a, k):
        for side, peer in enumerate((one, two)):
            for order in range(2):
                j = (order + side) % 2
                target = (U, R)[a].at[j, rows_of(k, me)]
                source = target if a else up_rows.at[j, rows_of(k, me)]
                sent[a, k, side, j] = remote(
                    "seq", peer, source, target, s_send.at[a, k, side, j], s_recv.at[a, k, side, j]
                )

    def relay(a, k):
        for side, (origin, peer) in enumerate(((one, two), (two, one))):
            sent[a, k, side, side].wait_recv()
            block = (U, R)[a].at[side, rows_of(k, origin)]
            sent[a, k, 2, side] = remote("seq", peer, block, block, y_send.at[a, k, side], y_recv.at[a, k, side])

    def all_arrived(a, k):
        for side in range(2):
            sent[a, k, side, 1 - side].wait_recv()
            sent[a, k, 2, side].wait_recv()

    def experts(k, j):
        rows = pl.ds(k * chunk, chunk)
        logits = times(R[j, rows, :], RT[...])
        lane = lax.broadcasted_iota(jnp.int32, logits.shape, 1)
        logits = jnp.where(lane < experts_all, logits, MASKED)
        powers = jnp.exp(logits - jnp.max(logits, axis=1, keepdims=True))
        picked = jnp.sum(jnp.where(lane == place * 2 + j, powers, 0.0), axis=1, keepdims=True)
        gate = picked / jnp.sum(powers, axis=1, keepdims=True)
        G[j, rows, :] = (U[j, rows, :].astype(jnp.float32) * gate).astype(G.dtype)

        @pl.loop(0, W1.shape[2] // TILE)
        def _(t):
            cols = pl.ds(pl.multiple_of(t * TILE, TILE), TILE)
            v = times(R[j, rows, :], W1[j, :, cols])
            grad = times_transposed(G[j, rows, :], W2[j, cols, :])
            square = v * v
            t = jnp.tanh(ROOT * v * (1.0 + 0.044715 * square))
            half = 0.5 * (1.0 + t)
            A[j, rows, cols] = (v * half).astype(A.dtype)
            slope = half + 0.5 * v * (1.0 - t * t) * (ROOT * (1.0 + 0.134145 * square))
            I[j, rows, cols] = (grad * slope).astype(I.dtype)

        @pl.loop(0, W1.shape[1] // TILE)
        def _(t):
            cols = pl.ds(pl.multiple_of(t * TILE, TILE), TILE)
            PB[0, j, rows, cols] = times(A[j, rows, :], W2[j, :, cols]).astype(PB.dtype)
            PB[1, j, rows, cols] = times_transposed(I[j, rows, :], W1[j, cols, :]).astype(PB.dtype)

    summed = {}

    def near_of(j):
        return (one, two) if j == 0 else (two, one)

    def collect_one(k, j):
        near, rest = near_of(j)
        for a in range(2):
            for order, block in enumerate((both, near)):
                summed[a, k, j, order] = remote(
                    "seq", near, PB.at[a, j, rows_of(k, block)], first.at[a, j, k, order],
                    c_send.at[a, j, k, order], c_recv.at[a, j, k, order],
                )

    def collect_two(k, j):
        near, rest = near_of(j)
        for a in range(2):
            summed[a, k, j, 0].wait_recv()
            first[a, j, k, 0] = (
                first[a, j, k, 0].astype(jnp.float32) + PB[a, j, rows_of(k, rest), :].astype(jnp.float32)
            ).astype(first.dtype)
            summed[a, k, j, 2] = remote(
                "seq", rest, first.at[a, j, k, 0], second.at[a, j, k], d_send.at[a, j, k], d_recv.at[a, j, k]
            )

    returns = {}

    def collect_three(k, j):
        for a in range(2):
            summed[a, k, j, 1].wait_recv()
            summed[a, k, j, 2].wait_recv()
            first[a, j, k, 1] = (
                first[a, j, k, 1].astype(jnp.float32)
                + PB[a, j, rows_of(k, me), :].astype(jnp.float32)
                + second[a, j, k].astype(jnp.float32)
            ).astype(first.dtype)
            to = chip ^ k
            target = ret.at[a, place, j]
            for c in range(2):
                if k == 0:
                    if c == 0:
                        returns[a, k, j, 0] = local(
                            first.at[a, j, k, 1, pl.ds(core * cap, cap)], target, own.at[1 + a * 2 + j]
                        )
                        returns[a, k, j, 1] = remote(
                            "fsdp", sibling, first.at[a, j, k, 1, pl.ds((core ^ 1) * cap, cap)], target,
                            r_send.at[a, j, k, 1], r_recv.at[a, j, k, 1],
                        )
                    continue
                returns[a, k, j, c] = remote(
                    "fsdp", to * 2 + (core ^ c), first.at[a, j, k, 1, pl.ds((core ^ c) * cap, cap)], target,
                    r_send.at[a, j, k, c], r_recv.at[a, j, k, c],
                )

    staged = {}

    def weight_grads(j, which, tiles):
        left, right, out = ((R, I, dw_in), (A, G, dw_out))[which]
        for m in tiles:
            slot = m % 2
            lanes = slice(m * GRAD, (m + 1) * GRAD)
            if slot in staged:
                staged.pop(slot).wait()

            @pl.loop(0, right.shape[2] // TILE)
            def _(t):
                cols = pl.ds(pl.multiple_of(t * TILE, TILE), TILE)
                stage[slot, :, cols] = transposed_times(left[j, :, lanes], right[j, :, cols]).astype(stage.dtype)

            staged[slot] = local(stage.at[slot], out.at[j, lanes], store.at[slot])

    later = range(spread_first, chips)
    turn = TURN
    away = [k for k in turn if k]
    dispatch(0)
    dispatch(away[0])
    dispatch(away[1])
    for j in range(2):
        loads.append(local(w_in.at[j], W1.at[j], load.at[j]))
        loads.append(local(w_out.at[j], W2.at[j], load.at[2 + j]))
    loads.append(local(route, RT, load.at[4]))
    early = spread_first * chunk
    for j in range(2):
        loads.append(local(up_rows.at[j, pl.ds(0, early)], U.at[j, pl.ds(0, early)], load.at[5 + j]))
    for n, k in enumerate(later):
        for j in range(2):
            block = rows_of(k, me)
            loads.append(local(up_rows.at[j, block], U.at[j, block], load.at[7 + 2 * n + j]))
    if turn[0]:
        for k in later:
            spread_out(0, k)
    z_arrived(turn[0])
    spread_out(1, turn[0])
    if not turn[0]:
        for k in later:
            spread_out(0, k)
    z_arrived(turn[1])
    spread_out(1, turn[1])
    dispatch(away[2])
    relay(1, turn[0])
    for copy in loads:
        copy.wait()
    for k in later:
        relay(0, k)
    z_arrived(turn[2])
    spread_out(1, turn[2])
    for n in range(chips):
        k = turn[n]
        all_arrived(1, k)
        if k >= spread_first:
            all_arrived(0, k)
        if n == 0:
            relay(1, turn[1])
        experts(k, 0)
        collect_one(k, 0)
        if n == 1:
            relay(1, turn[3])
        if n == 0:
            z_arrived(turn[3])
            spread_out(1, turn[3])
        else:
            collect_two(turn[n - 1], 0)
        if n > 1:
            collect_three(turn[n - 2], 0)
        experts(k, 1)
        collect_one(k, 1)
        if n == 0:
            relay(1, turn[2])
        else:
            collect_two(turn[n - 1], 1)
        if n > 1:
            collect_three(turn[n - 2], 1)
    weight_grads(0, 0, range(4))
    collect_two(turn[3], 0)
    collect_three(turn[2], 0)
    collect_two(turn[3], 1)
    collect_three(turn[2], 1)
    weight_grads(0, 1, range(4))
    weight_grads(1, 0, range(2))
    collect_three(turn[3], 0)
    weight_grads(1, 0, range(2, 4))
    collect_three(turn[3], 1)
    weight_grads(1, 1, range(4))
    for copy in staged.values():
        copy.wait()
    for copy in dispatched.values():
        copy.wait_send()
    for copy in sent.values():
        copy.wait_send()
    for copy in summed.values():
        copy.wait_send()
    for (a, k, j, c), copy in returns.items():
        copy.wait()


def moe(send_rows, up_rows, route, w_in, w_out, experts_all, number):
    S, low, dma = jax.ShapeDtypeStruct, jnp.bfloat16, pltpu.SemaphoreType.DMA
    owners, _, cap, width = send_rows.shape
    chips = owners // 2
    hidden_units = w_in.shape[2]
    count = owners * cap * 4
    part = 2 * cap

    def vmem(*shape, dtype=low):
        return pltpu.VMEM(shape, dtype)

    return pl.pallas_call(
        functools.partial(moe_kernel, chips, cap, experts_all, SPREAD_FIRST),
        out_shape=(
            S((2, owners, 2, cap, width), low),
            S(w_in.shape, low),
            S(w_out.shape, low),
        ),
        in_specs=[ANY] * 5,
        out_specs=(ANY,) * 3,
        scratch_shapes=[
            vmem(2, count, width),
            vmem(2, count, width),
            vmem(2, count, width),
            vmem(2, count, hidden_units),
            vmem(2, count, hidden_units),
            vmem(2, 2, count, width),
            vmem(2, 2, chips, 2, part, width),
            vmem(2, 2, chips, part, width),
            vmem(*w_in.shape),
            vmem(*w_out.shape),
            vmem(*route.shape),
            vmem(2, GRAD, max(width, hidden_units)),
            dma((7 + 2 * (chips - SPREAD_FIRST),)),
            dma((5,)),
            dma((chips, 2)),
            dma((chips, 2)),
            dma((2, chips, 2, 2)),
            dma((2, chips, 2, 2)),
            dma((2, chips, 2)),
            dma((2, chips, 2)),
            dma((2, 2, chips, 2)),
            dma((2, 2, chips, 2)),
            dma((2, 2, chips)),
            dma((2, 2, chips)),
            dma((2, 2, chips, 2)),
            dma((2, 2, chips, 2)),
            dma((2,)),
        ],
        compiler_params=pltpu.CompilerParams(
            collective_id=number, has_side_effects=True, vmem_limit_bytes=60 * 2**20
        ),
        cost_estimate=pl.CostEstimate(
            flops=12 * 2 * count * width * hidden_units, bytes_accessed=2**25, transcendentals=0
        ),
    )(send_rows, up_rows, route, w_in, w_out)


def front_kernel(
    count, cap, experts_all, spread_here, hidden, qkv_weight, mix, out_grad, router, gain_a, gain_b, ids, length,
    normed_out, heads_out, mix_out, small_out, gains_out, up, projected_out, attended_out, sums_out,
    middle_out, low_out, logits_out, sent_out, hit_out,
    staged, hid, heads_all, small_own, small_all, gains, normed, proj, attended, sums, acc, stat,
    mix_all, up_low, rows, hit, mixed, middle, normed_low, logits, sent_rows, pile,
    h_send, h_recv, q_send, q_recv, f_send, f_recv, n_send, n_recv, u_send, u_recv, m_send, m_recv,
    s_send, s_recv, x_send, x_recv, y_send, y_recv, local,
):
    me, place = lax.axis_index("seq"), lax.axis_index("fsdp")
    one, two, both = me ^ 1, me ^ 2, me ^ 3
    others = (one, two, both)
    chips = count // 2
    chip, core = place // 2, lax.rem(place, 2)
    sibling = place ^ 1
    share = mix.shape[0]
    tokens = hidden.shape[0]
    group = attended.shape[1]
    part, chunk = 2 * cap, 8 * cap
    barrier = pltpu.get_barrier_semaphore()
    for peer in others:
        pl.semaphore_signal(barrier, inc=1, device_id={"seq": peer}, device_id_type=MESH)
    for step in range(1, count):
        pl.semaphore_signal(
            barrier, inc=1, device_id={"fsdp": lax.rem(place + step, count)}, device_id_type=MESH
        )
    pl.semaphore_wait(barrier, 3 + count - 1)

    def keep(source, target, number):
        copy = pltpu.make_async_copy(source, target, local.at[number])
        copy.start()
        return copy

    def far(k):
        return (chip ^ k) * 2 + core

    away, near = {}, {}

    def block(a, owner):
        if a == 0:
            return mix_all.at[me, owner // 2, core]
        if a == 1:
            return small_all.at[pl.ds(pl.multiple_of((me * count + owner) * share, share), share)]
        return heads_all.at[:, owner]

    own_of = (mix, small_own, staged)

    def send_far(a):
        for k in range(1, chips):
            away[a, k] = remote("fsdp", far(k), own_of[a], block(a, place), f_send.at[a, k], f_recv.at[a, k])

    def send_near(a):
        near[a, 0] = remote("fsdp", sibling, own_of[a], block(a, place), n_send.at[a, 0], n_recv.at[a, 0])

    def pass_on(a):
        for k in range(1, chips):
            away[a, k].wait_recv()
            arrived = block(a, far(k))
            near[a, k] = remote("fsdp", sibling, arrived, arrived, n_send.at[a, k], n_recv.at[a, k])

    direct = {}

    def both_ways(name, views, sources, send, receive):
        for side, peer in enumerate((one, two)):
            for order in range(2):
                p = (order + side) % 2
                direct[name, side, p] = remote(
                    "seq", peer, sources[p], views[p](me), send.at[side, p], receive.at[side, p]
                )

    def relay(name, views, send, receive):
        for side, (origin, peer) in enumerate(((one, two), (two, one))):
            direct[name, side, side].wait_recv()
            source = views[side](origin)
            direct[name, 2, side] = remote("seq", peer, source, source, send.at[2, side], receive.at[2, side])

    def arrived(name):
        for side in range(2):
            direct[name, side, 1 - side].wait_recv()
            direct[name, 2, side].wait_recv()

    moved = {}

    def send_rows(k):
        for c in range(2):
            if k == 0 and c == 0:
                continue
            peer = (chip ^ k) * 2 + (core ^ c)
            moved[k, c] = remote(
                "fsdp", peer, rows.at[peer], up.at[:, pl.ds(k * chunk + me * part + core * cap, cap)],
                u_send.at[k, c], u_recv.at[k, c],
            )

    columns = [
        (pl.ds(p * group, group), lambda to, p=p: pl.ds(pl.multiple_of((p * 4 + to) * group, group), group))
        for p in range(3)
    ]
    exchanged = [
        remote(
            "seq", peer, qkv_weight.at[:, view(peer)], staged.at[me, :, into], q_send.at[i, p], q_recv.at[i, p]
        )
        for i, peer in enumerate(others)
        for p, (into, view) in enumerate(columns)
    ]
    half = tokens // 2
    hidden_views = [
        lambda origin, p=p: hid.at[pl.ds(origin * tokens + p * half, half)] for p in range(2)
    ]
    both_ways("hidden", hidden_views, [hidden.at[pl.ds(p * half, half)] for p in range(2)], h_send, h_recv)
    send_far(0)
    own_heads = [
        keep(qkv_weight.at[:, view(me)], staged.at[me, :, into], 14 + p) for p, (into, view) in enumerate(columns)
    ]
    own_hidden = keep(hidden, hid.at[pl.ds(me * tokens, tokens)], 1)
    own_mix = keep(mix, block(0, place), 2)
    own_grad = keep(out_grad, up_low, 13)
    pile[...] = jnp.zeros_like(pile)
    pile[:experts_all, :share] = router[...].astype(jnp.float32)
    for n, gain in enumerate((gain_a, gain_b)):
        pile[experts_all + n : experts_all + n + 1, :share] = gain[...].astype(jnp.float32)
    small_own[...] = jnp.transpose(pile[...])[:share].astype(small_own.dtype)
    send_far(1)
    send_near(1)
    own_small = keep(small_own, block(1, place), 3)
    across = ids[...].astype(jnp.float32)
    chosen = jnp.transpose(jnp.broadcast_to(across, (128, tokens)))[:, :1]
    first = lax.broadcasted_iota(jnp.int32, (tokens, tokens), 0)
    second = lax.broadcasted_iota(jnp.int32, (tokens, tokens), 1)
    ranks = jnp.sum(jnp.where((chosen == across) & (first < second), 1.0, 0.0), axis=0, keepdims=True)
    slot = (across * cap + ranks).astype(jnp.int32)
    hit[...] = jnp.where(lax.broadcasted_iota(jnp.int32, hit.shape, 0) == slot, 1.0, 0.0).astype(hit.dtype)
    own_grad.wait()
    position = me * tokens + lax.broadcasted_iota(jnp.int32, (tokens, 1), 0)
    up_low[...] = jnp.where(position < length[0], up_low[...].astype(jnp.float32), 0.0).astype(up_low.dtype)

    def to_slots(values, target):
        @pl.loop(0, count)
        def _(owner):
            picked = hit[pl.ds(pl.multiple_of(owner * 2 * cap, 2 * cap), 2 * cap), :]
            target[owner] = times(picked, values[...]).astype(target.dtype).reshape(target.shape[1:])

    to_slots(up_low, rows)
    own_rows = keep(rows.at[place], up.at[:, pl.ds(me * part + core * cap, cap)], 4)
    send_rows(0)
    hit_kept = keep(hit, hit_out, 0)
    pass_on(1)
    for copy in own_heads:
        copy.wait()
    for copy in exchanged:
        copy.wait_recv()
    own_block = keep(staged, heads_all.at[:, place], 5)
    send_far(2)
    send_near(2)
    own_small.wait()
    for k in range(chips):
        near[1, k].wait_recv()
    mine = small_all.at[pl.ds(pl.multiple_of(me * count * share, share), count * share)]
    smalls = [remote("seq", peer, mine, mine, q_send.at[3, i], q_recv.at[3, i]) for i, peer in enumerate(others)]

    def up_views(k):
        return [lambda origin, j=j: up.at[j, pl.ds(k * chunk + origin * part, part)] for j in range(2)]

    def up_out(k):
        if k == 0:
            own_rows.wait()
        for c in range(2):
            if (k, c) in moved:
                moved[k, c].wait_recv()
        if k < spread_here:
            views = up_views(k)
            both_ways(("up", k), views, [views[0](me), views[1](me)], s_send.at[k], s_recv.at[k])

    def up_relay(k):
        if k < spread_here:
            relay(("up", k), up_views(k), s_send.at[k], s_recv.at[k])

    up_out(0)
    relay("hidden", hidden_views, h_send, h_recv)
    own_mix.wait()
    for k in range(1, chips):
        away[0, k].wait_recv()
    mix_views = [
        lambda origin, p=p: mix_all.at[origin, pl.ds(p * (chips // 2), chips // 2), core] for p in range(2)
    ]
    both_ways("mix", mix_views, [mix_views[p](me) for p in range(2)], m_send, m_recv)
    for copy in smalls:
        copy.wait_recv()
    small_kept = keep(small_all, small_out, 6)
    own_hidden.wait()
    arrived("hidden")
    turned = jnp.transpose(small_all[...].astype(jnp.float32))
    gains[0:1, :] = turned[experts_all : experts_all + 1]
    gains[1:2, :] = turned[experts_all + 1 : experts_all + 2]
    gains_kept = keep(gains, gains_out, 17)
    gain = gains[0:1, :]

    @pl.loop(0, hid.shape[0] // 128)
    def _(t):
        place_rows = pl.ds(pl.multiple_of(t * 128, 128), 128)
        value = hid[place_rows, :].astype(jnp.float32)
        scale = lax.rsqrt(jnp.mean(value * value, axis=-1, keepdims=True) + EPS)
        normed[place_rows, :] = (value * scale * gain).astype(normed.dtype)

    normed_kept = keep(normed, normed_out, 7)
    pass_on(2)
    for k in range(1, chips):
        send_rows(k)
    up_relay(0)
    relay("mix", mix_views, m_send, m_recv)
    own_block.wait()
    for k in range(chips):
        near[2, k].wait_recv()
    heads_kept = keep(heads_all, heads_out, 8)
    width = hid.shape[1]

    for p in range(3):

        @pl.loop(0, hid.shape[0] // TILE)
        def _(t):
            place_rows = pl.ds(pl.multiple_of(t * TILE, TILE), TILE)
            weights = heads_all[:, :, :, p * group : (p + 1) * group].reshape(width, group)
            proj[place_rows, p * group : (p + 1) * group] = times(normed[place_rows, :], weights).astype(proj.dtype)

    projected_kept = keep(proj, projected_out, 9)
    head_of = lax.broadcasted_iota(jnp.int32, (tokens, group), 1) // HEAD_DIM
    sent = []
    for i in range(4):
        own = slice(i * tokens, (i + 1) * tokens)
        reach = (i + 1) * tokens

        @pl.loop(0, group // HEAD_DIM)
        def _(h):
            query = jnp.where(head_of == h, proj[own, :group] * (HEAD_DIM**-0.5), 0).astype(proj.dtype)
            scores = times_transposed(query, proj[:reach, group : 2 * group])
            column = lax.broadcasted_iota(jnp.int32, scores.shape, 1)
            row = lax.broadcasted_iota(jnp.int32, scores.shape, 0) + i * tokens
            scores = jnp.where((column <= row) & (column < length[0]), scores, MASKED)
            top = jnp.max(scores, axis=1, keepdims=True)
            powers = jnp.exp(scores - top)
            total = jnp.sum(powers, axis=1, keepdims=True)
            probs = (powers * (1.0 / total)).astype(proj.dtype)
            out = times(probs, proj[:reach, 2 * group :])
            acc[...] = jnp.where(head_of == h, out, acc[...])
            lane = lax.broadcasted_iota(jnp.int32, stat.shape, 1)
            stat[...] = jnp.where(lane == h, top + jnp.log(total), stat[...])

        attended[own, :] = acc[...].astype(attended.dtype)
        sums[:, own] = jnp.transpose(stat[...])[:8]
        target = mixed.at[:, pl.ds(pl.multiple_of(me * group, group), group)]

        @pl.when(me != i)
        def _():
            remote("seq", i, attended.at[own], target, x_send.at[i], x_recv.at[me])

        @pl.when(me == i)
        def _():
            pltpu.make_async_copy(attended.at[own], target, local.at[10]).start()

        if i == 1:
            up_relay(1)
        if i == 0:
            up_out(1)
            arrived("mix")
            both_cores = [
                remote(
                    "fsdp", sibling, mix_all.at[s, :, core], mix_all.at[s, :, core], y_send.at[s], y_recv.at[s]
                )
                for s in range(4)
            ]
    up_out(2)
    attended_kept = keep(attended, attended_out, 11)
    sums_kept = keep(sums, sums_out, 12)
    for i in range(4):
        target = mixed.at[:, pl.ds(i * group, group)]

        @pl.when(me != i)
        def _():
            copy = pltpu.make_async_remote_copy(
                attended.at[pl.ds(i * tokens, tokens)], target, x_send.at[i], x_recv.at[i],
                device_id={"seq": i}, device_id_type=MESH,
            )
            copy.wait()

        @pl.when(me == i)
        def _():
            pltpu.make_async_copy(attended.at[pl.ds(i * tokens, tokens)], target, local.at[10]).wait()

    up_relay(2)
    for copy in both_cores:
        copy.wait()
    mix_kept = keep(mix_all.at[me], mix_out, 18)
    for n in range(width // TILE):
        lanes = slice(n * TILE, (n + 1) * TILE)
        total = hid[pl.ds(pl.multiple_of(me * tokens, tokens), tokens), lanes].astype(jnp.float32)
        for s in range(4):
            weights = mix_all[s, :, :, :, lanes].reshape(group, TILE)
            total = total + times(mixed[:, s * group : (s + 1) * group], weights)
        middle[:, lanes] = total
    middle_kept = keep(middle, middle_out, 19)
    for t in range(tokens // 128):
        span = slice(t * 128, (t + 1) * 128)
        value = middle[span, :]
        scale = lax.rsqrt(jnp.mean(value * value, axis=-1, keepdims=True) + EPS)
        normed_low[span, :] = (value * scale * gains[1:2, :]).astype(normed_low.dtype)
    logits[...] = times(normed_low[...], small_all[...])
    to_slots(normed_low, sent_rows)
    last = [
        keep(normed_low, low_out, 20),
        keep(logits, logits_out, 21),
        keep(sent_rows, sent_out, 22),
    ]
    for k in range(3, chips):
        up_out(k)
        up_relay(k)
    for k in range(spread_here):
        arrived(("up", k))
    for copy in (*direct.values(), *exchanged, *smalls, *away.values(), *near.values(), *moved.values()):
        copy.wait_send()
    for copy in (
        small_kept, normed_kept, heads_kept, projected_kept, attended_kept, sums_kept,
        hit_kept, gains_kept, mix_kept, middle_kept, *last,
    ):
        copy.wait()


def front(hidden, qkv_weight, mix, out_grad, router, gain_a, gain_b, ids, lengths, count, cap, spread_here, number):
    S, dma, low, f32 = jax.ShapeDtypeStruct, pltpu.SemaphoreType.DMA, jnp.bfloat16, jnp.float32
    chips = count // 2
    tokens, width = hidden.shape
    experts_all = router.shape[0]
    group = qkv_weight.shape[1] // 12
    share = qkv_weight.shape[0]
    full = 4 * tokens
    lanes = -(-(experts_all + 2) // 128) * 128
    all_heads = (4, count, share, 3 * group)
    slots = experts_all * cap

    def vmem(*shape, dtype=low):
        return pltpu.VMEM(shape, dtype)

    near = pl.BlockSpec(memory_space=pltpu.VMEM)
    return pl.pallas_call(
        functools.partial(front_kernel, count, cap, experts_all, spread_here),
        out_shape=(
            S((full, width), low),
            S(all_heads, low),
            S((chips, 2, share, width), low),
            S((width, lanes), low),
            S((8, width), f32),
            S((2, 4 * count * cap, width), low),
            S((full, 3 * group), low),
            S((full, group), low),
            S((8, full), f32),
            S((tokens, width), f32),
            S((tokens, width), low),
            S((tokens, lanes), f32),
            S((count, 2, cap, width), low),
            S((slots, tokens), low),
        ),
        in_specs=[ANY] * 4 + [near] * 4 + [pl.BlockSpec(memory_space=pltpu.SMEM)],
        out_specs=(ANY,) * 14,
        scratch_shapes=[
            vmem(4, share, 3 * group),
            vmem(full, width),
            vmem(*all_heads),
            vmem(share, lanes),
            vmem(width, lanes),
            vmem(8, width, dtype=f32),
            vmem(full, width),
            vmem(full, 3 * group),
            vmem(full, group),
            vmem(8, full, dtype=f32),
            vmem(tokens, group, dtype=f32),
            vmem(tokens, 128, dtype=f32),
            vmem(4, chips, 2, share, width),
            vmem(tokens, width),
            vmem(count, 2, cap, width),
            vmem(slots, tokens),
            vmem(tokens, width),
            vmem(tokens, width, dtype=f32),
            vmem(tokens, width),
            vmem(tokens, lanes, dtype=f32),
            vmem(count, 2, cap, width),
            vmem(lanes, 128, dtype=f32),
            dma((3, 2)), dma((3, 2)), dma((4, 3)), dma((4, 3)),
            dma((3, chips)), dma((3, chips)), dma((3, chips)), dma((3, chips)),
            dma((chips, 2)), dma((chips, 2)), dma((3, 2)), dma((3, 2)),
            dma((chips, 3, 2)), dma((chips, 3, 2)), dma((4,)), dma((4,)), dma((4,)), dma((4,)), dma((23,)),
        ],
        compiler_params=pltpu.CompilerParams(
            collective_id=number, has_side_effects=True, vmem_limit_bytes=60 * 2**20
        ),
    )(hidden, qkv_weight, mix, out_grad, router, gain_a, gain_b, ids, lengths)


def finish_kernel(
    experts_all, experts, output, input_grad, heads, mix, small, gain, *refs
):
    wide, refs = refs[:experts], refs[experts:]
    output_out, input_out, heads_out, mix_out, route_out, gain_a, gain_b = refs[:7]
    wide_out, kinds = refs[7 : 7 + experts], refs[7 + experts]
    for source, target in zip(wide, wide_out):
        target[...] = source[...].astype(target.dtype)
    output_out[...] = output[...]
    input_out[...] = input_grad[...]
    heads_out[...] = heads[...].astype(heads_out.dtype)
    mix_out[...] = mix[...]

    @pl.when(pl.program_id(0) == 0)
    def _():
        share = route_out.shape[1]
        start = lax.rem(lax.axis_index("fsdp") * share, 128)
        total = small[0] + small[1] + small[2] + small[3]
        own = jnp.zeros((total.shape[0], share), jnp.float32)
        for place in range(0, 128, share):
            own = own + jnp.where(start == place, total[:, place : place + share], 0.0)
        kinds[...] = own
        route_out[...] = kinds[:experts_all]
        gain_a[...] = kinds[experts_all : experts_all + 1] / gain[...].astype(jnp.float32)
        gain_b[...] = kinds[experts_all + 1 : experts_all + 2]


def finish(output, input_grad, heads, mix, small, gain, experts_all, wide):
    S, f32 = jax.ShapeDtypeStruct, jnp.float32
    steps = 4
    share = heads.shape[0]

    def part(x, dim):
        shape = tuple(size // steps if d == dim else size for d, size in enumerate(x.shape))
        return pl.BlockSpec(shape, lambda n: tuple(n if d == dim else 0 for d in range(len(shape))))

    def same(*shape):
        return pl.BlockSpec(shape, lambda n: (0,) * len(shape))

    halves = [pl.BlockSpec((1, x.shape[1] * 2 // steps, x.shape[2]), lambda n: (n // (steps // 2), n % (steps // 2), 0)) for x in wide]
    return pl.pallas_call(
        functools.partial(finish_kernel, experts_all, len(wide)),
        grid=(steps,),
        out_shape=(
            S(output.shape, output.dtype),
            S(input_grad.shape, f32),
            S(heads.shape, f32),
            S(mix.shape, f32),
            S((experts_all, share), f32),
            S((1, share), f32),
            S((1, share), f32),
            *(S(x.shape, f32) for x in wide),
        ),
        in_specs=[
            part(output, 0), part(input_grad, 0), part(heads, 1), part(mix, 1), same(*small.shape), same(1, share), *halves
        ],
        out_specs=(
            part(output, 0), part(input_grad, 0), part(heads, 1), part(mix, 1),
            same(experts_all, share), same(1, share), same(1, share), *halves,
        ),
        scratch_shapes=[pltpu.VMEM((small.shape[1], share), f32)],
        compiler_params=pltpu.CompilerParams(vmem_limit_bytes=60 * 2**20),
    )(output, input_grad, heads, mix, small, gain, *wide)


def back_kernel(
    count, experts_all, ret_in, hit_in, middle_in, logits_in, low_in, out_grad, small_all, gains_in, hidden_in,
    proj_in, attended_in, sums_in, normed_in, heads_in, mix_in, ids, length,
    output_out, input_out, heads_out, mix_out, small_out,
    ret, hit, middle, logits, normed_two, up_low, route, gains, hid, output, grad_middle, grad_in, grad_logits, grad_two,
    grads, proj, attended, sums, normed, heads, mix, small, grad_heads, delta, masked_grad, masked_query,
    masked_key, masked_value, probs, slopes, grad_query, grad_key, grad_value, grad_proj, part, weights, weights_mix, gain_sum,
    sib_a, sib_b, sib_c, own_a, own_b, own_c, got_a, got_b, got_c, total_a, total_b, total_c, first, second,
    g_send, g_recv, b_send, b_recv, bb_send, bb_recv, z_send, z_recv, x_send, x_recv, w_send, w_recv, c_send, c_recv, load, keep,
):
    me, place = lax.axis_index("seq"), lax.axis_index("fsdp")
    one, two, both = me ^ 1, me ^ 2, me ^ 3
    others = (one, two, both)
    chips = count // 2
    chip, core = place // 2, lax.rem(place, 2)
    sibling = place ^ 1
    tokens, width = grad_in.shape
    gain_row = experts_all
    group = attended.shape[1]
    share = weights.shape[0] // (4 * count)
    heads_local = group // HEAD_DIM
    low = grads.dtype
    barrier = pltpu.get_barrier_semaphore()
    for peer in others:
        pl.semaphore_signal(barrier, inc=1, device_id={"seq": peer}, device_id_type=MESH)
    for k in range(1, chips):
        pl.semaphore_signal(
            barrier, inc=1, device_id={"fsdp": (chip ^ k) * 2 + core}, device_id_type=MESH
        )
    pl.semaphore_signal(barrier, inc=1, device_id={"fsdp": sibling}, device_id_type=MESH)

    def local(source, to, sem):
        copy = pltpu.make_async_copy(source, to, sem)
        copy.start()
        return copy

    heads_of = [
        local(source, to, load.at[9 + i])
        for i, (source, to) in enumerate(
            (
                (hit_in, hit),
                (ret_in, ret),
                (middle_in, middle),
                (logits_in, logits),
                (low_in, normed_two),
                (out_grad, up_low),
                (small_all, route),
                (gains_in, gains),
                (hidden_in, hid),
            )
        )
    ]
    loads = [
        local(source, to, load.at[1 + i])
        for i, (source, to) in enumerate(
            (
                (proj_in, proj),
                (attended_in, attended),
                (sums_in, sums),
                (mix_in, mix),
                (heads_in, heads),
                (normed_in, normed),
            )
        )
    ]
    for copy in heads_of:
        copy.wait()
    small[...] = jnp.zeros_like(small)
    grad_two[...] = jnp.zeros_like(grad_two)
    lane = lax.broadcasted_iota(jnp.int32, (tokens // 2, route.shape[1]), 1)
    chosen = jnp.transpose(jnp.broadcast_to(ids[...].astype(jnp.float32), (128, tokens)))[:, :1].astype(jnp.int32)
    half = tokens // 2
    direct = {}
    for t in range(2):
        span = slice(t * half, (t + 1) * half)
        position = me * tokens + t * half + lax.broadcasted_iota(jnp.int32, (half, 1), 0)
        valid = jnp.where(position < length[0], 1.0, 0.0)
        scores = jnp.where(lane < experts_all, logits[span, :], MASKED)
        powers = jnp.exp(scores - jnp.max(scores, axis=1, keepdims=True))
        share_of = powers / jnp.sum(powers, axis=1, keepdims=True)
        choose = lane == chosen[span]
        gate = jnp.sum(jnp.where(choose, share_of, 0.0), axis=1, keepdims=True)
        back_rows = transposed_times(hit[:, span], ret[0])
        value = middle[span, :]
        output[span, :] = (valid * (value + gate * back_rows)).astype(low)
        upstream = valid * up_low[span, :].astype(jnp.float32)
        grad_gate = jnp.sum(upstream * back_rows, axis=1, keepdims=True)
        slope = grad_gate * gate * (jnp.where(choose, 1.0, 0.0) - share_of)
        grad_logits[span, :] = slope.astype(low)
        incoming = times_transposed(grad_logits[span, :], route[...]) + transposed_times(hit[:, span], ret[1])
        scale = lax.rsqrt(jnp.mean(value * value, axis=-1, keepdims=True) + EPS)
        shrunk = value * scale
        grad_two[...] += jnp.sum(incoming * shrunk, axis=0, keepdims=True)
        scaled = incoming * gains[1:2, :]
        total = upstream + scale * (scaled - shrunk * jnp.mean(scaled * shrunk, axis=-1, keepdims=True))
        grad_middle[span, :] = total
        grad_in[span, :] = total.astype(low)
        if t == 0:
            pl.semaphore_wait(barrier, 3 + chips)
        for side, peer in enumerate((one, two)):
            direct[side, t] = remote(
                "seq", peer, grad_in.at[pl.ds(t * half, half)], grads.at[pl.ds(me * tokens + t * half, half)],
                g_send.at[side, t], g_recv.at[side, t],
            )
    output_kept = local(output, output_out, load.at[8])
    own_grad = local(grad_in, grads.at[pl.ds(me * tokens, tokens)], load.at[0])
    for n in range(width // 128):
        lanes = slice(n * 128, (n + 1) * 128)
        kinds = transposed_times(grad_logits[...], normed_two[:, lanes])
        small[n // 2, n % 2, :experts_all, :] = kinds[:experts_all]
        small[n // 2, n % 2, gain_row + 1 : gain_row + 2, :] = grad_two[:, lanes]
    for copy in loads:
        copy.wait()
    head_of = lax.broadcasted_iota(jnp.int32, (tokens, group), 1) // HEAD_DIM
    key_at = lax.broadcasted_iota(jnp.int32, (tokens, tokens), 0)
    for j in range(4):
        rows = slice(j * tokens, (j + 1) * tokens)
        for h in range(heads_local):
            key = proj[rows, group : 2 * group] * (HEAD_DIM**-0.5)
            masked_key[j * heads_local + h] = jnp.where(head_of == h, key, 0).astype(low)
            masked_value[j * heads_local + h] = jnp.where(head_of == h, proj[rows, 2 * group :], 0).astype(low)
    grad_key[...] = jnp.zeros_like(grad_key)
    grad_value[...] = jnp.zeros_like(grad_value)
    gain_sum[...] = jnp.zeros_like(gain_sum)

    def block(i, j, masked):
        rows = pl.ds(pl.multiple_of(i * tokens, tokens), tokens)
        keys = pl.ds(pl.multiple_of(j * tokens, tokens), tokens)
        hidden = j * tokens + key_at >= length[0]
        if masked:
            hidden = hidden | (key_at > lax.broadcasted_iota(jnp.int32, (tokens, tokens), 1))
        total = None
        for h in range(heads_local):
            lanes = slice(h * tokens, (h + 1) * tokens)
            key = masked_key[j * heads_local + h]
            scores = times_transposed(key, proj[rows, :group])
            scores = jnp.where(hidden, MASKED, scores)
            p = jnp.exp(scores - sums[h : h + 1, rows])
            probs[:, lanes] = p.astype(low)
            grad = times_transposed(masked_value[j * heads_local + h], grad_heads[...])
            slopes[:, lanes] = (p * (grad - delta[h : h + 1, :])).astype(low)
            term = transposed_times(slopes[:, lanes], key)
            total = term if total is None else total + term
        grad_query[...] += total
        grad_value[keys, :] += times(probs[...], masked_grad[...])
        grad_key[keys, :] += times(slopes[...], masked_query[...])

    def queries(i):
        rows = pl.ds(pl.multiple_of(i * tokens, tokens), tokens)
        grad_heads[...] = times_transposed(grads[rows, :], mix[...]).astype(low)
        out = grad_heads[...].astype(jnp.float32)
        turned = jnp.transpose(out * attended[rows, :].astype(jnp.float32))
        query = proj[rows, :group]
        for h in range(heads_local):
            delta[h : h + 1, :] = jnp.sum(turned[h * HEAD_DIM : (h + 1) * HEAD_DIM], axis=0, keepdims=True)
            masked_grad[h * tokens : (h + 1) * tokens, :] = jnp.where(head_of == h, out, 0).astype(low)
            masked_query[h * tokens : (h + 1) * tokens, :] = jnp.where(head_of == h, query, 0).astype(low)
        grad_query[...] = jnp.zeros_like(grad_query)

        @pl.loop(0, i)
        def _(j):
            block(i, j, False)

        block(i, i, True)
        grad_proj[rows, :group] = grad_query[...].astype(low)

    own_grad.wait()
    queries(me)
    for side, (origin, peer) in enumerate(((one, two), (two, one))):
        direct[side, side].wait_recv()
        source = grads.at[pl.ds(origin * tokens + side * half, half)]
        direct[2, side] = remote("seq", peer, source, source, g_send.at[2, side], g_recv.at[2, side])
    for side, origin in enumerate((one, two)):
        direct[side, 1 - side].wait_recv()
        queries(origin)
    for side in range(2):
        direct[2, side].wait_recv()
    for n in range(width // TILE):
        lanes = slice(n * TILE, (n + 1) * TILE)
        weights_mix[:, lanes] = transposed_times(attended[...], grads[:, lanes]).astype(low)
    order_of = [*range(1, chips), 0]
    to_sibling, away = {}, {}

    def rows_at(s, owner):
        return pl.ds(pl.multiple_of((s * count + owner) * share, share), share)

    def start_sibling(a, k, core_of):
        owner = (chip ^ k) * 2 + core_of
        if a == 1:
            return [
                remote(
                    "fsdp", sibling, weights_mix.at[pl.ds(pl.multiple_of(owner * share, share), share)], sib_b.at[k],
                    b_send.at[0, k], b_recv.at[0, k],
                )
            ]
        if a == 2:
            return [
                remote(
                    "fsdp", sibling, small.at[:, owner * share // 128], sib_c.at[k], b_send.at[1, k], b_recv.at[1, k]
                )
            ]
        raise ValueError(a)

    sib, own, got = (sib_a, sib_b, sib_c), (own_a, own_b, own_c), (got_a, got_b, got_c)
    totals = (total_a, total_b, total_c)

    def pair_sum(a, k):
        owner = (chip ^ k) * 2 + core
        for copy in to_sibling[a, k]:
            copy.wait_recv()
        if a == 1:
            mine = weights_mix[pl.ds(pl.multiple_of(owner * share, share), share), :]
            own_b[k] = (mine.astype(jnp.float32) + sib_b[k].astype(jnp.float32)).astype(low)
        else:
            for s in range(4):
                own_c[k, s] = small[s, owner * share // 128] + sib_c[k, s]
        if k:
            away[a, k] = remote(
                "fsdp", (chip ^ k) * 2 + core, own[a].at[k], got[a].at[k], z_send.at[a, k], z_recv.at[a, k]
            )

    for k in order_of:
        to_sibling[1, k] = start_sibling(1, k, core ^ 1)
    queries(both)
    for k in order_of:
        pair_sum(1, k)
    grad_proj[:, group : 2 * group] = (grad_key[...] * (HEAD_DIM**-0.5)).astype(low)
    grad_proj[:, 2 * group :] = grad_value[...].astype(low)

    def partial(j):
        own_rows = pl.ds(pl.multiple_of(j * tokens, tokens), tokens)
        for n in range(width // TILE):
            lanes = slice(n * TILE, (n + 1) * TILE)
            back = times_transposed(grad_proj[own_rows, :], heads[lanes, :])
            gain_sum[:, lanes] += jnp.sum(back * normed[own_rows, lanes].astype(jnp.float32), axis=0, keepdims=True)
            part[j, :, lanes] = back.astype(low)

    summed = {}

    def send_part(side, order):
        near = (one, two)[side]
        block_of = near if order else both
        summed[side, order] = remote(
            "seq", near, part.at[block_of, pl.ds(side * half, half)], first.at[side, order],
            c_send.at[side, order], c_recv.at[side, order],
        )

    partial(both)
    send_part(0, 0)
    send_part(1, 0)
    partial(one)
    send_part(0, 1)
    partial(two)
    send_part(1, 1)
    for s in range(4):
        lanes = slice(s * group, (s + 1) * group)
        weights[lanes, :] = transposed_times(normed[:, lanes], grad_proj[...]).astype(low)
        for k in order_of:
            owner = (chip ^ k) * 2
            to_sibling[s + 3, k] = [
                remote(
                    "fsdp", sibling, weights.at[rows_at(s, owner + (core ^ 1))], sib_a.at[k, pl.ds(s * share, share)],
                    bb_send.at[s, k], bb_recv.at[s, k],
                )
            ]
    for s in range(4):
        rows = slice(s * share, (s + 1) * share)
        for k in order_of:
            owner = (chip ^ k) * 2 + core
            to_sibling[s + 3, k][0].wait_recv()
            own_a[k, rows, :] = (
                weights[rows_at(s, owner), :].astype(jnp.float32) + sib_a[k, rows, :].astype(jnp.float32)
            ).astype(low)
            if k:
                away[s + 3, k] = remote(
                    "fsdp", owner, own_a.at[k, pl.ds(s * share, share)], got_a.at[k, pl.ds(s * share, share)],
                    z_send.at[s + 3, k], z_recv.at[s + 3, k],
                )
    partial(me)
    for b in range(width // 128):
        small[b // 2, b % 2, gain_row : gain_row + 1, :] = gain_sum[:, b * 128 : (b + 1) * 128]
    for k in order_of:
        to_sibling[2, k] = start_sibling(2, k, core ^ 1)
    for k in order_of:
        pair_sum(2, k)
    for side, rest in enumerate((two, one)):
        rows = slice(side * half, (side + 1) * half)
        summed[side, 0].wait_recv()
        first[side, 0] = (first[side, 0].astype(jnp.float32) + part[rest, rows, :].astype(jnp.float32)).astype(low)
        summed[side, 2] = remote("seq", rest, first.at[side, 0], second.at[side], c_send.at[2, side], c_recv.at[2, side])
    stored = []
    for side in range(2):
        rows = slice(side * half, (side + 1) * half)
        summed[side, 1].wait_recv()
        summed[side, 2].wait_recv()
        incoming = (
            part[me, rows, :].astype(jnp.float32)
            + first[side, 1].astype(jnp.float32)
            + second[side].astype(jnp.float32)
        )
        value = hid[rows, :].astype(jnp.float32)
        scale = lax.rsqrt(jnp.mean(value * value, axis=-1, keepdims=True) + EPS)
        shrunk = value * scale
        scaled = incoming * gains[0:1, :]
        grad_middle[rows, :] += scale * (scaled - shrunk * jnp.mean(scaled * shrunk, axis=-1, keepdims=True))
        stored.append(
            local(grad_middle.at[pl.ds(side * half, half)], input_out.at[pl.ds(side * half, half)], keep.at[side])
        )
    for a in (1, 0, 2):
        if a == 0:
            for s in range(4):
                rows = slice(s * share, (s + 1) * share)
                total = own_a[0, rows, :].astype(jnp.float32)
                for k in range(1, chips):
                    away[s + 3, k].wait_recv()
                    total = total + got_a[k, rows, :].astype(jnp.float32)
                total_a[s] = total.astype(low)
        else:
            total = own[a][0].astype(jnp.float32)
            for k in range(1, chips):
                away[a, k].wait_recv()
                total = total + got[a][k].astype(jnp.float32)
            totals[a][...] = total
    crossed = []
    for p in range(3):
        lanes = pl.ds(p * group, group)
        target = heads_out.at[:, pl.ds(pl.multiple_of((p * 4 + me) * group, group), group)]
        for i, peer in enumerate(others):
            crossed.append(
                remote("seq", peer, total_a.at[peer, :, lanes], target, w_send.at[p, i], w_recv.at[p, i])
            )
        stored.append(local(total_a.at[me, :, lanes], target, load.at[18 + p]))
    for i, peer in enumerate(others):
        crossed.append(remote("seq", peer, total_c.at[peer], small_out.at[me], x_send.at[i], x_recv.at[i]))
    stored.append(local(total_c.at[me], small_out.at[me], keep.at[3]))
    stored.append(local(total_b, mix_out, keep.at[2]))
    for copy in (*stored, *crossed, output_kept):
        copy.wait()
    for copy in (*summed.values(), *away.values(), *direct.values()):
        copy.wait_send()
    for copies in to_sibling.values():
        for copy in copies:
            copy.wait_send()


def back(
    ret, hit, middle, logits, normed_two, out_grad, route, gains, hidden,
    proj, attended, sums, normed, heads, mix, ids, lengths, count, experts_all, number,
):
    S, dma, f32, low = jax.ShapeDtypeStruct, pltpu.SemaphoreType.DMA, jnp.float32, jnp.bfloat16
    tokens, width = out_grad.shape
    group = attended.shape[1]
    chips = count // 2
    full = 4 * tokens
    share = width // (4 * count)
    local_heads = group // HEAD_DIM
    kinds = -(-(experts_all + 2) // 8) * 8

    def vmem(*shape, dtype=low):
        return pltpu.VMEM(shape, dtype)

    sets = [
        vmem(chips, 4 * share, 3 * group),
        vmem(chips, share, width),
        vmem(chips, 4, kinds, 128, dtype=f32),
    ]
    return pl.pallas_call(
        functools.partial(back_kernel, count, experts_all),
        out_shape=(
            S((tokens, width), low),
            S((tokens, width), f32),
            S((share, 12 * group), low),
            S((share, width), f32),
            S((4, kinds, 128), f32),
        ),
        in_specs=[ANY] * 15 + [pl.BlockSpec(memory_space=pltpu.VMEM), pl.BlockSpec(memory_space=pltpu.SMEM)],
        out_specs=(ANY,) * 5,
        scratch_shapes=[
            vmem(*ret.shape),
            vmem(*hit.shape),
            vmem(tokens, width, dtype=f32),
            vmem(*logits.shape, dtype=f32),
            vmem(tokens, width),
            vmem(tokens, width),
            vmem(*route.shape),
            vmem(*gains.shape, dtype=f32),
            vmem(tokens, width),
            vmem(tokens, width),
            vmem(tokens, width, dtype=f32),
            vmem(tokens, width),
            vmem(*logits.shape),
            vmem(1, width, dtype=f32),
            vmem(full, width),
            vmem(*proj.shape),
            vmem(*attended.shape),
            vmem(*sums.shape, dtype=f32),
            vmem(*normed.shape),
            vmem(*heads.shape),
            vmem(group, width),
            vmem(4, group // 128, kinds, 128, dtype=f32),
            vmem(tokens, group),
            vmem(8, tokens, dtype=f32),
            vmem(local_heads * tokens, group),
            vmem(local_heads * tokens, group),
            vmem(4 * local_heads, tokens, group),
            vmem(4 * local_heads, tokens, group),
            vmem(tokens, local_heads * tokens),
            vmem(tokens, local_heads * tokens),
            vmem(tokens, group, dtype=f32),
            vmem(full, group, dtype=f32),
            vmem(full, group, dtype=f32),
            vmem(full, 3 * group),
            vmem(4, tokens, width),
            vmem(width, 3 * group),
            vmem(group, width),
            vmem(1, width, dtype=f32),
            *sets,
            *sets,
            *sets,
            vmem(4, share, 3 * group),
            vmem(share, width, dtype=f32),
            vmem(4, kinds, 128, dtype=f32),
            vmem(2, 2, tokens // 2, width),
            vmem(2, tokens // 2, width),
            dma((3, 2)), dma((3, 2)),
            dma((2, chips)), dma((2, chips)), dma((4, chips)), dma((4, chips)),
            dma((7, chips)), dma((7, chips)),
            dma((3,)), dma((3,)), dma((3, 3)), dma((3, 3)), dma((3, 2)), dma((3, 2)), dma((21,)), dma((5,)),
        ],
        compiler_params=pltpu.CompilerParams(
            collective_id=number, has_side_effects=True, vmem_limit_bytes=60 * 2**20
        ),
    )(
        ret, hit, middle, logits, normed_two, out_grad, route, gains, hidden,
        proj, attended, sums, normed, heads, mix, ids, lengths,
    )


def shards(
    hidden,
    lengths,
    expert_ids,
    attn_gain,
    qkv_weight,
    out_weight,
    moe_gain,
    router_weight,
    expert_in,
    expert_out,
    out_grad,
):
    S = jax.ShapeDtypeStruct
    low = jnp.bfloat16
    owners = lax.axis_size("fsdp")
    seq_count = lax.axis_size("seq")
    tokens, width = hidden.shape[1], hidden.shape[2]
    full_len = tokens * seq_count
    group_width = width // seq_count
    experts_all = router_weight.shape[1]
    expert_local = expert_in.shape[0]
    capacity = -(-max(2, 2 * tokens // experts_all) // 16) * 16
    slots = experts_all * capacity

    chosen = expert_ids[0, :, 0]

    def to_owners(rows, number):
        return exchange(
            "fsdp",
            owners,
            (rows.reshape(owners, expert_local, capacity, width),),
            (S((expert_local, owners, capacity, width), low),),
            ((lead, second),),
            number,
        )[0].reshape(expert_local, owners * capacity, width)

    def to_sources(rows, number):
        return exchange(
            "fsdp",
            owners,
            (rows.reshape(expert_local, owners, capacity, width),),
            (S((owners, expert_local, capacity, width), low),),
            ((second, lead),),
            number,
        )[0].reshape(slots, width)

    chips = owners // 2
    fused = 4 * owners * capacity <= 1024
    (
        normed,
        weight_qkv,
        mix_rows,
        small,
        gains,
        up_all,
        projected,
        attended,
        totals,
        middle,
        normed_two,
        logits,
        sent,
        dispatch,
    ) = front(
        hidden[0],
        qkv_weight,
        out_weight,
        out_grad[0],
        router_weight.T,
        attn_gain[None],
        moe_gain[None],
        expert_ids[0].T,
        lengths,
        owners,
        capacity,
        SPREAD_FIRST if fused else chips,
        0,
    )
    weight_qkv = weight_qkv.reshape(width, 3 * group_width)
    mix_rows = mix_rows.reshape(group_width, width)
    if not fused:
        up_all = up_all.reshape(expert_local, chips, seq_count, 2 * capacity, width)
        chip, bit = lax.axis_index("fsdp") // 2, 1
        while bit < chips:
            pairs = up_all.reshape(expert_local, chips // (2 * bit), 2, bit, seq_count, 2 * capacity, width)
            up_all = jnp.where((chip // bit) % 2 == 1, pairs[:, :, ::-1], pairs)
            bit *= 2
        up_all = up_all.reshape(expert_local, chips, seq_count, 2 * capacity, width)
        up_all = up_all.transpose(0, 2, 1, 3, 4)
    if fused:
        returned, *expert_grads = moe(
            sent,
            up_all,
            small,
            expert_in,
            expert_out,
            experts_all,
            5,
        )
        returned = returned.reshape(2, slots, width)
    else:
        choose = chosen[:, None] == jnp.arange(experts_all, dtype=jnp.int32)[None, :]
        weights = jax.nn.softmax(logits[:, :experts_all], axis=-1)
        gate = jnp.sum(jnp.where(choose, weights, 0.0), axis=-1)
        gate_rows = jnp.sum(jnp.where(dispatch > 0, gate[None, :], 0.0), axis=1)
        gates = lax.all_to_all(
            gate_rows.reshape(owners, expert_local, capacity), "fsdp", split_axis=0, concat_axis=0, tiled=True
        )
        gates = lax.all_gather(gates, "seq", axis=0)
        gates = gates.transpose(2, 0, 1, 3).reshape(expert_local, seq_count * owners * capacity, 1)

        rows_all = spread(to_owners(sent, 5), 6)
        count = seq_count * owners * capacity
        rows_all = rows_all.reshape(expert_local, count, width)
        up_all = up_all.reshape(expert_local, count, width)
        grad_rows = (up_all.astype(jnp.float32) * gates).astype(low)

        def per_expert(form, left, right):
            return jnp.einsum(form, left, right, preferred_element_type=jnp.float32)

        inner = per_expert("jrd,jdf->jrf", rows_all, expert_in)
        active, active_back = jax.vjp(gelu_tanh, inner)
        active = active.astype(low)
        partial_out = per_expert("jrf,jfd->jrd", active, expert_out).astype(low)
        grad_active = per_expert("jrd,jfd->jrf", grad_rows, expert_out)
        grad_inner = active_back(grad_active)[0].astype(low)
        partial_back = per_expert("jrf,jdf->jrd", grad_inner, expert_in).astype(low)
        expert_out_grad = per_expert("jrf,jrd->jfd", active, grad_rows)
        expert_in_grad = per_expert("jrd,jrf->jdf", rows_all, grad_inner)

        shape = (expert_local, seq_count, owners * capacity, width)
        returned = to_sources(collect(partial_out.reshape(shape), 7), 8)
        grad_back = to_sources(collect(partial_back.reshape(shape), 9), 10)
        returned, expert_grads = jnp.stack([returned, grad_back]), ()
    output, grad_inputs, qkv_sum, mix_grad, small_sum = back(
        returned,
        dispatch,
        middle,
        logits,
        normed_two,
        out_grad[0],
        small,
        gains,
        hidden[0],
        projected,
        attended,
        totals,
        normed,
        weight_qkv,
        mix_rows,
        expert_ids[0].T,
        lengths,
        owners,
        experts_all,
        12,
    )
    output, grad_inputs, qkv_grad, mix_grad, route_grad, gain_one_grad, gain_two_grad, *wide = finish(
        output, grad_inputs, qkv_sum, mix_grad, small_sum, attn_gain[None], experts_all, expert_grads
    )
    if fused:
        expert_in_grad, expert_out_grad = wide
    return (
        output[None],
        grad_inputs[None],
        gain_one_grad[0],
        qkv_grad,
        mix_grad,
        gain_two_grad[0],
        route_grad.T,
        expert_in_grad,
        expert_out_grad,
    )


def solution(mesh):
    placed = (
        P("fsdp", "seq", None),
        P("fsdp"),
        P("fsdp", "seq", None),
        P(("seq", "fsdp")),
        P(("seq", "fsdp"), None),
        P(("seq", "fsdp"), None),
        P(("seq", "fsdp")),
        P(("seq", "fsdp"), None),
        P("fsdp", None, "seq"),
        P("fsdp", "seq", None),
        P("fsdp", "seq", None),
    )
    return jax.shard_map(
        shards,
        mesh=mesh,
        in_specs=placed,
        out_specs=(
            P("fsdp", "seq", None),
            P("fsdp", "seq", None),
            P(("seq", "fsdp")),
            P(("seq", "fsdp"), None),
            P(("seq", "fsdp"), None),
            P(("seq", "fsdp")),
            P(("seq", "fsdp"), None),
            P("fsdp", None, "seq"),
            P("fsdp", "seq", None),
        ),
        check_vma=False,
    )
```
